32 devices in a mesh: dp: 8 (over z, y), vocab: 4 (over x, core).
Axes of the slice: x: 2, y: 2, z: 4, core: 2. Of those that a mesh axis runs over, the one named last changes fastest.
Arguments:
- enc_ids: int32 [8, 512], P('dp'), may hold values from 0 to 96102
- labels: int32 [8, 256], P('dp'), may hold values from 0 to 96102
- target_lengths: int32 [8], P('dp'), may hold values from 1 to 256, as said below
- loss_positions: int32 [8, 64], P('dp'), may hold values from 0 to 255, as said below
- embedding: float32 [96104, 768], P('vocab', 'dp'), as said below
- attn_in: float32 [3, 768, 2304], P(None, 'dp'), may hold values from -0.21875 to 0.21875
- attn_out: float32 [3, 768, 768], P(None, 'dp'), may hold values from -1.75 to 1.75
- ffn_up: float32 [2, 768, 3072], P(None, 'dp'), may hold values from -0.21875 to 0.21875
- ffn_down: float32 [2, 3072, 768], P(None, 'dp'), may hold values from -0.109375 to 0.109375
- norms: float32 [14, 768], P(None, 'dp'), as said below
- embedding_first: float32 [96104, 768], P('vocab', 'dp'), may hold values from -1.4305115e-06 to 1.4305115e-06
- attn_in_first: float32 [3, 768, 2304], P(None, 'dp'), may hold values from -1.4305115e-06 to 1.4305115e-06
- attn_out_first: float32 [3, 768, 768], P(None, 'dp'), may hold values from -1.4305115e-06 to 1.4305115e-06
- ffn_up_first: float32 [2, 768, 3072], P(None, 'dp'), may hold values from -1.4305115e-06 to 1.4305115e-06
- ffn_down_first: float32 [2, 3072, 768], P(None, 'dp'), may hold values from -1.4305115e-06 to 1.4305115e-06
- norms_first: float32 [14, 768], P(None, 'dp'), may hold values from -5.722046e-06 to 5.722046e-06
- embedding_second: float32 [96104, 768], P('vocab', 'dp'), may hold values from 2.2140133e-15 to 3.5424212e-14
- attn_in_second: float32 [3, 768, 2304], P(None, 'dp'), may hold values from 2.2140133e-15 to 3.5424212e-14
- attn_out_second: float32 [3, 768, 768], P(None, 'dp'), may hold values from 2.2140133e-15 to 3.5424212e-14
- ffn_up_second: float32 [2, 768, 3072], P(None, 'dp'), may hold values from 2.2140133e-15 to 3.5424212e-14
- ffn_down_second: float32 [2, 3072, 768], P(None, 'dp'), may hold values from 2.2140133e-15 to 3.5424212e-14
- norms_second: float32 [14, 768], P(None, 'dp'), may hold values from 3.5424212e-14 to 5.667874e-13
Outputs:
- loss_sum: float32 [], replicated
- token_count: float32 [], replicated
- grad_norm: float32 [], replicated
- new_embedding: float32 [96104, 768], P('vocab', 'dp')
- new_attn_in: float32 [3, 768, 2304], P(None, 'dp')
- new_attn_out: float32 [3, 768, 768], P(None, 'dp')
- new_ffn_up: float32 [2, 768, 3072], P(None, 'dp')
- new_ffn_down: float32 [2, 3072, 768], P(None, 'dp')
- new_norms: float32 [14, 768], P(None, 'dp')
- embedding_first_out: float32 [96104, 768], P('vocab', 'dp')
- attn_in_first_out: float32 [3, 768, 2304], P(None, 'dp')
- attn_out_first_out: float32 [3, 768, 768], P(None, 'dp')
- ffn_up_first_out: float32 [2, 768, 3072], P(None, 'dp')
- ffn_down_first_out: float32 [2, 3072, 768], P(None, 'dp')
- norms_first_out: float32 [14, 768], P(None, 'dp')
- embedding_second_out: float32 [96104, 768], P('vocab', 'dp')
- attn_in_second_out: float32 [3, 768, 2304], P(None, 'dp')
- attn_out_second_out: float32 [3, 768, 768], P(None, 'dp')
- ffn_up_second_out: float32 [2, 768, 3072], P(None, 'dp')
- ffn_down_second_out: float32 [2, 3072, 768], P(None, 'dp')
- norms_second_out: float32 [14, 768], P(None, 'dp')
The draws below stay inside these ranges and needn't reach their ends.
Inputs may be any that keep to these rules, and one draw needn't show every extreme that they name: `target_lengths`: the last example's length is 256. `loss_positions`: each row holds 64 different positions. `embedding`: entries are of order 768^(-1/2) up to a factor of a few. `norms`: gains are positive and of order one; biases are of order a few tenths.
All inputs are finite; a program needn't handle non-finite values.
Results may differ from the reference program's by a relative error of at most 0.02.
Values may be sent and summed in bfloat16 or wider, within the bound.
A program may use at most 576 MiB of HBM per device.

```python
import math
from functools import partial
import jax
import jax.numpy as jnp
import numpy as np
from jax import lax

D = 768
HEADS = 12
HEAD_DIM = 64
FF = 3072
V = 96104
S_ENC = 512
S_DEC = 256
LOSS_POS = 64
STEP = 10
EXAMPLES = 8
PARAMS = 90333696


def draw_embedding(key, part):
    key = jax.random.fold_in(key, 11)
    row_place = jnp.arange(V, dtype=jnp.float32)[:, None] / (V - 1)
    base_draw = jax.random.normal(key, (V, D), jnp.float32)
    row_scale = 1.0 + 2.0 * row_place
    common = (24.0 * row_place - 12.0) / D
    return base_draw * row_scale * D ** (-0.5) + common


def draw_norms(key, part):
    key = jax.random.fold_in(key, 12)
    gain_key, shift_key = jax.random.split(key)
    column = jnp.arange(D, dtype=jnp.float32)[None, :] / (D - 1)
    gain_rows = (0.5 + column) * jax.random.uniform(gain_key, (7, D), jnp.float32, 0.8, 1.2)
    shifts = 0.3 + 0.3 * jax.random.normal(shift_key, (7, D), jnp.float32)
    return jnp.concatenate([gain_rows, shifts], axis=0)


def draw_target_lengths(key, part):
    key = jax.random.fold_in(key, 13)
    example_place = jnp.arange(EXAMPLES)
    base_len = S_DEC * (EXAMPLES - 1 + 2 * example_place) // (3 * (EXAMPLES - 1))
    least_len = jnp.maximum(1, base_len * 4 // 5)
    upper_len = jnp.minimum(S_DEC, base_len * 6 // 5) + 1
    drawn = jax.random.randint(key, (EXAMPLES,), least_len, upper_len)
    return jnp.where(example_place == EXAMPLES - 1, S_DEC, drawn).astype(jnp.int32)


def draw_loss_positions(key, part):
    key = jax.random.fold_in(key, 14)
    example_keys = jax.random.split(key, EXAMPLES)
    picked = jax.vmap(lambda single: jax.random.permutation(single, S_DEC)[:LOSS_POS])(example_keys)
    return picked.astype(jnp.int32)


def plant(values, rng, low, largest):
    extent = values.shape
    place = [jax.random.randint(jax.random.fold_in(rng, axis), (), 0, extent[axis]) for axis in range(len(extent))]
    values = values.at[tuple(place)].set(low)
    longest = extent.index(max(extent))
    place[longest] = (place[longest] + 1) % extent[longest]
    return values.at[tuple(place)].set(largest)


def steps_of(stream_key, shape, shards, least, top_value):
    def one(position, parts):
        steps = jax.random.uniform(jax.random.fold_in(jax.random.fold_in(stream_key, 6), position), (parts,), jnp.float32, least / len(shards), top_value / len(shards))
        return jnp.repeat(jnp.exp(steps), shape[position] // parts).reshape((-1,) + (1,) * (len(shape) - position - 1))

    factor_of = one(*shards[0])
    for cut in shards[1:]:
        factor_of = factor_of * one(*cut)
    return factor_of


def ranked_wide(own_key, shape, count, skew):
    weights = [min(1 << octave, count + 1 - (1 << octave)) * (1 << 20) // math.isqrt((1 << octave) ** skew) + 1 for octave in range((count + 1).bit_length()) if 1 << octave <= count]
    spread = 1 + sum(weights) // (1 << 30)
    grid = np.cumsum(np.array([max(1, weight // spread) for weight in weights]))
    pick = jax.random.randint(jax.random.fold_in(own_key, 1), shape, 0, int(grid[len(weights) - 1]))
    start = jnp.left_shift(1, jnp.searchsorted(jnp.asarray(grid, jnp.int32), pick, side="right").astype(jnp.int32))
    rank = start - 1 + jax.random.randint(jax.random.fold_in(own_key, 4), shape, 0, 1 << 30) % jnp.minimum(start, count + 1 - start)
    return jax.random.permutation(jax.random.fold_in(own_key, 2), count)[rank].astype(jnp.int32)


def bell_draw(own_key, extent, spread, most, shards=(), kind=jnp.bfloat16):
    array = jax.random.normal(own_key, extent, jnp.float32) * spread
    if len(shards) > 0:
        array = steps_of(own_key, extent, shards, -0.22, 0.18) * array
    return jnp.clip(array, min=-most, max=most).astype(kind)


def setup_inputs(seed: int = 0) -> dict:
    arg_keys = jax.random.split(jax.random.key(seed), 23)
    return {
        "enc_ids": plant(ranked_wide(arg_keys[0], (EXAMPLES, S_ENC), V - 1, 2), jax.random.fold_in(arg_keys[0], 3), 0, (V - 1) - 1).astype(jnp.int32),
        "labels": plant(ranked_wide(arg_keys[1], (EXAMPLES, S_DEC), V - 1, 2), jax.random.fold_in(arg_keys[1], 3), 0, (V - 1) - 1).astype(jnp.int32),
        "target_lengths": draw_target_lengths(jax.random.fold_in(arg_keys[22], 71), 0),
        "loss_positions": draw_loss_positions(jax.random.fold_in(arg_keys[22], 71), 0),
        "embedding": draw_embedding(jax.random.fold_in(arg_keys[22], 71), 0),
        "attn_in": bell_draw(arg_keys[5], (3, D, 3 * D), D ** -0.5, 0.21875, ((1, 8),), jnp.float32),
        "attn_out": bell_draw(arg_keys[6], (3, D, D), (D // 64) ** -0.5, 1.75, ((1, 8),), jnp.float32),
        "ffn_up": bell_draw(arg_keys[7], (2, D, FF), D ** -0.5, 0.21875, ((1, 8),), jnp.float32),
        "ffn_down": bell_draw(arg_keys[8], (2, FF, D), FF ** -0.5, 0.109375, ((1, 8),), jnp.float32),
        "norms": draw_norms(jax.random.fold_in(arg_keys[22], 71), 0),
        "embedding_first": bell_draw(arg_keys[10], (V, D), (0.0022 / PARAMS ** 0.5), 1.430511474609375e-06, ((0, 4), (1, 8)), jnp.float32),
        "attn_in_first": bell_draw(arg_keys[11], (3, D, 3 * D), (0.0022 / PARAMS ** 0.5), 1.430511474609375e-06, ((1, 8),), jnp.float32),
        "attn_out_first": bell_draw(arg_keys[12], (3, D, D), (0.0022 / PARAMS ** 0.5), 1.430511474609375e-06, ((1, 8),), jnp.float32),
        "ffn_up_first": bell_draw(arg_keys[13], (2, D, FF), (0.0022 / PARAMS ** 0.5), 1.430511474609375e-06, ((1, 8),), jnp.float32),
        "ffn_down_first": bell_draw(arg_keys[14], (2, FF, D), (0.0022 / PARAMS ** 0.5), 1.430511474609375e-06, ((1, 8),), jnp.float32),
        "norms_first": bell_draw(arg_keys[15], (14, D), (0.0088 / PARAMS ** 0.5), 5.7220458984375e-06, ((1, 8),), jnp.float32),
        "embedding_second": jnp.clip(jnp.exp(math.log(3.5424212120518245e-14) - 2.7725887 * jax.random.uniform(arg_keys[16], (V, D), jnp.float32) ** steps_of(arg_keys[16], (V, D), ((0, 4), (1, 8)), -0.2, 0.2)), 2.2140132575323903e-15, 3.5424212120518245e-14),
        "attn_in_second": jnp.clip(jnp.exp(math.log(3.5424212120518245e-14) - 2.7725887 * jax.random.uniform(arg_keys[17], (3, D, 3 * D), jnp.float32) ** steps_of(arg_keys[17], (3, D, 3 * D), ((1, 8),), -0.2, 0.2)), 2.2140132575323903e-15, 3.5424212120518245e-14),
        "attn_out_second": jnp.clip(jnp.exp(math.log(3.5424212120518245e-14) - 2.7725887 * jax.random.uniform(arg_keys[18], (3, D, D), jnp.float32) ** steps_of(arg_keys[18], (3, D, D), ((1, 8),), -0.2, 0.2)), 2.2140132575323903e-15, 3.5424212120518245e-14),
        "ffn_up_second": jnp.clip(jnp.exp(math.log(3.5424212120518245e-14) - 2.7725887 * jax.random.uniform(arg_keys[19], (2, D, FF), jnp.float32) ** steps_of(arg_keys[19], (2, D, FF), ((1, 8),), -0.2, 0.2)), 2.2140132575323903e-15, 3.5424212120518245e-14),
        "ffn_down_second": jnp.clip(jnp.exp(math.log(3.5424212120518245e-14) - 2.7725887 * jax.random.uniform(arg_keys[20], (2, FF, D), jnp.float32) ** steps_of(arg_keys[20], (2, FF, D), ((1, 8),), -0.2, 0.2)), 2.2140132575323903e-15, 3.5424212120518245e-14),
        "norms_second": jnp.clip(jnp.exp(math.log(5.667873939282919e-13) - 2.7725887 * jax.random.uniform(arg_keys[21], (14, D), jnp.float32) ** steps_of(arg_keys[21], (14, D), ((1, 8),), -0.2, 0.2)), 3.5424212120518245e-14, 5.667873939282919e-13),
    }


EPS_NORM = 1e-05
SMOOTH = 0.1
CLIP = 0.02
RATES = (0.05, 0.05, 0.4, 0.05, 0.05, 0.8)
BETA_ONE = 0.9
BETA_TWO = 0.999
ADAM_EPS = 1e-08
DECAY = 0.01
HIGHEST = lax.Precision.HIGHEST

@jax.custom_vjp
def low(v):
    return lax.optimization_barrier(v.astype(jnp.bfloat16)).astype(jnp.float32)

@jax.custom_vjp
def low_back(v):
    return v

def low_keep(v):
    return (low(v), None)

def low_pass(kept, grad):
    return (grad,)

def back_keep(v):
    return (v, None)

def back_low(kept, grad):
    return (low(grad),)
low.defvjp(low_keep, low_pass)
low_back.defvjp(back_keep, back_low)

def matmul(left_side, right_side):
    return jnp.matmul(left_side, right_side, precision=HIGHEST)

def positions_table(length, model_width):
    position_col = jnp.arange(length, dtype=jnp.float32)[:, None]
    freq_index = jnp.arange(model_width // 2, dtype=jnp.float32)[None, :]
    angles = position_col * jnp.exp(freq_index * (-2.0 * math.log(10000.0) / model_width))
    return jnp.concatenate([jnp.sin(angles), jnp.cos(angles)], axis=1)

def norm_apply(tensor, gain_row, shift_row):
    center = tensor - lax.optimization_barrier(jnp.mean(tensor, axis=-1, keepdims=True))
    return center * lax.rsqrt(lax.optimization_barrier(jnp.mean(center * center, axis=-1, keepdims=True)) + EPS_NORM) * gain_row + shift_row

def attend(queries, key_rows, value_rows, causal):
    batch_size, query_len, model_width = queries.shape

    def single_example(block_args):
        query_block, key_block, value_block = block_args
        scores = low_back(jnp.einsum('qhe,khe->hqk', query_block, key_block, precision=HIGHEST) * HEAD_DIM ** (-0.5))
        if causal:
            allowed = jnp.arange(query_block.shape[0])[:, None] >= jnp.arange(key_block.shape[0])[None, :]
            scores = jnp.where(allowed[None], scores, -1e+30)
        softmax_out = low(jax.nn.softmax(scores, axis=-1))
        return jnp.einsum('hqk,khe->qhe', softmax_out, value_block, precision=HIGHEST)

    def to_heads(tensor):
        return tensor.reshape(batch_size, tensor.shape[1], HEADS, HEAD_DIM)
    context = lax.map(jax.checkpoint(single_example), (to_heads(queries), to_heads(key_rows), to_heads(value_rows)))
    return low(low_back(context.reshape(batch_size, query_len, model_width)))

def layer(stream, memory, blocks, feed_parts, gain_rows, shifts):
    for block_order, (w_in, w_out, norm_row) in enumerate(blocks):
        normed = low(norm_apply(stream, gain_rows[norm_row], shifts[norm_row]))
        model_width = w_out.shape[0]
        if block_order == 0:
            projected = low(low_back(matmul(normed, w_in)))
            queries = projected[..., :model_width]
            key_rows = projected[..., model_width:2 * model_width]
            value_rows = projected[..., 2 * model_width:]
        else:
            queries = low(low_back(matmul(normed, w_in[:, :model_width])))
            paired = low(low_back(matmul(memory, w_in[:, model_width:])))
            key_rows, value_rows = (paired[..., :model_width], paired[..., model_width:])
        context = attend(queries, key_rows, value_rows, memory is not None and block_order == 0)
        stream = stream + low_back(matmul(context, w_out))
    w_up, w_down, norm_row = feed_parts
    normed = low(norm_apply(stream, gain_rows[norm_row], shifts[norm_row]))
    hidden_pre = low_back(matmul(normed, w_up))
    activated = low(jax.nn.silu(hidden_pre))
    return stream + low_back(matmul(activated, w_down))

def head_block(block_args, emb_table):
    rows, targets, weight = block_args
    logits = low_back(matmul(low(rows), emb_table.T))
    padding = jnp.arange(V) == V - 1
    masked = jnp.where(padding[None, :], -1e+30, logits)
    log_total = jax.nn.logsumexp(masked, axis=-1)
    target_logit = jnp.take_along_axis(logits, targets[:, None], axis=1)[:, 0]
    smooth_sum = lax.optimization_barrier(jnp.sum(jnp.where(padding[None, :], 0.0, logits), axis=-1))
    per_row = log_total - (1.0 - SMOOTH) * target_logit - SMOOTH * smooth_sum / (V - 1)
    return jnp.sum(weight * per_row)

def adam_update(weight, first_moment, second_moment, gradient, factor, rate):
    clipped = gradient * factor
    new_first = BETA_ONE * first_moment + (1.0 - BETA_ONE) * clipped
    new_second = BETA_TWO * second_moment + (1.0 - BETA_TWO) * clipped * clipped
    corrected = new_first / (1.0 - BETA_ONE ** STEP) / (jnp.sqrt(new_second / (1.0 - BETA_TWO ** STEP)) + ADAM_EPS)
    return (weight - rate * (corrected + DECAY * weight), new_first, new_second)

def reference(enc_ids, labels, target_lengths, loss_positions, embedding, attn_in, attn_out, ffn_up, ffn_down, norms, embedding_first, attn_in_first, attn_out_first, ffn_up_first, ffn_down_first, norms_first, embedding_second, attn_in_second, attn_out_second, ffn_up_second, ffn_down_second, norms_second):
    dec_ids = jnp.concatenate([jnp.zeros((labels.shape[0], 1), jnp.int32), labels[:, :-1]], axis=1)
    counted = (loss_positions < target_lengths[:, None]).astype(jnp.float32)
    token_count = jnp.sum(counted)
    targets = jnp.take_along_axis(labels, loss_positions, axis=1)

    def objective(params):
        emb_table, w_in_all, w_out_all, w_up_all, w_down_all, norm_values = [low(member) for member in params]
        gain_rows, shifts = (norm_values[:7], norm_values[7:])
        enc_stream = emb_table[enc_ids] * math.sqrt(D) + positions_table(S_ENC, D)
        dec_stream = emb_table[dec_ids] * math.sqrt(D) + positions_table(S_DEC, D)
        enc_out = layer(enc_stream, None, [(w_in_all[0], w_out_all[0], 0)], (w_up_all[0], w_down_all[0], 1), gain_rows, shifts)
        memory = low(norm_apply(enc_out, gain_rows[2], shifts[2]))
        dec_out = layer(dec_stream, memory, [(w_in_all[1], w_out_all[1], 3), (w_in_all[2], w_out_all[2], 4)], (w_up_all[1], w_down_all[1], 5), gain_rows, shifts)
        final = norm_apply(dec_out, gain_rows[6], shifts[6])
        selected = jnp.take_along_axis(final, loss_positions[:, :, None], axis=1)
        per_example = lax.map(jax.checkpoint(partial(head_block, emb_table=emb_table)), (selected, targets, counted))
        loss_total = jnp.sum(per_example)
        return (loss_total / token_count, loss_total)
    params = (embedding, attn_in, attn_out, ffn_up, ffn_down, norms)
    _, pullback, loss_sum = jax.vjp(objective, params, has_aux=True)
    gradients, = pullback(jnp.ones((), jnp.float32))
    squares = sum((jnp.sum(member * member) for member in gradients))
    grad_norm = jnp.sqrt(squares)
    factor = jnp.minimum(1.0, CLIP / (grad_norm + 1e-06))
    firsts = (embedding_first, attn_in_first, attn_out_first, ffn_up_first, ffn_down_first, norms_first)
    seconds = (embedding_second, attn_in_second, attn_out_second, ffn_up_second, ffn_down_second, norms_second)
    updated = [adam_update(params[slot], firsts[slot], seconds[slot], gradients[slot], factor, RATES[slot]) for slot in range(6)]
    return (loss_sum, token_count, grad_norm, updated[0][0], updated[1][0], updated[2][0], updated[3][0], updated[4][0], updated[5][0], updated[0][1], updated[1][1], updated[2][1], updated[3][1], updated[4][1], updated[5][1], updated[0][2], updated[1][2], updated[2][2], updated[3][2], updated[4][2], updated[5][2])
```

```python
from functools import partial
import math

import jax
import jax.numpy as jnp
import numpy as np
from jax import lax
from jax.experimental import pallas as pl
from jax.experimental.pallas import tpu as pltpu
from jax.sharding import PartitionSpec as P

HEADS = 12
HEAD_DIM = 64
STEP = 10


EPS_NORM = 1e-05
SMOOTH = 0.1
CLIP = 0.02
RATES = (0.05, 0.05, 0.4, 0.05, 0.05, 0.8)
BETA_ONE = 0.9
BETA_TWO = 0.999
ADAM_EPS = 1e-08
DECAY = 0.01


def lowered(tensor):
    return tensor.astype(jnp.bfloat16)


def matmul(left_side, right_side):
    return jnp.dot(left_side, right_side, preferred_element_type=jnp.float32)


def times_transposed(left_side, right_side):
    return lax.dot_general(
        left_side, right_side, (((1,), (1,)), ((), ())), preferred_element_type=jnp.float32
    )


def contract_rows(left_side, right_side):
    return lax.dot_general(
        left_side, right_side, (((0,), (0,)), ((), ())), preferred_element_type=jnp.float32
    )


def positions_table(length, model_width):
    position_col = jnp.arange(length, dtype=jnp.float32)[:, None]
    freq_index = jnp.arange(model_width // 2, dtype=jnp.float32)[None, :]
    angles = position_col * jnp.exp(freq_index * (-2.0 * math.log(10000.0) / model_width))
    return jnp.concatenate([jnp.sin(angles), jnp.cos(angles)], axis=1)


def norm_forward(tensor, gain_row, shift_row):
    center = tensor - jnp.mean(tensor, axis=-1, keepdims=True)
    scale_inv = lax.rsqrt(jnp.mean(center * center, axis=-1, keepdims=True) + EPS_NORM)
    normed = center * scale_inv
    return (normed * gain_row + shift_row, (normed, scale_inv))


def norm_backward_rows(grad_out, saved_parts, gain_row):
    normed, scale_inv = saved_parts
    grad_normed = grad_out * gain_row
    grad_in = scale_inv * (
        grad_normed
        - jnp.mean(grad_normed, axis=-1, keepdims=True)
        - normed * jnp.mean(grad_normed * normed, axis=-1, keepdims=True)
    )
    return (grad_in, jnp.sum(grad_out * normed, axis=0), jnp.sum(grad_out, axis=0))


def split_heads(rows, batch_size):
    return rows.reshape(batch_size, -1, HEADS, rows.shape[1] // HEADS)


def score_block(queries, key_rows, causal):
    scores = jnp.einsum(
        "qhe,khe->hqk", queries, key_rows, preferred_element_type=jnp.float32
    ) * HEAD_DIM ** (-0.5)
    if causal:
        allowed = jnp.arange(queries.shape[0])[:, None] >= jnp.arange(key_rows.shape[0])[None, :]
        scores = jnp.where(allowed[None], scores, -1e30)
    return scores


def attend_one(block_args, causal):
    queries, key_rows, value_rows = block_args
    scores = score_block(queries, key_rows, causal)
    row_top = jnp.max(scores, axis=-1, keepdims=True)
    exponent = jnp.exp(scores - row_top)
    row_total = jnp.sum(exponent, axis=-1, keepdims=True)
    softmax_out = lowered(exponent / row_total)
    context = jnp.einsum(
        "hqk,khe->qhe", softmax_out, value_rows, preferred_element_type=jnp.float32
    )
    return (lowered(context), (row_top + jnp.log(row_total))[..., 0])


def attend_back(block_args, causal):
    queries, key_rows, value_rows, log_total, grad_context = block_args
    scores = score_block(queries, key_rows, causal)
    softmax_out = jnp.exp(scores - log_total[..., None])
    grad_values = jnp.einsum(
        "hqk,qhe->khe", lowered(softmax_out), grad_context, preferred_element_type=jnp.float32
    )
    grad_softmax = jnp.einsum(
        "qhe,khe->hqk", grad_context, value_rows, preferred_element_type=jnp.float32
    )
    grad_scores = lowered(
        softmax_out * (grad_softmax - jnp.sum(grad_softmax * softmax_out, axis=-1, keepdims=True))
    )
    grad_queries = jnp.einsum(
        "hqk,khe->qhe", grad_scores, key_rows, preferred_element_type=jnp.float32
    ) * HEAD_DIM ** (-0.5)
    grad_keys = jnp.einsum(
        "hqk,qhe->khe", grad_scores, queries, preferred_element_type=jnp.float32
    ) * HEAD_DIM ** (-0.5)
    return (lowered(grad_queries), lowered(grad_keys), lowered(grad_values))


def layer_forward(stream, memory, blocks, feed_parts, gain_rows, shifts, batch_size):
    kept_values = []
    for block_order, (w_in, w_out, norm_row) in enumerate(blocks):
        normed, norm_kept = norm_forward(stream, gain_rows[norm_row], shifts[norm_row])
        query_in = lowered(normed)
        model_width = w_out.shape[0]
        if block_order == 0:
            projected = lowered(matmul(query_in, w_in))
            queries = projected[:, :model_width]
            key_rows = projected[:, model_width : 2 * model_width]
            value_rows = projected[:, 2 * model_width :]
            memory_in = query_in
        else:
            memory_in = memory
            queries = lowered(matmul(query_in, w_in[:, :model_width]))
            paired = lowered(matmul(memory, w_in[:, model_width:]))
            key_rows, value_rows = (paired[:, :model_width], paired[:, model_width:])
        causal = memory is not None and block_order == 0
        heads = (
            split_heads(queries, batch_size),
            split_heads(key_rows, batch_size),
            split_heads(value_rows, batch_size),
        )
        context, log_total = lax.map(partial(attend_one, causal=causal), heads)
        context = context.reshape(-1, model_width)
        stream = stream + matmul(context, w_out)
        kept_values.append((norm_kept, query_in, memory_in, heads, context, log_total))
    w_up, w_down, norm_row = feed_parts
    normed, norm_kept = norm_forward(stream, gain_rows[norm_row], shifts[norm_row])
    hidden_in = lowered(normed)
    hidden_pre = matmul(hidden_in, w_up)
    activated = lowered(jax.nn.silu(hidden_pre))
    stream = stream + matmul(activated, w_down)
    kept_values.append((norm_kept, hidden_in, hidden_pre, activated))
    return (stream, kept_values)


def layer_backward(grad_stream, memory, blocks, feed_parts, gain_rows, kept_values, batch_size):
    w_up, w_down, norm_row = feed_parts
    norm_kept, hidden_in, hidden_pre, activated = kept_values[-1]
    grad_low = lowered(grad_stream)
    grad_down = contract_rows(activated, grad_low)
    sigmoid_pre = jax.nn.sigmoid(hidden_pre)
    grad_pre = lowered(
        times_transposed(grad_low, w_down) * sigmoid_pre * (1.0 + hidden_pre * (1.0 - sigmoid_pre))
    )
    grad_up = contract_rows(hidden_in, grad_pre)
    grad_in, grad_gain, grad_shift = norm_backward_rows(
        times_transposed(grad_pre, w_up), norm_kept, gain_rows[norm_row]
    )
    grad_stream = grad_stream + grad_in
    norm_grads = [(norm_row, grad_gain, grad_shift)]
    block_grads = [None] * len(blocks)
    grad_memory = None
    for block_order in reversed(range(len(blocks))):
        w_in, w_out, norm_row = blocks[block_order]
        norm_kept, query_in, memory_in, heads, context, log_total = kept_values[block_order]
        model_width = w_out.shape[0]
        grad_low = lowered(grad_stream)
        grad_w_out = contract_rows(context, grad_low)
        grad_context = split_heads(lowered(times_transposed(grad_low, w_out)), batch_size)
        causal = memory is not None and block_order == 0
        grad_heads = lax.map(partial(attend_back, causal=causal), heads + (log_total, grad_context))
        grad_queries, grad_keys, grad_values = [
            member.reshape(-1, model_width) for member in grad_heads
        ]
        if block_order == 0:
            grad_proj = jnp.concatenate([grad_queries, grad_keys, grad_values], axis=1)
            grad_w_in = contract_rows(query_in, grad_proj)
            grad_normed = times_transposed(grad_proj, w_in)
        else:
            grad_pair = jnp.concatenate([grad_keys, grad_values], axis=1)
            grad_w_in = jnp.concatenate(
                [contract_rows(query_in, grad_queries), contract_rows(memory_in, grad_pair)], axis=1
            )
            grad_normed = times_transposed(grad_queries, w_in[:, :model_width])
            grad_memory = times_transposed(grad_pair, w_in[:, model_width:])
        grad_in, grad_gain, grad_shift = norm_backward_rows(grad_normed, norm_kept, gain_rows[norm_row])
        grad_stream = grad_stream + grad_in
        norm_grads.append((norm_row, grad_gain, grad_shift))
        block_grads[block_order] = (grad_w_in, grad_w_out)
    return (grad_stream, grad_memory, block_grads, (grad_up, grad_down), norm_grads)


def adam_update(weight, first_moment, second_moment, gradient, factor, rate):
    clipped = gradient * factor
    new_first = BETA_ONE * first_moment + (1.0 - BETA_ONE) * clipped
    new_second = BETA_TWO * second_moment + (1.0 - BETA_TWO) * clipped * clipped
    corrected = (
        new_first
        / (1.0 - BETA_ONE**STEP)
        / (jnp.sqrt(new_second / (1.0 - BETA_TWO**STEP)) + ADAM_EPS)
    )
    return (weight - rate * (corrected + DECAY * weight), new_first, new_second)


def local_copied(
    enc_ids,
    labels,
    target_lengths,
    loss_positions,
    embedding,
    attn_in,
    attn_out,
    ffn_up,
    ffn_down,
    norms,
    embedding_first,
    attn_in_first,
    attn_out_first,
    ffn_up_first,
    ffn_down_first,
    norms_first,
    embedding_second,
    attn_in_second,
    attn_out_second,
    ffn_up_second,
    ffn_down_second,
    norms_second,
):
    batch_size, enc_len = enc_ids.shape
    dec_len = labels.shape[1]
    emb_table, w_in_all, w_out_all, w_up_all, w_down_all, norm_table = (
        lax.all_gather(lowered(embedding), "dp", axis=1, tiled=True),
        lax.all_gather(lowered(attn_in), "dp", axis=1, tiled=True),
        lax.all_gather(lowered(attn_out), "dp", axis=1, tiled=True),
        lax.all_gather(lowered(ffn_up), "dp", axis=1, tiled=True),
        lax.all_gather(lowered(ffn_down), "dp", axis=1, tiled=True),
        lax.all_gather(lowered(norms), "dp", axis=1, tiled=True),
    )
    model_width = emb_table.shape[1]
    shard_rows = emb_table.shape[0]
    vocab_total = shard_rows * lax.axis_size("vocab")
    row_start = lax.axis_index("vocab") * shard_rows
    norm_values = norm_table.astype(jnp.float32)
    gain_rows, shifts = (norm_values[:7], norm_values[7:])
    dec_ids = jnp.concatenate([jnp.zeros((batch_size, 1), jnp.int32), labels[:, :-1]], axis=1)
    token_list = jnp.concatenate([enc_ids.reshape(-1), dec_ids.reshape(-1)])
    local_rows = token_list - row_start
    inside = (local_rows >= 0) & (local_rows < shard_rows)
    safe_rows = jnp.clip(local_rows, 0, shard_rows - 1)
    picked = jnp.where(
        inside[:, None], jnp.take(emb_table, safe_rows, axis=0).astype(jnp.float32), 0.0
    )
    looked = lax.psum(picked.astype(jnp.bfloat16), "vocab").astype(jnp.float32)
    root_width = math.sqrt(model_width)
    enc_tokens = batch_size * enc_len
    enc_stream = (
        looked[:enc_tokens].reshape(batch_size, enc_len, model_width) * root_width
        + positions_table(enc_len, model_width)
    ).reshape(enc_tokens, model_width)
    dec_stream = (
        looked[enc_tokens:].reshape(batch_size, dec_len, model_width) * root_width
        + positions_table(dec_len, model_width)
    ).reshape(batch_size * dec_len, model_width)
    enc_blocks = [(w_in_all[0], w_out_all[0], 0)]
    dec_blocks = [(w_in_all[1], w_out_all[1], 3), (w_in_all[2], w_out_all[2], 4)]
    enc_feed = (w_up_all[0], w_down_all[0], 1)
    dec_feed = (w_up_all[1], w_down_all[1], 5)
    enc_out, enc_kept = layer_forward(
        enc_stream, None, enc_blocks, enc_feed, gain_rows, shifts, batch_size
    )
    memory, memory_kept = norm_forward(enc_out, gain_rows[2], shifts[2])
    memory_low = lowered(memory)
    dec_out, dec_kept = layer_forward(
        dec_stream, memory_low, dec_blocks, dec_feed, gain_rows, shifts, batch_size
    )
    final, final_kept = norm_forward(dec_out, gain_rows[6], shifts[6])
    chosen = (jnp.arange(batch_size)[:, None] * dec_len + loss_positions).reshape(-1)
    selected = lowered(jnp.take(final, chosen, axis=0))
    logits = times_transposed(selected, emb_table)
    columns = row_start + jnp.arange(shard_rows)
    padding = columns == vocab_total - 1
    masked = jnp.where(padding[None, :], -1e30, logits)
    target_local = jnp.take_along_axis(labels, loss_positions, axis=1).reshape(-1) - row_start
    target_hit = (jnp.arange(shard_rows)[None, :] == target_local[:, None]).astype(jnp.float32)
    target_term = jnp.sum(target_hit * logits, axis=1)
    smooth_term = jnp.sum(jnp.where(padding[None, :], 0.0, logits), axis=1)
    local_max = jnp.max(masked, axis=1)
    row_max = lax.pmax(local_max, "vocab")
    exp_local = jnp.sum(jnp.exp(masked - row_max[:, None]), axis=1)
    exp_total, smooth_total, target_total = lax.psum((exp_local, smooth_term, target_term), "vocab")
    log_total = row_max + jnp.log(exp_total)
    per_row = log_total - (1.0 - SMOOTH) * target_total - SMOOTH * smooth_total / (vocab_total - 1)
    counted = (loss_positions < target_lengths[:, None]).reshape(-1).astype(jnp.float32)
    loss_sum, token_count = lax.psum((jnp.sum(counted * per_row), jnp.sum(counted)), "dp")
    softmax_rows = jnp.exp(masked - log_total[:, None])
    grad_logits = (counted / token_count)[:, None] * (
        softmax_rows - (1.0 - SMOOTH) * target_hit - SMOOTH / (vocab_total - 1)
    )
    grad_logits = lowered(jnp.where(padding[None, :], 0.0, grad_logits))
    grad_selected = lax.psum(matmul(grad_logits, emb_table).astype(jnp.bfloat16), "vocab").astype(
        jnp.float32
    )
    grad_final = jnp.zeros_like(final).at[chosen].add(grad_selected)
    grad_dec_out, gain_six, shift_six = norm_backward_rows(grad_final, final_kept, gain_rows[6])
    grad_dec_stream, grad_memory, dec_block_grads, dec_feed_grads, dec_norm_grads = layer_backward(
        grad_dec_out, memory_low, dec_blocks, dec_feed, gain_rows, dec_kept, batch_size
    )
    grad_enc_out, gain_two, shift_two = norm_backward_rows(grad_memory, memory_kept, gain_rows[2])
    grad_enc_stream, _, enc_block_grads, enc_feed_grads, enc_norm_grads = layer_backward(
        grad_enc_out, None, enc_blocks, enc_feed, gain_rows, enc_kept, batch_size
    )
    grad_attn_in = jnp.stack([enc_block_grads[0][0], dec_block_grads[0][0], dec_block_grads[1][0]])
    grad_attn_out = jnp.stack([enc_block_grads[0][1], dec_block_grads[0][1], dec_block_grads[1][1]])
    grad_up_all = jnp.stack([enc_feed_grads[0], dec_feed_grads[0]])
    grad_down_all = jnp.stack([enc_feed_grads[1], dec_feed_grads[1]])
    grad_norms = jnp.zeros((14, model_width), jnp.float32)
    for norm_row, grad_gain, grad_shift in (
        enc_norm_grads + dec_norm_grads + [(2, gain_two, shift_two), (6, gain_six, shift_six)]
    ):
        grad_norms = grad_norms.at[norm_row].set(grad_gain).at[norm_row + 7].set(grad_shift)
    grad_tokens = jnp.concatenate([grad_enc_stream, grad_dec_stream], axis=0) * root_width
    head_term = contract_rows(grad_logits, selected)
    lookup_term = (
        jnp.zeros((shard_rows, model_width), jnp.float32)
        .at[safe_rows]
        .add(jnp.where(inside[:, None], grad_tokens, 0.0))
    )
    g_attn_in, g_attn_out, g_up, g_down, g_norms, g_embedding = (
        lax.psum_scatter(
            grad_attn_in.astype(jnp.bfloat16), "dp", scatter_dimension=1, tiled=True
        ).astype(jnp.float32),
        lax.psum_scatter(
            grad_attn_out.astype(jnp.bfloat16), "dp", scatter_dimension=1, tiled=True
        ).astype(jnp.float32),
        lax.psum_scatter(
            grad_up_all.astype(jnp.bfloat16), "dp", scatter_dimension=1, tiled=True
        ).astype(jnp.float32),
        lax.psum_scatter(
            grad_down_all.astype(jnp.bfloat16), "dp", scatter_dimension=1, tiled=True
        ).astype(jnp.float32),
        lax.psum_scatter(
            grad_norms.astype(jnp.bfloat16), "dp", scatter_dimension=1, tiled=True
        ).astype(jnp.float32),
        lax.psum_scatter(
            (head_term + lookup_term).astype(jnp.bfloat16), "dp", scatter_dimension=1, tiled=True
        ).astype(jnp.float32),
    )
    gradients = (g_embedding, g_attn_in, g_attn_out, g_up, g_down, g_norms)
    dense_squares = sum((jnp.sum(member * member) for member in gradients[1:]))
    squares = lax.psum(
        dense_squares / lax.axis_size("vocab") + jnp.sum(g_embedding * g_embedding), ("dp", "vocab")
    )
    grad_norm = jnp.sqrt(squares)
    factor = jnp.minimum(1.0, CLIP / (grad_norm + 1e-06))
    params = (embedding, attn_in, attn_out, ffn_up, ffn_down, norms)
    firsts = (
        embedding_first,
        attn_in_first,
        attn_out_first,
        ffn_up_first,
        ffn_down_first,
        norms_first,
    )
    seconds = (
        embedding_second,
        attn_in_second,
        attn_out_second,
        ffn_up_second,
        ffn_down_second,
        norms_second,
    )
    updated = [
        adam_update(params[slot], firsts[slot], seconds[slot], gradients[slot], factor, RATES[slot])
        for slot in range(6)
    ]
    return (
        loss_sum,
        token_count,
        grad_norm,
        updated[0][0],
        updated[1][0],
        updated[2][0],
        updated[3][0],
        updated[4][0],
        updated[5][0],
        updated[0][1],
        updated[1][1],
        updated[2][1],
        updated[3][1],
        updated[4][1],
        updated[5][1],
        updated[0][2],
        updated[1][2],
        updated[2][2],
        updated[3][2],
        updated[4][2],
        updated[5][2],
    )


VMEM_BYTES = 60 * 1024 * 1024


def positions_numpy(length, model_width):
    place = np.arange(length, dtype=np.float32)[:, None]
    index = np.arange(model_width // 2, dtype=np.float32)[None, :]
    angles = place * np.exp(index * np.float32(-2.0 * math.log(10000.0) / model_width))
    return np.concatenate([np.sin(angles), np.cos(angles)], axis=1).astype(np.float32)


def pick_kernel(ids_ref, table_ref, out_ref, list_ref, count_ref, wide_ref):
    count, rows = wide_ref.shape[0], table_ref.shape[0]

    def one(step, found):
        for inner in range(8):
            slot = step * 8 + inner
            row = ids_ref[slot]
            hit = (row >= 0) & (row < rows)
            safe = jnp.where(hit, row, 0)
            wide_ref[pl.ds(slot, 1), :] = table_ref[pl.ds(safe, 1), :] * jnp.where(hit, 1.0, 0.0)
            list_ref[found] = slot
            found = found + jnp.where(hit, 1, 0)
        return found

    count_ref[0] = lax.fori_loop(0, count // 8, one, 0)
    out_ref[...] = wide_ref[...].astype(jnp.bfloat16)


def pick_rows(local_ids, table):
    count, width = local_ids.shape[0], table.shape[1]
    return pl.pallas_call(
        pick_kernel,
        out_shape=(
            jax.ShapeDtypeStruct((count, width), jnp.bfloat16),
            jax.ShapeDtypeStruct((count + 8,), jnp.int32),
            jax.ShapeDtypeStruct((1,), jnp.int32),
        ),
        in_specs=[
            pl.BlockSpec(memory_space=pltpu.SMEM),
            pl.BlockSpec(memory_space=pltpu.VMEM),
        ],
        out_specs=(
            pl.BlockSpec(memory_space=pltpu.VMEM),
            pl.BlockSpec(memory_space=pltpu.SMEM),
            pl.BlockSpec(memory_space=pltpu.SMEM),
        ),
        scratch_shapes=[pltpu.VMEM((count, width), jnp.float32)],
        compiler_params=pltpu.CompilerParams(vmem_limit_bytes=VMEM_BYTES),
        name="pick_rows",
    )(local_ids, table)


def spread_kernel(ids_ref, list_ref, count_ref, grads_ref, zero_ref, one_ref, two_ref, out_ref, squares_ref, wide_ref, rows_ref):
    width = grads_ref.shape[1]
    chunks, _, piece_columns = zero_ref.shape
    chunk = 3 * piece_columns
    rows_ref[...] = grads_ref[...].astype(jnp.float32)
    wide_ref[...] = jnp.zeros_like(wide_ref)

    def one(step, carry):
        slot = list_ref[step]
        row = ids_ref[slot]
        wide_ref[pl.ds(row, 1), 0:width] += rows_ref[pl.ds(slot, 1), :]
        return carry

    lax.fori_loop(0, count_ref[0], one, 0)

    def turn(piece, total):
        for part in range(chunk // 128):
            start = pl.multiple_of(piece * chunk + part * 128, 128)
            head_ref = (zero_ref, one_ref, two_ref)[part * 128 // piece_columns]
            column = part * 128 % piece_columns
            block = jnp.transpose(wide_ref[pl.ds(start, 128), :])[:width]
            block = block + head_ref[piece, :, column : column + 128].astype(jnp.float32)
            out_ref[:, pl.ds(start, 128)] = block
            total = total + block * block
        return total

    total = lax.fori_loop(0, chunks, turn, jnp.zeros((width, 128), jnp.float32))
    squares_ref[...] = jnp.sum(total, axis=0, keepdims=True)


def spread_rows(local_ids, hit_list, hit_count, grads, head):
    chunks, width, piece_columns = head[0].shape
    chunk = 3 * piece_columns
    return pl.pallas_call(
        spread_kernel,
        out_shape=(
            jax.ShapeDtypeStruct((width, chunks * chunk), jnp.float32),
            jax.ShapeDtypeStruct((1, 128), jnp.float32),
        ),
        in_specs=[pl.BlockSpec(memory_space=pltpu.SMEM)] * 3
        + [pl.BlockSpec(memory_space=pltpu.VMEM)] * 4,
        out_specs=(
            pl.BlockSpec(memory_space=pltpu.VMEM),
            pl.BlockSpec(memory_space=pltpu.VMEM),
        ),
        scratch_shapes=[
            pltpu.VMEM((chunks * chunk, 128), jnp.float32),
            pltpu.VMEM(grads.shape, jnp.float32),
        ],
        compiler_params=pltpu.CompilerParams(vmem_limit_bytes=VMEM_BYTES),
        name="spread_rows",
    )(local_ids, hit_list, hit_count, grads, *head)


MESH = pl.DeviceIdType.MESH


def meet(devices):
    barrier = pltpu.get_barrier_semaphore()
    for device in devices:
        pl.semaphore_signal(barrier, inc=1, device_id=device, device_id_type=MESH)
    pl.semaphore_wait(barrier, len(devices))


def send(source, target, send_sem, recv_sem, device):
    copy = pltpu.make_async_remote_copy(
        src_ref=source,
        dst_ref=target,
        send_sem=send_sem,
        recv_sem=recv_sem,
        device_id=device,
        device_id_type=MESH,
    )
    copy.start()
    return copy


def places():
    group, share = lax.axis_index("dp"), lax.axis_index("vocab")
    core = lax.rem(share, 2)
    core_peer = (group, share + 1 - 2 * core)
    side_peer = (group, lax.rem(share + 2, 4))
    return group, share, core, core_peer, side_peer


def group_peers(group, share, groups):
    return [(lax.rem(group + step, groups), share) for step in range(1, groups)]


def share_peers(group, share, shares):
    return [(group, lax.rem(share + step, shares)) for step in range(1, shares)]


def total_scratch(rows, width):
    half = rows // 2
    return [
        pltpu.VMEM((rows, width), jnp.float32),
        pltpu.VMEM((4, half, width), jnp.bfloat16),
        pltpu.VMEM((rows, width), jnp.bfloat16),
        pltpu.SemaphoreType.DMA((6,)),
    ]


class Total:
    def __init__(self, refs):
        self.part, self.bufs, self.total, self.sems = refs
        _, _, core, self.core_peer, self.side_peer = places()
        half = self.part.shape[0] // 2
        self.mine = pl.ds(pl.multiple_of(core * half, half), half)
        self.other = pl.ds(pl.multiple_of((1 - core) * half, half), half)

    def begin(self, partial_rows):
        self.part[...] = partial_rows
        self.bufs[0] = lowered(self.part[self.other, :])
        self.one = send(
            self.bufs.at[0], self.bufs.at[1], self.sems.at[0], self.sems.at[1], self.core_peer
        )

    def middle(self):
        self.one.wait_recv()
        self.bufs[2] = lowered(self.part[self.mine, :] + self.bufs[1].astype(jnp.float32))
        self.two = send(
            self.bufs.at[2], self.bufs.at[3], self.sems.at[2], self.sems.at[3], self.side_peer
        )

    def last(self):
        self.two.wait_recv()
        self.total[self.mine, :] = lowered(
            self.bufs[2].astype(jnp.float32) + self.bufs[3].astype(jnp.float32)
        )
        piece = self.total.at[self.mine, :]
        self.three = send(piece, piece, self.sems.at[4], self.sems.at[5], self.core_peer)

    def finish(self):
        self.three.wait()
        self.one.wait_send()
        self.two.wait_send()
        return self.total[...].astype(jnp.float32)

    def rest(self):
        self.middle()
        self.last()
        return self.finish()


class Exchange:
    def __init__(self, source_ref, target_ref, sems, groups, index):
        group, share = lax.axis_index("dp"), lax.axis_index("vocab")
        columns = target_ref.shape[2]
        at = pl.ds(index * columns, columns)
        self.copies = [
            send(
                source_ref.at[peer[0], :, at],
                target_ref.at[group],
                sems.at[0, step],
                sems.at[1, step],
                peer,
            )
            for step, peer in enumerate(group_peers(group, share, groups))
        ]
        self.keep = pltpu.make_async_copy(
            source_ref.at[group, :, at], target_ref.at[group], sems.at[0, groups - 1]
        )
        self.keep.start()

    def finish(self):
        self.keep.wait()
        for copy in self.copies:
            copy.wait()


def in_vmem(count, at_rest=()):
    return [
        pl.BlockSpec(memory_space=pl.ANY if index in at_rest else pltpu.VMEM)
        for index in range(count)
    ]


def call(kernel, name, number, inputs, out_shape, scratch, flops, rest_in=(), rest_out=()):
    moved = sum(math.prod(member.shape) * member.dtype.itemsize for member in (*inputs, *out_shape))
    return pl.pallas_call(
        kernel,
        out_shape=tuple(out_shape),
        in_specs=in_vmem(len(inputs), rest_in),
        out_specs=tuple(in_vmem(len(out_shape), rest_out)),
        scratch_shapes=scratch,
        compiler_params=pltpu.CompilerParams(
            collective_id=number, has_side_effects=True, vmem_limit_bytes=VMEM_BYTES
        ),
        cost_estimate=pl.CostEstimate(flops=flops, bytes_accessed=moved, transcendentals=0),
        name=name,
    )(*inputs)


def shape_of(shape, dtype):
    return jax.ShapeDtypeStruct(shape, dtype)


def head_slice(ref, start, index):
    low = start + index * HEAD_DIM
    return ref[:, low : low + HEAD_DIM]


def masked_scores(query, key, causal):
    scores = times_transposed(query, key) * HEAD_DIM ** (-0.5)
    if causal:
        down = lax.broadcasted_iota(jnp.int32, scores.shape, 0)
        across = lax.broadcasted_iota(jnp.int32, scores.shape, 1)
        scores = jnp.where(down >= across, scores, -1e30)
    return scores


def heads_forward(q_ref, kv_ref, starts, context_ref, logs_ref, causal):
    q_start, k_start, v_start = starts
    for index in range(context_ref.shape[1] // HEAD_DIM):
        query = head_slice(q_ref, q_start, index)
        key = head_slice(kv_ref, k_start, index)
        value = head_slice(kv_ref, v_start, index)
        scores = masked_scores(query, key, causal)
        row_top = jnp.max(scores, axis=-1, keepdims=True)
        exponent = jnp.exp(scores - row_top)
        row_total = jnp.sum(exponent, axis=-1, keepdims=True)
        context = lowered(matmul(lowered(exponent / row_total), value))
        context_ref[:, index * HEAD_DIM : (index + 1) * HEAD_DIM] = context
        logs_ref[:, index : index + 1] = row_top + jnp.log(row_total)


def heads_backward(q_ref, kv_ref, starts, logs_ref, grad_ref, gq_ref, gkv_ref, g_starts, causal):
    q_start, k_start, v_start = starts
    gq_start, gk_start, gv_start = g_starts
    scale = HEAD_DIM ** (-0.5)
    for index in range(grad_ref.shape[1] // HEAD_DIM):
        low, high = index * HEAD_DIM, (index + 1) * HEAD_DIM
        query = head_slice(q_ref, q_start, index)
        key = head_slice(kv_ref, k_start, index)
        value = head_slice(kv_ref, v_start, index)
        grad = grad_ref[:, low:high]
        softmax_out = jnp.exp(
            masked_scores(query, key, causal) - logs_ref[:, index : index + 1]
        )
        gkv_ref[:, gv_start + low : gv_start + high] = lowered(
            contract_rows(lowered(softmax_out), grad)
        )
        grad_softmax = times_transposed(grad, value)
        inner = jnp.sum(grad_softmax * softmax_out, axis=-1, keepdims=True)
        grad_scores = lowered(softmax_out * (grad_softmax - inner))
        gq_ref[:, gq_start + low : gq_start + high] = lowered(matmul(grad_scores, key) * scale)
        gkv_ref[:, gk_start + low : gk_start + high] = lowered(
            contract_rows(grad_scores, query) * scale
        )


def norm_backward(grad_out, saved_parts, gain_row):
    normed, scale_inv = saved_parts
    grad_normed = grad_out * gain_row
    grad_in = scale_inv * (
        grad_normed
        - jnp.mean(grad_normed, axis=-1, keepdims=True)
        - normed * jnp.mean(grad_normed * normed, axis=-1, keepdims=True)
    )
    return (
        grad_in,
        jnp.sum(grad_out * normed, axis=0, keepdims=True),
        jnp.sum(grad_out, axis=0, keepdims=True),
    )


def gain_of(norms_ref, row):
    return norms_ref[row : row + 1, :], norms_ref[row + 7 : row + 8, :]


def stream_of(looked_ref, start, place_ref):
    rows, width = place_ref.shape
    looked = looked_ref[start : start + rows, :].astype(jnp.float32)
    return looked * math.sqrt(width) + place_ref[...]


def first_kernel(
    shares,
    looked_ref, place_enc_ref, place_dec_ref, w_ref,
    qkv_enc_ref, context_enc_ref, logs_enc_ref, stream_enc_ref,
    qkv_dec_ref, context_dec_ref, logs_dec_ref, stream_dec_ref,
    out_rows_ref, norms_ref,
    blocks_ref, block_sems, local_sem, *total_refs,
):
    group, share, _, _, _ = places()
    peers = share_peers(group, share, shares)
    meet(peers)
    _, rows, wide = blocks_ref.shape
    own = qkv_enc_ref.shape[1] // 3
    padded = w_ref.shape[1] - wide
    enc_start, dec_start, out_start = 0, padded // 2, padded
    window = pl.ds(out_start, wide)
    copies = []
    for step, (_, peer) in enumerate(peers):
        source = w_ref.at[pl.ds(pl.multiple_of(peer * rows, 64), rows), window]
        copies.append(
            send(source, blocks_ref.at[share], block_sems.at[0, step], block_sems.at[1, step], (group, peer))
        )
    keep = pltpu.make_async_copy(
        w_ref.at[pl.ds(pl.multiple_of(share * rows, 64), rows), window], blocks_ref.at[share], local_sem
    )
    keep.start()

    turned = jnp.transpose(w_ref[:, w_ref.shape[1] - 128 :].astype(jnp.float32))
    norms_ref[...] = turned[64:80]

    enc_total, dec_total = Total(total_refs[:4]), Total(total_refs[4:])
    enc_len, dec_len = place_enc_ref.shape[0], place_dec_ref.shape[0]
    stream = stream_of(looked_ref, 0, place_enc_ref)
    normed, _ = norm_forward(stream, *gain_of(norms_ref, 0))
    qkv_enc_ref[...] = lowered(matmul(lowered(normed), w_ref[:, enc_start : enc_start + 3 * own]))
    stream_enc_ref[...] = stream
    starts = (0, own, 2 * own)
    logs_enc_ref[...] = jnp.zeros_like(logs_enc_ref)
    heads_forward(qkv_enc_ref, qkv_enc_ref, starts, context_enc_ref, logs_enc_ref, False)
    keep.wait()
    for copy in copies:
        copy.wait()
    for matrix in range(3):
        for piece in range(shares):
            out_rows_ref[matrix, :, piece * own : (piece + 1) * own] = blocks_ref[
                piece, :, matrix * own : (matrix + 1) * own
            ]
    enc_total.begin(matmul(context_enc_ref[...], out_rows_ref[0]))
    stream = stream_of(looked_ref, enc_len, place_dec_ref)
    stream_dec_ref[...] = stream
    normed, _ = norm_forward(stream, *gain_of(norms_ref, 3))
    enc_total.middle()
    qkv_dec_ref[...] = lowered(matmul(lowered(normed), w_ref[:, dec_start : dec_start + 3 * own]))
    logs_dec_ref[...] = jnp.zeros_like(logs_dec_ref)
    heads_forward(qkv_dec_ref, qkv_dec_ref, starts, context_dec_ref, logs_dec_ref, True)
    enc_total.last()
    dec_total.begin(matmul(context_dec_ref[...], out_rows_ref[1]))
    dec_total.middle()
    stream_enc_ref[...] += enc_total.finish()
    dec_total.last()
    stream_dec_ref[...] += dec_total.finish()


def enc_feed_kernel(stream_in_ref, norms_ref, w_ref, pre_ref, stream_ref, memory_ref, *total_refs):
    group, share, _, core_peer, side_peer = places()
    meet([core_peer, side_peer])
    width = stream_in_ref.shape[1]
    total = Total(total_refs)
    normed, _ = norm_forward(stream_in_ref[...], *gain_of(norms_ref, 1))
    hidden = w_ref.shape[1] - width
    pre_ref[...] = matmul(lowered(normed), w_ref[:, :hidden])
    activated = lowered(jax.nn.silu(pre_ref[...]))
    total.begin(matmul(activated, w_ref[:, hidden:]))
    stream_ref[...] = stream_in_ref[...] + total.rest()
    memory, _ = norm_forward(stream_ref[...], *gain_of(norms_ref, 2))
    memory_ref[...] = lowered(memory)


def dec_kernel(
    groups,
    stream_in_ref, memory_ref, norms_ref, w_ref, out_rows_ref, positions_ref,
    q_ref, kv_ref, context_ref, logs_ref, stream_mid_ref, pre_ref, stream_ref, selected_ref,
    own_ref, select_sems, *total_refs,
):
    group, share, _, core_peer, side_peer = places()
    peers = group_peers(group, share, groups)
    meet([core_peer, side_peer] + peers)
    width = stream_in_ref.shape[1]
    own = q_ref.shape[1]
    hidden = pre_ref.shape[1]
    in_start = hidden + width
    cross_total, feed_total = Total(total_refs[:4]), Total(total_refs[4:])
    kv_ref[...] = lowered(matmul(memory_ref[...], w_ref[:, in_start + own : in_start + 3 * own]))
    normed, _ = norm_forward(stream_in_ref[...], *gain_of(norms_ref, 4))
    q_ref[...] = lowered(matmul(lowered(normed), w_ref[:, in_start : in_start + own]))
    logs_ref[...] = jnp.zeros_like(logs_ref)
    heads_forward(q_ref, kv_ref, (0, 0, own), context_ref, logs_ref, False)
    cross_total.begin(matmul(context_ref[...], out_rows_ref[2]))
    stream_mid_ref[...] = stream_in_ref[...] + cross_total.rest()
    normed, _ = norm_forward(stream_mid_ref[...], *gain_of(norms_ref, 5))
    pre_ref[...] = matmul(lowered(normed), w_ref[:, :hidden])
    activated = lowered(jax.nn.silu(pre_ref[...]))
    feed_total.begin(matmul(activated, w_ref[:, hidden : hidden + width]))
    stream_ref[...] = stream_mid_ref[...] + feed_total.rest()
    final, _ = norm_forward(stream_ref[...], *gain_of(norms_ref, 6))
    places_down = lax.broadcasted_iota(jnp.int32, (own_ref.shape[0], stream_ref.shape[0]), 1)
    chosen = lowered(jnp.where(places_down == positions_ref[...], 1.0, 0.0))
    own_ref[...] = lowered(matmul(chosen, lowered(final)))
    selected_ref[group] = own_ref[...]
    copies = [
        send(own_ref, selected_ref.at[group], select_sems.at[0, step], select_sems.at[1, step], peer)
        for step, peer in enumerate(peers)
    ]
    for copy in copies:
        copy.wait()


def combine_stats(stats):
    row_max = stats[0][0:1]
    for member in stats[1:]:
        row_max = jnp.maximum(row_max, member[0:1])
    exp_total = smooth = target = 0.0
    for member in stats:
        exp_total = exp_total + member[1:2] * jnp.exp(member[0:1] - row_max)
        smooth = smooth + member[2:3]
        target = target + member[3:4]
    return row_max, exp_total, smooth, target


def head_kernel(
    groups, shares, shard_rows,
    selected_ref, table_ref, targets_ref, weights_ref, counted_ref,
    loss_ref, grad_out_ref, head_ref,
    logits_ref, dz_ref, stats_ref, turned_ref, share_stats_ref, group_stats_ref, stat_sems,
    part_ref, core_ref, side_ref, group_ref, sum_ref, sems,
):
    group, share, core, core_peer, side_peer = places()
    side = share // 2
    near, far = share_peers(group, share, shares), group_peers(group, share, groups)
    meet(near + far)
    rows, width = selected_ref.shape
    chunk = table_ref.shape[1]
    vocab_total = shard_rows * shares
    first = group * chunk
    limit = jnp.minimum(shard_rows - first, vocab_total - 1 - share * shard_rows - first)
    block = 512
    step_rows = 32

    for part in range(chunk // block):
        logits_ref[:, part * block : (part + 1) * block] = matmul(
            selected_ref[...], table_ref[:, part * block : (part + 1) * block]
        )
    stats_ref[...] = jnp.zeros_like(stats_ref)

    def gather_stats(step, carry):
        at = pl.ds(pl.multiple_of(step * step_rows, step_rows), step_rows)
        logits = logits_ref[at, :]
        column = lax.broadcasted_iota(jnp.int32, logits.shape, 1)
        real = column < limit
        masked = jnp.where(real, logits, -1e30)
        top = jnp.max(masked, axis=1, keepdims=True)
        stats_ref[at, 0:1] = top
        stats_ref[at, 1:2] = jnp.sum(jnp.exp(masked - top), axis=1, keepdims=True)
        stats_ref[at, 2:3] = jnp.sum(jnp.where(real, logits, 0.0), axis=1, keepdims=True)
        hit = column == targets_ref[at, :]
        stats_ref[at, 3:4] = jnp.sum(jnp.where(hit, logits, 0.0), axis=1, keepdims=True)
        return carry

    lax.fori_loop(0, rows // step_rows, gather_stats, 0)
    share_stats_ref[share] = jnp.transpose(stats_ref[...])[0:8]
    copies = [
        send(share_stats_ref.at[share], share_stats_ref.at[share], stat_sems.at[0, step], stat_sems.at[1, step], peer)
        for step, peer in enumerate(near)
    ]
    for copy in copies:
        copy.wait()
    merged = combine_stats([share_stats_ref[index] for index in range(shares)])
    group_stats_ref[group] = jnp.concatenate(merged + (jnp.zeros((4, rows), jnp.float32),), axis=0)
    copies = [
        send(group_stats_ref.at[group], group_stats_ref.at[group], stat_sems.at[2, step], stat_sems.at[3, step], peer)
        for step, peer in enumerate(far)
    ]
    for copy in copies:
        copy.wait()
    row_max, exp_total, smooth, target = combine_stats(
        [group_stats_ref[index] for index in range(groups)]
    )
    log_total = row_max + jnp.log(exp_total)
    per_row = log_total - (1.0 - SMOOTH) * target - SMOOTH * smooth / (vocab_total - 1)
    loss = jnp.sum(counted_ref[...] * per_row, axis=1, keepdims=True)
    loss_ref[...] = jnp.broadcast_to(loss, loss_ref.shape)
    turned_ref[...] = jnp.zeros_like(turned_ref)
    turned_ref[0:1, :] = log_total
    stats_ref[...] = jnp.transpose(turned_ref[...])

    def make_dz(step, carry):
        at = pl.ds(pl.multiple_of(step * step_rows, step_rows), step_rows)
        logits = logits_ref[at, :]
        column = lax.broadcasted_iota(jnp.int32, logits.shape, 1)
        softmax_rows = jnp.exp(logits - stats_ref[at, 0:1])
        hit = jnp.where(column == targets_ref[at, :], 1.0 - SMOOTH, 0.0)
        grad = weights_ref[at, :] * (softmax_rows - hit - SMOOTH / (vocab_total - 1))
        dz_ref[at, :] = lowered(jnp.where(column < limit, grad, 0.0))
        return carry

    lax.fori_loop(0, rows // step_rows, make_dz, 0)
    loss_rows = rows // groups
    half, quarter = loss_rows // 2, loss_rows // 4
    part_ref[...] = lowered(times_transposed(dz_ref[...], table_ref[...])).reshape(part_ref.shape)
    mine = pl.ds(pl.multiple_of(core * half, 16), half)
    other = pl.ds(pl.multiple_of((1 - core) * half, 16), half)
    copy = send(part_ref.at[:, other, :], core_ref, sems.at[0, 0], sems.at[1, 0], core_peer)

    def head_part(index):
        at = slice(index * block, (index + 1) * block)
        head_ref[:, at] = lowered(contract_rows(selected_ref[...], dz_ref[:, at]))

    parts = chunk // block
    head_part(0)
    copy.wait()
    part_ref[:, mine, :] = lowered(
        part_ref[:, mine, :].astype(jnp.float32) + core_ref[...].astype(jnp.float32)
    )
    base = core * half
    my_quarter = pl.ds(pl.multiple_of(base + side * quarter, 16), quarter)
    other_quarter = pl.ds(pl.multiple_of(base + (1 - side) * quarter, 16), quarter)
    copy = send(part_ref.at[:, other_quarter, :], side_ref, sems.at[0, 1], sems.at[1, 1], side_peer)
    for index in range(1, parts // 2):
        head_part(index)
    copy.wait()
    side_ref[...] = lowered(
        part_ref[:, my_quarter, :].astype(jnp.float32) + side_ref[...].astype(jnp.float32)
    )
    group_ref[group] = side_ref[group]
    copies = [
        send(side_ref.at[peer[0]], group_ref.at[group], sems.at[0, 2 + step], sems.at[1, 2 + step], peer)
        for step, peer in enumerate(far)
    ]
    for index in range(parts // 2, parts):
        head_part(index)
    for copy in copies:
        copy.wait()
    summed = group_ref[0].astype(jnp.float32)
    for index in range(1, groups):
        summed = summed + group_ref[index].astype(jnp.float32)
    sum_ref[...] = lowered(summed)
    grad_out_ref[my_quarter, :] = sum_ref[...]
    base_sem = 1 + groups
    copies = [
        send(sum_ref, grad_out_ref.at[my_quarter, :], sems.at[0, base_sem + step], sems.at[1, base_sem + step], peer)
        for step, peer in enumerate(near)
    ]
    for copy in copies:
        copy.wait()


def feed_grads(grad_ref, stream_ref, pre_ref, norms_ref, row, w_ref, grads_ref, total):
    width = stream_ref.shape[1]
    hidden = pre_ref.shape[1]
    normed, _ = norm_forward(stream_ref[...], *gain_of(norms_ref, row))
    grad_low = lowered(grad_ref[...])
    pre = pre_ref[...]
    sigmoid_pre = jax.nn.sigmoid(pre)
    grad_pre = lowered(
        times_transposed(grad_low, w_ref[:, hidden : hidden + width])
        * sigmoid_pre
        * (1.0 + pre * (1.0 - sigmoid_pre))
    )
    total.begin(times_transposed(grad_pre, w_ref[:, :hidden]))
    activated = lowered(pre * sigmoid_pre)
    grads_ref[:, hidden : hidden + width] = lowered(contract_rows(activated, grad_low))
    total.middle()
    grads_ref[:, :hidden] = lowered(contract_rows(lowered(normed), grad_pre))


def norm_step(grad_ref, stream_ref, norms_ref, row, summed, rows_ref, slot):
    gain, shift = gain_of(norms_ref, row)
    _, kept = norm_forward(stream_ref[...], gain, shift)
    grad_in, grad_gain, grad_shift = norm_backward(summed, kept, gain)
    rows_ref[slot : slot + 1, :] = grad_gain
    rows_ref[slot + 1 : slot + 2, :] = grad_shift
    if grad_ref is None:
        return grad_in
    return grad_ref[...] + grad_in


def dec_back_kernel(
    groups,
    grad_selected_ref, positions_ref, stream_in_ref, stream_mid_ref, stream_ref, pre_ref, memory_ref,
    norms_ref, w_ref, out_rows_ref, q_ref, kv_ref, context_ref, logs_ref, head_in_ref,
    grads_ref, grad_out_rows_ref, grad_ref, grad_memory_ref, rows_ref, head_out_ref,
    head_sems, grad_context_ref, gq_ref, gkv_ref, *total_refs,
):
    group, share, _, core_peer, side_peer = places()
    meet([core_peer, side_peer] + group_peers(group, share, groups))
    exchange = Exchange(head_in_ref, head_out_ref, head_sems, groups, 0)
    width = stream_ref.shape[1]
    own = q_ref.shape[1]
    hidden = pre_ref.shape[1]
    in_start = hidden + width
    feed_total, cross_total, memory_total = [Total(total_refs[4 * k : 4 * k + 4]) for k in range(3)]
    rows_ref[...] = jnp.zeros_like(rows_ref)
    down = lax.broadcasted_iota(jnp.int32, (stream_ref.shape[0], grad_selected_ref.shape[0]), 0)
    chosen = lowered(jnp.where(down == positions_ref[...], 1.0, 0.0))
    grad_final = matmul(chosen, grad_selected_ref[...])
    grad_ref[...] = norm_step(None, stream_ref, norms_ref, 6, grad_final, rows_ref, 0)
    feed_grads(grad_ref, stream_mid_ref, pre_ref, norms_ref, 5, w_ref, grads_ref, feed_total)
    feed_total.last()
    grad_ref[...] = norm_step(
        grad_ref, stream_mid_ref, norms_ref, 5, feed_total.finish(), rows_ref, 2
    )
    grad_low = lowered(grad_ref[...])
    grad_context_ref[...] = lowered(times_transposed(grad_low, out_rows_ref[2]))
    heads_backward(
        q_ref, kv_ref, (0, 0, own), logs_ref, grad_context_ref, gq_ref, gkv_ref, (0, 0, own), False
    )
    memory_total.begin(
        times_transposed(gkv_ref[...], w_ref[:, in_start + own : in_start + 3 * own])
    )
    cross_total.begin(times_transposed(gq_ref[...], w_ref[:, in_start : in_start + own]))
    grad_out_rows_ref[...] = lowered(contract_rows(context_ref[...], grad_low))
    memory_total.middle()
    cross_total.middle()
    normed, _ = norm_forward(stream_in_ref[...], *gain_of(norms_ref, 4))
    grads_ref[:, in_start:] = jnp.zeros((width, grads_ref.shape[1] - in_start), jnp.bfloat16)
    grads_ref[:, in_start : in_start + own] = lowered(contract_rows(lowered(normed), gq_ref[...]))
    grads_ref[:, in_start + own : in_start + 3 * own] = lowered(
        contract_rows(memory_ref[...], gkv_ref[...])
    )
    memory_total.last()
    cross_total.last()
    grad_memory_ref[...] = memory_total.finish()
    grad_ref[...] = norm_step(
        grad_ref, stream_in_ref, norms_ref, 4, cross_total.finish(), rows_ref, 4
    )
    exchange.finish()


def mid_back_kernel(
    groups,
    grad_memory_ref, stream_enc_ref, stream_mid_ref, pre_ref, norms_ref, w_ref,
    grad_dec_in_ref, looked_ref, place_dec_ref, w_first_ref, out_rows_ref, qkv_ref, context_ref, logs_ref, head_in_ref,
    grads_ref, grad_out_rows_ref, grad_enc_ref, tokens_ref, rows_ref, head_out_ref,
    head_sems, stream_dec_ref, grad_context_ref, gqkv_ref, *total_refs,
):
    group, share, _, core_peer, side_peer = places()
    meet([core_peer, side_peer] + group_peers(group, share, groups))
    exchange = Exchange(head_in_ref, head_out_ref, head_sems, groups, 1)
    width = stream_enc_ref.shape[1]
    own = context_ref.shape[1]
    hidden = pre_ref.shape[1]
    in_start = hidden + width
    w_start = w_first_ref.shape[1] // 3
    dec_start = looked_ref.shape[0] - place_dec_ref.shape[0]
    feed_total, self_total = Total(total_refs[:4]), Total(total_refs[4:])
    rows_ref[...] = jnp.zeros_like(rows_ref)
    grad_enc_ref[...] = norm_step(
        None, stream_enc_ref, norms_ref, 2, grad_memory_ref[...], rows_ref, 0
    )
    feed_grads(grad_enc_ref, stream_mid_ref, pre_ref, norms_ref, 1, w_ref, grads_ref, feed_total)
    grad_low = lowered(grad_dec_in_ref[...])
    grad_context_ref[...] = lowered(times_transposed(grad_low, out_rows_ref[1]))
    starts = (0, own, 2 * own)
    heads_backward(
        qkv_ref, qkv_ref, starts, logs_ref, grad_context_ref, gqkv_ref, gqkv_ref, starts, True
    )
    feed_total.last()
    self_total.begin(times_transposed(gqkv_ref[...], w_first_ref[:, w_start : w_start + 3 * own]))
    grad_out_rows_ref[...] = lowered(contract_rows(context_ref[...], grad_low))
    self_total.middle()
    stream_dec_ref[...] = stream_of(looked_ref, dec_start, place_dec_ref)
    normed, _ = norm_forward(stream_dec_ref[...], *gain_of(norms_ref, 3))
    grads_ref[:, in_start:] = jnp.zeros((width, grads_ref.shape[1] - in_start), jnp.bfloat16)
    grads_ref[:, in_start : in_start + 3 * own] = lowered(
        contract_rows(lowered(normed), gqkv_ref[...])
    )
    grad_enc_ref[...] = norm_step(
        grad_enc_ref, stream_mid_ref, norms_ref, 1, feed_total.finish(), rows_ref, 2
    )
    self_total.last()
    grad_dec = norm_step(
        grad_dec_in_ref, stream_dec_ref, norms_ref, 3, self_total.finish(), rows_ref, 4
    )
    tokens_ref[...] = lowered(grad_dec * math.sqrt(width))
    exchange.finish()


def last_back_kernel(
    groups, shares,
    grad_in_ref, looked_ref, place_enc_ref, norms_ref, w_ref, out_rows_ref, qkv_ref, context_ref, logs_ref,
    g_self_ref, g_cross_ref, rows_dec_ref, rows_mid_ref, head_in_ref,
    grads_ref, tokens_ref, head_out_ref,
    head_sems, stream_ref, grad_context_ref, gqkv_ref, g_rows_ref, norm_rows_ref, turned_ref, blocks_ref, rows_ref, block_sems, local_sem, *total_refs,
):
    group, share, _, core_peer, side_peer = places()
    peers = share_peers(group, share, shares)
    meet(peers + group_peers(group, share, groups))
    exchange = Exchange(head_in_ref, head_out_ref, head_sems, groups, 2)
    width = stream_ref.shape[1]
    own = context_ref.shape[1]
    wide = blocks_ref.shape[2]
    total = Total(total_refs)
    grad_low = lowered(grad_in_ref[...])
    grad_context_ref[...] = lowered(times_transposed(grad_low, out_rows_ref[0]))
    starts = (0, own, 2 * own)
    heads_backward(
        qkv_ref, qkv_ref, starts, logs_ref, grad_context_ref, gqkv_ref, gqkv_ref, starts, False
    )
    total.begin(times_transposed(gqkv_ref[...], w_ref[:, : 3 * own]))
    g_rows_ref[...] = lowered(contract_rows(context_ref[...], grad_low))
    total.middle()
    stream_ref[...] = stream_of(looked_ref, 0, place_enc_ref)
    normed, _ = norm_forward(stream_ref[...], *gain_of(norms_ref, 0))
    in_wide = grads_ref.shape[1] - wide
    grads_ref[:, :in_wide] = jnp.zeros((width, in_wide), jnp.bfloat16)
    grads_ref[:, : 3 * own] = lowered(contract_rows(lowered(normed), gqkv_ref[...]))
    blocks_ref[...] = jnp.zeros_like(blocks_ref)
    for piece in range(shares):
        at = slice(piece * own, (piece + 1) * own)
        for matrix, source in enumerate((g_rows_ref, g_self_ref, g_cross_ref)):
            blocks_ref[piece, :, matrix * own : (matrix + 1) * own] = source[:, at]
    total.last()
    rows_ref[...] = jnp.zeros_like(rows_ref)
    grad_enc = norm_step(grad_in_ref, stream_ref, norms_ref, 0, total.finish(), rows_ref, 0)
    tokens_ref[...] = lowered(grad_enc * math.sqrt(width))
    norm_rows_ref[...] = jnp.zeros_like(norm_rows_ref)
    order = (
        (0, rows_ref, 0),
        (1, rows_mid_ref, 2),
        (2, rows_mid_ref, 0),
        (3, rows_mid_ref, 4),
        (4, rows_dec_ref, 4),
        (5, rows_dec_ref, 2),
        (6, rows_dec_ref, 0),
    )
    for row, source, slot in order:
        norm_rows_ref[64 + row : 65 + row, :] = source[slot : slot + 1, :]
        norm_rows_ref[71 + row : 72 + row, :] = source[slot + 1 : slot + 2, :]
    turned_ref[...] = jnp.transpose(norm_rows_ref[...])
    own_rows = turned_ref[pl.ds(pl.multiple_of(share * own, 64), own), :]
    for piece in range(shares):
        tail = blocks_ref[piece, :, wide - 128 :].astype(jnp.float32)
        blocks_ref[piece, :, wide - 128 :] = lowered(tail + own_rows)
    target = grads_ref.at[pl.ds(pl.multiple_of(share * own, 64), own), pl.ds(in_wide, wide)]
    copies = [
        send(blocks_ref.at[peer[1]], target, block_sems.at[0, step], block_sems.at[1, step], peer)
        for step, peer in enumerate(peers)
    ]
    keep = pltpu.make_async_copy(blocks_ref.at[share], target, local_sem)
    keep.start()
    keep.wait()
    for copy in copies:
        copy.wait()
    exchange.finish()


def numbers_kernel(groups, own_ref, out_ref, sems, local_sem):
    group, share, _, _, _ = places()
    peers = group_peers(group, share, groups)
    meet(peers)
    copies = [
        send(own_ref, out_ref.at[group], sems.at[0, step], sems.at[1, step], peer)
        for step, peer in enumerate(peers)
    ]
    keep = pltpu.make_async_copy(own_ref, out_ref.at[group], local_sem)
    keep.start()
    keep.wait()
    for copy in copies:
        copy.wait()


def look_kernel(groups, picked_ref, looked_ref, send_ref, core_ref, side_ref, group_ref, sems):
    group, share, core, core_peer, side_peer = places()
    side = share // 2
    far = group_peers(group, share, groups)
    meet([core_peer, side_peer] + far)
    _, tokens, width = picked_ref.shape
    half, quarter = tokens // 2, tokens // 4
    mine = pl.ds(pl.multiple_of(core * half, 16), half)
    other = pl.ds(pl.multiple_of((1 - core) * half, 16), half)
    send(picked_ref.at[:, other, :], core_ref, sems.at[0, 0], sems.at[1, 0], core_peer).wait()
    core_ref[...] = core_ref[...] + picked_ref[:, mine, :]
    own_quarter = pl.ds(pl.multiple_of(side * quarter, 16), quarter)
    other_quarter = pl.ds(pl.multiple_of((1 - side) * quarter, 16), quarter)
    send(core_ref.at[:, other_quarter, :], side_ref, sems.at[0, 1], sems.at[1, 1], side_peer).wait()
    side_ref[...] = side_ref[...] + core_ref[:, own_quarter, :]
    group_ref[group] = side_ref[group]
    copies = [
        send(side_ref.at[peer[0]], group_ref.at[group], sems.at[0, 2 + step], sems.at[1, 2 + step], peer)
        for step, peer in enumerate(far)
    ]
    for copy in copies:
        copy.wait()
    for index in range(groups):
        send_ref[:, index * width : (index + 1) * width] = group_ref[index]
    at = pl.ds(pl.multiple_of(core * half + side * quarter, 16), quarter)
    looked_ref[at, :] = send_ref[...]
    end = 1 + groups
    send(send_ref, looked_ref.at[at, :], sems.at[0, end], sems.at[1, end], side_peer).wait()
    end = end + 1
    both = looked_ref.at[mine, :]
    send(both, both, sems.at[0, end], sems.at[1, end], core_peer).wait()


def squares_kernel(
    groups, shares, norm_start, norm_count,
    embedding_ref, one_ref, two_ref, three_ref, out_ref, share_ref, group_ref, sems,
):
    group, share, _, _, _ = places()
    near, far = share_peers(group, share, shares), group_peers(group, share, groups)
    meet(near + far)
    total = 0.0
    for ref in (one_ref, two_ref, three_ref):
        value = ref[...].astype(jnp.float32)
        value = value * value
        if ref is three_ref:
            column = lax.broadcasted_iota(jnp.int32, value.shape, 1)
            norm_part = (column >= norm_start) & (column < norm_start + norm_count)
            value = jnp.where(norm_part, value / shares, value)
        total = total + jnp.sum(value)
    lane = lax.broadcasted_iota(jnp.int32, (8, 128), 1)
    down = lax.broadcasted_iota(jnp.int32, (8, 128), 0)
    share_ref[share] = jnp.where((lane == 0) & (down == 0), total, 0.0) + jnp.where(
        down == 1, embedding_ref[...], 0.0
    )
    copies = [
        send(share_ref.at[share], share_ref.at[share], sems.at[0, step], sems.at[1, step], peer)
        for step, peer in enumerate(near)
    ]
    for copy in copies:
        copy.wait()
    summed = share_ref[0]
    for index in range(1, shares):
        summed = summed + share_ref[index]
    group_ref[group] = summed
    copies = [
        send(group_ref.at[group], group_ref.at[group], sems.at[2, step], sems.at[3, step], peer)
        for step, peer in enumerate(far)
    ]
    for copy in copies:
        copy.wait()
    summed = group_ref[0]
    for index in range(1, groups):
        summed = summed + group_ref[index]
    out_ref[...] = jnp.broadcast_to(jnp.sum(summed), out_ref.shape)


def share_of_columns(array, groups, shares, index):
    lead, columns = array.shape[:-1], array.shape[-1]
    cut = array.reshape(lead + (groups, shares, columns // groups // shares))
    own = lax.dynamic_index_in_dim(cut, index, axis=len(lead) + 1, keepdims=False)
    return own.reshape(lead + (columns // shares,))


def whole_of_shares(shares_first, groups):
    shares, rows, columns = shares_first.shape
    cut = shares_first.reshape(shares, rows, groups, columns // groups)
    return cut.transpose(1, 2, 0, 3).reshape(rows, shares * columns)


def local(
    enc_ids,
    labels,
    target_lengths,
    loss_positions,
    embedding,
    attn_in,
    attn_out,
    ffn_up,
    ffn_down,
    norms,
    embedding_first,
    attn_in_first,
    attn_out_first,
    ffn_up_first,
    ffn_down_first,
    norms_first,
    embedding_second,
    attn_in_second,
    attn_out_second,
    ffn_up_second,
    ffn_down_second,
    norms_second,
):
    groups, shares = lax.axis_size("dp"), lax.axis_size("vocab")
    group, share = lax.axis_index("dp"), lax.axis_index("vocab")
    enc_len, dec_len = enc_ids.shape[1], labels.shape[1]
    loss_count = loss_positions.shape[1]
    shard_rows, part_width = embedding.shape
    model_width = part_width * groups
    vocab_total = shard_rows * shares
    row_start = share * shard_rows
    root_width = math.sqrt(model_width)
    tokens = enc_len + dec_len

    bf16, f32 = jnp.bfloat16, jnp.float32
    sems = pltpu.SemaphoreType.DMA
    numbers = jnp.concatenate(
        [enc_ids, labels, loss_positions, target_lengths[:, None]], axis=1
    )
    number_count = numbers.shape[1]
    number_lanes = -(-number_count // 1024) * 128
    numbers = jnp.pad(numbers, ((0, 0), (0, 8 * number_lanes - number_count)))
    (numbers,) = call(
        partial(numbers_kernel, groups),
        "numbers",
        1,
        [numbers.reshape(8, number_lanes)],
        [shape_of((groups, 8, number_lanes), jnp.int32)],
        [sems((2, groups - 1)), sems],
        0,
    )
    numbers = numbers.reshape(groups, 8 * number_lanes)
    all_enc = numbers[:, :enc_len]
    all_labels = numbers[:, enc_len:tokens]
    all_positions = numbers[:, tokens : tokens + loss_count]
    all_lengths = numbers[:, tokens + loss_count : number_count]
    all_tokens = jnp.concatenate(
        [all_enc, jnp.zeros((groups, 1), jnp.int32), all_labels[:, :-1]], axis=1
    )
    all_targets = jnp.take_along_axis(all_labels, all_positions, axis=1).reshape(-1)
    all_counted = (all_positions < all_lengths).reshape(-1).astype(f32)
    token_count = jnp.sum(all_counted)

    local_ids = all_tokens.reshape(-1) - row_start
    picked, hit_list, hit_count = pick_rows(local_ids, embedding)
    (looked,) = call(
        partial(look_kernel, groups),
        "look",
        2,
        [picked.reshape(groups, tokens, part_width)],
        [shape_of((tokens, model_width), bf16)],
        [
            pltpu.VMEM((tokens // 4, model_width), bf16),
            pltpu.VMEM((groups, tokens // 2, part_width), bf16),
            pltpu.VMEM((groups, tokens // 4, part_width), bf16),
            pltpu.VMEM((groups, tokens // 4, part_width), bf16),
            sems((2, groups + 3)),
        ],
        0,
    )

    mine_in = share_of_columns(lowered(attn_in), 3, shares, share)
    mine_out = share_of_columns(lowered(attn_out), 1, shares, share)
    mine_up = share_of_columns(lowered(ffn_up), groups, shares, share)
    down_rows = ffn_down.shape[1] // shares
    mine_down = lax.dynamic_slice_in_dim(ffn_down, share * down_rows, down_rows, axis=1)
    mine_down = lowered(mine_down)
    norm_rows = norms.shape[0]
    own_in, own, own_up = mine_in.shape[2], mine_out.shape[2], mine_up.shape[2]
    gap = -own_in % 128

    def wider(array, columns):
        return jnp.pad(array, ((0, 0), (0, columns)))

    mine_first = jnp.concatenate(
        [wider(mine_in[0], gap), wider(mine_in[1], gap), mine_out[0], mine_out[1], mine_out[2]]
        + [wider(lowered(norms).T, gap - norm_rows)],
        axis=1,
    )
    mine_enc = jnp.concatenate([mine_up[0], mine_down[0]], axis=1)
    mine_dec = jnp.concatenate([mine_up[1], mine_down[1], wider(mine_in[2], gap)], axis=1)
    mine_first, mine_enc, mine_dec, _ = lax.optimization_barrier(
        (mine_first, mine_enc, mine_dec, all_lengths)
    )
    w_first = lax.all_gather(mine_first, "dp", axis=0, tiled=True)
    w_enc = lax.all_gather(mine_enc, "dp", axis=0, tiled=True)
    w_dec = lax.all_gather(mine_dec, "dp", axis=0, tiled=True)
    in_wide = own_in + gap

    chunk = -(-shard_rows // (groups * 512)) * 512
    across = jnp.pad(lowered(embedding.T), ((0, 0), (0, groups * chunk - shard_rows)))
    across = across.reshape(part_width, groups, chunk).transpose(1, 0, 2)
    across, looked = lax.optimization_barrier((across, looked))
    table = lax.all_to_all(across, "dp", 0, 0).reshape(model_width, chunk)

    place_enc = positions_numpy(enc_len, model_width)
    place_dec = positions_numpy(dec_len, model_width)
    enc_macs, dec_macs = enc_len * model_width, dec_len * model_width
    total_enc, total_dec = total_scratch(enc_len, model_width), total_scratch(dec_len, model_width)
    (
        qkv_enc, context_enc, logs_enc, stream_enc,
        qkv_dec, context_dec, logs_dec, stream_dec,
        out_rows, norm_values,
    ) = call(
        partial(first_kernel, shares),
        "first",
        3,
        [looked, place_enc, place_dec, w_first],
        [
            shape_of((enc_len, 3 * own), bf16),
            shape_of((enc_len, own), bf16),
            shape_of((enc_len, 128), f32),
            shape_of((enc_len, model_width), f32),
            shape_of((dec_len, 3 * own), bf16),
            shape_of((dec_len, own), bf16),
            shape_of((dec_len, 128), f32),
            shape_of((dec_len, model_width), f32),
            shape_of((3, own, model_width), bf16),
            shape_of((16, model_width), f32),
        ],
        [
            pltpu.VMEM((shares, own, in_wide), bf16),
            sems((2, shares - 1)),
            sems,
        ]
        + total_enc
        + total_dec,
        8 * (enc_macs + dec_macs) * own,
    )
    pre_enc, stream_two, memory = call(
        enc_feed_kernel,
        "enc_feed",
        4,
        [stream_enc, norm_values, w_enc],
        [
            shape_of((enc_len, own_up), f32),
            shape_of((enc_len, model_width), f32),
            shape_of((enc_len, model_width), bf16),
        ],
        total_enc,
        4 * enc_macs * own_up,
    )
    (
        q_cross, kv_cross, context_cross, logs_cross, stream_mid, pre_dec, stream_out, selected
    ) = call(
        partial(dec_kernel, groups),
        "dec",
        5,
        [stream_dec, memory, norm_values, w_dec, out_rows, loss_positions.reshape(-1, 1)],
        [
            shape_of((dec_len, own), bf16),
            shape_of((enc_len, 2 * own), bf16),
            shape_of((dec_len, own), bf16),
            shape_of((dec_len, 128), f32),
            shape_of((dec_len, model_width), f32),
            shape_of((dec_len, own_up), f32),
            shape_of((dec_len, model_width), f32),
            shape_of((groups, loss_count, model_width), bf16),
        ],
        [pltpu.VMEM((loss_count, model_width), bf16), sems((2, groups - 1))] + total_dec + total_dec,
        4 * dec_macs * own_up + 8 * enc_macs * own,
    )

    rows_all = groups * loss_count
    first_row = row_start + group * chunk
    targets = all_targets - first_row
    inside = (targets >= 0) & (targets < jnp.minimum(chunk, shard_rows - group * chunk))
    targets = jnp.where(inside, targets, -1)[:, None]
    loss, grad_selected, head_grad = call(
        partial(head_kernel, groups, shares, shard_rows),
        "head",
        6,
        [
            selected.reshape(rows_all, model_width),
            table,
            targets,
            (all_counted / token_count)[:, None],
            all_counted[None, :],
        ],
        [
            shape_of((1, 128), f32),
            shape_of((loss_count, model_width), bf16),
            shape_of((model_width, chunk), bf16),
        ],
        [
            pltpu.VMEM((rows_all, chunk), f32),
            pltpu.VMEM((rows_all, chunk), bf16),
            pltpu.VMEM((rows_all, 128), f32),
            pltpu.VMEM((128, rows_all), f32),
            pltpu.VMEM((shares, 8, rows_all), f32),
            pltpu.VMEM((groups, 8, rows_all), f32),
            sems((4, max(groups, shares))),
            pltpu.VMEM((groups, loss_count, model_width), bf16),
            pltpu.VMEM((groups, loss_count // 2, model_width), bf16),
            pltpu.VMEM((groups, loss_count // 4, model_width), bf16),
            pltpu.VMEM((groups, loss_count // 4, model_width), bf16),
            pltpu.VMEM((loss_count // 4, model_width), bf16),
            sems((2, groups + shares)),
        ],
        6 * rows_all * chunk * model_width,
    )
    loss_sum = loss[0, 0]
    head_grad = head_grad.reshape(groups, part_width, chunk)
    pieces = chunk // 3

    dec_grads, g_out_cross, grad_dec, grad_memory, rows_dec, head_zero = call(
        partial(dec_back_kernel, groups),
        "dec_back",
        7,
        [
            grad_selected, loss_positions.reshape(1, -1), stream_dec, stream_mid, stream_out, pre_dec,
            memory, norm_values, w_dec, out_rows, q_cross, kv_cross, context_cross, logs_cross,
            head_grad,
        ],
        [
            shape_of((model_width, own_up + model_width + in_wide), bf16),
            shape_of((own, model_width), bf16),
            shape_of((dec_len, model_width), f32),
            shape_of((enc_len, model_width), f32),
            shape_of((8, model_width), f32),
            shape_of((groups, part_width, pieces), bf16),
        ],
        [
            sems((2, groups)),
            pltpu.VMEM((dec_len, own), bf16),
            pltpu.VMEM((dec_len, own), bf16),
            pltpu.VMEM((enc_len, 2 * own), bf16),
        ]
        + total_dec
        + total_dec
        + total_enc,
        8 * dec_macs * own_up + 16 * enc_macs * own,
        (14,),
        (5,),
    )
    dec_own = lax.psum_scatter(dec_grads, "dp", scatter_dimension=0, tiled=True)
    mid_grads, g_out_self, grad_enc, tokens_dec, rows_mid, head_one = call(
        partial(mid_back_kernel, groups),
        "mid_back",
        8,
        [
            grad_memory, stream_two, stream_enc, pre_enc, norm_values, w_enc,
            grad_dec, looked, place_dec, w_first, out_rows, qkv_dec, context_dec, logs_dec,
            head_grad,
        ],
        [
            shape_of((model_width, own_up + model_width + in_wide), bf16),
            shape_of((own, model_width), bf16),
            shape_of((enc_len, model_width), f32),
            shape_of((dec_len, model_width), bf16),
            shape_of((8, model_width), f32),
            shape_of((groups, part_width, pieces), bf16),
        ],
        [
            sems((2, groups)),
            pltpu.VMEM((dec_len, model_width), f32),
            pltpu.VMEM((dec_len, own), bf16),
            pltpu.VMEM((dec_len, 3 * own), bf16),
        ]
        + total_enc
        + total_dec,
        8 * enc_macs * own_up + 16 * dec_macs * own,
        (14,),
        (5,),
    )
    mid_own = lax.psum_scatter(mid_grads, "dp", scatter_dimension=0, tiled=True)
    last_grads, tokens_enc, head_two = call(
        partial(last_back_kernel, groups, shares),
        "last_back",
        9,
        [
            grad_enc, looked, place_enc, norm_values, w_first, out_rows, qkv_enc, context_enc, logs_enc,
            g_out_self, g_out_cross, rows_dec, rows_mid, head_grad,
        ],
        [
            shape_of((model_width, 2 * in_wide), bf16),
            shape_of((enc_len, model_width), bf16),
            shape_of((groups, part_width, pieces), bf16),
        ],
        [
            sems((2, groups)),
            pltpu.VMEM((enc_len, model_width), f32),
            pltpu.VMEM((enc_len, own), bf16),
            pltpu.VMEM((enc_len, 3 * own), bf16),
            pltpu.VMEM((own, model_width), bf16),
            pltpu.VMEM((128, model_width), f32),
            pltpu.VMEM((model_width, 128), f32),
            pltpu.VMEM((shares, own, in_wide), bf16),
            pltpu.VMEM((8, model_width), f32),
            sems((2, shares - 1)),
            sems,
        ]
        + total_enc,
        16 * enc_macs * own,
        (13,),
        (2,),
    )
    last_own = lax.psum_scatter(last_grads, "dp", scatter_dimension=0, tiled=True)

    grad_tokens = jnp.concatenate([tokens_enc, tokens_dec], axis=0)
    grad_tokens = grad_tokens.reshape(tokens, groups, part_width).transpose(1, 0, 2)
    grad_tokens = lax.all_to_all(grad_tokens, "dp", 0, 0).reshape(groups * tokens, part_width)
    g_embedding, embedding_squares = spread_rows(
        local_ids, hit_list, hit_count, grad_tokens, (head_zero, head_one, head_two)
    )
    g_embedding = g_embedding[:, :shard_rows].T
    norm_start = in_wide + own_in
    (squares,) = call(
        partial(squares_kernel, groups, shares, norm_start, norm_rows),
        "squares",
        10,
        [embedding_squares, dec_own, mid_own, last_own],
        [shape_of((1, 128), f32)],
        [
            pltpu.VMEM((shares, 8, 128), f32),
            pltpu.VMEM((groups, 8, 128), f32),
            sems((4, max(groups, shares))),
        ],
        0,
    )
    grad_norm = jnp.sqrt(squares[0, 0])
    factor = jnp.minimum(1.0, CLIP / (grad_norm + 1e-06))
    dec_shares = lax.all_gather(dec_own, "vocab", axis=0, tiled=False)
    mid_shares = lax.all_gather(mid_own, "vocab", axis=0, tiled=False)
    last_shares = lax.all_gather(last_own, "vocab", axis=0, tiled=False)

    def shares_cut(array, *sizes):
        edges = np.cumsum((0,) + sizes)
        return [array[:, :, low:high].astype(f32) for low, high in zip(edges[:-1], edges[1:])]

    s_up_dec, s_down_dec, s_in_cross = shares_cut(dec_shares, own_up, model_width, own_in)
    s_up_enc, s_down_enc, s_in_self = shares_cut(mid_shares, own_up, model_width, own_in)
    s_in_enc, _, s_out_enc, s_out_self, s_out_cross = shares_cut(
        last_shares, own_in, gap, own, own, own
    )
    gradients = (
        g_embedding,
        jnp.stack([whole_of_shares(member, 3) for member in (s_in_enc, s_in_self, s_in_cross)]),
        jnp.stack([whole_of_shares(member, 1) for member in (s_out_enc, s_out_self, s_out_cross)]),
        jnp.stack([whole_of_shares(member, groups) for member in (s_up_enc, s_up_dec)]),
        jnp.stack([member.reshape(-1, model_width) for member in (s_down_enc, s_down_dec)]),
        last_own[:, norm_start : norm_start + norm_rows].astype(f32).T,
    )
    params = (embedding, attn_in, attn_out, ffn_up, ffn_down, norms)
    firsts = (
        embedding_first,
        attn_in_first,
        attn_out_first,
        ffn_up_first,
        ffn_down_first,
        norms_first,
    )
    seconds = (
        embedding_second,
        attn_in_second,
        attn_out_second,
        ffn_up_second,
        ffn_down_second,
        norms_second,
    )
    updated = [
        adam_update(params[slot], firsts[slot], seconds[slot], gradients[slot], factor, RATES[slot])
        for slot in range(6)
    ]
    return (loss_sum, token_count, grad_norm) + tuple(
        updated[slot][kind] for kind in range(3) for slot in range(6)
    )


def splits_evenly(mesh):
    return HEADS % mesh.shape["vocab"] == 0


def solution(mesh):
    placed = (
        P("dp", None),
        P("dp", None),
        P("dp"),
        P("dp", None),
        P("vocab", "dp"),
        P(None, "dp", None),
        P(None, "dp", None),
        P(None, "dp", None),
        P(None, "dp", None),
        P(None, "dp"),
        P("vocab", "dp"),
        P(None, "dp", None),
        P(None, "dp", None),
        P(None, "dp", None),
        P(None, "dp", None),
        P(None, "dp"),
        P("vocab", "dp"),
        P(None, "dp", None),
        P(None, "dp", None),
        P(None, "dp", None),
        P(None, "dp", None),
        P(None, "dp"),
    )
    return jax.shard_map(
        local if splits_evenly(mesh) else local_copied,
        mesh=mesh,
        in_specs=placed,
        out_specs=(
            P(),
            P(),
            P(),
            P("vocab", "dp"),
            P(None, "dp", None),
            P(None, "dp", None),
            P(None, "dp", None),
            P(None, "dp", None),
            P(None, "dp"),
            P("vocab", "dp"),
            P(None, "dp", None),
            P(None, "dp", None),
            P(None, "dp", None),
            P(None, "dp", None),
            P(None, "dp"),
            P("vocab", "dp"),
            P(None, "dp", None),
            P(None, "dp", None),
            P(None, "dp", None),
            P(None, "dp", None),
            P(None, "dp"),
        ),
        check_vma=False,
    )
```

```python
from functools import partial
import math

import jax
import jax.numpy as jnp
import numpy as np
from jax import lax
from jax.experimental import pallas as pl
from jax.experimental.pallas import tpu as pltpu
from jax.sharding import PartitionSpec as P

HEADS = 12
HEAD_DIM = 64
STEP = 10


EPS_NORM = 1e-05
SMOOTH = 0.1
CLIP = 0.02
RATES = (0.05, 0.05, 0.4, 0.05, 0.05, 0.8)
BETA_ONE = 0.9
BETA_TWO = 0.999
ADAM_EPS = 1e-08
DECAY = 0.01


def lowered(tensor):
    return tensor.astype(jnp.bfloat16)


def matmul(left_side, right_side):
    return jnp.dot(left_side, right_side, preferred_element_type=jnp.float32)


def times_transposed(left_side, right_side):
    return lax.dot_general(
        left_side, right_side, (((1,), (1,)), ((), ())), preferred_element_type=jnp.float32
    )


def contract_rows(left_side, right_side):
    return lax.dot_general(
        left_side, right_side, (((0,), (0,)), ((), ())), preferred_element_type=jnp.float32
    )


def positions_table(length, model_width):
    position_col = jnp.arange(length, dtype=jnp.float32)[:, None]
    freq_index = jnp.arange(model_width // 2, dtype=jnp.float32)[None, :]
    angles = position_col * jnp.exp(freq_index * (-2.0 * math.log(10000.0) / model_width))
    return jnp.concatenate([jnp.sin(angles), jnp.cos(angles)], axis=1)


def norm_forward(tensor, gain_row, shift_row):
    center = tensor - jnp.mean(tensor, axis=-1, keepdims=True)
    scale_inv = lax.rsqrt(jnp.mean(center * center, axis=-1, keepdims=True) + EPS_NORM)
    normed = center * scale_inv
    return (normed * gain_row + shift_row, (normed, scale_inv))


def norm_backward_rows(grad_out, saved_parts, gain_row):
    normed, scale_inv = saved_parts
    grad_normed = grad_out * gain_row
    grad_in = scale_inv * (
        grad_normed
        - jnp.mean(grad_normed, axis=-1, keepdims=True)
        - normed * jnp.mean(grad_normed * normed, axis=-1, keepdims=True)
    )
    return (grad_in, jnp.sum(grad_out * normed, axis=0), jnp.sum(grad_out, axis=0))


def split_heads(rows, batch_size):
    return rows.reshape(batch_size, -1, HEADS, rows.shape[1] // HEADS)


def score_block(queries, key_rows, causal):
    scores = jnp.einsum(
        "qhe,khe->hqk", queries, key_rows, preferred_element_type=jnp.float32
    ) * HEAD_DIM ** (-0.5)
    if causal:
        allowed = jnp.arange(queries.shape[0])[:, None] >= jnp.arange(key_rows.shape[0])[None, :]
        scores = jnp.where(allowed[None], scores, -1e30)
    return scores


def attend_one(block_args, causal):
    queries, key_rows, value_rows = block_args
    scores = score_block(queries, key_rows, causal)
    row_top = jnp.max(scores, axis=-1, keepdims=True)
    exponent = jnp.exp(scores - row_top)
    row_total = jnp.sum(exponent, axis=-1, keepdims=True)
    softmax_out = lowered(exponent / row_total)
    context = jnp.einsum(
        "hqk,khe->qhe", softmax_out, value_rows, preferred_element_type=jnp.float32
    )
    return (lowered(context), (row_top + jnp.log(row_total))[..., 0])


def attend_back(block_args, causal):
    queries, key_rows, value_rows, log_total, grad_context = block_args
    scores = score_block(queries, key_rows, causal)
    softmax_out = jnp.exp(scores - log_total[..., None])
    grad_values = jnp.einsum(
        "hqk,qhe->khe", lowered(softmax_out), grad_context, preferred_element_type=jnp.float32
    )
    grad_softmax = jnp.einsum(
        "qhe,khe->hqk", grad_context, value_rows, preferred_element_type=jnp.float32
    )
    grad_scores = lowered(
        softmax_out * (grad_softmax - jnp.sum(grad_softmax * softmax_out, axis=-1, keepdims=True))
    )
    grad_queries = jnp.einsum(
        "hqk,khe->qhe", grad_scores, key_rows, preferred_element_type=jnp.float32
    ) * HEAD_DIM ** (-0.5)
    grad_keys = jnp.einsum(
        "hqk,qhe->khe", grad_scores, queries, preferred_element_type=jnp.float32
    ) * HEAD_DIM ** (-0.5)
    return (lowered(grad_queries), lowered(grad_keys), lowered(grad_values))


def layer_forward(stream, memory, blocks, feed_parts, gain_rows, shifts, batch_size):
    kept_values = []
    for block_order, (w_in, w_out, norm_row) in enumerate(blocks):
        normed, norm_kept = norm_forward(stream, gain_rows[norm_row], shifts[norm_row])
        query_in = lowered(normed)
        model_width = w_out.shape[0]
        if block_order == 0:
            projected = lowered(matmul(query_in, w_in))
            queries = projected[:, :model_width]
            key_rows = projected[:, model_width : 2 * model_width]
            value_rows = projected[:, 2 * model_width :]
            memory_in = query_in
        else:
            memory_in = memory
            queries = lowered(matmul(query_in, w_in[:, :model_width]))
            paired = lowered(matmul(memory, w_in[:, model_width:]))
            key_rows, value_rows = (paired[:, :model_width], paired[:, model_width:])
        causal = memory is not None and block_order == 0
        heads = (
            split_heads(queries, batch_size),
            split_heads(key_rows, batch_size),
            split_heads(value_rows, batch_size),
        )
        context, log_total = lax.map(partial(attend_one, causal=causal), heads)
        context = context.reshape(-1, model_width)
        stream = stream + matmul(context, w_out)
        kept_values.append((norm_kept, query_in, memory_in, heads, context, log_total))
    w_up, w_down, norm_row = feed_parts
    normed, norm_kept = norm_forward(stream, gain_rows[norm_row], shifts[norm_row])
    hidden_in = lowered(normed)
    hidden_pre = matmul(hidden_in, w_up)
    activated = lowered(jax.nn.silu(hidden_pre))
    stream = stream + matmul(activated, w_down)
    kept_values.append((norm_kept, hidden_in, hidden_pre, activated))
    return (stream, kept_values)


def layer_backward(grad_stream, memory, blocks, feed_parts, gain_rows, kept_values, batch_size):
    w_up, w_down, norm_row = feed_parts
    norm_kept, hidden_in, hidden_pre, activated = kept_values[-1]
    grad_low = lowered(grad_stream)
    grad_down = contract_rows(activated, grad_low)
    sigmoid_pre = jax.nn.sigmoid(hidden_pre)
    grad_pre = lowered(
        times_transposed(grad_low, w_down) * sigmoid_pre * (1.0 + hidden_pre * (1.0 - sigmoid_pre))
    )
    grad_up = contract_rows(hidden_in, grad_pre)
    grad_in, grad_gain, grad_shift = norm_backward_rows(
        times_transposed(grad_pre, w_up), norm_kept, gain_rows[norm_row]
    )
    grad_stream = grad_stream + grad_in
    norm_grads = [(norm_row, grad_gain, grad_shift)]
    block_grads = [None] * len(blocks)
    grad_memory = None
    for block_order in reversed(range(len(blocks))):
        w_in, w_out, norm_row = blocks[block_order]
        norm_kept, query_in, memory_in, heads, context, log_total = kept_values[block_order]
        model_width = w_out.shape[0]
        grad_low = lowered(grad_stream)
        grad_w_out = contract_rows(context, grad_low)
        grad_context = split_heads(lowered(times_transposed(grad_low, w_out)), batch_size)
        causal = memory is not None and block_order == 0
        grad_heads = lax.map(partial(attend_back, causal=causal), heads + (log_total, grad_context))
        grad_queries, grad_keys, grad_values = [
            member.reshape(-1, model_width) for member in grad_heads
        ]
        if block_order == 0:
            grad_proj = jnp.concatenate([grad_queries, grad_keys, grad_values], axis=1)
            grad_w_in = contract_rows(query_in, grad_proj)
            grad_normed = times_transposed(grad_proj, w_in)
        else:
            grad_pair = jnp.concatenate([grad_keys, grad_values], axis=1)
            grad_w_in = jnp.concatenate(
                [contract_rows(query_in, grad_queries), contract_rows(memory_in, grad_pair)], axis=1
            )
            grad_normed = times_transposed(grad_queries, w_in[:, :model_width])
            grad_memory = times_transposed(grad_pair, w_in[:, model_width:])
        grad_in, grad_gain, grad_shift = norm_backward_rows(grad_normed, norm_kept, gain_rows[norm_row])
        grad_stream = grad_stream + grad_in
        norm_grads.append((norm_row, grad_gain, grad_shift))
        block_grads[block_order] = (grad_w_in, grad_w_out)
    return (grad_stream, grad_memory, block_grads, (grad_up, grad_down), norm_grads)


def adam_update(weight, first_moment, second_moment, gradient, factor, rate):
    clipped = gradient * factor
    new_first = BETA_ONE * first_moment + (1.0 - BETA_ONE) * clipped
    new_second = BETA_TWO * second_moment + (1.0 - BETA_TWO) * clipped * clipped
    corrected = (
        new_first
        / (1.0 - BETA_ONE**STEP)
        / (jnp.sqrt(new_second / (1.0 - BETA_TWO**STEP)) + ADAM_EPS)
    )
    return (weight - rate * (corrected + DECAY * weight), new_first, new_second)


def local_copied(
    enc_ids,
    labels,
    target_lengths,
    loss_positions,
    embedding,
    attn_in,
    attn_out,
    ffn_up,
    ffn_down,
    norms,
    embedding_first,
    attn_in_first,
    attn_out_first,
    ffn_up_first,
    ffn_down_first,
    norms_first,
    embedding_second,
    attn_in_second,
    attn_out_second,
    ffn_up_second,
    ffn_down_second,
    norms_second,
):
    batch_size, enc_len = enc_ids.shape
    dec_len = labels.shape[1]
    emb_table, w_in_all, w_out_all, w_up_all, w_down_all, norm_table = (
        lax.all_gather(lowered(embedding), "dp", axis=1, tiled=True),
        lax.all_gather(lowered(attn_in), "dp", axis=1, tiled=True),
        lax.all_gather(lowered(attn_out), "dp", axis=1, tiled=True),
        lax.all_gather(lowered(ffn_up), "dp", axis=1, tiled=True),
        lax.all_gather(lowered(ffn_down), "dp", axis=1, tiled=True),
        lax.all_gather(lowered(norms), "dp", axis=1, tiled=True),
    )
    model_width = emb_table.shape[1]
    shard_rows = emb_table.shape[0]
    vocab_total = shard_rows * lax.axis_size("vocab")
    row_start = lax.axis_index("vocab") * shard_rows
    norm_values = norm_table.astype(jnp.float32)
    gain_rows, shifts = (norm_values[:7], norm_values[7:])
    dec_ids = jnp.concatenate([jnp.zeros((batch_size, 1), jnp.int32), labels[:, :-1]], axis=1)
    token_list = jnp.concatenate([enc_ids.reshape(-1), dec_ids.reshape(-1)])
    local_rows = token_list - row_start
    inside = (local_rows >= 0) & (local_rows < shard_rows)
    safe_rows = jnp.clip(local_rows, 0, shard_rows - 1)
    picked = jnp.where(
        inside[:, None], jnp.take(emb_table, safe_rows, axis=0).astype(jnp.float32), 0.0
    )
    looked = lax.psum(picked.astype(jnp.bfloat16), "vocab").astype(jnp.float32)
    root_width = math.sqrt(model_width)
    enc_tokens = batch_size * enc_len
    enc_stream = (
        looked[:enc_tokens].reshape(batch_size, enc_len, model_width) * root_width
        + positions_table(enc_len, model_width)
    ).reshape(enc_tokens, model_width)
    dec_stream = (
        looked[enc_tokens:].reshape(batch_size, dec_len, model_width) * root_width
        + positions_table(dec_len, model_width)
    ).reshape(batch_size * dec_len, model_width)
    enc_blocks = [(w_in_all[0], w_out_all[0], 0)]
    dec_blocks = [(w_in_all[1], w_out_all[1], 3), (w_in_all[2], w_out_all[2], 4)]
    enc_feed = (w_up_all[0], w_down_all[0], 1)
    dec_feed = (w_up_all[1], w_down_all[1], 5)
    enc_out, enc_kept = layer_forward(
        enc_stream, None, enc_blocks, enc_feed, gain_rows, shifts, batch_size
    )
    memory, memory_kept = norm_forward(enc_out, gain_rows[2], shifts[2])
    memory_low = lowered(memory)
    dec_out, dec_kept = layer_forward(
        dec_stream, memory_low, dec_blocks, dec_feed, gain_rows, shifts, batch_size
    )
    final, final_kept = norm_forward(dec_out, gain_rows[6], shifts[6])
    chosen = (jnp.arange(batch_size)[:, None] * dec_len + loss_positions).reshape(-1)
    selected = lowered(jnp.take(final, chosen, axis=0))
    logits = times_transposed(selected, emb_table)
    columns = row_start + jnp.arange(shard_rows)
    padding = columns == vocab_total - 1
    masked = jnp.where(padding[None, :], -1e30, logits)
    target_local = jnp.take_along_axis(labels, loss_positions, axis=1).reshape(-1) - row_start
    target_hit = (jnp.arange(shard_rows)[None, :] == target_local[:, None]).astype(jnp.float32)
    target_term = jnp.sum(target_hit * logits, axis=1)
    smooth_term = jnp.sum(jnp.where(padding[None, :], 0.0, logits), axis=1)
    local_max = jnp.max(masked, axis=1)
    row_max = lax.pmax(local_max, "vocab")
    exp_local = jnp.sum(jnp.exp(masked - row_max[:, None]), axis=1)
    exp_total, smooth_total, target_total = lax.psum((exp_local, smooth_term, target_term), "vocab")
    log_total = row_max + jnp.log(exp_total)
    per_row = log_total - (1.0 - SMOOTH) * target_total - SMOOTH * smooth_total / (vocab_total - 1)
    counted = (loss_positions < target_lengths[:, None]).reshape(-1).astype(jnp.float32)
    loss_sum, token_count = lax.psum((jnp.sum(counted * per_row), jnp.sum(counted)), "dp")
    softmax_rows = jnp.exp(masked - log_total[:, None])
    grad_logits = (counted / token_count)[:, None] * (
        softmax_rows - (1.0 - SMOOTH) * target_hit - SMOOTH / (vocab_total - 1)
    )
    grad_logits = lowered(jnp.where(padding[None, :], 0.0, grad_logits))
    grad_selected = lax.psum(matmul(grad_logits, emb_table).astype(jnp.bfloat16), "vocab").astype(
        jnp.float32
    )
    grad_final = jnp.zeros_like(final).at[chosen].add(grad_selected)
    grad_dec_out, gain_six, shift_six = norm_backward_rows(grad_final, final_kept, gain_rows[6])
    grad_dec_stream, grad_memory, dec_block_grads, dec_feed_grads, dec_norm_grads = layer_backward(
        grad_dec_out, memory_low, dec_blocks, dec_feed, gain_rows, dec_kept, batch_size
    )
    grad_enc_out, gain_two, shift_two = norm_backward_rows(grad_memory, memory_kept, gain_rows[2])
    grad_enc_stream, _, enc_block_grads, enc_feed_grads, enc_norm_grads = layer_backward(
        grad_enc_out, None, enc_blocks, enc_feed, gain_rows, enc_kept, batch_size
    )
    grad_attn_in = jnp.stack([enc_block_grads[0][0], dec_block_grads[0][0], dec_block_grads[1][0]])
    grad_attn_out = jnp.stack([enc_block_grads[0][1], dec_block_grads[0][1], dec_block_grads[1][1]])
    grad_up_all = jnp.stack([enc_feed_grads[0], dec_feed_grads[0]])
    grad_down_all = jnp.stack([enc_feed_grads[1], dec_feed_grads[1]])
    grad_norms = jnp.zeros((14, model_width), jnp.float32)
    for norm_row, grad_gain, grad_shift in (
        enc_norm_grads + dec_norm_grads + [(2, gain_two, shift_two), (6, gain_six, shift_six)]
    ):
        grad_norms = grad_norms.at[norm_row].set(grad_gain).at[norm_row + 7].set(grad_shift)
    grad_tokens = jnp.concatenate([grad_enc_stream, grad_dec_stream], axis=0) * root_width
    head_term = contract_rows(grad_logits, selected)
    lookup_term = (
        jnp.zeros((shard_rows, model_width), jnp.float32)
        .at[safe_rows]
        .add(jnp.where(inside[:, None], grad_tokens, 0.0))
    )
    g_attn_in, g_attn_out, g_up, g_down, g_norms, g_embedding = (
        lax.psum_scatter(
            grad_attn_in.astype(jnp.bfloat16), "dp", scatter_dimension=1, tiled=True
        ).astype(jnp.float32),
        lax.psum_scatter(
            grad_attn_out.astype(jnp.bfloat16), "dp", scatter_dimension=1, tiled=True
        ).astype(jnp.float32),
        lax.psum_scatter(
            grad_up_all.astype(jnp.bfloat16), "dp", scatter_dimension=1, tiled=True
        ).astype(jnp.float32),
        lax.psum_scatter(
            grad_down_all.astype(jnp.bfloat16), "dp", scatter_dimension=1, tiled=True
        ).astype(jnp.float32),
        lax.psum_scatter(
            grad_norms.astype(jnp.bfloat16), "dp", scatter_dimension=1, tiled=True
        ).astype(jnp.float32),
        lax.psum_scatter(
            (head_term + lookup_term).astype(jnp.bfloat16), "dp", scatter_dimension=1, tiled=True
        ).astype(jnp.float32),
    )
    gradients = (g_embedding, g_attn_in, g_attn_out, g_up, g_down, g_norms)
    dense_squares = sum((jnp.sum(member * member) for member in gradients[1:]))
    squares = lax.psum(
        dense_squares / lax.axis_size("vocab") + jnp.sum(g_embedding * g_embedding), ("dp", "vocab")
    )
    grad_norm = jnp.sqrt(squares)
    factor = jnp.minimum(1.0, CLIP / (grad_norm + 1e-06))
    params = (embedding, attn_in, attn_out, ffn_up, ffn_down, norms)
    firsts = (
        embedding_first,
        attn_in_first,
        attn_out_first,
        ffn_up_first,
        ffn_down_first,
        norms_first,
    )
    seconds = (
        embedding_second,
        attn_in_second,
        attn_out_second,
        ffn_up_second,
        ffn_down_second,
        norms_second,
    )
    updated = [
        adam_update(params[slot], firsts[slot], seconds[slot], gradients[slot], factor, RATES[slot])
        for slot in range(6)
    ]
    return (
        loss_sum,
        token_count,
        grad_norm,
        updated[0][0],
        updated[1][0],
        updated[2][0],
        updated[3][0],
        updated[4][0],
        updated[5][0],
        updated[0][1],
        updated[1][1],
        updated[2][1],
        updated[3][1],
        updated[4][1],
        updated[5][1],
        updated[0][2],
        updated[1][2],
        updated[2][2],
        updated[3][2],
        updated[4][2],
        updated[5][2],
    )


VMEM_BYTES = 60 * 1024 * 1024


def positions_numpy(length, model_width):
    place = np.arange(length, dtype=np.float32)[:, None]
    index = np.arange(model_width // 2, dtype=np.float32)[None, :]
    angles = place * np.exp(index * np.float32(-2.0 * math.log(10000.0) / model_width))
    return np.concatenate([np.sin(angles), np.cos(angles)], axis=1).astype(np.float32)


def hits_kernel(rows, span, ids_ref, list_ref):
    def one(step, found):
        for inner in range(8):
            slot = step * 8 + inner
            row = ids_ref[slot]
            list_ref[found] = row * span + slot
            found = found + jnp.where((row >= 0) & (row < rows), 1, 0)
        return found

    list_ref[list_ref.shape[0] - 1] = lax.fori_loop(0, ids_ref.shape[0] // 8, one, 0)


def list_hits(local_ids, rows, span):
    return pl.pallas_call(
        partial(hits_kernel, rows, span),
        out_shape=jax.ShapeDtypeStruct((span,), jnp.int32),
        in_specs=[pl.BlockSpec(memory_space=pltpu.SMEM)],
        out_specs=pl.BlockSpec(memory_space=pltpu.SMEM),
        name="list_hits",
    )(local_ids)


def over_hits(lists_ref, visit):
    groups, span = lists_ref.shape
    for group in range(groups):

        def one(step, carry):
            entry = lists_ref[group, step]
            visit(group, entry // span, lax.rem(entry, span))
            return carry

        lax.fori_loop(0, lists_ref[group, span - 1], one, 0)


def pick_kernel(lists_ref, table_ref, out_ref, across_ref, wide_ref, turned_ref):
    tokens = wide_ref.shape[0] // lists_ref.shape[0]
    width, rows = table_ref.shape
    total = across_ref.shape[1]
    wide_ref[...] = jnp.zeros_like(wide_ref)
    step = 1024
    for low in range(0, total, step):
        high = max(min(low + step, rows), low)
        if high > low:
            across_ref[:, low:high] = lowered(table_ref[:, low:high])
        if high < low + step:
            across_ref[:, high : low + step] = jnp.zeros((width, low + step - high), jnp.bfloat16)

    def turn(piece, carry):
        for part in range(8):
            start = pl.multiple_of(piece * step + part * 128, 128)
            block = across_ref[:, pl.ds(start, 128)].astype(jnp.float32)
            turned_ref[pl.ds(start, 128), :] = jnp.transpose(block)
        return carry

    lax.fori_loop(0, total // step, turn, 0)

    def visit(group, row, slot):
        wide_ref[pl.ds(group * tokens + slot, 1), :] = turned_ref[pl.ds(row, 1), :]

    over_hits(lists_ref, visit)
    out_ref[...] = wide_ref[...].astype(jnp.bfloat16)


def pick_rows(lists, count, table, total):
    width = table.shape[0]
    return pl.pallas_call(
        pick_kernel,
        out_shape=(
            jax.ShapeDtypeStruct((count, width), jnp.bfloat16),
            jax.ShapeDtypeStruct((width, total), jnp.bfloat16),
        ),
        in_specs=[
            pl.BlockSpec(memory_space=pltpu.SMEM),
            pl.BlockSpec(memory_space=pltpu.VMEM),
        ],
        out_specs=(
            pl.BlockSpec(memory_space=pltpu.VMEM),
            pl.BlockSpec(memory_space=pltpu.VMEM),
        ),
        scratch_shapes=[
            pltpu.VMEM((count, width), jnp.float32),
            pltpu.VMEM((total, width), jnp.float32),
        ],
        compiler_params=pltpu.CompilerParams(vmem_limit_bytes=VMEM_BYTES),
        name="pick_rows",
    )(lists, table)


def spread_kernel(
    lists_ref, grads_ref, head_ref, out_ref, squares_ref, wide_ref, rows_ref
):
    shares, groups, quarter, width = grads_ref.shape
    tokens = shares * quarter
    chunks, _, chunk = head_ref.shape
    for index in range(shares):
        for number in range(groups):
            start = number * tokens + index * quarter
            rows_ref[start : start + quarter, :] = grads_ref[index, number].astype(jnp.float32)
    wide_ref[...] = jnp.zeros_like(wide_ref)

    def visit(group, row, slot):
        wide_ref[pl.ds(row, 1), 0:width] += rows_ref[pl.ds(group * tokens + slot, 1), :]

    over_hits(lists_ref, visit)

    def turn(piece, total):
        for part in range(chunk // 128):
            column = part * 128
            start = pl.multiple_of(piece * chunk + part * 128, 128)
            block = jnp.transpose(wide_ref[pl.ds(start, 128), :])[:width]
            block = block + head_ref[piece, :, column : column + 128].astype(jnp.float32)
            out_ref[:, pl.ds(start, 128)] = block
            total = total + block * block
        return total

    total = lax.fori_loop(0, chunks, turn, jnp.zeros((width, 128), jnp.float32))
    squares_ref[...] = jnp.sum(total, axis=0, keepdims=True)


def spread_rows(lists, grads, head):
    chunks, width, chunk = head.shape
    shares, groups, quarter, _ = grads.shape
    return pl.pallas_call(
        spread_kernel,
        out_shape=(
            jax.ShapeDtypeStruct((width, chunks * chunk), jnp.float32),
            jax.ShapeDtypeStruct((1, 128), jnp.float32),
        ),
        in_specs=[pl.BlockSpec(memory_space=pltpu.SMEM)]
        + [pl.BlockSpec(memory_space=pltpu.VMEM)] * 2,
        out_specs=(
            pl.BlockSpec(memory_space=pltpu.VMEM),
            pl.BlockSpec(memory_space=pltpu.VMEM),
        ),
        scratch_shapes=[
            pltpu.VMEM((chunks * chunk, 128), jnp.float32),
            pltpu.VMEM((shares * groups * quarter, width), jnp.float32),
        ],
        compiler_params=pltpu.CompilerParams(vmem_limit_bytes=VMEM_BYTES),
        name="spread_rows",
    )(lists, grads, head)


MESH = pl.DeviceIdType.MESH


def meet(devices):
    barrier = pltpu.get_barrier_semaphore()
    for device in devices:
        pl.semaphore_signal(barrier, inc=1, device_id=device, device_id_type=MESH)
    pl.semaphore_wait(barrier, len(devices))


def send(source, target, send_sem, recv_sem, device):
    copy = pltpu.make_async_remote_copy(
        src_ref=source,
        dst_ref=target,
        send_sem=send_sem,
        recv_sem=recv_sem,
        device_id=device,
        device_id_type=MESH,
    )
    copy.start()
    return copy


def places():
    group, share = lax.axis_index("dp"), lax.axis_index("vocab")
    core = lax.rem(share, 2)
    core_peer = (group, share + 1 - 2 * core)
    side_peer = (group, lax.rem(share + 2, 4))
    return group, share, core, core_peer, side_peer


def group_peers(group, share, groups):
    return [(lax.rem(group + step, groups), share) for step in range(1, groups)]


def share_peers(group, share, shares):
    return [(group, lax.rem(share + step, shares)) for step in range(1, shares)]


def total_scratch(rows, width):
    half = rows // 2
    return [
        pltpu.VMEM((rows, width), jnp.float32),
        pltpu.VMEM((4, half, width), jnp.bfloat16),
        pltpu.VMEM((rows, width), jnp.bfloat16),
        pltpu.SemaphoreType.DMA((6,)),
    ]


class Total:
    def __init__(self, refs):
        self.part, self.bufs, self.total, self.sems = refs
        _, _, core, self.core_peer, self.side_peer = places()
        half = self.part.shape[0] // 2
        self.mine = pl.ds(pl.multiple_of(core * half, half), half)
        self.other = pl.ds(pl.multiple_of((1 - core) * half, half), half)

    def begin(self, partial_rows):
        self.part[...] = partial_rows
        self.bufs[0] = lowered(self.part[self.other, :])
        self.one = send(
            self.bufs.at[0], self.bufs.at[1], self.sems.at[0], self.sems.at[1], self.core_peer
        )

    def middle(self):
        self.one.wait_recv()
        self.bufs[2] = lowered(self.part[self.mine, :] + self.bufs[1].astype(jnp.float32))
        self.two = send(
            self.bufs.at[2], self.bufs.at[3], self.sems.at[2], self.sems.at[3], self.side_peer
        )

    def last(self):
        self.two.wait_recv()
        self.total[self.mine, :] = lowered(
            self.bufs[2].astype(jnp.float32) + self.bufs[3].astype(jnp.float32)
        )
        piece = self.total.at[self.mine, :]
        self.three = send(piece, piece, self.sems.at[4], self.sems.at[5], self.core_peer)

    def finish(self):
        self.three.wait()
        self.one.wait_send()
        self.two.wait_send()
        return self.total[...].astype(jnp.float32)

    def rest(self):
        self.middle()
        self.last()
        return self.finish()


class Exchange:
    def __init__(self, block_of, target_ref, sems, groups):
        group, share = lax.axis_index("dp"), lax.axis_index("vocab")
        self.copies = [
            send(
                block_of(peer[0]), target_ref.at[group], sems.at[0, step], sems.at[1, step], peer
            )
            for step, peer in enumerate(group_peers(group, share, groups))
        ]
        self.keep = pltpu.make_async_copy(
            block_of(group), target_ref.at[group], sems.at[0, groups - 1]
        )
        self.keep.start()

    def finish(self):
        self.keep.wait()
        for copy in self.copies:
            copy.wait()


def head_blocks(source_ref, start, columns):
    return lambda group: source_ref.at[group, :, pl.ds(start, columns)]


def table_blocks(source_ref, chunk, start, columns):
    return lambda group: source_ref.at[:, pl.ds(pl.multiple_of(group * chunk + start, 128), columns)]


def pair_of(group, share):
    place = lax.rem(group, 2)
    return (group + 1 - 2 * place, share), place


def line_places(group):
    pair, place = group // 2, lax.rem(group, 2)
    high, low = pair // 2, lax.rem(pair, 2)
    far = ((1 - high) * 2 + low) * 2 + place
    near = (high * 2 + 1 - low) * 2 + place
    return high, low, far, near


def line_scratch(width, columns):
    return [
        pltpu.VMEM((2, 2, width, columns), jnp.bfloat16),
        pltpu.VMEM((2, width, columns), jnp.bfloat16),
        pltpu.VMEM((width, columns), jnp.bfloat16),
        pltpu.SemaphoreType.DMA((6,)),
    ]


class Owned:
    def __init__(self, blocks, refs):
        group, self.share = lax.axis_index("dp"), lax.axis_index("vocab")
        self.high, self.low, self.far, self.near = line_places(group)
        self.pair, self.place = pair_of(group, self.share)
        self.blocks = blocks
        self.pair_in, self.near_in, self.far_in, self.sems = refs

    def begin(self):
        source = self.blocks.at[:, :, 1 - self.place]
        self.zero = send(source, self.pair_in, self.sems.at[0], self.sems.at[1], self.pair)

    def beside(self):
        self.zero.wait()
        self.blocks[:, :, self.place] = lowered(
            self.blocks[:, :, self.place].astype(jnp.float32) + self.pair_in[...].astype(jnp.float32)
        )
        self.one = send(
            self.blocks.at[:, 1 - self.low, self.place],
            self.near_in,
            self.sems.at[2],
            self.sems.at[3],
            (self.near, self.share),
        )

    def beyond(self):
        self.one.wait()
        self.blocks[:, self.low, self.place] = lowered(
            self.blocks[:, self.low, self.place].astype(jnp.float32)
            + self.near_in[...].astype(jnp.float32)
        )
        self.two = send(
            self.blocks.at[1 - self.high, self.low, self.place],
            self.far_in,
            self.sems.at[4],
            self.sems.at[5],
            (self.far, self.share),
        )

    def finish(self):
        self.two.wait()
        return lowered(
            self.blocks[self.high, self.low, self.place].astype(jnp.float32)
            + self.far_in[...].astype(jnp.float32)
        )


class Late:
    def __init__(self, source, buffer, sem):
        self.copy, self.buffer, self.waiting = pltpu.make_async_copy(source, buffer, sem), buffer, True
        self.copy.start()

    def __call__(self):
        if self.waiting:
            self.copy.wait()
            self.waiting = False
        return self.buffer


class ShareGather:
    def __init__(self, target_ref, sems):
        _, self.share, _, self.core_peer, self.side_peer = places()
        self.target, self.sems = target_ref, sems
        block = target_ref.at[self.share]
        self.one = send(block, block, sems.at[0, 0], sems.at[1, 0], self.side_peer)

    def middle(self):
        self.one.wait()
        both = [self.target.at[index] for index in (self.share, self.side_peer[1])]
        self.two = [
            send(block, block, self.sems.at[0, 1 + step], self.sems.at[1, 1 + step], self.core_peer)
            for step, block in enumerate(both)
        ]

    def finish(self):
        for copy in self.two:
            copy.wait()


def in_vmem(count, at_rest=()):
    return [
        pl.BlockSpec(memory_space=pl.ANY if index in at_rest else pltpu.VMEM)
        for index in range(count)
    ]


def call(kernel, name, number, inputs, out_shape, scratch, flops, rest_in=(), rest_out=()):
    moved = sum(math.prod(member.shape) * member.dtype.itemsize for member in (*inputs, *out_shape))
    return pl.pallas_call(
        kernel,
        out_shape=tuple(out_shape),
        in_specs=in_vmem(len(inputs), rest_in),
        out_specs=tuple(in_vmem(len(out_shape), rest_out)),
        scratch_shapes=scratch,
        compiler_params=pltpu.CompilerParams(
            collective_id=number, has_side_effects=True, vmem_limit_bytes=VMEM_BYTES
        ),
        cost_estimate=pl.CostEstimate(flops=flops, bytes_accessed=moved, transcendentals=0),
        name=name,
    )(*inputs)


def shape_of(shape, dtype):
    return jax.ShapeDtypeStruct(shape, dtype)


def head_slice(ref, start, index):
    low = start + index * HEAD_DIM
    return ref[:, low : low + HEAD_DIM]


def masked_scores(query, key, causal):
    scores = times_transposed(query, key) * HEAD_DIM ** (-0.5)
    if causal:
        down = lax.broadcasted_iota(jnp.int32, scores.shape, 0)
        across = lax.broadcasted_iota(jnp.int32, scores.shape, 1)
        scores = jnp.where(down >= across, scores, -1e30)
    return scores


def heads_forward(q_ref, kv_ref, starts, context_ref, logs_ref, causal):
    q_start, k_start, v_start = starts
    for index in range(context_ref.shape[1] // HEAD_DIM):
        query = head_slice(q_ref, q_start, index)
        key = head_slice(kv_ref, k_start, index)
        value = head_slice(kv_ref, v_start, index)
        scores = masked_scores(query, key, causal)
        row_top = jnp.max(scores, axis=-1, keepdims=True)
        exponent = jnp.exp(scores - row_top)
        row_total = jnp.sum(exponent, axis=-1, keepdims=True)
        context = lowered(matmul(lowered(exponent / row_total), value))
        context_ref[:, index * HEAD_DIM : (index + 1) * HEAD_DIM] = context
        logs_ref[:, index : index + 1] = row_top + jnp.log(row_total)


def heads_backward(q_ref, kv_ref, starts, logs_ref, grad_ref, gq_ref, gkv_ref, g_starts, causal):
    q_start, k_start, v_start = starts
    gq_start, gk_start, gv_start = g_starts
    scale = HEAD_DIM ** (-0.5)
    for index in range(grad_ref.shape[1] // HEAD_DIM):
        low, high = index * HEAD_DIM, (index + 1) * HEAD_DIM
        query = head_slice(q_ref, q_start, index)
        key = head_slice(kv_ref, k_start, index)
        value = head_slice(kv_ref, v_start, index)
        grad = grad_ref[:, low:high]
        softmax_out = jnp.exp(
            masked_scores(query, key, causal) - logs_ref[:, index : index + 1]
        )
        gkv_ref[:, gv_start + low : gv_start + high] = lowered(
            contract_rows(lowered(softmax_out), grad)
        )
        grad_softmax = times_transposed(grad, value)
        inner = jnp.sum(grad_softmax * softmax_out, axis=-1, keepdims=True)
        grad_scores = lowered(softmax_out * (grad_softmax - inner))
        gq_ref[:, gq_start + low : gq_start + high] = lowered(matmul(grad_scores, key) * scale)
        gkv_ref[:, gk_start + low : gk_start + high] = lowered(
            contract_rows(grad_scores, query) * scale
        )


def norm_backward(grad_out, saved_parts, gain_row):
    normed, scale_inv = saved_parts
    grad_normed = grad_out * gain_row
    grad_in = scale_inv * (
        grad_normed
        - jnp.mean(grad_normed, axis=-1, keepdims=True)
        - normed * jnp.mean(grad_normed * normed, axis=-1, keepdims=True)
    )
    return (
        grad_in,
        jnp.sum(grad_out * normed, axis=0, keepdims=True),
        jnp.sum(grad_out, axis=0, keepdims=True),
    )


def gain_of(norms_ref, row):
    return norms_ref[row : row + 1, :], norms_ref[row + 7 : row + 8, :]


def stream_of(looked_ref, start, place_ref):
    rows, width = place_ref.shape
    looked = looked_ref[start : start + rows, :].astype(jnp.float32)
    return looked * math.sqrt(width) + place_ref[...]


def first_kernel(
    groups, shares, start, first_wide,
    looked_ref, place_enc_ref, place_dec_ref, w_ref, across_ref,
    qkv_enc_ref, context_enc_ref, logs_enc_ref, stream_enc_ref,
    qkv_dec_ref, context_dec_ref, logs_dec_ref, stream_dec_ref,
    out_rows_ref, norms_ref, table_ref,
    table_sems, blocks_ref, block_sems, local_sem, *total_refs,
):
    group, share, _, _, _ = places()
    peers = share_peers(group, share, shares)
    meet(peers + group_peers(group, share, groups))
    chunk, columns = across_ref.shape[1] // groups, table_ref.shape[2]
    exchange = Exchange(
        table_blocks(across_ref, chunk, start, columns), table_ref, table_sems, groups
    )
    _, rows, wide = blocks_ref.shape
    own = qkv_enc_ref.shape[1] // 3
    padded = first_wide - wide
    enc_start, dec_start, out_start = 0, padded // 2, padded
    window = pl.ds(out_start, wide)
    copies = []
    for step, (_, peer) in enumerate(peers):
        source = w_ref.at[pl.ds(pl.multiple_of(peer * rows, 64), rows), window]
        copies.append(
            send(source, blocks_ref.at[share], block_sems.at[0, step], block_sems.at[1, step], (group, peer))
        )
    keep = pltpu.make_async_copy(
        w_ref.at[pl.ds(pl.multiple_of(share * rows, 64), rows), window], blocks_ref.at[share], local_sem
    )
    keep.start()

    turned = jnp.transpose(w_ref[:, first_wide - 128 : first_wide].astype(jnp.float32))
    norms_ref[...] = turned[64:80]

    enc_total, dec_total = Total(total_refs[:4]), Total(total_refs[4:])
    enc_len, dec_len = place_enc_ref.shape[0], place_dec_ref.shape[0]
    stream = stream_of(looked_ref, 0, place_enc_ref)
    normed, _ = norm_forward(stream, *gain_of(norms_ref, 0))
    qkv_enc_ref[...] = lowered(matmul(lowered(normed), w_ref[:, enc_start : enc_start + 3 * own]))
    stream_enc_ref[...] = stream
    starts = (0, own, 2 * own)
    logs_enc_ref[...] = jnp.zeros_like(logs_enc_ref)
    heads_forward(qkv_enc_ref, qkv_enc_ref, starts, context_enc_ref, logs_enc_ref, False)
    keep.wait()
    for copy in copies:
        copy.wait()
    for matrix in range(3):
        for piece in range(shares):
            out_rows_ref[matrix, :, piece * own : (piece + 1) * own] = blocks_ref[
                piece, :, matrix * own : (matrix + 1) * own
            ]
    enc_total.begin(matmul(context_enc_ref[...], out_rows_ref[0]))
    stream = stream_of(looked_ref, enc_len, place_dec_ref)
    stream_dec_ref[...] = stream
    normed, _ = norm_forward(stream, *gain_of(norms_ref, 3))
    enc_total.middle()
    qkv_dec_ref[...] = lowered(matmul(lowered(normed), w_ref[:, dec_start : dec_start + 3 * own]))
    logs_dec_ref[...] = jnp.zeros_like(logs_dec_ref)
    heads_forward(qkv_dec_ref, qkv_dec_ref, starts, context_dec_ref, logs_dec_ref, True)
    enc_total.last()
    dec_total.begin(matmul(context_dec_ref[...], out_rows_ref[1]))
    dec_total.middle()
    stream_enc_ref[...] += enc_total.finish()
    dec_total.last()
    stream_dec_ref[...] += dec_total.finish()
    exchange.finish()


def enc_feed_kernel(
    groups, start, first_wide,
    stream_in_ref, norms_ref, w_early_ref, across_ref,
    pre_ref, stream_ref, memory_ref, table_ref,
    table_sems, w_ref, w_sem, *total_refs,
):
    group, share, _, core_peer, side_peer = places()
    load = Late(w_early_ref.at[:, pl.ds(first_wide, w_ref.shape[1])], w_ref, w_sem)
    meet([core_peer, side_peer] + group_peers(group, share, groups))
    chunk, columns = across_ref.shape[1] // groups, table_ref.shape[2]
    exchange = Exchange(
        table_blocks(across_ref, chunk, start, columns), table_ref, table_sems, groups
    )
    width = stream_in_ref.shape[1]
    total = Total(total_refs)
    normed, _ = norm_forward(stream_in_ref[...], *gain_of(norms_ref, 1))
    hidden = w_ref.shape[1] - width
    load()
    pre_ref[...] = matmul(lowered(normed), w_ref[:, :hidden])
    activated = lowered(jax.nn.silu(pre_ref[...]))
    total.begin(matmul(activated, w_ref[:, hidden:]))
    stream_ref[...] = stream_in_ref[...] + total.rest()
    memory, _ = norm_forward(stream_ref[...], *gain_of(norms_ref, 2))
    memory_ref[...] = lowered(memory)
    exchange.finish()


def dec_kernel(
    groups, start,
    stream_in_ref, memory_ref, norms_ref, w_ref, out_rows_ref, positions_ref, across_ref,
    q_ref, kv_ref, context_ref, logs_ref, stream_mid_ref, pre_ref, stream_ref, selected_ref, table_ref,
    own_ref, select_sems, table_sems, *total_refs,
):
    group, share, _, core_peer, side_peer = places()
    peers = group_peers(group, share, groups)
    meet([core_peer, side_peer] + peers)
    chunk, columns = across_ref.shape[1] // groups, table_ref.shape[2]
    exchange = Exchange(
        table_blocks(across_ref, chunk, start, columns), table_ref, table_sems, groups
    )
    width = stream_in_ref.shape[1]
    own = q_ref.shape[1]
    hidden = pre_ref.shape[1]
    in_start = hidden + width
    cross_total, feed_total = Total(total_refs[:4]), Total(total_refs[4:])
    kv_ref[...] = lowered(matmul(memory_ref[...], w_ref[:, in_start + own : in_start + 3 * own]))
    normed, _ = norm_forward(stream_in_ref[...], *gain_of(norms_ref, 4))
    q_ref[...] = lowered(matmul(lowered(normed), w_ref[:, in_start : in_start + own]))
    logs_ref[...] = jnp.zeros_like(logs_ref)
    heads_forward(q_ref, kv_ref, (0, 0, own), context_ref, logs_ref, False)
    cross_total.begin(matmul(context_ref[...], out_rows_ref[2]))
    stream_mid_ref[...] = stream_in_ref[...] + cross_total.rest()
    normed, _ = norm_forward(stream_mid_ref[...], *gain_of(norms_ref, 5))
    pre_ref[...] = matmul(lowered(normed), w_ref[:, :hidden])
    activated = lowered(jax.nn.silu(pre_ref[...]))
    feed_total.begin(matmul(activated, w_ref[:, hidden : hidden + width]))
    stream_ref[...] = stream_mid_ref[...] + feed_total.rest()
    final, _ = norm_forward(stream_ref[...], *gain_of(norms_ref, 6))
    places_down = lax.broadcasted_iota(jnp.int32, (own_ref.shape[0], stream_ref.shape[0]), 1)
    chosen = lowered(jnp.where(places_down == positions_ref[...], 1.0, 0.0))
    own_ref[...] = lowered(matmul(chosen, lowered(final)))
    selected_ref[group] = own_ref[...]
    copies = [
        send(own_ref, selected_ref.at[group], select_sems.at[0, step], select_sems.at[1, step], peer)
        for step, peer in enumerate(peers)
    ]
    exchange.finish()
    for copy in copies:
        copy.wait()


def combine_stats(stats):
    row_max = stats[0][0:1]
    for member in stats[1:]:
        row_max = jnp.maximum(row_max, member[0:1])
    exp_total = smooth = target = 0.0
    for member in stats:
        exp_total = exp_total + member[1:2] * jnp.exp(member[0:1] - row_max)
        smooth = smooth + member[2:3]
        target = target + member[3:4]
    return row_max, exp_total, smooth, target


def head_kernel(
    groups, shares, shard_rows,
    selected_ref, zero_ref, one_ref, two_ref, three_ref, targets_ref, weights_ref, counted_ref,
    loss_ref, grad_out_ref, head_ref,
    logits_ref, dz_ref, stats_ref, turned_ref, share_stats_ref, group_stats_ref, stat_sems,
    part_ref, core_ref, side_ref, group_ref, sum_ref, sems,
):
    group, share, core, core_peer, side_peer = places()
    side = share // 2
    near, far = share_peers(group, share, shares), group_peers(group, share, groups)
    meet(near + far)
    rows, width = selected_ref.shape
    chunk = logits_ref.shape[1]
    tables = (zero_ref, one_ref, two_ref, three_ref)
    starts = np.cumsum([0] + [ref.shape[1] for ref in tables])
    vocab_total = shard_rows * shares
    first = group * chunk
    limit = jnp.minimum(shard_rows - first, vocab_total - 1 - share * shard_rows - first)
    block = 384
    step_rows = 32

    for ref, start in zip(tables, starts):
        step = 512 if ref.shape[1] % 512 == 0 else 384
        for low in range(0, ref.shape[1], step):
            logits_ref[:, start + low : start + low + step] = matmul(
                selected_ref[...], ref[:, low : low + step]
            )
    stats_ref[...] = jnp.zeros_like(stats_ref)

    def gather_stats(step, carry):
        at = pl.ds(pl.multiple_of(step * step_rows, step_rows), step_rows)
        logits = logits_ref[at, :]
        column = lax.broadcasted_iota(jnp.int32, logits.shape, 1)
        real = column < limit
        masked = jnp.where(real, logits, -1e30)
        top = jnp.max(masked, axis=1, keepdims=True)
        stats_ref[at, 0:1] = top
        stats_ref[at, 1:2] = jnp.sum(jnp.exp(masked - top), axis=1, keepdims=True)
        stats_ref[at, 2:3] = jnp.sum(jnp.where(real, logits, 0.0), axis=1, keepdims=True)
        hit = column == targets_ref[at, :]
        stats_ref[at, 3:4] = jnp.sum(jnp.where(hit, logits, 0.0), axis=1, keepdims=True)
        return carry

    lax.fori_loop(0, rows // step_rows, gather_stats, 0)
    share_stats_ref[share] = jnp.transpose(stats_ref[...])[0:8]
    copies = [
        send(share_stats_ref.at[share], share_stats_ref.at[share], stat_sems.at[0, step], stat_sems.at[1, step], peer)
        for step, peer in enumerate(near)
    ]
    for copy in copies:
        copy.wait()
    merged = combine_stats([share_stats_ref[index] for index in range(shares)])
    group_stats_ref[group] = jnp.concatenate(merged + (jnp.zeros((4, rows), jnp.float32),), axis=0)
    copies = [
        send(group_stats_ref.at[group], group_stats_ref.at[group], stat_sems.at[2, step], stat_sems.at[3, step], peer)
        for step, peer in enumerate(far)
    ]
    for copy in copies:
        copy.wait()
    row_max, exp_total, smooth, target = combine_stats(
        [group_stats_ref[index] for index in range(groups)]
    )
    log_total = row_max + jnp.log(exp_total)
    per_row = log_total - (1.0 - SMOOTH) * target - SMOOTH * smooth / (vocab_total - 1)
    loss = jnp.sum(counted_ref[...] * per_row, axis=1, keepdims=True)
    loss_ref[...] = jnp.broadcast_to(loss, loss_ref.shape)
    turned_ref[...] = jnp.zeros_like(turned_ref)
    turned_ref[0:1, :] = log_total
    stats_ref[...] = jnp.transpose(turned_ref[...])

    def make_dz(step, carry):
        at = pl.ds(pl.multiple_of(step * step_rows, step_rows), step_rows)
        logits = logits_ref[at, :]
        column = lax.broadcasted_iota(jnp.int32, logits.shape, 1)
        softmax_rows = jnp.exp(logits - stats_ref[at, 0:1])
        hit = jnp.where(column == targets_ref[at, :], 1.0 - SMOOTH, 0.0)
        grad = weights_ref[at, :] * (softmax_rows - hit - SMOOTH / (vocab_total - 1))
        dz_ref[at, :] = lowered(jnp.where(column < limit, grad, 0.0))
        return carry

    lax.fori_loop(0, rows // step_rows, make_dz, 0)
    loss_rows = rows // groups
    half, quarter = loss_rows // 2, loss_rows // 4
    grad_rows = 0.0
    for ref, start in zip(tables, starts):
        grad_rows = grad_rows + times_transposed(dz_ref[:, start : start + ref.shape[1]], ref[...])
    part_ref[...] = lowered(grad_rows).reshape(part_ref.shape)
    mine = pl.ds(pl.multiple_of(core * half, 16), half)
    other = pl.ds(pl.multiple_of((1 - core) * half, 16), half)
    copy = send(part_ref.at[:, other, :], core_ref, sems.at[0, 0], sems.at[1, 0], core_peer)

    def head_part(index):
        at = slice(index * block, (index + 1) * block)
        head_ref[:, at] = lowered(contract_rows(selected_ref[...], dz_ref[:, at]))

    parts = chunk // block
    head_part(0)
    copy.wait()
    part_ref[:, mine, :] = lowered(
        part_ref[:, mine, :].astype(jnp.float32) + core_ref[...].astype(jnp.float32)
    )
    base = core * half
    my_quarter = pl.ds(pl.multiple_of(base + side * quarter, 16), quarter)
    other_quarter = pl.ds(pl.multiple_of(base + (1 - side) * quarter, 16), quarter)
    copy = send(part_ref.at[:, other_quarter, :], side_ref, sems.at[0, 1], sems.at[1, 1], side_peer)
    for index in range(1, parts // 2):
        head_part(index)
    copy.wait()
    side_ref[...] = lowered(
        part_ref[:, my_quarter, :].astype(jnp.float32) + side_ref[...].astype(jnp.float32)
    )
    group_ref[group] = side_ref[group]
    copies = [
        send(side_ref.at[peer[0]], group_ref.at[group], sems.at[0, 2 + step], sems.at[1, 2 + step], peer)
        for step, peer in enumerate(far)
    ]
    for index in range(parts // 2, parts):
        head_part(index)
    for copy in copies:
        copy.wait()
    summed = group_ref[0].astype(jnp.float32)
    for index in range(1, groups):
        summed = summed + group_ref[index].astype(jnp.float32)
    sum_ref[...] = lowered(summed)
    grad_out_ref[my_quarter, :] = sum_ref[...]
    base_sem = 1 + groups
    copies = [
        send(sum_ref, grad_out_ref.at[my_quarter, :], sems.at[0, base_sem + step], sems.at[1, base_sem + step], peer)
        for step, peer in enumerate(near)
    ]
    for copy in copies:
        copy.wait()


def put_grads(grads_ref, start, value):
    shape = grads_ref.shape[:4] + (value.shape[1],)
    grads_ref[:, :, :, :, start : start + value.shape[1]] = lowered(value).reshape(shape)


def feed_grads(grad_ref, stream_ref, pre_ref, norms_ref, row, w_ref, grads_ref, total):
    width = stream_ref.shape[1]
    hidden = pre_ref.shape[1]
    normed, _ = norm_forward(stream_ref[...], *gain_of(norms_ref, row))
    grad_low = lowered(grad_ref[...])
    pre = pre_ref[...]
    sigmoid_pre = jax.nn.sigmoid(pre)
    grad_pre = lowered(
        times_transposed(grad_low, w_ref[:, hidden : hidden + width])
        * sigmoid_pre
        * (1.0 + pre * (1.0 - sigmoid_pre))
    )
    total.begin(times_transposed(grad_pre, w_ref[:, :hidden]))
    activated = lowered(pre * sigmoid_pre)
    put_grads(grads_ref, hidden, contract_rows(activated, grad_low))
    total.middle()
    put_grads(grads_ref, 0, contract_rows(lowered(normed), grad_pre))


def norm_step(grad_ref, stream_ref, norms_ref, row, summed, rows_ref, slot):
    gain, shift = gain_of(norms_ref, row)
    _, kept = norm_forward(stream_ref[...], gain, shift)
    grad_in, grad_gain, grad_shift = norm_backward(summed, kept, gain)
    rows_ref[slot : slot + 1, :] = grad_gain
    rows_ref[slot + 1 : slot + 2, :] = grad_shift
    if grad_ref is None:
        return grad_in
    return grad_ref[...] + grad_in


def back_kernel(
    groups, shares, first_wide, norm_start, norm_count, refs_in, refs_out, *refs
):
    inputs, outputs, scratch = refs[:refs_in], refs[refs_in : refs_in + refs_out], refs[refs_in + refs_out :]
    (
        grad_selected_ref, positions_ref, stream_out_ref, stream_mid_ref, pre_dec_ref, norms_ref, w_dec_hbm,
        out_rows_hbm, memory_hbm, stream_dec_hbm, q_ref, kv_ref, context_cross_ref, logs_cross_ref,
        stream_two_hbm, stream_enc_hbm, pre_enc_hbm, w_early_hbm, looked_hbm, place_enc_hbm, place_dec_ref,
        qkv_dec_ref, context_dec_ref, logs_dec_ref, qkv_enc_ref, context_enc_ref, logs_enc_ref,
        head_in_ref,
    ) = inputs
    head_out_ref, own_tokens_ref, dec_shares_ref, own_ref, squares_ref = outputs
    (
        head_sems, load_sems, w_ref, w_enc_ref, out_rows_ref, memory_ref, stream_dec_ref, stream_two_ref,
        stream_enc_ref, pre_enc_ref, looked_ref,
        dec_grads_ref, mid_grads_ref, last_grads_ref,
        grad_ref, grad_enc_ref,
        context_ref, gq_ref, gkv_ref, gqkv_ref, gqkv_enc_ref, context_enc_grad_ref,
        g_enc_ref, g_self_ref, g_cross_ref, rows_dec_ref, rows_mid_ref, rows_ref,
        norm_rows_ref, turned_ref, blocks_ref, block_sems, cut_ref, token_sems, share_sems, dec_sems, dec_own_ref,
        local_sems,
    ) = scratch[:38]
    rest = scratch[38:]
    stream_ref = pre_enc_ref
    small_one, large_one = rest[:4], rest[4:8]
    small_two, large_two = small_one[:1] + rest[8:11], large_one[:1] + rest[11:14]
    dec_line = Owned(dec_grads_ref, rest[14:18])
    mid_line = Owned(mid_grads_ref, rest[18:22])
    last_line = Owned(last_grads_ref, rest[22:26])
    group, share, core, core_peer, side_peer = places()
    peers = share_peers(group, share, shares)
    load_w_dec = Late(w_dec_hbm, w_ref, load_sems.at[0])
    load_rows = Late(out_rows_hbm, out_rows_ref, load_sems.at[1])
    load_memory = Late(memory_hbm, memory_ref, load_sems.at[2])
    load_dec = Late(stream_dec_hbm, stream_dec_ref, load_sems.at[3])
    load_two = Late(stream_two_hbm, stream_two_ref, load_sems.at[4])
    load_enc = Late(stream_enc_hbm, stream_enc_ref, load_sems.at[5])
    load_pre = Late(pre_enc_hbm, pre_enc_ref, load_sems.at[6])
    load_w_enc = Late(
        w_early_hbm.at[:, pl.ds(first_wide, w_enc_ref.shape[1])], w_enc_ref, load_sems.at[7]
    )
    load_looked = Late(looked_hbm, looked_ref, load_sems.at[8])
    meet(peers + group_peers(group, share, groups))
    exchange = Exchange(
        head_blocks(head_in_ref, 0, head_out_ref.shape[2]), head_out_ref, head_sems, groups
    )
    width = stream_out_ref.shape[1]
    own = q_ref.shape[1]
    hidden = pre_dec_ref.shape[1]
    in_start = hidden + width
    starts = (0, own, 2 * own)
    for rows in (rows_dec_ref, rows_mid_ref, rows_ref):
        rows[...] = jnp.zeros_like(rows)

    total = Total(small_one)
    down = lax.broadcasted_iota(jnp.int32, (stream_out_ref.shape[0], grad_selected_ref.shape[0]), 0)
    chosen = lowered(jnp.where(down == positions_ref[...], 1.0, 0.0))
    grad_final = matmul(chosen, grad_selected_ref[...])
    grad_ref[...] = norm_step(None, stream_out_ref, norms_ref, 6, grad_final, rows_dec_ref, 0)
    load_w_dec()
    feed_grads(grad_ref, stream_mid_ref, pre_dec_ref, norms_ref, 5, w_ref, dec_grads_ref, total)
    total.last()
    grad_ref[...] = norm_step(
        grad_ref, stream_mid_ref, norms_ref, 5, total.finish(), rows_dec_ref, 2
    )

    cross_total, memory_total = Total(small_two), Total(large_one)
    grad_low = lowered(grad_ref[...])
    load_rows()
    context_ref[...] = lowered(times_transposed(grad_low, out_rows_ref[2]))
    heads_backward(
        q_ref, kv_ref, (0, 0, own), logs_cross_ref, context_ref, gq_ref, gkv_ref, (0, 0, own), False
    )
    memory_total.begin(
        times_transposed(gkv_ref[...], w_ref[:, in_start + own : in_start + 3 * own])
    )
    cross_total.begin(times_transposed(gq_ref[...], w_ref[:, in_start : in_start + own]))
    load_w_first = Late(
        w_early_hbm.at[:, pl.ds(0, first_wide)], w_ref.at[:, pl.ds(0, first_wide)], load_sems.at[9]
    )
    g_cross_ref[...] = lowered(contract_rows(context_cross_ref[...], grad_low))
    memory_total.middle()
    cross_total.middle()
    load_dec()
    load_memory()
    normed, _ = norm_forward(stream_dec_ref[...], *gain_of(norms_ref, 4))
    gap = dec_grads_ref.shape[4] - in_start - 3 * own
    put_grads(dec_grads_ref, in_start, contract_rows(lowered(normed), gq_ref[...]))
    put_grads(dec_grads_ref, in_start + own, contract_rows(memory_ref[...], gkv_ref[...]))
    put_grads(dec_grads_ref, in_start + 3 * own, jnp.zeros((width, gap), jnp.float32))
    dec_line.begin()
    memory_total.last()
    cross_total.last()
    summed = memory_total.finish()
    load_two()
    grad_enc_ref[...] = norm_step(None, stream_two_ref, norms_ref, 2, summed, rows_mid_ref, 0)
    load_place = Late(place_enc_hbm, stream_two_ref, load_sems.at[10])
    grad_ref[...] = norm_step(
        grad_ref, stream_dec_ref, norms_ref, 4, cross_total.finish(), rows_dec_ref, 4
    )

    feed_total, self_total = Total(large_two), Total(small_one)
    load_enc()
    load_pre()
    load_w_enc()
    feed_grads(
        grad_enc_ref, stream_enc_ref, pre_enc_ref, norms_ref, 1, w_enc_ref, mid_grads_ref, feed_total
    )
    grad_low = lowered(grad_ref[...])
    context_ref[...] = lowered(times_transposed(grad_low, out_rows_ref[1]))
    feed_total.last()
    heads_backward(
        qkv_dec_ref, qkv_dec_ref, starts, logs_dec_ref, context_ref, gqkv_ref, gqkv_ref, starts, True
    )
    load_w_first()
    w_start = first_wide // 3
    self_total.begin(times_transposed(gqkv_ref[...], w_ref[:, w_start : w_start + 3 * own]))
    g_self_ref[...] = lowered(contract_rows(context_dec_ref[...], grad_low))
    self_total.middle()
    load_looked()
    enc_len = stream_enc_ref.shape[0]
    stream_dec_ref[...] = stream_of(looked_ref, enc_len, place_dec_ref)
    normed, _ = norm_forward(stream_dec_ref[...], *gain_of(norms_ref, 3))
    put_grads(mid_grads_ref, in_start, contract_rows(lowered(normed), gqkv_ref[...]))
    put_grads(mid_grads_ref, in_start + 3 * own, jnp.zeros((width, gap), jnp.float32))
    mid_line.begin()
    grad_enc_ref[...] = norm_step(
        grad_enc_ref, stream_enc_ref, norms_ref, 1, feed_total.finish(), rows_mid_ref, 2
    )
    self_total.last()
    tokens = cut_ref.shape[1]
    part = cut_ref.shape[2]
    grad_dec = norm_step(
        grad_ref, stream_dec_ref, norms_ref, 3, self_total.finish(), rows_mid_ref, 4
    )
    grad_low = lowered(grad_dec * math.sqrt(width))
    for index in range(groups):
        cut_ref[index, enc_len:tokens] = grad_low[:, index * part : (index + 1) * part]

    total = Total(large_one)
    grad_low = lowered(grad_enc_ref[...])
    context_enc_grad_ref[...] = lowered(times_transposed(grad_low, out_rows_ref[0]))
    heads_backward(
        qkv_enc_ref, qkv_enc_ref, starts, logs_enc_ref, context_enc_grad_ref, gqkv_enc_ref, gqkv_enc_ref, starts,
        False,
    )
    total.begin(times_transposed(gqkv_enc_ref[...], w_ref[:, : 3 * own]))
    dec_line.beside()
    g_enc_ref[...] = lowered(contract_rows(context_enc_ref[...], grad_low))
    total.middle()
    load_place()
    stream_ref[...] = stream_of(looked_ref, 0, stream_two_ref)
    normed, _ = norm_forward(stream_ref[...], *gain_of(norms_ref, 0))
    wide = blocks_ref.shape[2]
    in_wide = last_grads_ref.shape[4] - wide
    put_grads(last_grads_ref, 0, contract_rows(lowered(normed), gqkv_enc_ref[...]))
    put_grads(last_grads_ref, 3 * own, jnp.zeros((width, in_wide - 3 * own), jnp.float32))
    blocks_ref[...] = jnp.zeros_like(blocks_ref)
    for piece in range(shares):
        at = slice(piece * own, (piece + 1) * own)
        for matrix, source in enumerate((g_enc_ref, g_self_ref, g_cross_ref)):
            blocks_ref[piece, :, matrix * own : (matrix + 1) * own] = source[:, at]
    total.last()
    grad_enc = norm_step(grad_enc_ref, stream_ref, norms_ref, 0, total.finish(), rows_ref, 0)
    grad_low = lowered(grad_enc * math.sqrt(width))
    for index in range(groups):
        cut_ref[index, 0:enc_len] = grad_low[:, index * part : (index + 1) * part]
    quarter = tokens // shares
    own_rows = pl.ds(pl.multiple_of(share * quarter, 64), quarter)
    to_groups = Exchange(
        lambda index: cut_ref.at[index, own_rows, :], own_tokens_ref.at[share], token_sems, groups
    )
    norm_rows_ref[...] = jnp.zeros_like(norm_rows_ref)
    order = (
        (0, rows_ref, 0),
        (1, rows_mid_ref, 2),
        (2, rows_mid_ref, 0),
        (3, rows_mid_ref, 4),
        (4, rows_dec_ref, 4),
        (5, rows_dec_ref, 2),
        (6, rows_dec_ref, 0),
    )
    for row, source, slot in order:
        norm_rows_ref[64 + row : 65 + row, :] = source[slot : slot + 1, :]
        norm_rows_ref[71 + row : 72 + row, :] = source[slot + 1 : slot + 2, :]
    turned_ref[...] = jnp.transpose(norm_rows_ref[...])
    own_norms = turned_ref[pl.ds(pl.multiple_of(share * own, 64), own), :]
    for piece in range(shares):
        tail = blocks_ref[piece, :, wide - 128 :].astype(jnp.float32)
        blocks_ref[piece, :, wide - 128 :] = lowered(tail + own_norms)
    copies = []
    for half in range(2):
        target = last_grads_ref.at[share // 2, lax.rem(share, 2), half, :, pl.ds(in_wide, wide)]
        source_rows = pl.ds(half * part, part)
        for step, peer in enumerate(peers):
            copies.append(
                send(
                    blocks_ref.at[peer[1], source_rows, :],
                    target,
                    block_sems.at[half, 0, step],
                    block_sems.at[half, 1, step],
                    peer,
                )
            )
        keep = pltpu.make_async_copy(
            blocks_ref.at[share, source_rows, :], target, local_sems.at[half]
        )
        keep.start()
        copies.append(keep)
    for copy in copies:
        copy.wait()
    last_line.begin()
    mid_line.beside()
    dec_line.beyond()
    to_groups.finish()
    token_gather = ShareGather(own_tokens_ref, share_sems)
    last_line.beside()
    mid_line.beyond()
    dec_own_ref[...] = dec_line.finish()
    keep = pltpu.make_async_copy(dec_own_ref, dec_shares_ref.at[share], local_sems.at[2])
    keep.start()
    keep.wait()
    dec_gather = ShareGather(dec_shares_ref, dec_sems)
    token_gather.middle()
    last_line.beyond()
    middle = mid_grads_ref.shape[4]
    own_ref[:, :middle] = mid_line.finish()
    dec_gather.middle()
    token_gather.finish()
    own_ref[:, middle:] = last_line.finish()
    squares = 0.0
    for ref in (dec_own_ref, own_ref):
        value = ref[...].astype(jnp.float32)
        value = value * value
        if ref is own_ref:
            column = lax.broadcasted_iota(jnp.int32, value.shape, 1)
            norm_part = (column >= norm_start) & (column < norm_start + norm_count)
            value = jnp.where(norm_part, value / shares, value)
        squares = squares + jnp.sum(jnp.sum(value, axis=0, keepdims=True), axis=1, keepdims=True)
    lane = lax.broadcasted_iota(jnp.int32, squares_ref.shape, 1)
    squares_ref[...] = jnp.where(lane == 0, squares, 0.0)
    dec_gather.finish()
    exchange.finish()


def look_kernel(
    groups,
    picked_ref, across_ref,
    looked_ref, table_ref,
    send_ref, core_ref, side_ref, group_ref, sems, table_sems,
):
    group, share, core, core_peer, side_peer = places()
    side = share // 2
    far = group_peers(group, share, groups)
    meet([core_peer, side_peer] + far)
    _, tokens, width = picked_ref.shape
    half, quarter = tokens // 2, tokens // 4
    mine = pl.ds(pl.multiple_of(core * half, 16), half)
    other = pl.ds(pl.multiple_of((1 - core) * half, 16), half)
    send(picked_ref.at[:, other, :], core_ref, sems.at[0, 0], sems.at[1, 0], core_peer).wait()
    core_ref[...] = core_ref[...] + picked_ref[:, mine, :]
    own_quarter = pl.ds(pl.multiple_of(side * quarter, 16), quarter)
    other_quarter = pl.ds(pl.multiple_of((1 - side) * quarter, 16), quarter)
    send(core_ref.at[:, other_quarter, :], side_ref, sems.at[0, 1], sems.at[1, 1], side_peer).wait()
    side_ref[...] = side_ref[...] + core_ref[:, own_quarter, :]
    group_ref[group] = side_ref[group]
    copies = [
        send(side_ref.at[peer[0]], group_ref.at[group], sems.at[0, 2 + step], sems.at[1, 2 + step], peer)
        for step, peer in enumerate(far)
    ]
    for copy in copies:
        copy.wait()
    chunk, columns = across_ref.shape[1] // groups, table_ref.shape[2]
    exchange = Exchange(
        table_blocks(across_ref, chunk, 0, columns), table_ref, table_sems, groups
    )
    for index in range(groups):
        send_ref[:, index * width : (index + 1) * width] = group_ref[index]
    at = pl.ds(pl.multiple_of(core * half + side * quarter, 16), quarter)
    looked_ref[at, :] = send_ref[...]
    end = 1 + groups
    send(send_ref, looked_ref.at[at, :], sems.at[0, end], sems.at[1, end], side_peer).wait()
    end = end + 1
    both = looked_ref.at[mine, :]
    send(both, both, sems.at[0, end], sems.at[1, end], core_peer).wait()
    exchange.finish()


def squares_kernel(
    groups, shares,
    embedding_ref, dense_ref,
    out_ref,
    share_ref, group_ref, sems,
):
    group, share, _, _, _ = places()
    near, far = share_peers(group, share, shares), group_peers(group, share, groups)
    meet(near + far)
    down = lax.broadcasted_iota(jnp.int32, (8, 128), 0)
    share_ref[share] = jnp.where(down == 0, embedding_ref[...] + dense_ref[...], 0.0)
    copies = [
        send(share_ref.at[share], share_ref.at[share], sems.at[0, step], sems.at[1, step], peer)
        for step, peer in enumerate(near)
    ]
    for copy in copies:
        copy.wait()
    summed = share_ref[0]
    for index in range(1, shares):
        summed = summed + share_ref[index]
    group_ref[group] = summed
    copies = [
        send(group_ref.at[group], group_ref.at[group], sems.at[2, step], sems.at[3, step], peer)
        for step, peer in enumerate(far)
    ]
    for copy in copies:
        copy.wait()
    summed = group_ref[0]
    for index in range(1, groups):
        summed = summed + group_ref[index]
    out_ref[...] = jnp.broadcast_to(jnp.sum(summed), out_ref.shape)


def dense_kernel(
    rate, place_grads, factor_ref, *refs
):
    *grad_refs, w_ref, first_ref, second_ref, new_w_ref, new_first_ref, new_second_ref, wide_ref = refs
    place_grads(wide_ref, *grad_refs)
    updated = adam_update(
        w_ref[0],
        first_ref[0],
        second_ref[0],
        wide_ref[...].astype(jnp.float32),
        factor_ref[0],
        rate,
    )
    for out, value in zip((new_w_ref, new_first_ref, new_second_ref), updated):
        out[0] = value


def dense_update(name, rate, place_grads, factor, grads, w, first, second, parts):
    matrices, rows, columns = w.shape
    rows = rows // parts
    own = pl.BlockSpec((1, rows, columns), lambda matrix, part: (matrix, part, 0))
    shares, width = grads[0].shape[:2]
    grad_specs = [
        pl.BlockSpec((shares, width, member.shape[2]), lambda matrix, part: (0, 0, 0))
        for member in grads
    ]
    return pl.pallas_call(
        partial(dense_kernel, rate, place_grads),
        grid=(matrices, parts),
        out_shape=[jax.ShapeDtypeStruct(w.shape, w.dtype)] * 3,
        in_specs=[pl.BlockSpec(memory_space=pltpu.SMEM)] + grad_specs + [own] * 3,
        out_specs=[own] * 3,
        scratch_shapes=[pltpu.VMEM((rows, columns), jnp.bfloat16)],
        compiler_params=pltpu.CompilerParams(vmem_limit_bytes=VMEM_BYTES),
        name=name,
    )(factor, *grads, w, first, second)


def place_columns(groups, matrix, source_ref, start):
    def place(wide_ref):
        @pl.when(pl.program_id(0) == matrix)
        def _():
            rows, columns = wide_ref.shape
            shares = source_ref.shape[0]
            piece = columns // groups // shares
            at = pl.ds(pl.multiple_of(pl.program_id(1) * rows, 16), rows)
            for number in range(groups):
                for share in range(shares):
                    low = (number * shares + share) * piece
                    wide_ref[:, low : low + piece] = source_ref[
                        share, at, start + number * piece : start + (number + 1) * piece
                    ]

    return place


def prepare_kernel(
    groups, shares, gap,
    numbers_ref, hits_ref, in_ref, out_ref, up_ref, down_ref, norms_ref,
    all_numbers_ref, all_hits_ref, early_ref, dec_ref,
    square_ref, sems, local_sems,
):
    group, share, _, _, _ = places()
    peers = group_peers(group, share, groups)
    meet(peers)
    copies = []
    for number, (source, target) in enumerate(
        ((numbers_ref, all_numbers_ref), (hits_ref, all_hits_ref))
    ):
        copies += [
            send(source, target.at[group], sems.at[number, 0, step], sems.at[number, 1, step], peer)
            for step, peer in enumerate(peers)
        ]
        keep = pltpu.make_async_copy(source, target.at[group], local_sems.at[number])
        keep.start()
        copies.append(keep)
    width, model_width = in_ref.shape[1], out_ref.shape[2]
    own = model_width // shares
    piece = up_ref.shape[2] // groups // shares
    hidden = groups * piece
    early_ref[...] = jnp.zeros_like(early_ref)
    dec_ref[...] = jnp.zeros_like(dec_ref)

    def put(index):
        def columns(target, start, source, groups_in, size):
            step = shares * size
            for number in range(groups_in):
                low = number * step + index * size
                target[:, start + number * size : start + (number + 1) * size] = lowered(
                    source[:, low : low + size]
                )

        in_wide = 3 * own + gap
        columns(early_ref, 0, in_ref.at[0], 3, own)
        columns(early_ref, in_wide, in_ref.at[1], 3, own)
        for matrix in range(3):
            columns(early_ref, 2 * in_wide + matrix * own, out_ref.at[matrix], 1, own)
        rows = slice(index * (down_ref.shape[1] // shares), (index + 1) * (down_ref.shape[1] // shares))
        for matrix, (target, start) in enumerate(((early_ref, 3 * in_wide), (dec_ref, 0))):
            columns(target, start, up_ref.at[matrix], groups, piece)
            start = start + hidden
            target[:, start : start + model_width] = lowered(down_ref[matrix, rows, :])
        columns(dec_ref, hidden + model_width, in_ref.at[2], 3, own)

    for index in range(shares):
        pl.when(share == index)(partial(put, index))
    square_ref[...] = jnp.zeros_like(square_ref)
    square_ref[0 : norms_ref.shape[0], 0:width] = norms_ref[...]
    end = 3 * (3 * own + gap)
    early_ref[:, end - gap : end] = lowered(jnp.transpose(square_ref[...])[0:width, 0:gap])
    for copy in copies:
        copy.wait()


def local(
    enc_ids,
    labels,
    target_lengths,
    loss_positions,
    embedding,
    attn_in,
    attn_out,
    ffn_up,
    ffn_down,
    norms,
    embedding_first,
    attn_in_first,
    attn_out_first,
    ffn_up_first,
    ffn_down_first,
    norms_first,
    embedding_second,
    attn_in_second,
    attn_out_second,
    ffn_up_second,
    ffn_down_second,
    norms_second,
):
    groups, shares = lax.axis_size("dp"), lax.axis_size("vocab")
    group, share = lax.axis_index("dp"), lax.axis_index("vocab")
    enc_len, dec_len = enc_ids.shape[1], labels.shape[1]
    loss_count = loss_positions.shape[1]
    shard_rows, part_width = embedding.shape
    model_width = part_width * groups
    vocab_total = shard_rows * shares
    row_start = share * shard_rows
    root_width = math.sqrt(model_width)
    tokens = enc_len + dec_len

    bf16, f32 = jnp.bfloat16, jnp.float32
    sems = pltpu.SemaphoreType.DMA
    numbers = jnp.concatenate(
        [enc_ids, labels, loss_positions, target_lengths[:, None]], axis=1
    )
    number_count = numbers.shape[1]
    number_lanes = -(-number_count // 1024) * 128
    numbers = jnp.pad(numbers, ((0, 0), (0, 8 * number_lanes - number_count)))
    span = 1 << tokens.bit_length()
    own_tokens = jnp.concatenate([enc_ids[0], jnp.zeros((1,), jnp.int32), labels[0, :-1]])
    hits = list_hits(own_tokens - row_start, shard_rows, span)
    own = model_width // shares
    own_in, own_up = 3 * own, ffn_up.shape[2] // shares
    norm_rows = norms.shape[0]
    gap = -own_in % 128
    in_wide = own_in + gap
    dec_wide = own_up + model_width + in_wide
    first_wide = 3 * in_wide
    early_wide = first_wide + own_up + model_width
    chunk = -(-shard_rows // (groups * 3072)) * 3072
    table_cuts = (chunk // 8, chunk // 3, chunk // 6, 3 * chunk // 8)
    table_starts = np.cumsum((0,) + table_cuts).tolist()
    numbers, hits, mine_early, mine_dec = call(
        partial(prepare_kernel, groups, shares, gap),
        "prepare",
        1,
        [
            numbers.reshape(8, number_lanes), hits.reshape(8, span // 8),
            attn_in, attn_out, ffn_up, ffn_down, norms,
        ],
        [
            shape_of((groups, 8, number_lanes), jnp.int32),
            shape_of((groups, 8, span // 8), jnp.int32),
            shape_of((part_width, early_wide), bf16),
            shape_of((part_width, dec_wide), bf16),
        ],
        [pltpu.VMEM((128, 128), f32), sems((2, 2, groups - 1)), sems((2,))],
        0,
    )
    hits = hits.reshape(groups, span)
    w_early = lax.all_gather(mine_early, "dp", axis=0, tiled=True)
    w_dec = lax.all_gather(mine_dec, "dp", axis=0, tiled=True)
    numbers = numbers.reshape(groups, 8 * number_lanes)
    all_labels = numbers[:, enc_len:tokens]
    all_positions = numbers[:, tokens : tokens + loss_count]
    all_lengths = numbers[:, tokens + loss_count : number_count]
    at_place = all_positions[:, :, None] == jnp.arange(dec_len)
    all_targets = jnp.sum(jnp.where(at_place, all_labels[:, None, :], 0), axis=2).reshape(-1)
    all_counted = (all_positions < all_lengths).reshape(-1).astype(f32)
    token_count = jnp.sum(all_counted)

    picked, across = pick_rows(hits, groups * tokens, embedding.T, groups * chunk)
    looked, table_zero = call(
        partial(look_kernel, groups),
        "look",
        2,
        [picked.reshape(groups, tokens, part_width), across],
        [
            shape_of((tokens, model_width), bf16),
            shape_of((groups, part_width, table_cuts[0]), bf16),
        ],
        [
            pltpu.VMEM((tokens // 4, model_width), bf16),
            pltpu.VMEM((groups, tokens // 2, part_width), bf16),
            pltpu.VMEM((groups, tokens // 4, part_width), bf16),
            pltpu.VMEM((groups, tokens // 4, part_width), bf16),
            sems((2, groups + 3)),
            sems((2, groups)),
        ],
        0,
        (1,),
        (1,),
    )


    place_enc = positions_numpy(enc_len, model_width)
    place_dec = positions_numpy(dec_len, model_width)
    enc_macs, dec_macs = enc_len * model_width, dec_len * model_width
    total_enc, total_dec = total_scratch(enc_len, model_width), total_scratch(dec_len, model_width)
    (
        qkv_enc, context_enc, logs_enc, stream_enc,
        qkv_dec, context_dec, logs_dec, stream_dec,
        out_rows, norm_values, table_one,
    ) = call(
        partial(first_kernel, groups, shares, table_starts[1], first_wide),
        "first",
        3,
        [looked, place_enc, place_dec, w_early, across],
        [
            shape_of((enc_len, 3 * own), bf16),
            shape_of((enc_len, own), bf16),
            shape_of((enc_len, 128), f32),
            shape_of((enc_len, model_width), f32),
            shape_of((dec_len, 3 * own), bf16),
            shape_of((dec_len, own), bf16),
            shape_of((dec_len, 128), f32),
            shape_of((dec_len, model_width), f32),
            shape_of((3, own, model_width), bf16),
            shape_of((16, model_width), f32),
            shape_of((groups, part_width, table_cuts[1]), bf16),
        ],
        [
            sems((2, groups)),
            pltpu.VMEM((shares, own, in_wide), bf16),
            sems((2, shares - 1)),
            sems,
        ]
        + total_enc
        + total_dec,
        8 * (enc_macs + dec_macs) * own,
        (4,),
        (10,),
    )
    pre_enc, stream_two, memory, table_two = call(
        partial(enc_feed_kernel, groups, table_starts[2], first_wide),
        "enc_feed",
        4,
        [stream_enc, norm_values, w_early, across],
        [
            shape_of((enc_len, own_up), f32),
            shape_of((enc_len, model_width), f32),
            shape_of((enc_len, model_width), bf16),
            shape_of((groups, part_width, table_cuts[2]), bf16),
        ],
        [sems((2, groups)), pltpu.VMEM((model_width, own_up + model_width), bf16), sems] + total_enc,
        4 * enc_macs * own_up,
        (2, 3),
        (3,),
    )
    (
        q_cross, kv_cross, context_cross, logs_cross, stream_mid, pre_dec, stream_out, selected,
        table_three,
    ) = call(
        partial(dec_kernel, groups, table_starts[3]),
        "dec",
        5,
        [stream_dec, memory, norm_values, w_dec, out_rows, loss_positions.reshape(-1, 1), across],
        [
            shape_of((dec_len, own), bf16),
            shape_of((enc_len, 2 * own), bf16),
            shape_of((dec_len, own), bf16),
            shape_of((dec_len, 128), f32),
            shape_of((dec_len, model_width), f32),
            shape_of((dec_len, own_up), f32),
            shape_of((dec_len, model_width), f32),
            shape_of((groups, loss_count, model_width), bf16),
            shape_of((groups, part_width, table_cuts[3]), bf16),
        ],
        [
            pltpu.VMEM((loss_count, model_width), bf16),
            sems((2, groups - 1)),
            sems((2, groups)),
        ]
        + total_dec
        + total_dec,
        4 * dec_macs * own_up + 8 * enc_macs * own,
        (6,),
        (8,),
    )

    rows_all = groups * loss_count
    first_row = row_start + group * chunk
    targets = all_targets - first_row
    inside = (targets >= 0) & (targets < jnp.minimum(chunk, shard_rows - group * chunk))
    targets = jnp.where(inside, targets, -1)[:, None]
    loss, grad_selected, head_grad = call(
        partial(head_kernel, groups, shares, shard_rows),
        "head",
        6,
        [
            selected.reshape(rows_all, model_width),
            table_zero.reshape(model_width, -1),
            table_one.reshape(model_width, -1),
            table_two.reshape(model_width, -1),
            table_three.reshape(model_width, -1),
            targets,
            (all_counted / token_count)[:, None],
            all_counted[None, :],
        ],
        [
            shape_of((1, 128), f32),
            shape_of((loss_count, model_width), bf16),
            shape_of((model_width, chunk), bf16),
        ],
        [
            pltpu.VMEM((rows_all, chunk), f32),
            pltpu.VMEM((rows_all, chunk), bf16),
            pltpu.VMEM((rows_all, 128), f32),
            pltpu.VMEM((128, rows_all), f32),
            pltpu.VMEM((shares, 8, rows_all), f32),
            pltpu.VMEM((groups, 8, rows_all), f32),
            sems((4, max(groups, shares))),
            pltpu.VMEM((groups, loss_count, model_width), bf16),
            pltpu.VMEM((groups, loss_count // 2, model_width), bf16),
            pltpu.VMEM((groups, loss_count // 4, model_width), bf16),
            pltpu.VMEM((groups, loss_count // 4, model_width), bf16),
            pltpu.VMEM((loss_count // 4, model_width), bf16),
            sems((2, groups + shares)),
        ],
        6 * rows_all * chunk * model_width,
    )
    loss_sum = loss[0, 0]
    head_grad = head_grad.reshape(groups, part_width, chunk)
    late_wide = dec_wide + 2 * in_wide
    norm_start = dec_wide + in_wide + own_in
    quarter = tokens // shares
    block_shape = (2, 2, 2, part_width)
    back_inputs = [
        grad_selected, loss_positions.reshape(1, -1), stream_out, stream_mid, pre_dec, norm_values, w_dec,
        out_rows, memory, stream_dec, q_cross, kv_cross, context_cross, logs_cross,
        stream_two, stream_enc, pre_enc, w_early, looked, place_enc, place_dec,
        qkv_dec, context_dec, logs_dec, qkv_enc, context_enc, logs_enc,
        head_grad,
    ]

    head_grad, grad_tokens, dec_shares, late_own, dense_squares = call(
        partial(
            back_kernel, groups, shares, first_wide, norm_start, norm_rows, len(back_inputs), 5
        ),
        "backward",
        7,
        back_inputs,
        [
            shape_of((groups, part_width, chunk), bf16),
            shape_of((shares, groups, quarter, part_width), bf16),
            shape_of((shares, part_width, dec_wide), bf16),
            shape_of((part_width, late_wide), bf16),
            shape_of((1, 128), f32),
        ],
        [
            sems((2, groups)),
            sems((11,)),
            pltpu.VMEM((model_width, dec_wide), bf16),
            pltpu.VMEM((model_width, own_up + model_width), bf16),
            pltpu.VMEM(out_rows.shape, bf16),
            pltpu.VMEM((enc_len, model_width), bf16),
            pltpu.VMEM((dec_len, model_width), f32),
            pltpu.VMEM((enc_len, model_width), f32),
            pltpu.VMEM((enc_len, model_width), f32),
            pltpu.VMEM((enc_len, own_up), f32),
            pltpu.VMEM((tokens, model_width), bf16),
            pltpu.VMEM(block_shape + (dec_wide,), bf16),
            pltpu.VMEM(block_shape + (dec_wide,), bf16),
            pltpu.VMEM(block_shape + (2 * in_wide,), bf16),
            pltpu.VMEM((dec_len, model_width), f32),
            pltpu.VMEM((enc_len, model_width), f32),
            pltpu.VMEM((dec_len, own), bf16),
            pltpu.VMEM((dec_len, own), bf16),
            pltpu.VMEM((enc_len, 2 * own), bf16),
            pltpu.VMEM((dec_len, 3 * own), bf16),
            pltpu.VMEM((enc_len, 3 * own), bf16),
            pltpu.VMEM((enc_len, own), bf16),
            pltpu.VMEM((own, model_width), bf16),
            pltpu.VMEM((own, model_width), bf16),
            pltpu.VMEM((own, model_width), bf16),
            pltpu.VMEM((8, model_width), f32),
            pltpu.VMEM((8, model_width), f32),
            pltpu.VMEM((8, model_width), f32),
            pltpu.VMEM((128, model_width), f32),
            pltpu.VMEM((model_width, 128), f32),
            pltpu.VMEM((shares, own, in_wide), bf16),
            sems((2, 2, shares - 1)),
            pltpu.VMEM((groups, tokens, part_width), bf16),
            sems((2, groups)),
            sems((2, 3)),
            sems((2, 3)),
            pltpu.VMEM((part_width, dec_wide), bf16),
            sems((3,)),
            *total_dec,
            *total_enc,
            *total_dec[1:],
            *total_enc[1:],
            *line_scratch(part_width, dec_wide),
            *line_scratch(part_width, dec_wide),
            *line_scratch(part_width, 2 * in_wide),
        ],
        16 * (enc_macs + dec_macs) * own_up,
        (6, 7, 8, 9, 14, 15, 16, 17, 18, 19, 27),
        (0, 1, 2),
    )
    late_shares = lax.all_gather(late_own, "vocab", axis=0, tiled=False)
    g_embedding, embedding_squares = spread_rows(hits, grad_tokens, head_grad)
    g_embedding = g_embedding[:, :shard_rows].T
    (squares,) = call(
        partial(squares_kernel, groups, shares),
        "squares",
        10,
        [embedding_squares, dense_squares],
        [shape_of((1, 128), f32)],
        [
            pltpu.VMEM((shares, 8, 128), f32),
            pltpu.VMEM((groups, 8, 128), f32),
            sems((4, max(groups, shares))),
        ],
        0,
    )
    grad_norm = jnp.sqrt(squares[0, 0])
    factor = jnp.minimum(1.0, CLIP / (grad_norm + 1e-06))
    grad_pair = [late_shares, dec_shares]
    in_start, late_in, late_out = own_up + model_width, dec_wide, dec_wide + in_wide

    def place_in(wide_ref, late_ref, dec_ref):
        place_columns(3, 0, late_ref, late_in)(wide_ref)
        place_columns(3, 1, late_ref, in_start)(wide_ref)
        place_columns(3, 2, dec_ref, in_start)(wide_ref)

    def place_out(wide_ref, late_ref):
        for matrix in range(3):
            place_columns(1, matrix, late_ref, late_out + matrix * own)(wide_ref)

    def place_up(wide_ref, late_ref, dec_ref):
        place_columns(groups, 0, late_ref, 0)(wide_ref)
        place_columns(groups, 1, dec_ref, 0)(wide_ref)

    def place_down(wide_ref, late_ref, dec_ref):
        for matrix, ref in enumerate((late_ref, dec_ref)):

            @pl.when(pl.program_id(0) == matrix)
            def _(ref=ref):
                wide_ref[...] = ref[pl.program_id(1), :, own_up : own_up + model_width]

    scale = factor.reshape(1)
    new_in = dense_update(
        "adam_in", RATES[1], place_in, scale, grad_pair, attn_in, attn_in_first, attn_in_second, 2
    )
    new_out = dense_update(
        "adam_out", RATES[2], place_out, scale, grad_pair[:1], attn_out, attn_out_first, attn_out_second, 1
    )
    new_up = dense_update(
        "adam_up", RATES[3], place_up, scale, grad_pair, ffn_up, ffn_up_first, ffn_up_second, 2
    )
    new_down = dense_update(
        "adam_down", RATES[4], place_down, scale, grad_pair, ffn_down, ffn_down_first, ffn_down_second, shares
    )
    g_norms = late_own[:, norm_start : norm_start + norm_rows].astype(f32).T
    new_embedding = adam_update(
        embedding, embedding_first, embedding_second, g_embedding, factor, RATES[0]
    )
    new_norms = adam_update(norms, norms_first, norms_second, g_norms, factor, RATES[5])
    updated = (new_embedding, new_in, new_out, new_up, new_down, new_norms)
    return (loss_sum, token_count, grad_norm) + tuple(
        updated[slot][kind] for kind in range(3) for slot in range(6)
    )


def splits_evenly(mesh):
    return HEADS % mesh.shape["vocab"] == 0 and mesh.shape["dp"] == 8


def solution(mesh):
    placed = (
        P("dp", None),
        P("dp", None),
        P("dp"),
        P("dp", None),
        P("vocab", "dp"),
        P(None, "dp", None),
        P(None, "dp", None),
        P(None, "dp", None),
        P(None, "dp", None),
        P(None, "dp"),
        P("vocab", "dp"),
        P(None, "dp", None),
        P(None, "dp", None),
        P(None, "dp", None),
        P(None, "dp", None),
        P(None, "dp"),
        P("vocab", "dp"),
        P(None, "dp", None),
        P(None, "dp", None),
        P(None, "dp", None),
        P(None, "dp", None),
        P(None, "dp"),
    )
    return jax.shard_map(
        local if splits_evenly(mesh) else local_copied,
        mesh=mesh,
        in_specs=placed,
        out_specs=(
            P(),
            P(),
            P(),
            P("vocab", "dp"),
            P(None, "dp", None),
            P(None, "dp", None),
            P(None, "dp", None),
            P(None, "dp", None),
            P(None, "dp"),
            P("vocab", "dp"),
            P(None, "dp", None),
            P(None, "dp", None),
            P(None, "dp", None),
            P(None, "dp", None),
            P(None, "dp"),
            P("vocab", "dp"),
            P(None, "dp", None),
            P(None, "dp", None),
            P(None, "dp", None),
            P(None, "dp", None),
            P(None, "dp"),
        ),
        check_vma=False,
    )
```

```python
from functools import partial
import math

import jax
import jax.numpy as jnp
import numpy as np
from jax import lax
from jax.experimental import pallas as pl
from jax.experimental.pallas import tpu as pltpu
from jax.sharding import PartitionSpec as P

HEADS = 12
HEAD_DIM = 64
STEP = 10


EPS_NORM = 1e-05
SMOOTH = 0.1
CLIP = 0.02
RATES = (0.05, 0.05, 0.4, 0.05, 0.05, 0.8)
BETA_ONE = 0.9
BETA_TWO = 0.999
ADAM_EPS = 1e-08
DECAY = 0.01


def lowered(tensor):
    return tensor.astype(jnp.bfloat16)


def matmul(left_side, right_side):
    return jnp.dot(left_side, right_side, preferred_element_type=jnp.float32)


def times_transposed(left_side, right_side):
    return lax.dot_general(
        left_side, right_side, (((1,), (1,)), ((), ())), preferred_element_type=jnp.float32
    )


def contract_rows(left_side, right_side):
    return lax.dot_general(
        left_side, right_side, (((0,), (0,)), ((), ())), preferred_element_type=jnp.float32
    )


def positions_table(length, model_width):
    position_col = jnp.arange(length, dtype=jnp.float32)[:, None]
    freq_index = jnp.arange(model_width // 2, dtype=jnp.float32)[None, :]
    angles = position_col * jnp.exp(freq_index * (-2.0 * math.log(10000.0) / model_width))
    return jnp.concatenate([jnp.sin(angles), jnp.cos(angles)], axis=1)


def norm_forward(tensor, gain_row, shift_row):
    center = tensor - jnp.mean(tensor, axis=-1, keepdims=True)
    scale_inv = lax.rsqrt(jnp.mean(center * center, axis=-1, keepdims=True) + EPS_NORM)
    normed = center * scale_inv
    return (normed * gain_row + shift_row, (normed, scale_inv))


def norm_backward_rows(grad_out, saved_parts, gain_row):
    normed, scale_inv = saved_parts
    grad_normed = grad_out * gain_row
    grad_in = scale_inv * (
        grad_normed
        - jnp.mean(grad_normed, axis=-1, keepdims=True)
        - normed * jnp.mean(grad_normed * normed, axis=-1, keepdims=True)
    )
    return (grad_in, jnp.sum(grad_out * normed, axis=0), jnp.sum(grad_out, axis=0))


def split_heads(rows, batch_size):
    return rows.reshape(batch_size, -1, HEADS, rows.shape[1] // HEADS)


def score_block(queries, key_rows, causal):
    scores = jnp.einsum(
        "qhe,khe->hqk", queries, key_rows, preferred_element_type=jnp.float32
    ) * HEAD_DIM ** (-0.5)
    if causal:
        allowed = jnp.arange(queries.shape[0])[:, None] >= jnp.arange(key_rows.shape[0])[None, :]
        scores = jnp.where(allowed[None], scores, -1e30)
    return scores


def attend_one(block_args, causal):
    queries, key_rows, value_rows = block_args
    scores = score_block(queries, key_rows, causal)
    row_top = jnp.max(scores, axis=-1, keepdims=True)
    exponent = jnp.exp(scores - row_top)
    row_total = jnp.sum(exponent, axis=-1, keepdims=True)
    softmax_out = lowered(exponent / row_total)
    context = jnp.einsum(
        "hqk,khe->qhe", softmax_out, value_rows, preferred_element_type=jnp.float32
    )
    return (lowered(context), (row_top + jnp.log(row_total))[..., 0])


def attend_back(block_args, causal):
    queries, key_rows, value_rows, log_total, grad_context = block_args
    scores = score_block(queries, key_rows, causal)
    softmax_out = jnp.exp(scores - log_total[..., None])
    grad_values = jnp.einsum(
        "hqk,qhe->khe", lowered(softmax_out), grad_context, preferred_element_type=jnp.float32
    )
    grad_softmax = jnp.einsum(
        "qhe,khe->hqk", grad_context, value_rows, preferred_element_type=jnp.float32
    )
    grad_scores = lowered(
        softmax_out * (grad_softmax - jnp.sum(grad_softmax * softmax_out, axis=-1, keepdims=True))
    )
    grad_queries = jnp.einsum(
        "hqk,khe->qhe", grad_scores, key_rows, preferred_element_type=jnp.float32
    ) * HEAD_DIM ** (-0.5)
    grad_keys = jnp.einsum(
        "hqk,qhe->khe", grad_scores, queries, preferred_element_type=jnp.float32
    ) * HEAD_DIM ** (-0.5)
    return (lowered(grad_queries), lowered(grad_keys), lowered(grad_values))


def layer_forward(stream, memory, blocks, feed_parts, gain_rows, shifts, batch_size):
    kept_values = []
    for block_order, (w_in, w_out, norm_row) in enumerate(blocks):
        normed, norm_kept = norm_forward(stream, gain_rows[norm_row], shifts[norm_row])
        query_in = lowered(normed)
        model_width = w_out.shape[0]
        if block_order == 0:
            projected = lowered(matmul(query_in, w_in))
            queries = projected[:, :model_width]
            key_rows = projected[:, model_width : 2 * model_width]
            value_rows = projected[:, 2 * model_width :]
            memory_in = query_in
        else:
            memory_in = memory
            queries = lowered(matmul(query_in, w_in[:, :model_width]))
            paired = lowered(matmul(memory, w_in[:, model_width:]))
            key_rows, value_rows = (paired[:, :model_width], paired[:, model_width:])
        causal = memory is not None and block_order == 0
        heads = (
            split_heads(queries, batch_size),
            split_heads(key_rows, batch_size),
            split_heads(value_rows, batch_size),
        )
        context, log_total = lax.map(partial(attend_one, causal=causal), heads)
        context = context.reshape(-1, model_width)
        stream = stream + matmul(context, w_out)
        kept_values.append((norm_kept, query_in, memory_in, heads, context, log_total))
    w_up, w_down, norm_row = feed_parts
    normed, norm_kept = norm_forward(stream, gain_rows[norm_row], shifts[norm_row])
    hidden_in = lowered(normed)
    hidden_pre = matmul(hidden_in, w_up)
    activated = lowered(jax.nn.silu(hidden_pre))
    stream = stream + matmul(activated, w_down)
    kept_values.append((norm_kept, hidden_in, hidden_pre, activated))
    return (stream, kept_values)


def layer_backward(grad_stream, memory, blocks, feed_parts, gain_rows, kept_values, batch_size):
    w_up, w_down, norm_row = feed_parts
    norm_kept, hidden_in, hidden_pre, activated = kept_values[-1]
    grad_low = lowered(grad_stream)
    grad_down = contract_rows(activated, grad_low)
    sigmoid_pre = jax.nn.sigmoid(hidden_pre)
    grad_pre = lowered(
        times_transposed(grad_low, w_down) * sigmoid_pre * (1.0 + hidden_pre * (1.0 - sigmoid_pre))
    )
    grad_up = contract_rows(hidden_in, grad_pre)
    grad_in, grad_gain, grad_shift = norm_backward_rows(
        times_transposed(grad_pre, w_up), norm_kept, gain_rows[norm_row]
    )
    grad_stream = grad_stream + grad_in
    norm_grads = [(norm_row, grad_gain, grad_shift)]
    block_grads = [None] * len(blocks)
    grad_memory = None
    for block_order in reversed(range(len(blocks))):
        w_in, w_out, norm_row = blocks[block_order]
        norm_kept, query_in, memory_in, heads, context, log_total = kept_values[block_order]
        model_width = w_out.shape[0]
        grad_low = lowered(grad_stream)
        grad_w_out = contract_rows(context, grad_low)
        grad_context = split_heads(lowered(times_transposed(grad_low, w_out)), batch_size)
        causal = memory is not None and block_order == 0
        grad_heads = lax.map(partial(attend_back, causal=causal), heads + (log_total, grad_context))
        grad_queries, grad_keys, grad_values = [
            member.reshape(-1, model_width) for member in grad_heads
        ]
        if block_order == 0:
            grad_proj = jnp.concatenate([grad_queries, grad_keys, grad_values], axis=1)
            grad_w_in = contract_rows(query_in, grad_proj)
            grad_normed = times_transposed(grad_proj, w_in)
        else:
            grad_pair = jnp.concatenate([grad_keys, grad_values], axis=1)
            grad_w_in = jnp.concatenate(
                [contract_rows(query_in, grad_queries), contract_rows(memory_in, grad_pair)], axis=1
            )
            grad_normed = times_transposed(grad_queries, w_in[:, :model_width])
            grad_memory = times_transposed(grad_pair, w_in[:, model_width:])
        grad_in, grad_gain, grad_shift = norm_backward_rows(grad_normed, norm_kept, gain_rows[norm_row])
        grad_stream = grad_stream + grad_in
        norm_grads.append((norm_row, grad_gain, grad_shift))
        block_grads[block_order] = (grad_w_in, grad_w_out)
    return (grad_stream, grad_memory, block_grads, (grad_up, grad_down), norm_grads)


def adam_update(weight, first_moment, second_moment, gradient, factor, rate):
    clipped = gradient * factor
    new_first = BETA_ONE * first_moment + (1.0 - BETA_ONE) * clipped
    new_second = BETA_TWO * second_moment + (1.0 - BETA_TWO) * clipped * clipped
    corrected = (
        new_first
        / (1.0 - BETA_ONE**STEP)
        / (jnp.sqrt(new_second / (1.0 - BETA_TWO**STEP)) + ADAM_EPS)
    )
    return (weight - rate * (corrected + DECAY * weight), new_first, new_second)


def local_copied(
    enc_ids,
    labels,
    target_lengths,
    loss_positions,
    embedding,
    attn_in,
    attn_out,
    ffn_up,
    ffn_down,
    norms,
    embedding_first,
    attn_in_first,
    attn_out_first,
    ffn_up_first,
    ffn_down_first,
    norms_first,
    embedding_second,
    attn_in_second,
    attn_out_second,
    ffn_up_second,
    ffn_down_second,
    norms_second,
):
    batch_size, enc_len = enc_ids.shape
    dec_len = labels.shape[1]
    emb_table, w_in_all, w_out_all, w_up_all, w_down_all, norm_table = (
        lax.all_gather(lowered(embedding), "dp", axis=1, tiled=True),
        lax.all_gather(lowered(attn_in), "dp", axis=1, tiled=True),
        lax.all_gather(lowered(attn_out), "dp", axis=1, tiled=True),
        lax.all_gather(lowered(ffn_up), "dp", axis=1, tiled=True),
        lax.all_gather(lowered(ffn_down), "dp", axis=1, tiled=True),
        lax.all_gather(lowered(norms), "dp", axis=1, tiled=True),
    )
    model_width = emb_table.shape[1]
    shard_rows = emb_table.shape[0]
    vocab_total = shard_rows * lax.axis_size("vocab")
    row_start = lax.axis_index("vocab") * shard_rows
    norm_values = norm_table.astype(jnp.float32)
    gain_rows, shifts = (norm_values[:7], norm_values[7:])
    dec_ids = jnp.concatenate([jnp.zeros((batch_size, 1), jnp.int32), labels[:, :-1]], axis=1)
    token_list = jnp.concatenate([enc_ids.reshape(-1), dec_ids.reshape(-1)])
    local_rows = token_list - row_start
    inside = (local_rows >= 0) & (local_rows < shard_rows)
    safe_rows = jnp.clip(local_rows, 0, shard_rows - 1)
    picked = jnp.where(
        inside[:, None], jnp.take(emb_table, safe_rows, axis=0).astype(jnp.float32), 0.0
    )
    looked = lax.psum(picked.astype(jnp.bfloat16), "vocab").astype(jnp.float32)
    root_width = math.sqrt(model_width)
    enc_tokens = batch_size * enc_len
    enc_stream = (
        looked[:enc_tokens].reshape(batch_size, enc_len, model_width) * root_width
        + positions_table(enc_len, model_width)
    ).reshape(enc_tokens, model_width)
    dec_stream = (
        looked[enc_tokens:].reshape(batch_size, dec_len, model_width) * root_width
        + positions_table(dec_len, model_width)
    ).reshape(batch_size * dec_len, model_width)
    enc_blocks = [(w_in_all[0], w_out_all[0], 0)]
    dec_blocks = [(w_in_all[1], w_out_all[1], 3), (w_in_all[2], w_out_all[2], 4)]
    enc_feed = (w_up_all[0], w_down_all[0], 1)
    dec_feed = (w_up_all[1], w_down_all[1], 5)
    enc_out, enc_kept = layer_forward(
        enc_stream, None, enc_blocks, enc_feed, gain_rows, shifts, batch_size
    )
    memory, memory_kept = norm_forward(enc_out, gain_rows[2], shifts[2])
    memory_low = lowered(memory)
    dec_out, dec_kept = layer_forward(
        dec_stream, memory_low, dec_blocks, dec_feed, gain_rows, shifts, batch_size
    )
    final, final_kept = norm_forward(dec_out, gain_rows[6], shifts[6])
    chosen = (jnp.arange(batch_size)[:, None] * dec_len + loss_positions).reshape(-1)
    selected = lowered(jnp.take(final, chosen, axis=0))
    logits = times_transposed(selected, emb_table)
    columns = row_start + jnp.arange(shard_rows)
    padding = columns == vocab_total - 1
    masked = jnp.where(padding[None, :], -1e30, logits)
    target_local = jnp.take_along_axis(labels, loss_positions, axis=1).reshape(-1) - row_start
    target_hit = (jnp.arange(shard_rows)[None, :] == target_local[:, None]).astype(jnp.float32)
    target_term = jnp.sum(target_hit * logits, axis=1)
    smooth_term = jnp.sum(jnp.where(padding[None, :], 0.0, logits), axis=1)
    local_max = jnp.max(masked, axis=1)
    row_max = lax.pmax(local_max, "vocab")
    exp_local = jnp.sum(jnp.exp(masked - row_max[:, None]), axis=1)
    exp_total, smooth_total, target_total = lax.psum((exp_local, smooth_term, target_term), "vocab")
    log_total = row_max + jnp.log(exp_total)
    per_row = log_total - (1.0 - SMOOTH) * target_total - SMOOTH * smooth_total / (vocab_total - 1)
    counted = (loss_positions < target_lengths[:, None]).reshape(-1).astype(jnp.float32)
    loss_sum, token_count = lax.psum((jnp.sum(counted * per_row), jnp.sum(counted)), "dp")
    softmax_rows = jnp.exp(masked - log_total[:, None])
    grad_logits = (counted / token_count)[:, None] * (
        softmax_rows - (1.0 - SMOOTH) * target_hit - SMOOTH / (vocab_total - 1)
    )
    grad_logits = lowered(jnp.where(padding[None, :], 0.0, grad_logits))
    grad_selected = lax.psum(matmul(grad_logits, emb_table).astype(jnp.bfloat16), "vocab").astype(
        jnp.float32
    )
    grad_final = jnp.zeros_like(final).at[chosen].add(grad_selected)
    grad_dec_out, gain_six, shift_six = norm_backward_rows(grad_final, final_kept, gain_rows[6])
    grad_dec_stream, grad_memory, dec_block_grads, dec_feed_grads, dec_norm_grads = layer_backward(
        grad_dec_out, memory_low, dec_blocks, dec_feed, gain_rows, dec_kept, batch_size
    )
    grad_enc_out, gain_two, shift_two = norm_backward_rows(grad_memory, memory_kept, gain_rows[2])
    grad_enc_stream, _, enc_block_grads, enc_feed_grads, enc_norm_grads = layer_backward(
        grad_enc_out, None, enc_blocks, enc_feed, gain_rows, enc_kept, batch_size
    )
    grad_attn_in = jnp.stack([enc_block_grads[0][0], dec_block_grads[0][0], dec_block_grads[1][0]])
    grad_attn_out = jnp.stack([enc_block_grads[0][1], dec_block_grads[0][1], dec_block_grads[1][1]])
    grad_up_all = jnp.stack([enc_feed_grads[0], dec_feed_grads[0]])
    grad_down_all = jnp.stack([enc_feed_grads[1], dec_feed_grads[1]])
    grad_norms = jnp.zeros((14, model_width), jnp.float32)
    for norm_row, grad_gain, grad_shift in (
        enc_norm_grads + dec_norm_grads + [(2, gain_two, shift_two), (6, gain_six, shift_six)]
    ):
        grad_norms = grad_norms.at[norm_row].set(grad_gain).at[norm_row + 7].set(grad_shift)
    grad_tokens = jnp.concatenate([grad_enc_stream, grad_dec_stream], axis=0) * root_width
    head_term = contract_rows(grad_logits, selected)
    lookup_term = (
        jnp.zeros((shard_rows, model_width), jnp.float32)
        .at[safe_rows]
        .add(jnp.where(inside[:, None], grad_tokens, 0.0))
    )
    g_attn_in, g_attn_out, g_up, g_down, g_norms, g_embedding = (
        lax.psum_scatter(
            grad_attn_in.astype(jnp.bfloat16), "dp", scatter_dimension=1, tiled=True
        ).astype(jnp.float32),
        lax.psum_scatter(
            grad_attn_out.astype(jnp.bfloat16), "dp", scatter_dimension=1, tiled=True
        ).astype(jnp.float32),
        lax.psum_scatter(
            grad_up_all.astype(jnp.bfloat16), "dp", scatter_dimension=1, tiled=True
        ).astype(jnp.float32),
        lax.psum_scatter(
            grad_down_all.astype(jnp.bfloat16), "dp", scatter_dimension=1, tiled=True
        ).astype(jnp.float32),
        lax.psum_scatter(
            grad_norms.astype(jnp.bfloat16), "dp", scatter_dimension=1, tiled=True
        ).astype(jnp.float32),
        lax.psum_scatter(
            (head_term + lookup_term).astype(jnp.bfloat16), "dp", scatter_dimension=1, tiled=True
        ).astype(jnp.float32),
    )
    gradients = (g_embedding, g_attn_in, g_attn_out, g_up, g_down, g_norms)
    dense_squares = sum((jnp.sum(member * member) for member in gradients[1:]))
    squares = lax.psum(
        dense_squares / lax.axis_size("vocab") + jnp.sum(g_embedding * g_embedding), ("dp", "vocab")
    )
    grad_norm = jnp.sqrt(squares)
    factor = jnp.minimum(1.0, CLIP / (grad_norm + 1e-06))
    params = (embedding, attn_in, attn_out, ffn_up, ffn_down, norms)
    firsts = (
        embedding_first,
        attn_in_first,
        attn_out_first,
        ffn_up_first,
        ffn_down_first,
        norms_first,
    )
    seconds = (
        embedding_second,
        attn_in_second,
        attn_out_second,
        ffn_up_second,
        ffn_down_second,
        norms_second,
    )
    updated = [
        adam_update(params[slot], firsts[slot], seconds[slot], gradients[slot], factor, RATES[slot])
        for slot in range(6)
    ]
    return (
        loss_sum,
        token_count,
        grad_norm,
        updated[0][0],
        updated[1][0],
        updated[2][0],
        updated[3][0],
        updated[4][0],
        updated[5][0],
        updated[0][1],
        updated[1][1],
        updated[2][1],
        updated[3][1],
        updated[4][1],
        updated[5][1],
        updated[0][2],
        updated[1][2],
        updated[2][2],
        updated[3][2],
        updated[4][2],
        updated[5][2],
    )


VMEM_BYTES = 60 * 1024 * 1024


def positions_numpy(length, model_width):
    place = np.arange(length, dtype=np.float32)[:, None]
    index = np.arange(model_width // 2, dtype=np.float32)[None, :]
    angles = place * np.exp(index * np.float32(-2.0 * math.log(10000.0) / model_width))
    return np.concatenate([np.sin(angles), np.cos(angles)], axis=1).astype(np.float32)


def hits_kernel(rows, span, ids_ref, list_ref):
    def one(step, found):
        for inner in range(8):
            slot = step * 8 + inner
            row = ids_ref[slot]
            list_ref[found] = row * span + slot
            found = found + jnp.where((row >= 0) & (row < rows), 1, 0)
        return found

    list_ref[list_ref.shape[0] - 1] = lax.fori_loop(0, ids_ref.shape[0] // 8, one, 0)


def list_hits(local_ids, rows, span):
    return pl.pallas_call(
        partial(hits_kernel, rows, span),
        out_shape=jax.ShapeDtypeStruct((span,), jnp.int32),
        in_specs=[pl.BlockSpec(memory_space=pltpu.SMEM)],
        out_specs=pl.BlockSpec(memory_space=pltpu.SMEM),
        name="list_hits",
    )(local_ids)


def over_hits(lists_ref, visit):
    groups, span = lists_ref.shape
    for group in range(groups):

        def one(step, carry):
            entry = lists_ref[group, step]
            visit(group, entry // span, lax.rem(entry, span))
            return carry

        lax.fori_loop(0, lists_ref[group, span - 1], one, 0)


def pick_kernel(lists_ref, table_ref, out_ref, across_ref, wide_ref, turned_ref):
    tokens = wide_ref.shape[0] // lists_ref.shape[0]
    width, rows = table_ref.shape
    total = across_ref.shape[1]
    wide_ref[...] = jnp.zeros_like(wide_ref)
    step = 1024
    for low in range(0, total, step):
        high = max(min(low + step, rows), low)
        if high > low:
            across_ref[:, low:high] = lowered(table_ref[:, low:high])
        if high < low + step:
            across_ref[:, high : low + step] = jnp.zeros((width, low + step - high), jnp.bfloat16)

    def turn(piece, carry):
        for part in range(8):
            start = pl.multiple_of(piece * step + part * 128, 128)
            block = across_ref[:, pl.ds(start, 128)].astype(jnp.float32)
            turned_ref[pl.ds(start, 128), :] = jnp.transpose(block)
        return carry

    lax.fori_loop(0, total // step, turn, 0)

    def visit(group, row, slot):
        wide_ref[pl.ds(group * tokens + slot, 1), :] = turned_ref[pl.ds(row, 1), :]

    over_hits(lists_ref, visit)
    out_ref[...] = wide_ref[...].astype(jnp.bfloat16)


def pick_rows(lists, count, table, total):
    width = table.shape[0]
    return pl.pallas_call(
        pick_kernel,
        out_shape=(
            jax.ShapeDtypeStruct((count, width), jnp.bfloat16),
            jax.ShapeDtypeStruct((width, total), jnp.bfloat16),
        ),
        in_specs=[
            pl.BlockSpec(memory_space=pltpu.SMEM),
            pl.BlockSpec(memory_space=pltpu.VMEM),
        ],
        out_specs=(
            pl.BlockSpec(memory_space=pltpu.VMEM),
            pl.BlockSpec(memory_space=pltpu.VMEM),
        ),
        scratch_shapes=[
            pltpu.VMEM((count, width), jnp.float32),
            pltpu.VMEM((total, width), jnp.float32),
        ],
        compiler_params=pltpu.CompilerParams(vmem_limit_bytes=VMEM_BYTES),
        name="pick_rows",
    )(lists, table)


def spread_kernel(
    lists_ref, grads_ref, zero_ref, one_ref, out_ref, squares_ref, wide_ref, rows_ref
):
    shares, groups, _, width = grads_ref.shape
    tokens = rows_ref.shape[0] // groups
    quarter = tokens // shares
    chunks = zero_ref.shape[0]
    parts = [(ref, low) for ref in (zero_ref, one_ref) for low in range(0, ref.shape[2], 128)]
    chunk = 128 * len(parts)
    for index in range(shares):
        for number in range(groups):
            start = number * tokens + index * quarter
            rows_ref[start : start + quarter, :] = grads_ref[index, number, 0:quarter].astype(jnp.float32)
    wide_ref[...] = jnp.zeros_like(wide_ref)

    def visit(group, row, slot):
        wide_ref[pl.ds(row, 1), 0:width] += rows_ref[pl.ds(group * tokens + slot, 1), :]

    over_hits(lists_ref, visit)

    def turn(piece, total):
        for part, (head_ref, column) in enumerate(parts):
            start = pl.multiple_of(piece * chunk + part * 128, 128)
            block = jnp.transpose(wide_ref[pl.ds(start, 128), :])[:width]
            block = block + head_ref[piece, :, column : column + 128].astype(jnp.float32)
            out_ref[:, pl.ds(start, 128)] = lowered(block)
            total = total + block * block
        return total

    total = lax.fori_loop(0, chunks, turn, jnp.zeros((width, 128), jnp.float32))
    squares_ref[...] = jnp.sum(total, axis=0, keepdims=True)


def spread_rows(lists, count, grads, head):
    chunks, width, _ = head[0].shape
    chunk = sum(member.shape[2] for member in head)
    return pl.pallas_call(
        spread_kernel,
        out_shape=(
            jax.ShapeDtypeStruct((width, chunks * chunk), jnp.bfloat16),
            jax.ShapeDtypeStruct((1, 128), jnp.float32),
        ),
        in_specs=[pl.BlockSpec(memory_space=pltpu.SMEM)]
        + [pl.BlockSpec(memory_space=pltpu.VMEM)] * 3,
        out_specs=(
            pl.BlockSpec(memory_space=pltpu.VMEM),
            pl.BlockSpec(memory_space=pltpu.VMEM),
        ),
        scratch_shapes=[
            pltpu.VMEM((chunks * chunk, 128), jnp.float32),
            pltpu.VMEM((count, width), jnp.float32),
        ],
        compiler_params=pltpu.CompilerParams(vmem_limit_bytes=VMEM_BYTES),
        name="spread_rows",
    )(lists, grads, *head)


MESH = pl.DeviceIdType.MESH


def meet(devices):
    barrier = pltpu.get_barrier_semaphore()
    for device in devices:
        pl.semaphore_signal(barrier, inc=1, device_id=device, device_id_type=MESH)
    pl.semaphore_wait(barrier, len(devices))


def send(source, target, send_sem, recv_sem, device):
    copy = pltpu.make_async_remote_copy(
        src_ref=source,
        dst_ref=target,
        send_sem=send_sem,
        recv_sem=recv_sem,
        device_id=device,
        device_id_type=MESH,
    )
    copy.start()
    return copy


def places():
    group, share = lax.axis_index("dp"), lax.axis_index("vocab")
    core = lax.rem(share, 2)
    core_peer = (group, share + 1 - 2 * core)
    side_peer = (group, lax.rem(share + 2, 4))
    return group, share, core, core_peer, side_peer


def group_peers(group, share, groups):
    return [(lax.rem(group + step, groups), share) for step in range(1, groups)]


def share_peers(group, share, shares):
    return [(group, lax.rem(share + step, shares)) for step in range(1, shares)]


def total_scratch(rows, width):
    half = rows // 2
    return [
        pltpu.VMEM((rows, width), jnp.float32),
        pltpu.VMEM((4, half, width), jnp.bfloat16),
        pltpu.VMEM((rows, width), jnp.bfloat16),
        pltpu.SemaphoreType.DMA((6,)),
    ]


class Total:
    def __init__(self, refs):
        self.part, self.bufs, self.total, self.sems = refs
        _, _, core, self.core_peer, self.side_peer = places()
        half = self.part.shape[0] // 2
        self.mine = pl.ds(pl.multiple_of(core * half, half), half)
        self.other = pl.ds(pl.multiple_of((1 - core) * half, half), half)

    def begin(self, partial_rows):
        self.part[...] = partial_rows
        self.bufs[0] = lowered(self.part[self.other, :])
        self.one = send(
            self.bufs.at[0], self.bufs.at[1], self.sems.at[0], self.sems.at[1], self.core_peer
        )

    def middle(self):
        self.one.wait_recv()
        self.bufs[2] = lowered(self.part[self.mine, :] + self.bufs[1].astype(jnp.float32))
        self.two = send(
            self.bufs.at[2], self.bufs.at[3], self.sems.at[2], self.sems.at[3], self.side_peer
        )

    def last(self):
        self.two.wait_recv()
        self.total[self.mine, :] = lowered(
            self.bufs[2].astype(jnp.float32) + self.bufs[3].astype(jnp.float32)
        )
        piece = self.total.at[self.mine, :]
        self.three = send(piece, piece, self.sems.at[4], self.sems.at[5], self.core_peer)

    def finish(self):
        self.three.wait()
        self.one.wait_send()
        self.two.wait_send()
        return self.total[...].astype(jnp.float32)

    def rest(self):
        self.middle()
        self.last()
        return self.finish()


class Exchange:
    def __init__(self, block_of, target_ref, sems, groups):
        group, share = lax.axis_index("dp"), lax.axis_index("vocab")
        self.copies = [
            send(
                block_of(peer[0]), target_ref.at[group], sems.at[0, step], sems.at[1, step], peer
            )
            for step, peer in enumerate(group_peers(group, share, groups))
        ]
        self.keep = pltpu.make_async_copy(
            block_of(group), target_ref.at[group], sems.at[0, groups - 1]
        )
        self.keep.start()

    def finish(self):
        self.keep.wait()
        for copy in self.copies:
            copy.wait()


def head_blocks(source_ref, start, columns):
    return lambda group: source_ref.at[group, :, pl.ds(start, columns)]


def table_blocks(source_ref, chunk, start, columns):
    return lambda group: source_ref.at[:, pl.ds(pl.multiple_of(group * chunk + start, 128), columns)]


def pair_of(group, share):
    place = lax.rem(group, 2)
    return (group + 1 - 2 * place, share), place


def line_places(group):
    pair, place = group // 2, lax.rem(group, 2)
    high, low = pair // 2, lax.rem(pair, 2)
    far = ((1 - high) * 2 + low) * 2 + place
    near = (high * 2 + 1 - low) * 2 + place
    return high, low, far, near


def line_scratch(width, columns):
    return [
        pltpu.VMEM((2, 2, width, columns), jnp.bfloat16),
        pltpu.VMEM((2, width, columns), jnp.bfloat16),
        pltpu.VMEM((width, columns), jnp.bfloat16),
        pltpu.SemaphoreType.DMA((6,)),
    ]


class Owned:
    def __init__(self, blocks, refs):
        group, self.share = lax.axis_index("dp"), lax.axis_index("vocab")
        self.high, self.low, self.far, self.near = line_places(group)
        self.pair, self.place = pair_of(group, self.share)
        self.blocks = blocks
        self.pair_in, self.near_in, self.far_in, self.sems = refs

    def begin(self):
        source = self.blocks.at[:, :, 1 - self.place]
        self.zero = send(source, self.pair_in, self.sems.at[0], self.sems.at[1], self.pair)

    def beside(self):
        self.zero.wait()
        self.blocks[:, :, self.place] = lowered(
            self.blocks[:, :, self.place].astype(jnp.float32) + self.pair_in[...].astype(jnp.float32)
        )
        self.one = send(
            self.blocks.at[:, 1 - self.low, self.place],
            self.near_in,
            self.sems.at[2],
            self.sems.at[3],
            (self.near, self.share),
        )

    def beyond(self):
        self.one.wait()
        self.blocks[:, self.low, self.place] = lowered(
            self.blocks[:, self.low, self.place].astype(jnp.float32)
            + self.near_in[...].astype(jnp.float32)
        )
        self.two = send(
            self.blocks.at[1 - self.high, self.low, self.place],
            self.far_in,
            self.sems.at[4],
            self.sems.at[5],
            (self.far, self.share),
        )

    def finish(self):
        self.two.wait()
        return lowered(
            self.blocks[self.high, self.low, self.place].astype(jnp.float32)
            + self.far_in[...].astype(jnp.float32)
        )


class Late:
    def __init__(self, source, buffer, sem):
        self.copy, self.buffer, self.waiting = pltpu.make_async_copy(source, buffer, sem), buffer, True
        self.copy.start()

    def __call__(self):
        if self.waiting:
            self.copy.wait()
            self.waiting = False
        return self.buffer


class ShareGather:
    def __init__(self, target_ref, sems):
        _, self.share, _, self.core_peer, self.side_peer = places()
        self.target, self.sems = target_ref, sems
        block = target_ref.at[self.share]
        self.one = send(block, block, sems.at[0, 0], sems.at[1, 0], self.side_peer)

    def middle(self):
        self.one.wait()
        both = [self.target.at[index] for index in (self.share, self.side_peer[1])]
        self.two = [
            send(block, block, self.sems.at[0, 1 + step], self.sems.at[1, 1 + step], self.core_peer)
            for step, block in enumerate(both)
        ]

    def finish(self):
        for copy in self.two:
            copy.wait()


def in_vmem(count, at_rest=()):
    return [
        pl.BlockSpec(memory_space=pl.ANY if index in at_rest else pltpu.VMEM)
        for index in range(count)
    ]


def call(kernel, name, number, inputs, out_shape, scratch, flops, rest_in=(), rest_out=()):
    moved = sum(math.prod(member.shape) * member.dtype.itemsize for member in (*inputs, *out_shape))
    return pl.pallas_call(
        kernel,
        out_shape=tuple(out_shape),
        in_specs=in_vmem(len(inputs), rest_in),
        out_specs=tuple(in_vmem(len(out_shape), rest_out)),
        scratch_shapes=scratch,
        compiler_params=pltpu.CompilerParams(
            collective_id=number, has_side_effects=True, vmem_limit_bytes=VMEM_BYTES
        ),
        cost_estimate=pl.CostEstimate(flops=flops, bytes_accessed=moved, transcendentals=0),
        name=name,
    )(*inputs)


def shape_of(shape, dtype):
    return jax.ShapeDtypeStruct(shape, dtype)


def head_slice(ref, start, index):
    low = start + index * HEAD_DIM
    return ref[:, low : low + HEAD_DIM]


def masked_scores(query, key, causal):
    scores = times_transposed(query, key) * HEAD_DIM ** (-0.5)
    if causal:
        down = lax.broadcasted_iota(jnp.int32, scores.shape, 0)
        across = lax.broadcasted_iota(jnp.int32, scores.shape, 1)
        scores = jnp.where(down >= across, scores, -1e30)
    return scores


def heads_forward(q_ref, kv_ref, starts, context_ref, logs_ref, causal):
    q_start, k_start, v_start = starts
    for index in range(context_ref.shape[1] // HEAD_DIM):
        query = head_slice(q_ref, q_start, index)
        key = head_slice(kv_ref, k_start, index)
        value = head_slice(kv_ref, v_start, index)
        scores = masked_scores(query, key, causal)
        row_top = jnp.max(scores, axis=-1, keepdims=True)
        exponent = jnp.exp(scores - row_top)
        row_total = jnp.sum(exponent, axis=-1, keepdims=True)
        context = lowered(matmul(lowered(exponent / row_total), value))
        context_ref[:, index * HEAD_DIM : (index + 1) * HEAD_DIM] = context
        logs_ref[:, index : index + 1] = row_top + jnp.log(row_total)


def heads_backward(q_ref, kv_ref, starts, logs_ref, grad_ref, gq_ref, gkv_ref, g_starts, causal):
    q_start, k_start, v_start = starts
    gq_start, gk_start, gv_start = g_starts
    scale = HEAD_DIM ** (-0.5)
    for index in range(grad_ref.shape[1] // HEAD_DIM):
        low, high = index * HEAD_DIM, (index + 1) * HEAD_DIM
        query = head_slice(q_ref, q_start, index)
        key = head_slice(kv_ref, k_start, index)
        value = head_slice(kv_ref, v_start, index)
        grad = grad_ref[:, low:high]
        softmax_out = jnp.exp(
            masked_scores(query, key, causal) - logs_ref[:, index : index + 1]
        )
        gkv_ref[:, gv_start + low : gv_start + high] = lowered(
            contract_rows(lowered(softmax_out), grad)
        )
        grad_softmax = times_transposed(grad, value)
        inner = jnp.sum(grad_softmax * softmax_out, axis=-1, keepdims=True)
        grad_scores = lowered(softmax_out * (grad_softmax - inner))
        gq_ref[:, gq_start + low : gq_start + high] = lowered(matmul(grad_scores, key) * scale)
        gkv_ref[:, gk_start + low : gk_start + high] = lowered(
            contract_rows(grad_scores, query) * scale
        )


def norm_backward(grad_out, saved_parts, gain_row):
    normed, scale_inv = saved_parts
    grad_normed = grad_out * gain_row
    grad_in = scale_inv * (
        grad_normed
        - jnp.mean(grad_normed, axis=-1, keepdims=True)
        - normed * jnp.mean(grad_normed * normed, axis=-1, keepdims=True)
    )
    return (
        grad_in,
        jnp.sum(grad_out * normed, axis=0, keepdims=True),
        jnp.sum(grad_out, axis=0, keepdims=True),
    )


def gain_of(norms_ref, row):
    return norms_ref[row : row + 1, :], norms_ref[row + 7 : row + 8, :]


def stream_of(looked_ref, start, place_ref):
    rows, width = place_ref.shape
    looked = looked_ref[start : start + rows, :].astype(jnp.float32)
    return looked * math.sqrt(width) + place_ref[...]


def forward_kernel(groups, shares, base, cuts, refs_in, refs_out, *refs):
    inputs, outputs, scratch = refs[:refs_in], refs[refs_in : refs_in + refs_out], refs[refs_in + refs_out :]
    looked_ref, place_enc_ref, place_dec_ref, w_early_hbm, across_ref = inputs
    (
        table_ref, out_rows_ref, norms_ref,
        qkv_enc_ref, context_enc_ref, logs_enc_ref, stream_enc_hbm, pre_enc_hbm, stream_two_hbm, memory_ref,
        qkv_dec_ref, context_dec_ref, logs_dec_ref, stream_dec_ref,
    ) = outputs
    (
        table_sems, out_sems, load_sems, w_first_ref, w_enc_ref, stream_enc_ref, pre_enc_ref, stream_two_ref,
        blocks_ref, block_sems, local_sem,
    ) = scratch[:11]
    rest = scratch[11:]
    small_one, large_one = rest[:4], rest[4:8]
    large_two = large_one[:1] + rest[8:11]
    group, share, core, core_peer, side_peer = places()
    peers, far = share_peers(group, share, shares), group_peers(group, share, groups)
    first_wide = w_first_ref.shape[1]
    load_first = Late(w_early_hbm.at[:, pl.ds(0, first_wide)], w_first_ref, load_sems.at[0])
    load_enc = Late(
        w_early_hbm.at[:, pl.ds(first_wide, w_enc_ref.shape[1])], w_enc_ref, load_sems.at[1]
    )
    meet(peers + far)
    chunk = across_ref.shape[1] // groups
    starts = np.cumsum((0,) + cuts).tolist()

    def table_piece(index):
        at = pl.ds(starts[index], cuts[index])
        return Exchange(
            table_blocks(across_ref, chunk, base + starts[index], cuts[index]),
            table_ref.at[:, :, at],
            table_sems.at[index],
            groups,
        )

    outgoing = []

    def put_out(source, target):
        copy = pltpu.make_async_copy(source, target, out_sems.at[len(outgoing)])
        copy.start()
        outgoing.append(copy)

    table_zero = table_piece(0)
    load_first()

    own = qkv_enc_ref.shape[1] // 3
    rows, wide = blocks_ref.shape[1:]
    padded = first_wide - wide
    window = pl.ds(padded, wide)
    copies = []
    for step, (_, peer) in enumerate(peers):
        source = w_first_ref.at[pl.ds(pl.multiple_of(peer * rows, 64), rows), window]
        copies.append(
            send(source, blocks_ref.at[share], block_sems.at[0, step], block_sems.at[1, step], (group, peer))
        )
    keep = pltpu.make_async_copy(
        w_first_ref.at[pl.ds(pl.multiple_of(share * rows, 64), rows), window], blocks_ref.at[share], local_sem
    )
    keep.start()
    turned = jnp.transpose(w_first_ref[:, first_wide - 128 :].astype(jnp.float32))
    norms_ref[...] = turned[64:80]
    enc_total, dec_total = Total(large_one), Total(small_one)
    enc_len, dec_len = place_enc_ref.shape[0], place_dec_ref.shape[0]
    stream = stream_of(looked_ref, 0, place_enc_ref)
    normed, _ = norm_forward(stream, *gain_of(norms_ref, 0))
    qkv_enc_ref[...] = lowered(matmul(lowered(normed), w_first_ref[:, : 3 * own]))
    stream_enc_ref[...] = stream
    head_starts = (0, own, 2 * own)
    logs_enc_ref[...] = jnp.zeros_like(logs_enc_ref)
    heads_forward(qkv_enc_ref, qkv_enc_ref, head_starts, context_enc_ref, logs_enc_ref, False)
    table_one = table_piece(1)
    keep.wait()
    for copy in copies:
        copy.wait()
    for matrix in range(3):
        for piece in range(shares):
            out_rows_ref[matrix, :, piece * own : (piece + 1) * own] = blocks_ref[
                piece, :, matrix * own : (matrix + 1) * own
            ]
    enc_total.begin(matmul(context_enc_ref[...], out_rows_ref[0]))
    stream = stream_of(looked_ref, enc_len, place_dec_ref)
    stream_dec_ref[...] = stream
    normed, _ = norm_forward(stream, *gain_of(norms_ref, 3))
    enc_total.middle()
    dec_start = padded // 2
    qkv_dec_ref[...] = lowered(
        matmul(lowered(normed), w_first_ref[:, dec_start : dec_start + 3 * own])
    )
    logs_dec_ref[...] = jnp.zeros_like(logs_dec_ref)
    heads_forward(qkv_dec_ref, qkv_dec_ref, head_starts, context_dec_ref, logs_dec_ref, True)
    enc_total.last()
    dec_total.begin(matmul(context_dec_ref[...], out_rows_ref[1]))
    dec_total.middle()
    stream_enc_ref[...] += enc_total.finish()
    put_out(stream_enc_ref, stream_enc_hbm)
    dec_total.last()

    total = Total(large_two)
    normed, _ = norm_forward(stream_enc_ref[...], *gain_of(norms_ref, 1))
    hidden, width = pre_enc_ref.shape[1], stream_enc_ref.shape[1]
    load_enc()
    pre_enc_ref[...] = matmul(lowered(normed), w_enc_ref[:, :hidden])
    put_out(pre_enc_ref, pre_enc_hbm)
    activated = lowered(jax.nn.silu(pre_enc_ref[...]))
    total.begin(matmul(activated, w_enc_ref[:, hidden : hidden + width]))
    stream_dec_ref[...] += dec_total.finish()
    stream_two_ref[...] = stream_enc_ref[...] + total.rest()
    put_out(stream_two_ref, stream_two_hbm)
    memory, _ = norm_forward(stream_two_ref[...], *gain_of(norms_ref, 2))
    memory_ref[...] = lowered(memory)
    for piece in (table_zero, table_one):
        piece.finish()
    for copy in outgoing:
        copy.wait()


def dec_kernel(
    groups, start,
    stream_dec_ref, memory_ref, norms_ref, out_rows_ref, positions_ref, w_dec_hbm, across_ref,
    table_ref, q_ref, kv_ref, context_ref, logs_ref, stream_mid_ref, pre_dec_ref, stream_out_ref, selected_ref,
    w_dec_ref, load_sem, table_sems, own_ref, select_sems, *rest,
):
    small_one, small_two = rest[:4], rest[:1] + rest[4:7]
    group, share, core, core_peer, side_peer = places()
    far = group_peers(group, share, groups)
    load_dec = Late(w_dec_hbm, w_dec_ref, load_sem)
    meet([core_peer, side_peer] + far)
    chunk, columns = across_ref.shape[1] // groups, table_ref.shape[2]
    exchange = Exchange(
        table_blocks(across_ref, chunk, start, columns), table_ref, table_sems, groups
    )
    own, hidden = q_ref.shape[1], pre_dec_ref.shape[1]
    dec_len, width = stream_dec_ref.shape
    cross_total, feed_total = Total(small_two), Total(small_one)
    in_start = hidden + width
    normed, _ = norm_forward(stream_dec_ref[...], *gain_of(norms_ref, 4))
    load_dec()
    kv_ref[...] = lowered(
        matmul(memory_ref[...], w_dec_ref[:, in_start + own : in_start + 3 * own])
    )
    q_ref[...] = lowered(matmul(lowered(normed), w_dec_ref[:, in_start : in_start + own]))
    logs_ref[...] = jnp.zeros_like(logs_ref)
    heads_forward(q_ref, kv_ref, (0, 0, own), context_ref, logs_ref, False)
    cross_total.begin(matmul(context_ref[...], out_rows_ref[2]))
    stream_mid_ref[...] = stream_dec_ref[...] + cross_total.rest()
    normed, _ = norm_forward(stream_mid_ref[...], *gain_of(norms_ref, 5))
    pre_dec_ref[...] = matmul(lowered(normed), w_dec_ref[:, :hidden])
    activated = lowered(jax.nn.silu(pre_dec_ref[...]))
    feed_total.begin(matmul(activated, w_dec_ref[:, hidden:in_start]))
    stream_out_ref[...] = stream_mid_ref[...] + feed_total.rest()
    final, _ = norm_forward(stream_out_ref[...], *gain_of(norms_ref, 6))
    places_down = lax.broadcasted_iota(jnp.int32, (own_ref.shape[0], dec_len), 1)
    chosen = lowered(jnp.where(places_down == positions_ref[...], 1.0, 0.0))
    own_ref[...] = lowered(matmul(chosen, lowered(final)))
    selected_ref[group] = own_ref[...]
    copies = [
        send(own_ref, selected_ref.at[group], select_sems.at[0, step], select_sems.at[1, step], peer)
        for step, peer in enumerate(far)
    ]
    exchange.finish()
    for copy in copies:
        copy.wait()


def combine_stats(stats):
    row_max = stats[0][0:1]
    for member in stats[1:]:
        row_max = jnp.maximum(row_max, member[0:1])
    exp_total = smooth = target = 0.0
    for member in stats:
        exp_total = exp_total + member[1:2] * jnp.exp(member[0:1] - row_max)
        smooth = smooth + member[2:3]
        target = target + member[3:4]
    return row_max, exp_total, smooth, target


def head_kernel(
    groups, shares, shard_rows,
    selected_ref, zero_ref, one_ref, two_ref, targets_ref, weights_ref, counted_ref,
    loss_ref, grad_out_ref, head_ref, head_out_ref,
    head_sems, logits_ref, dz_ref, stats_ref, turned_ref, share_stats_ref, group_stats_ref, stat_sems,
    part_ref, core_ref, side_ref, group_ref, sum_ref, sems,
):
    group, share, core, core_peer, side_peer = places()
    side = share // 2
    near, far = share_peers(group, share, shares), group_peers(group, share, groups)
    meet(near + far)
    rows, width = selected_ref.shape
    chunk = logits_ref.shape[1]
    vocab_total = shard_rows * shares
    first = group * chunk
    limit = jnp.minimum(shard_rows - first, vocab_total - 1 - share * shard_rows - first)
    block = 384
    step_rows = 32

    tables = (zero_ref, one_ref, two_ref)
    starts = np.cumsum([0] + [ref.shape[1] for ref in tables]).tolist()
    for ref, start in zip(tables, starts):
        for low in range(0, ref.shape[1], block):
            logits_ref[:, start + low : start + low + block] = matmul(
                selected_ref[...], ref[:, low : low + block]
            )
    stats_ref[...] = jnp.zeros_like(stats_ref)

    def gather_stats(step, carry):
        at = pl.ds(pl.multiple_of(step * step_rows, step_rows), step_rows)
        logits = logits_ref[at, :]
        column = lax.broadcasted_iota(jnp.int32, logits.shape, 1)
        real = column < limit
        masked = jnp.where(real, logits, -1e30)
        top = jnp.max(masked, axis=1, keepdims=True)
        stats_ref[at, 0:1] = top
        stats_ref[at, 1:2] = jnp.sum(jnp.exp(masked - top), axis=1, keepdims=True)
        stats_ref[at, 2:3] = jnp.sum(jnp.where(real, logits, 0.0), axis=1, keepdims=True)
        hit = column == targets_ref[at, :]
        stats_ref[at, 3:4] = jnp.sum(jnp.where(hit, logits, 0.0), axis=1, keepdims=True)
        return carry

    lax.fori_loop(0, rows // step_rows, gather_stats, 0)
    share_stats_ref[share] = jnp.transpose(stats_ref[...])[0:8]
    copies = [
        send(share_stats_ref.at[share], share_stats_ref.at[share], stat_sems.at[0, step], stat_sems.at[1, step], peer)
        for step, peer in enumerate(near)
    ]
    for copy in copies:
        copy.wait()
    merged = combine_stats([share_stats_ref[index] for index in range(shares)])
    group_stats_ref[group] = jnp.concatenate(merged + (jnp.zeros((4, rows), jnp.float32),), axis=0)
    copies = [
        send(group_stats_ref.at[group], group_stats_ref.at[group], stat_sems.at[2, step], stat_sems.at[3, step], peer)
        for step, peer in enumerate(far)
    ]
    for copy in copies:
        copy.wait()
    row_max, exp_total, smooth, target = combine_stats(
        [group_stats_ref[index] for index in range(groups)]
    )
    log_total = row_max + jnp.log(exp_total)
    per_row = log_total - (1.0 - SMOOTH) * target - SMOOTH * smooth / (vocab_total - 1)
    loss = jnp.sum(counted_ref[...] * per_row, axis=1, keepdims=True)
    loss_ref[...] = jnp.broadcast_to(loss, loss_ref.shape)
    turned_ref[...] = jnp.zeros_like(turned_ref)
    turned_ref[0:1, :] = log_total
    stats_ref[...] = jnp.transpose(turned_ref[...])

    def make_dz(step, carry):
        at = pl.ds(pl.multiple_of(step * step_rows, step_rows), step_rows)
        logits = logits_ref[at, :]
        column = lax.broadcasted_iota(jnp.int32, logits.shape, 1)
        softmax_rows = jnp.exp(logits - stats_ref[at, 0:1])
        hit = jnp.where(column == targets_ref[at, :], 1.0 - SMOOTH, 0.0)
        grad = weights_ref[at, :] * (softmax_rows - hit - SMOOTH / (vocab_total - 1))
        dz_ref[at, :] = lowered(jnp.where(column < limit, grad, 0.0))
        return carry

    lax.fori_loop(0, rows // step_rows, make_dz, 0)
    loss_rows = rows // groups
    half, quarter = loss_rows // 2, loss_rows // 4

    def head_part(index):
        at = slice(index * block, (index + 1) * block)
        head_ref[:, at] = lowered(contract_rows(selected_ref[...], dz_ref[:, at]))

    early = head_out_ref.shape[2] // block
    for index in range(early):
        head_part(index)
    width_out = width // groups
    exchange = Exchange(
        lambda index: head_ref.at[
            pl.ds(pl.multiple_of(index * width_out, 16), width_out), pl.ds(0, early * block)
        ],
        head_out_ref,
        head_sems,
        groups,
    )
    grad_rows = 0.0
    for ref, start in zip(tables, starts):
        grad_rows = grad_rows + times_transposed(dz_ref[:, start : start + ref.shape[1]], ref[...])
    part_ref[...] = lowered(grad_rows).reshape(part_ref.shape)
    mine = pl.ds(pl.multiple_of(core * half, 16), half)
    other = pl.ds(pl.multiple_of((1 - core) * half, 16), half)
    copy = send(part_ref.at[:, other, :], core_ref, sems.at[0, 0], sems.at[1, 0], core_peer)
    parts = chunk // block
    middle = (early + parts) // 2
    copy.wait()
    part_ref[:, mine, :] = lowered(
        part_ref[:, mine, :].astype(jnp.float32) + core_ref[...].astype(jnp.float32)
    )
    base = core * half
    my_quarter = pl.ds(pl.multiple_of(base + side * quarter, 16), quarter)
    other_quarter = pl.ds(pl.multiple_of(base + (1 - side) * quarter, 16), quarter)
    copy = send(part_ref.at[:, other_quarter, :], side_ref, sems.at[0, 1], sems.at[1, 1], side_peer)
    for index in range(early, middle):
        head_part(index)
    copy.wait()
    side_ref[...] = lowered(
        part_ref[:, my_quarter, :].astype(jnp.float32) + side_ref[...].astype(jnp.float32)
    )
    group_ref[group] = side_ref[group]
    copies = [
        send(side_ref.at[peer[0]], group_ref.at[group], sems.at[0, 2 + step], sems.at[1, 2 + step], peer)
        for step, peer in enumerate(far)
    ]
    for index in range(middle, parts):
        head_part(index)
    for copy in copies:
        copy.wait()
    summed = group_ref[0].astype(jnp.float32)
    for index in range(1, groups):
        summed = summed + group_ref[index].astype(jnp.float32)
    sum_ref[...] = lowered(summed)
    grad_out_ref[my_quarter, :] = sum_ref[...]
    base_sem = 1 + groups
    copies = [
        send(sum_ref, grad_out_ref.at[my_quarter, :], sems.at[0, base_sem + step], sems.at[1, base_sem + step], peer)
        for step, peer in enumerate(near)
    ]
    for copy in copies:
        copy.wait()
    exchange.finish()


def put_grads(grads_ref, start, value):
    shape = grads_ref.shape[:4] + (value.shape[1],)
    grads_ref[:, :, :, :, start : start + value.shape[1]] = lowered(value).reshape(shape)


def feed_grads(grad_ref, stream_ref, pre_ref, norms_ref, row, w_ref, grads_ref, total):
    width = stream_ref.shape[1]
    hidden = pre_ref.shape[1]
    normed, _ = norm_forward(stream_ref[...], *gain_of(norms_ref, row))
    grad_low = lowered(grad_ref[...])
    pre = pre_ref[...]
    sigmoid_pre = jax.nn.sigmoid(pre)
    grad_pre = lowered(
        times_transposed(grad_low, w_ref[:, hidden : hidden + width])
        * sigmoid_pre
        * (1.0 + pre * (1.0 - sigmoid_pre))
    )
    total.begin(times_transposed(grad_pre, w_ref[:, :hidden]))
    activated = lowered(pre * sigmoid_pre)
    put_grads(grads_ref, hidden, contract_rows(activated, grad_low))
    total.middle()
    put_grads(grads_ref, 0, contract_rows(lowered(normed), grad_pre))


def norm_step(grad_ref, stream_ref, norms_ref, row, summed, rows_ref, slot):
    gain, shift = gain_of(norms_ref, row)
    _, kept = norm_forward(stream_ref[...], gain, shift)
    grad_in, grad_gain, grad_shift = norm_backward(summed, kept, gain)
    rows_ref[slot : slot + 1, :] = grad_gain
    rows_ref[slot + 1 : slot + 2, :] = grad_shift
    if grad_ref is None:
        return grad_in
    return grad_ref[...] + grad_in


def back_kernel(
    groups, shares, first_wide, refs_in, refs_out, *refs
):
    inputs, outputs, scratch = refs[:refs_in], refs[refs_in : refs_in + refs_out], refs[refs_in + refs_out :]
    (
        grad_selected_ref, positions_ref, stream_out_ref, stream_mid_ref, pre_dec_ref, norms_ref, w_dec_hbm,
        out_rows_hbm, memory_hbm, stream_dec_hbm, q_ref, kv_ref, context_cross_ref, logs_cross_ref,
        stream_two_hbm, stream_enc_hbm, pre_enc_hbm, w_early_hbm, looked_hbm, place_enc_hbm, place_dec_ref,
        qkv_dec_ref, context_dec_ref, logs_dec_ref, qkv_enc_ref, context_enc_ref, logs_enc_ref,
        head_in_ref,
    ) = inputs
    head_out_ref, own_tokens_ref, dec_shares_ref, own_ref, squares_ref = outputs
    (
        head_sems, load_sems, w_ref, w_enc_ref, out_rows_ref, memory_ref, stream_dec_ref, stream_two_ref,
        stream_enc_ref, pre_enc_ref, looked_ref,
        dec_grads_ref, mid_grads_ref, last_grads_ref,
        grad_ref, grad_enc_ref,
        context_ref, gq_ref, gkv_ref, gqkv_ref, gqkv_enc_ref, context_enc_grad_ref,
        g_enc_ref, g_self_ref, g_cross_ref, rows_dec_ref, rows_mid_ref, rows_ref,
        norm_rows_ref, blocks_ref, block_sems, cut_ref, token_sems, share_sems, dec_sems, dec_own_ref,
        local_sems,
    ) = scratch[:37]
    rest = scratch[37:]
    stream_ref = pre_enc_ref
    small_one, large_one = rest[:4], rest[4:8]
    small_two, large_two = small_one[:1] + rest[8:11], large_one[:1] + rest[11:14]
    dec_line = Owned(dec_grads_ref, rest[14:18])
    mid_line = Owned(mid_grads_ref, rest[18:22])
    last_line = Owned(last_grads_ref, rest[22:26])
    group, share, core, core_peer, side_peer = places()
    peers = share_peers(group, share, shares)
    load_w_dec = Late(w_dec_hbm, w_ref, load_sems.at[0])
    load_rows = Late(out_rows_hbm, out_rows_ref, load_sems.at[1])
    load_memory = Late(memory_hbm, memory_ref, load_sems.at[2])
    load_dec = Late(stream_dec_hbm, stream_dec_ref, load_sems.at[3])
    load_two = Late(stream_two_hbm, stream_two_ref, load_sems.at[4])
    load_enc = Late(stream_enc_hbm, stream_enc_ref, load_sems.at[5])
    load_pre = Late(pre_enc_hbm, pre_enc_ref, load_sems.at[6])
    load_w_enc = Late(
        w_early_hbm.at[:, pl.ds(first_wide, w_enc_ref.shape[1])], w_enc_ref, load_sems.at[7]
    )
    load_looked = Late(looked_hbm, looked_ref, load_sems.at[8])
    meet(peers + group_peers(group, share, groups))
    exchange = Exchange(
        head_blocks(head_in_ref, head_in_ref.shape[2] - head_out_ref.shape[2], head_out_ref.shape[2]),
        head_out_ref,
        head_sems,
        groups,
    )
    width = stream_out_ref.shape[1]
    own = q_ref.shape[1]
    hidden = pre_dec_ref.shape[1]
    in_start = hidden + width
    starts = (0, own, 2 * own)
    for rows in (rows_dec_ref, rows_mid_ref, rows_ref):
        rows[...] = jnp.zeros_like(rows)

    total = Total(small_one)
    down = lax.broadcasted_iota(jnp.int32, (stream_out_ref.shape[0], grad_selected_ref.shape[0]), 0)
    chosen = lowered(jnp.where(down == positions_ref[...], 1.0, 0.0))
    grad_final = matmul(chosen, grad_selected_ref[...])
    grad_ref[...] = norm_step(None, stream_out_ref, norms_ref, 6, grad_final, rows_dec_ref, 0)
    load_w_dec()
    feed_grads(grad_ref, stream_mid_ref, pre_dec_ref, norms_ref, 5, w_ref, dec_grads_ref, total)
    total.last()
    grad_ref[...] = norm_step(
        grad_ref, stream_mid_ref, norms_ref, 5, total.finish(), rows_dec_ref, 2
    )

    cross_total, memory_total = Total(small_two), Total(large_one)
    grad_low = lowered(grad_ref[...])
    load_rows()
    context_ref[...] = lowered(times_transposed(grad_low, out_rows_ref[2]))
    heads_backward(
        q_ref, kv_ref, (0, 0, own), logs_cross_ref, context_ref, gq_ref, gkv_ref, (0, 0, own), False
    )
    memory_total.begin(
        times_transposed(gkv_ref[...], w_ref[:, in_start + own : in_start + 3 * own])
    )
    cross_total.begin(times_transposed(gq_ref[...], w_ref[:, in_start : in_start + own]))
    load_w_first = Late(
        w_early_hbm.at[:, pl.ds(0, first_wide)], w_ref.at[:, pl.ds(0, first_wide)], load_sems.at[9]
    )
    g_cross_ref[...] = lowered(contract_rows(context_cross_ref[...], grad_low))
    memory_total.middle()
    cross_total.middle()
    load_dec()
    load_memory()
    normed, _ = norm_forward(stream_dec_ref[...], *gain_of(norms_ref, 4))
    gap = dec_grads_ref.shape[4] - in_start - 3 * own
    put_grads(dec_grads_ref, in_start, contract_rows(lowered(normed), gq_ref[...]))
    put_grads(dec_grads_ref, in_start + own, contract_rows(memory_ref[...], gkv_ref[...]))
    put_grads(dec_grads_ref, in_start + 3 * own, jnp.zeros((width, gap), jnp.float32))
    dec_line.begin()
    memory_total.last()
    cross_total.last()
    summed = memory_total.finish()
    load_two()
    grad_enc_ref[...] = norm_step(None, stream_two_ref, norms_ref, 2, summed, rows_mid_ref, 0)
    load_place = Late(place_enc_hbm, stream_two_ref, load_sems.at[10])
    grad_ref[...] = norm_step(
        grad_ref, stream_dec_ref, norms_ref, 4, cross_total.finish(), rows_dec_ref, 4
    )

    feed_total, self_total = Total(large_two), Total(small_one)
    load_enc()
    load_pre()
    load_w_enc()
    feed_grads(
        grad_enc_ref, stream_enc_ref, pre_enc_ref, norms_ref, 1, w_enc_ref, mid_grads_ref, feed_total
    )
    grad_low = lowered(grad_ref[...])
    context_ref[...] = lowered(times_transposed(grad_low, out_rows_ref[1]))
    feed_total.last()
    heads_backward(
        qkv_dec_ref, qkv_dec_ref, starts, logs_dec_ref, context_ref, gqkv_ref, gqkv_ref, starts, True
    )
    load_w_first()
    w_start = first_wide // 3
    self_total.begin(times_transposed(gqkv_ref[...], w_ref[:, w_start : w_start + 3 * own]))
    g_self_ref[...] = lowered(contract_rows(context_dec_ref[...], grad_low))
    self_total.middle()
    load_looked()
    enc_len = stream_enc_ref.shape[0]
    stream_dec_ref[...] = stream_of(looked_ref, enc_len, place_dec_ref)
    normed, _ = norm_forward(stream_dec_ref[...], *gain_of(norms_ref, 3))
    put_grads(mid_grads_ref, in_start, contract_rows(lowered(normed), gqkv_ref[...]))
    put_grads(mid_grads_ref, in_start + 3 * own, jnp.zeros((width, gap), jnp.float32))
    mid_line.begin()
    grad_enc_ref[...] = norm_step(
        grad_enc_ref, stream_enc_ref, norms_ref, 1, feed_total.finish(), rows_mid_ref, 2
    )
    self_total.last()
    tokens, part = looked_ref.shape[0], cut_ref.shape[2]
    quarter = tokens // shares
    block_rows = cut_ref.shape[1] // shares

    def put_tokens(first, rows):
        for index in range(groups):
            for piece in range(shares):
                low, high = max(first, piece * quarter), min(first + rows.shape[0], (piece + 1) * quarter)
                if low < high:
                    to = piece * block_rows - piece * quarter
                    cut_ref[index, to + low : to + high] = rows[
                        low - first : high - first, index * part : (index + 1) * part
                    ]

    grad_dec = norm_step(
        grad_ref, stream_dec_ref, norms_ref, 3, self_total.finish(), rows_mid_ref, 4
    )
    put_tokens(enc_len, lowered(grad_dec * math.sqrt(width)))

    total = Total(large_one)
    grad_low = lowered(grad_enc_ref[...])
    g_enc_ref[...] = lowered(contract_rows(context_enc_ref[...], grad_low))
    wide = blocks_ref.shape[2]
    in_wide = last_grads_ref.shape[4] - wide
    blocks_ref[...] = jnp.zeros_like(blocks_ref)
    for piece in range(shares):
        at = slice(piece * own, (piece + 1) * own)
        for matrix, source in enumerate((g_enc_ref, g_self_ref, g_cross_ref)):
            blocks_ref[piece, :, matrix * own : (matrix + 1) * own] = source[:, at]
    copies = []
    for half in range(2):
        target = last_grads_ref.at[share // 2, lax.rem(share, 2), half, :, pl.ds(in_wide, wide)]
        source_rows = pl.ds(half * part, part)
        for step, peer in enumerate(peers):
            copies.append(
                send(
                    blocks_ref.at[peer[1], source_rows, :],
                    target,
                    block_sems.at[half, 0, step],
                    block_sems.at[half, 1, step],
                    peer,
                )
            )
        keep = pltpu.make_async_copy(
            blocks_ref.at[share, source_rows, :], target, local_sems.at[half]
        )
        keep.start()
        copies.append(keep)
    context_enc_grad_ref[...] = lowered(times_transposed(grad_low, out_rows_ref[0]))
    heads_backward(
        qkv_enc_ref, qkv_enc_ref, starts, logs_enc_ref, context_enc_grad_ref, gqkv_enc_ref, gqkv_enc_ref, starts,
        False,
    )
    total.begin(times_transposed(gqkv_enc_ref[...], w_ref[:, : 3 * own]))
    load_place()
    stream_ref[...] = stream_of(looked_ref, 0, stream_two_ref)
    normed, _ = norm_forward(stream_ref[...], *gain_of(norms_ref, 0))
    total.middle()
    put_grads(last_grads_ref, 0, contract_rows(lowered(normed), gqkv_enc_ref[...]))
    put_grads(last_grads_ref, 3 * own, jnp.zeros((width, in_wide - 3 * own), jnp.float32))
    for copy in copies:
        copy.wait()
    last_line.begin()
    dec_line.beside()
    total.last()
    grad_enc = norm_step(grad_enc_ref, stream_ref, norms_ref, 0, total.finish(), rows_ref, 0)
    put_tokens(0, lowered(grad_enc * math.sqrt(width)))
    norm_rows_ref[...] = jnp.zeros_like(norm_rows_ref)
    order = (
        (0, rows_ref, 0),
        (1, rows_mid_ref, 2),
        (2, rows_mid_ref, 0),
        (3, rows_mid_ref, 4),
        (4, rows_dec_ref, 4),
        (5, rows_dec_ref, 2),
        (6, rows_dec_ref, 0),
    )
    for row, source, slot in order:
        norm_rows_ref[row : row + 1, :] = source[slot : slot + 1, :]
        norm_rows_ref[7 + row : 8 + row, :] = source[slot + 1 : slot + 2, :]
    norm_low = lowered(norm_rows_ref[...])
    for index in range(groups):
        for piece in range(shares):
            cut_ref[index, piece * block_rows + quarter : (piece + 1) * block_rows] = norm_low[
                :, index * part : (index + 1) * part
            ]
    own_rows = pl.ds(pl.multiple_of(share * block_rows, 16), block_rows)
    to_groups = Exchange(
        lambda index: cut_ref.at[index, own_rows, :], own_tokens_ref.at[share], token_sems, groups
    )
    mid_line.beside()
    dec_line.beyond()
    to_groups.finish()
    token_gather = ShareGather(own_tokens_ref, share_sems)
    last_line.beside()
    mid_line.beyond()
    dec_own_ref[...] = dec_line.finish()
    keep = pltpu.make_async_copy(dec_own_ref, dec_shares_ref.at[share], local_sems.at[2])
    keep.start()
    keep.wait()
    dec_gather = ShareGather(dec_shares_ref, dec_sems)
    token_gather.middle()
    last_line.beyond()
    middle = mid_grads_ref.shape[4]
    own_ref[:, :middle] = mid_line.finish()
    dec_gather.middle()
    token_gather.finish()
    own_ref[:, middle:] = last_line.finish()
    squares = 0.0
    for ref in (dec_own_ref, own_ref):
        value = ref[...].astype(jnp.float32)
        value = value * value
        squares = squares + jnp.sum(jnp.sum(value, axis=0, keepdims=True), axis=1, keepdims=True)
    lane = lax.broadcasted_iota(jnp.int32, squares_ref.shape, 1)
    squares_ref[...] = jnp.where(lane == 0, squares, 0.0)
    dec_gather.finish()
    exchange.finish()


def look_kernel(
    groups,
    picked_ref,
    looked_ref,
    send_ref, core_ref, side_ref, group_ref, sems,
):
    group, share, core, core_peer, side_peer = places()
    side = share // 2
    far = group_peers(group, share, groups)
    meet([core_peer, side_peer] + far)
    _, tokens, width = picked_ref.shape
    half, quarter = tokens // 2, tokens // 4
    mine = pl.ds(pl.multiple_of(core * half, 16), half)
    other = pl.ds(pl.multiple_of((1 - core) * half, 16), half)
    send(picked_ref.at[:, other, :], core_ref, sems.at[0, 0], sems.at[1, 0], core_peer).wait()
    core_ref[...] = core_ref[...] + picked_ref[:, mine, :]
    own_quarter = pl.ds(pl.multiple_of(side * quarter, 16), quarter)
    other_quarter = pl.ds(pl.multiple_of((1 - side) * quarter, 16), quarter)
    send(core_ref.at[:, other_quarter, :], side_ref, sems.at[0, 1], sems.at[1, 1], side_peer).wait()
    side_ref[...] = side_ref[...] + core_ref[:, own_quarter, :]
    group_ref[group] = side_ref[group]
    copies = [
        send(side_ref.at[peer[0]], group_ref.at[group], sems.at[0, 2 + step], sems.at[1, 2 + step], peer)
        for step, peer in enumerate(far)
    ]
    for copy in copies:
        copy.wait()
    for index in range(groups):
        send_ref[:, index * width : (index + 1) * width] = group_ref[index]
    at = pl.ds(pl.multiple_of(core * half + side * quarter, 16), quarter)
    looked_ref[at, :] = send_ref[...]
    end = 1 + groups
    send(send_ref, looked_ref.at[at, :], sems.at[0, end], sems.at[1, end], side_peer).wait()
    end = end + 1
    both = looked_ref.at[mine, :]
    send(both, both, sems.at[0, end], sems.at[1, end], core_peer).wait()


def squares_kernel(
    groups, shares,
    embedding_ref, dense_ref,
    out_ref,
    share_ref, group_ref, sems,
):
    group, share, _, _, _ = places()
    near, far = share_peers(group, share, shares), group_peers(group, share, groups)
    meet(near + far)
    down = lax.broadcasted_iota(jnp.int32, (8, 128), 0)
    share_ref[share] = jnp.where(down == 0, embedding_ref[...] + dense_ref[...], 0.0)
    copies = [
        send(share_ref.at[share], share_ref.at[share], sems.at[0, step], sems.at[1, step], peer)
        for step, peer in enumerate(near)
    ]
    for copy in copies:
        copy.wait()
    summed = share_ref[0]
    for index in range(1, shares):
        summed = summed + share_ref[index]
    group_ref[group] = summed
    copies = [
        send(group_ref.at[group], group_ref.at[group], sems.at[2, step], sems.at[3, step], peer)
        for step, peer in enumerate(far)
    ]
    for copy in copies:
        copy.wait()
    summed = group_ref[0]
    for index in range(1, groups):
        summed = summed + group_ref[index]
    out_ref[...] = jnp.broadcast_to(jnp.sum(summed), out_ref.shape)


def dense_kernel(
    rate, place_grads, factor_ref, *refs
):
    *grad_refs, w_ref, first_ref, second_ref, new_w_ref, new_first_ref, new_second_ref, wide_ref = refs
    place_grads(wide_ref, *grad_refs)
    updated = adam_update(
        w_ref[0],
        first_ref[0],
        second_ref[0],
        wide_ref[...].astype(jnp.float32),
        factor_ref[0],
        rate,
    )
    for out, value in zip((new_w_ref, new_first_ref, new_second_ref), updated):
        out[0] = value


def dense_update(name, rate, place_grads, factor, grads, w, first, second, parts, cut=None):
    matrices, rows, columns = w.shape
    rows = rows // parts
    own = pl.BlockSpec((1, rows, columns), lambda matrix, part: (matrix, part, 0))
    shares, width = grads[0].shape[:2]
    grad_specs = [
        pl.BlockSpec(
            (shares, width, cut[0] if cut else member.shape[2]),
            lambda matrix, part: (0, 0, cut[1] if cut else 0),
        )
        for member in grads
    ]
    return pl.pallas_call(
        partial(dense_kernel, rate, place_grads),
        grid=(matrices, parts),
        out_shape=[jax.ShapeDtypeStruct(w.shape, w.dtype)] * 3,
        in_specs=[pl.BlockSpec(memory_space=pltpu.SMEM)] + grad_specs + [own] * 3,
        out_specs=[own] * 3,
        scratch_shapes=[pltpu.VMEM((rows, columns), jnp.bfloat16)],
        compiler_params=pltpu.CompilerParams(vmem_limit_bytes=VMEM_BYTES),
        name=name,
    )(factor, *grads, w, first, second)


def place_columns(groups, matrix, source_ref, start):
    def place(wide_ref):
        @pl.when(pl.program_id(0) == matrix)
        def _():
            rows, columns = wide_ref.shape
            shares = source_ref.shape[0]
            piece = columns // groups // shares
            at = pl.ds(pl.multiple_of(pl.program_id(1) * rows, 16), rows)
            for number in range(groups):
                for share in range(shares):
                    low = (number * shares + share) * piece
                    wide_ref[:, low : low + piece] = source_ref[
                        share, at, start + number * piece : start + (number + 1) * piece
                    ]

    return place


def cut_kernel(groups, shares, gap, in_ref, out_ref, up_ref, down_ref, norms_ref, early_ref, dec_ref, square_ref):
    share = lax.axis_index("vocab")
    width, model_width = in_ref.shape[1], out_ref.shape[2]
    own = model_width // shares
    piece = up_ref.shape[2] // groups // shares
    hidden = groups * piece
    in_wide = 3 * own + gap
    early_ref[...] = jnp.zeros_like(early_ref)
    dec_ref[...] = jnp.zeros_like(dec_ref)

    def columns(target, start, source, groups_in, size, index):
        step = shares * size
        for number in range(groups_in):
            low = number * step + index * size
            target[:, start + number * size : start + (number + 1) * size] = lowered(
                source[:, low : low + size]
            )

    def put(index):
        columns(early_ref, 0, in_ref.at[0], 3, own, index)
        columns(early_ref, in_wide, in_ref.at[1], 3, own, index)
        for matrix in range(3):
            columns(early_ref, 2 * in_wide + matrix * own, out_ref.at[matrix], 1, own, index)
        rows = slice(index * (down_ref.shape[1] // shares), (index + 1) * (down_ref.shape[1] // shares))
        for matrix, (target, start) in enumerate(((early_ref, 3 * in_wide), (dec_ref, 0))):
            columns(target, start, up_ref.at[matrix], groups, piece, index)
            start = start + hidden
            target[:, start : start + model_width] = lowered(down_ref[matrix, rows, :])
        columns(dec_ref, hidden + model_width, in_ref.at[2], 3, own, index)

    for index in range(shares):
        pl.when(share == index)(partial(put, index))
    square_ref[...] = jnp.zeros_like(square_ref)
    square_ref[0 : norms_ref.shape[0], 0:width] = norms_ref[...]
    end = 3 * in_wide
    early_ref[:, end - gap : end] = lowered(jnp.transpose(square_ref[...])[0:width, 0:gap])


def cut_weights(groups, shares, gap, inputs, early_wide, dec_wide):
    width = inputs[0].shape[1]
    return pl.pallas_call(
        partial(cut_kernel, groups, shares, gap),
        out_shape=(
            jax.ShapeDtypeStruct((width, early_wide), jnp.bfloat16),
            jax.ShapeDtypeStruct((width, dec_wide), jnp.bfloat16),
        ),
        in_specs=[pl.BlockSpec(memory_space=pltpu.VMEM)] * len(inputs),
        out_specs=(pl.BlockSpec(memory_space=pltpu.VMEM),) * 2,
        scratch_shapes=[pltpu.VMEM((128, 128), jnp.float32)],
        compiler_params=pltpu.CompilerParams(vmem_limit_bytes=VMEM_BYTES),
        name="cut_weights",
    )(*inputs)


def numbers_kernel(
    groups, numbers_ref, hits_ref, all_numbers_ref, all_hits_ref, sems, local_sems
):
    group, share, _, _, _ = places()
    peers = group_peers(group, share, groups)
    meet(peers)
    copies = []
    for number, (source, target) in enumerate(
        ((numbers_ref, all_numbers_ref), (hits_ref, all_hits_ref))
    ):
        copies += [
            send(source, target.at[group], sems.at[number, 0, step], sems.at[number, 1, step], peer)
            for step, peer in enumerate(peers)
        ]
        keep = pltpu.make_async_copy(source, target.at[group], local_sems.at[number])
        keep.start()
        copies.append(keep)
    for copy in copies:
        copy.wait()


def local(
    enc_ids,
    labels,
    target_lengths,
    loss_positions,
    embedding,
    attn_in,
    attn_out,
    ffn_up,
    ffn_down,
    norms,
    embedding_first,
    attn_in_first,
    attn_out_first,
    ffn_up_first,
    ffn_down_first,
    norms_first,
    embedding_second,
    attn_in_second,
    attn_out_second,
    ffn_up_second,
    ffn_down_second,
    norms_second,
):
    groups, shares = lax.axis_size("dp"), lax.axis_size("vocab")
    group, share = lax.axis_index("dp"), lax.axis_index("vocab")
    enc_len, dec_len = enc_ids.shape[1], labels.shape[1]
    loss_count = loss_positions.shape[1]
    shard_rows, part_width = embedding.shape
    model_width = part_width * groups
    vocab_total = shard_rows * shares
    row_start = share * shard_rows
    root_width = math.sqrt(model_width)
    tokens = enc_len + dec_len

    bf16, f32 = jnp.bfloat16, jnp.float32
    sems = pltpu.SemaphoreType.DMA
    numbers = jnp.concatenate(
        [enc_ids, labels, loss_positions, target_lengths[:, None]], axis=1
    )
    number_count = numbers.shape[1]
    number_lanes = -(-number_count // 1024) * 128
    numbers = jnp.pad(numbers, ((0, 0), (0, 8 * number_lanes - number_count)))
    span = 1 << tokens.bit_length()
    own_tokens = jnp.concatenate([enc_ids[0], jnp.zeros((1,), jnp.int32), labels[0, :-1]])
    hits = list_hits(own_tokens - row_start, shard_rows, span)
    own = model_width // shares
    own_in, own_up = 3 * own, ffn_up.shape[2] // shares
    norm_rows = norms.shape[0]
    gap = -own_in % 128
    in_wide = own_in + gap
    dec_wide = own_up + model_width + in_wide
    first_wide = 3 * in_wide
    enc_wide = own_up + model_width
    chunk = -(-shard_rows // (groups * 3072)) * 3072
    table_cuts = (chunk // 4, 5 * chunk // 24, chunk // 6, 3 * chunk // 8)
    early_wide = first_wide + enc_wide
    mine_early, mine_dec = cut_weights(
        groups, shares, gap, (attn_in, attn_out, ffn_up, ffn_down, norms), early_wide, dec_wide
    )
    w_early = lax.all_gather(mine_early, "dp", axis=0, tiled=True)
    w_dec = lax.all_gather(mine_dec, "dp", axis=0, tiled=True)
    numbers, hits = call(
        partial(numbers_kernel, groups),
        "numbers",
        1,
        [numbers.reshape(8, number_lanes), hits.reshape(8, span // 8)],
        [
            shape_of((groups, 8, number_lanes), jnp.int32),
            shape_of((groups, 8, span // 8), jnp.int32),
        ],
        [sems((2, 2, groups - 1)), sems((2,))],
        0,
    )
    hits = hits.reshape(groups, span)
    numbers = numbers.reshape(groups, 8 * number_lanes)
    all_labels = numbers[:, enc_len:tokens]
    all_positions = numbers[:, tokens : tokens + loss_count]
    all_lengths = numbers[:, tokens + loss_count : number_count]
    at_place = all_positions[:, :, None] == jnp.arange(dec_len)
    all_targets = jnp.sum(jnp.where(at_place, all_labels[:, None, :], 0), axis=2).reshape(-1)
    all_counted = (all_positions < all_lengths).reshape(-1).astype(f32)
    token_count = jnp.sum(all_counted)

    picked, across = pick_rows(hits, groups * tokens, embedding.T, groups * chunk)
    place_enc = positions_numpy(enc_len, model_width)
    place_dec = positions_numpy(dec_len, model_width)
    enc_macs, dec_macs = enc_len * model_width, dec_len * model_width
    total_enc, total_dec = total_scratch(enc_len, model_width), total_scratch(dec_len, model_width)
    block_shape = (2, 2, 2, part_width)
    (looked,) = call(
        partial(look_kernel, groups),
        "look",
        2,
        [picked.reshape(groups, tokens, part_width)],
        [shape_of((tokens, model_width), bf16)],
        [
            pltpu.VMEM((tokens // 4, model_width), bf16),
            pltpu.VMEM((groups, tokens // 2, part_width), bf16),
            pltpu.VMEM((groups, tokens // 4, part_width), bf16),
            pltpu.VMEM((groups, tokens // 4, part_width), bf16),
            sems((2, groups + 3)),
        ],
        0,
    )
    table_zero = across.reshape(part_width, groups, chunk)[:, :, : table_cuts[0]]
    table_zero = lax.all_to_all(table_zero.transpose(1, 0, 2), "dp", 0, 0)
    forward_inputs = [looked, place_enc, place_dec, w_early, across]
    forward_outputs = [
        shape_of((groups, part_width, sum(table_cuts[1:3])), bf16),
        shape_of((3, own, model_width), bf16),
        shape_of((16, model_width), f32),
        shape_of((enc_len, 3 * own), bf16),
        shape_of((enc_len, own), bf16),
        shape_of((enc_len, 128), f32),
        shape_of((enc_len, model_width), f32),
        shape_of((enc_len, own_up), f32),
        shape_of((enc_len, model_width), f32),
        shape_of((enc_len, model_width), bf16),
        shape_of((dec_len, 3 * own), bf16),
        shape_of((dec_len, own), bf16),
        shape_of((dec_len, 128), f32),
        shape_of((dec_len, model_width), f32),
    ]
    (
        table_one, out_rows, norm_values,
        qkv_enc, context_enc, logs_enc, stream_enc, pre_enc, stream_two, memory,
        qkv_dec, context_dec, logs_dec, stream_dec,
    ) = call(
        partial(
            forward_kernel, groups, shares, table_cuts[0], table_cuts[1:3], len(forward_inputs),
            len(forward_outputs),
        ),
        "forward",
        3,
        forward_inputs,
        forward_outputs,
        [
            sems((2, 2, groups)),
            sems((3,)),
            sems((2,)),
            pltpu.VMEM((model_width, first_wide), bf16),
            pltpu.VMEM((model_width, enc_wide), bf16),
            pltpu.VMEM((enc_len, model_width), f32),
            pltpu.VMEM((enc_len, own_up), f32),
            pltpu.VMEM((enc_len, model_width), f32),
            pltpu.VMEM((shares, own, in_wide), bf16),
            sems((2, shares - 1)),
            sems,
            *total_dec,
            *total_enc,
            *total_enc[1:],
        ],
        8 * enc_macs * own_up,
        (3, 4),
        (0, 6, 7, 8),
    )
    (
        table_two, q_cross, kv_cross, context_cross, logs_cross, stream_mid, pre_dec, stream_out, selected,
    ) = call(
        partial(dec_kernel, groups, sum(table_cuts[:3])),
        "dec",
        4,
        [
            stream_dec, memory, norm_values, out_rows, loss_positions.reshape(-1, 1), w_dec, across,
        ],
        [
            shape_of((groups, part_width, table_cuts[3]), bf16),
            shape_of((dec_len, own), bf16),
            shape_of((enc_len, 2 * own), bf16),
            shape_of((dec_len, own), bf16),
            shape_of((dec_len, 128), f32),
            shape_of((dec_len, model_width), f32),
            shape_of((dec_len, own_up), f32),
            shape_of((dec_len, model_width), f32),
            shape_of((groups, loss_count, model_width), bf16),
        ],
        [
            pltpu.VMEM((model_width, dec_wide), bf16),
            sems,
            sems((2, groups)),
            pltpu.VMEM((loss_count, model_width), bf16),
            sems((2, groups - 1)),
            *total_dec,
            *total_dec[1:],
        ],
        8 * dec_macs * own_up,
        (5, 6),
        (0,),
    )

    rows_all = groups * loss_count
    first_row = row_start + group * chunk
    targets = all_targets - first_row
    inside = (targets >= 0) & (targets < jnp.minimum(chunk, shard_rows - group * chunk))
    targets = jnp.where(inside, targets, -1)[:, None]
    head_cut = chunk // 8
    loss, grad_selected, head_grad, head_zero = call(
        partial(head_kernel, groups, shares, shard_rows),
        "head",
        6,
        [
            selected.reshape(rows_all, model_width),
            table_zero.reshape(model_width, -1),
            table_one.reshape(model_width, -1),
            table_two.reshape(model_width, -1),
            targets,
            (all_counted / token_count)[:, None],
            all_counted[None, :],
        ],
        [
            shape_of((1, 128), f32),
            shape_of((loss_count, model_width), bf16),
            shape_of((model_width, chunk), bf16),
            shape_of((groups, part_width, head_cut), bf16),
        ],
        [
            sems((2, groups)),
            pltpu.VMEM((rows_all, chunk), f32),
            pltpu.VMEM((rows_all, chunk), bf16),
            pltpu.VMEM((rows_all, 128), f32),
            pltpu.VMEM((128, rows_all), f32),
            pltpu.VMEM((shares, 8, rows_all), f32),
            pltpu.VMEM((groups, 8, rows_all), f32),
            sems((4, max(groups, shares))),
            pltpu.VMEM((groups, loss_count, model_width), bf16),
            pltpu.VMEM((groups, loss_count // 2, model_width), bf16),
            pltpu.VMEM((groups, loss_count // 4, model_width), bf16),
            pltpu.VMEM((groups, loss_count // 4, model_width), bf16),
            pltpu.VMEM((loss_count // 4, model_width), bf16),
            sems((2, groups + shares)),
        ],
        6 * rows_all * chunk * model_width,
        (),
        (3,),
    )
    loss_sum = loss[0, 0]
    head_grad = head_grad.reshape(groups, part_width, chunk)
    late_wide = dec_wide + 2 * in_wide
    quarter = tokens // shares
    back_inputs = [
        grad_selected, loss_positions.reshape(1, -1), stream_out, stream_mid, pre_dec, norm_values, w_dec,
        out_rows, memory, stream_dec, q_cross, kv_cross, context_cross, logs_cross,
        stream_two, stream_enc, pre_enc, w_early, looked, place_enc, place_dec,
        qkv_dec, context_dec, logs_dec, qkv_enc, context_enc, logs_enc,
        head_grad,
    ]

    head_one, grad_tokens, dec_shares, late_own, dense_squares = call(
        partial(
            back_kernel, groups, shares, first_wide, len(back_inputs), 5
        ),
        "backward",
        7,
        back_inputs,
        [
            shape_of((groups, part_width, chunk - head_cut), bf16),
            shape_of((shares, groups, quarter + 16, part_width), bf16),
            shape_of((shares, part_width, dec_wide), bf16),
            shape_of((part_width, late_wide), bf16),
            shape_of((1, 128), f32),
        ],
        [
            sems((2, groups)),
            sems((11,)),
            pltpu.VMEM((model_width, dec_wide), bf16),
            pltpu.VMEM((model_width, own_up + model_width), bf16),
            pltpu.VMEM(out_rows.shape, bf16),
            pltpu.VMEM((enc_len, model_width), bf16),
            pltpu.VMEM((dec_len, model_width), f32),
            pltpu.VMEM((enc_len, model_width), f32),
            pltpu.VMEM((enc_len, model_width), f32),
            pltpu.VMEM((enc_len, own_up), f32),
            pltpu.VMEM((tokens, model_width), bf16),
            pltpu.VMEM(block_shape + (dec_wide,), bf16),
            pltpu.VMEM(block_shape + (dec_wide,), bf16),
            pltpu.VMEM(block_shape + (2 * in_wide,), bf16),
            pltpu.VMEM((dec_len, model_width), f32),
            pltpu.VMEM((enc_len, model_width), f32),
            pltpu.VMEM((dec_len, own), bf16),
            pltpu.VMEM((dec_len, own), bf16),
            pltpu.VMEM((enc_len, 2 * own), bf16),
            pltpu.VMEM((dec_len, 3 * own), bf16),
            pltpu.VMEM((enc_len, 3 * own), bf16),
            pltpu.VMEM((enc_len, own), bf16),
            pltpu.VMEM((own, model_width), bf16),
            pltpu.VMEM((own, model_width), bf16),
            pltpu.VMEM((own, model_width), bf16),
            pltpu.VMEM((8, model_width), f32),
            pltpu.VMEM((8, model_width), f32),
            pltpu.VMEM((8, model_width), f32),
            pltpu.VMEM((16, model_width), f32),
            pltpu.VMEM((shares, own, in_wide), bf16),
            sems((2, 2, shares - 1)),
            pltpu.VMEM((groups, tokens + 16 * shares, part_width), bf16),
            sems((2, groups)),
            sems((2, 3)),
            sems((2, 3)),
            pltpu.VMEM((part_width, dec_wide), bf16),
            sems((3,)),
            *total_dec,
            *total_enc,
            *total_dec[1:],
            *total_enc[1:],
            *line_scratch(part_width, dec_wide),
            *line_scratch(part_width, dec_wide),
            *line_scratch(part_width, 2 * in_wide),
        ],
        16 * (enc_macs + dec_macs) * own_up,
        (6, 7, 8, 9, 14, 15, 16, 17, 18, 19, 27),
        (0, 1, 2),
    )
    late_shares = lax.all_gather(late_own, "vocab", axis=0, tiled=False)
    g_embedding, embedding_squares = spread_rows(
        hits, groups * tokens, grad_tokens, (head_zero, head_one)
    )
    g_embedding = g_embedding[:, :shard_rows].astype(f32).T
    g_norms = jnp.sum(grad_tokens[0, :, quarter : quarter + norm_rows].astype(f32), axis=0)
    dense_squares = dense_squares + jnp.sum(g_norms * g_norms) / (shares * dense_squares.shape[1])
    (squares,) = call(
        partial(squares_kernel, groups, shares),
        "squares",
        10,
        [embedding_squares, dense_squares],
        [shape_of((1, 128), f32)],
        [
            pltpu.VMEM((shares, 8, 128), f32),
            pltpu.VMEM((groups, 8, 128), f32),
            sems((4, max(groups, shares))),
        ],
        0,
    )
    grad_norm = jnp.sqrt(squares[0, 0])
    factor = jnp.minimum(1.0, CLIP / (grad_norm + 1e-06))
    grad_pair = [late_shares, dec_shares]
    in_start, late_in, late_out = own_up + model_width, dec_wide, dec_wide + in_wide

    def place_in(wide_ref, late_ref, dec_ref):
        place_columns(3, 0, late_ref, late_in)(wide_ref)
        place_columns(3, 1, late_ref, in_start)(wide_ref)
        place_columns(3, 2, dec_ref, in_start)(wide_ref)

    def place_out(wide_ref, late_ref):
        for matrix in range(3):
            place_columns(1, matrix, late_ref, late_out + matrix * own)(wide_ref)

    def place_up(wide_ref, late_ref, dec_ref):
        place_columns(groups, 0, late_ref, 0)(wide_ref)
        place_columns(groups, 1, dec_ref, 0)(wide_ref)

    def place_down(wide_ref, late_ref, dec_ref):
        for matrix, ref in enumerate((late_ref, dec_ref)):

            @pl.when(pl.program_id(0) == matrix)
            def _(ref=ref):
                wide_ref[...] = ref[pl.program_id(1)]

    scale = factor.reshape(1)
    new_in = dense_update(
        "adam_in", RATES[1], place_in, scale, grad_pair, attn_in, attn_in_first, attn_in_second, 2
    )
    new_out = dense_update(
        "adam_out", RATES[2], place_out, scale, grad_pair[:1], attn_out, attn_out_first, attn_out_second, 1
    )
    new_up = dense_update(
        "adam_up", RATES[3], place_up, scale, grad_pair, ffn_up, ffn_up_first, ffn_up_second, 2,
        (own_up, 0),
    )
    new_down = dense_update(
        "adam_down", RATES[4], place_down, scale, grad_pair, ffn_down, ffn_down_first, ffn_down_second, shares,
        (model_width, 1),
    )
    new_embedding = adam_update(
        embedding, embedding_first, embedding_second, g_embedding, factor, RATES[0]
    )
    new_norms = adam_update(norms, norms_first, norms_second, g_norms, factor, RATES[5])
    updated = (new_embedding, new_in, new_out, new_up, new_down, new_norms)
    return (loss_sum, token_count, grad_norm) + tuple(
        updated[slot][kind] for kind in range(3) for slot in range(6)
    )


def splits_evenly(mesh):
    return HEADS % mesh.shape["vocab"] == 0 and mesh.shape["dp"] == 8


def solution(mesh):
    placed = (
        P("dp", None),
        P("dp", None),
        P("dp"),
        P("dp", None),
        P("vocab", "dp"),
        P(None, "dp", None),
        P(None, "dp", None),
        P(None, "dp", None),
        P(None, "dp", None),
        P(None, "dp"),
        P("vocab", "dp"),
        P(None, "dp", None),
        P(None, "dp", None),
        P(None, "dp", None),
        P(None, "dp", None),
        P(None, "dp"),
        P("vocab", "dp"),
        P(None, "dp", None),
        P(None, "dp", None),
        P(None, "dp", None),
        P(None, "dp", None),
        P(None, "dp"),
    )
    return jax.shard_map(
        local if splits_evenly(mesh) else local_copied,
        mesh=mesh,
        in_specs=placed,
        out_specs=(
            P(),
            P(),
            P(),
            P("vocab", "dp"),
            P(None, "dp", None),
            P(None, "dp", None),
            P(None, "dp", None),
            P(None, "dp", None),
            P(None, "dp"),
            P("vocab", "dp"),
            P(None, "dp", None),
            P(None, "dp", None),
            P(None, "dp", None),
            P(None, "dp", None),
            P(None, "dp"),
            P("vocab", "dp"),
            P(None, "dp", None),
            P(None, "dp", None),
            P(None, "dp", None),
            P(None, "dp", None),
            P(None, "dp"),
        ),
        check_vma=False,
    )
```

```python
from functools import partial
import math

import jax
import jax.numpy as jnp
import numpy as np
from jax import lax
from jax.experimental import pallas as pl
from jax.experimental.pallas import tpu as pltpu
from jax.sharding import PartitionSpec as P

HEADS = 12
HEAD_DIM = 64
STEP = 10


EPS_NORM = 1e-05
SMOOTH = 0.1
CLIP = 0.02
RATES = (0.05, 0.05, 0.4, 0.05, 0.05, 0.8)
BETA_ONE = 0.9
BETA_TWO = 0.999
ADAM_EPS = 1e-08
DECAY = 0.01


def lowered(tensor):
    return tensor.astype(jnp.bfloat16)


def matmul(left_side, right_side):
    return jnp.dot(left_side, right_side, preferred_element_type=jnp.float32)


def times_transposed(left_side, right_side):
    return lax.dot_general(
        left_side, right_side, (((1,), (1,)), ((), ())), preferred_element_type=jnp.float32
    )


def contract_rows(left_side, right_side):
    return lax.dot_general(
        left_side, right_side, (((0,), (0,)), ((), ())), preferred_element_type=jnp.float32
    )


def positions_table(length, model_width):
    position_col = jnp.arange(length, dtype=jnp.float32)[:, None]
    freq_index = jnp.arange(model_width // 2, dtype=jnp.float32)[None, :]
    angles = position_col * jnp.exp(freq_index * (-2.0 * math.log(10000.0) / model_width))
    return jnp.concatenate([jnp.sin(angles), jnp.cos(angles)], axis=1)


def norm_forward(tensor, gain_row, shift_row):
    center = tensor - jnp.mean(tensor, axis=-1, keepdims=True)
    scale_inv = lax.rsqrt(jnp.mean(center * center, axis=-1, keepdims=True) + EPS_NORM)
    normed = center * scale_inv
    return (normed * gain_row + shift_row, (normed, scale_inv))


def norm_backward_rows(grad_out, saved_parts, gain_row):
    normed, scale_inv = saved_parts
    grad_normed = grad_out * gain_row
    grad_in = scale_inv * (
        grad_normed
        - jnp.mean(grad_normed, axis=-1, keepdims=True)
        - normed * jnp.mean(grad_normed * normed, axis=-1, keepdims=True)
    )
    return (grad_in, jnp.sum(grad_out * normed, axis=0), jnp.sum(grad_out, axis=0))


def split_heads(rows, batch_size):
    return rows.reshape(batch_size, -1, HEADS, rows.shape[1] // HEADS)


def score_block(queries, key_rows, causal):
    scores = jnp.einsum(
        "qhe,khe->hqk", queries, key_rows, preferred_element_type=jnp.float32
    ) * HEAD_DIM ** (-0.5)
    if causal:
        allowed = jnp.arange(queries.shape[0])[:, None] >= jnp.arange(key_rows.shape[0])[None, :]
        scores = jnp.where(allowed[None], scores, -1e30)
    return scores


def attend_one(block_args, causal):
    queries, key_rows, value_rows = block_args
    scores = score_block(queries, key_rows, causal)
    row_top = jnp.max(scores, axis=-1, keepdims=True)
    exponent = jnp.exp(scores - row_top)
    row_total = jnp.sum(exponent, axis=-1, keepdims=True)
    softmax_out = lowered(exponent / row_total)
    context = jnp.einsum(
        "hqk,khe->qhe", softmax_out, value_rows, preferred_element_type=jnp.float32
    )
    return (lowered(context), (row_top + jnp.log(row_total))[..., 0])


def attend_back(block_args, causal):
    queries, key_rows, value_rows, log_total, grad_context = block_args
    scores = score_block(queries, key_rows, causal)
    softmax_out = jnp.exp(scores - log_total[..., None])
    grad_values = jnp.einsum(
        "hqk,qhe->khe", lowered(softmax_out), grad_context, preferred_element_type=jnp.float32
    )
    grad_softmax = jnp.einsum(
        "qhe,khe->hqk", grad_context, value_rows, preferred_element_type=jnp.float32
    )
    grad_scores = lowered(
        softmax_out * (grad_softmax - jnp.sum(grad_softmax * softmax_out, axis=-1, keepdims=True))
    )
    grad_queries = jnp.einsum(
        "hqk,khe->qhe", grad_scores, key_rows, preferred_element_type=jnp.float32
    ) * HEAD_DIM ** (-0.5)
    grad_keys = jnp.einsum(
        "hqk,qhe->khe", grad_scores, queries, preferred_element_type=jnp.float32
    ) * HEAD_DIM ** (-0.5)
    return (lowered(grad_queries), lowered(grad_keys), lowered(grad_values))


def layer_forward(stream, memory, blocks, feed_parts, gain_rows, shifts, batch_size):
    kept_values = []
    for block_order, (w_in, w_out, norm_row) in enumerate(blocks):
        normed, norm_kept = norm_forward(stream, gain_rows[norm_row], shifts[norm_row])
        query_in = lowered(normed)
        model_width = w_out.shape[0]
        if block_order == 0:
            projected = lowered(matmul(query_in, w_in))
            queries = projected[:, :model_width]
            key_rows = projected[:, model_width : 2 * model_width]
            value_rows = projected[:, 2 * model_width :]
            memory_in = query_in
        else:
            memory_in = memory
            queries = lowered(matmul(query_in, w_in[:, :model_width]))
            paired = lowered(matmul(memory, w_in[:, model_width:]))
            key_rows, value_rows = (paired[:, :model_width], paired[:, model_width:])
        causal = memory is not None and block_order == 0
        heads = (
            split_heads(queries, batch_size),
            split_heads(key_rows, batch_size),
            split_heads(value_rows, batch_size),
        )
        context, log_total = lax.map(partial(attend_one, causal=causal), heads)
        context = context.reshape(-1, model_width)
        stream = stream + matmul(context, w_out)
        kept_values.append((norm_kept, query_in, memory_in, heads, context, log_total))
    w_up, w_down, norm_row = feed_parts
    normed, norm_kept = norm_forward(stream, gain_rows[norm_row], shifts[norm_row])
    hidden_in = lowered(normed)
    hidden_pre = matmul(hidden_in, w_up)
    activated = lowered(jax.nn.silu(hidden_pre))
    stream = stream + matmul(activated, w_down)
    kept_values.append((norm_kept, hidden_in, hidden_pre, activated))
    return (stream, kept_values)


def layer_backward(grad_stream, memory, blocks, feed_parts, gain_rows, kept_values, batch_size):
    w_up, w_down, norm_row = feed_parts
    norm_kept, hidden_in, hidden_pre, activated = kept_values[-1]
    grad_low = lowered(grad_stream)
    grad_down = contract_rows(activated, grad_low)
    sigmoid_pre = jax.nn.sigmoid(hidden_pre)
    grad_pre = lowered(
        times_transposed(grad_low, w_down) * sigmoid_pre * (1.0 + hidden_pre * (1.0 - sigmoid_pre))
    )
    grad_up = contract_rows(hidden_in, grad_pre)
    grad_in, grad_gain, grad_shift = norm_backward_rows(
        times_transposed(grad_pre, w_up), norm_kept, gain_rows[norm_row]
    )
    grad_stream = grad_stream + grad_in
    norm_grads = [(norm_row, grad_gain, grad_shift)]
    block_grads = [None] * len(blocks)
    grad_memory = None
    for block_order in reversed(range(len(blocks))):
        w_in, w_out, norm_row = blocks[block_order]
        norm_kept, query_in, memory_in, heads, context, log_total = kept_values[block_order]
        model_width = w_out.shape[0]
        grad_low = lowered(grad_stream)
        grad_w_out = contract_rows(context, grad_low)
        grad_context = split_heads(lowered(times_transposed(grad_low, w_out)), batch_size)
        causal = memory is not None and block_order == 0
        grad_heads = lax.map(partial(attend_back, causal=causal), heads + (log_total, grad_context))
        grad_queries, grad_keys, grad_values = [
            member.reshape(-1, model_width) for member in grad_heads
        ]
        if block_order == 0:
            grad_proj = jnp.concatenate([grad_queries, grad_keys, grad_values], axis=1)
            grad_w_in = contract_rows(query_in, grad_proj)
            grad_normed = times_transposed(grad_proj, w_in)
        else:
            grad_pair = jnp.concatenate([grad_keys, grad_values], axis=1)
            grad_w_in = jnp.concatenate(
                [contract_rows(query_in, grad_queries), contract_rows(memory_in, grad_pair)], axis=1
            )
            grad_normed = times_transposed(grad_queries, w_in[:, :model_width])
            grad_memory = times_transposed(grad_pair, w_in[:, model_width:])
        grad_in, grad_gain, grad_shift = norm_backward_rows(grad_normed, norm_kept, gain_rows[norm_row])
        grad_stream = grad_stream + grad_in
        norm_grads.append((norm_row, grad_gain, grad_shift))
        block_grads[block_order] = (grad_w_in, grad_w_out)
    return (grad_stream, grad_memory, block_grads, (grad_up, grad_down), norm_grads)


def adam_update(weight, first_moment, second_moment, gradient, factor, rate):
    clipped = gradient * factor
    new_first = BETA_ONE * first_moment + (1.0 - BETA_ONE) * clipped
    new_second = BETA_TWO * second_moment + (1.0 - BETA_TWO) * clipped * clipped
    corrected = (
        new_first
        / (1.0 - BETA_ONE**STEP)
        / (jnp.sqrt(new_second / (1.0 - BETA_TWO**STEP)) + ADAM_EPS)
    )
    return (weight - rate * (corrected + DECAY * weight), new_first, new_second)


def local_copied(
    enc_ids,
    labels,
    target_lengths,
    loss_positions,
    embedding,
    attn_in,
    attn_out,
    ffn_up,
    ffn_down,
    norms,
    embedding_first,
    attn_in_first,
    attn_out_first,
    ffn_up_first,
    ffn_down_first,
    norms_first,
    embedding_second,
    attn_in_second,
    attn_out_second,
    ffn_up_second,
    ffn_down_second,
    norms_second,
):
    batch_size, enc_len = enc_ids.shape
    dec_len = labels.shape[1]
    emb_table, w_in_all, w_out_all, w_up_all, w_down_all, norm_table = (
        lax.all_gather(lowered(embedding), "dp", axis=1, tiled=True),
        lax.all_gather(lowered(attn_in), "dp", axis=1, tiled=True),
        lax.all_gather(lowered(attn_out), "dp", axis=1, tiled=True),
        lax.all_gather(lowered(ffn_up), "dp", axis=1, tiled=True),
        lax.all_gather(lowered(ffn_down), "dp", axis=1, tiled=True),
        lax.all_gather(lowered(norms), "dp", axis=1, tiled=True),
    )
    model_width = emb_table.shape[1]
    shard_rows = emb_table.shape[0]
    vocab_total = shard_rows * lax.axis_size("vocab")
    row_start = lax.axis_index("vocab") * shard_rows
    norm_values = norm_table.astype(jnp.float32)
    gain_rows, shifts = (norm_values[:7], norm_values[7:])
    dec_ids = jnp.concatenate([jnp.zeros((batch_size, 1), jnp.int32), labels[:, :-1]], axis=1)
    token_list = jnp.concatenate([enc_ids.reshape(-1), dec_ids.reshape(-1)])
    local_rows = token_list - row_start
    inside = (local_rows >= 0) & (local_rows < shard_rows)
    safe_rows = jnp.clip(local_rows, 0, shard_rows - 1)
    picked = jnp.where(
        inside[:, None], jnp.take(emb_table, safe_rows, axis=0).astype(jnp.float32), 0.0
    )
    looked = lax.psum(picked.astype(jnp.bfloat16), "vocab").astype(jnp.float32)
    root_width = math.sqrt(model_width)
    enc_tokens = batch_size * enc_len
    enc_stream = (
        looked[:enc_tokens].reshape(batch_size, enc_len, model_width) * root_width
        + positions_table(enc_len, model_width)
    ).reshape(enc_tokens, model_width)
    dec_stream = (
        looked[enc_tokens:].reshape(batch_size, dec_len, model_width) * root_width
        + positions_table(dec_len, model_width)
    ).reshape(batch_size * dec_len, model_width)
    enc_blocks = [(w_in_all[0], w_out_all[0], 0)]
    dec_blocks = [(w_in_all[1], w_out_all[1], 3), (w_in_all[2], w_out_all[2], 4)]
    enc_feed = (w_up_all[0], w_down_all[0], 1)
    dec_feed = (w_up_all[1], w_down_all[1], 5)
    enc_out, enc_kept = layer_forward(
        enc_stream, None, enc_blocks, enc_feed, gain_rows, shifts, batch_size
    )
    memory, memory_kept = norm_forward(enc_out, gain_rows[2], shifts[2])
    memory_low = lowered(memory)
    dec_out, dec_kept = layer_forward(
        dec_stream, memory_low, dec_blocks, dec_feed, gain_rows, shifts, batch_size
    )
    final, final_kept = norm_forward(dec_out, gain_rows[6], shifts[6])
    chosen = (jnp.arange(batch_size)[:, None] * dec_len + loss_positions).reshape(-1)
    selected = lowered(jnp.take(final, chosen, axis=0))
    logits = times_transposed(selected, emb_table)
    columns = row_start + jnp.arange(shard_rows)
    padding = columns == vocab_total - 1
    masked = jnp.where(padding[None, :], -1e30, logits)
    target_local = jnp.take_along_axis(labels, loss_positions, axis=1).reshape(-1) - row_start
    target_hit = (jnp.arange(shard_rows)[None, :] == target_local[:, None]).astype(jnp.float32)
    target_term = jnp.sum(target_hit * logits, axis=1)
    smooth_term = jnp.sum(jnp.where(padding[None, :], 0.0, logits), axis=1)
    local_max = jnp.max(masked, axis=1)
    row_max = lax.pmax(local_max, "vocab")
    exp_local = jnp.sum(jnp.exp(masked - row_max[:, None]), axis=1)
    exp_total, smooth_total, target_total = lax.psum((exp_local, smooth_term, target_term), "vocab")
    log_total = row_max + jnp.log(exp_total)
    per_row = log_total - (1.0 - SMOOTH) * target_total - SMOOTH * smooth_total / (vocab_total - 1)
    counted = (loss_positions < target_lengths[:, None]).reshape(-1).astype(jnp.float32)
    loss_sum, token_count = lax.psum((jnp.sum(counted * per_row), jnp.sum(counted)), "dp")
    softmax_rows = jnp.exp(masked - log_total[:, None])
    grad_logits = (counted / token_count)[:, None] * (
        softmax_rows - (1.0 - SMOOTH) * target_hit - SMOOTH / (vocab_total - 1)
    )
    grad_logits = lowered(jnp.where(padding[None, :], 0.0, grad_logits))
    grad_selected = lax.psum(matmul(grad_logits, emb_table).astype(jnp.bfloat16), "vocab").astype(
        jnp.float32
    )
    grad_final = jnp.zeros_like(final).at[chosen].add(grad_selected)
    grad_dec_out, gain_six, shift_six = norm_backward_rows(grad_final, final_kept, gain_rows[6])
    grad_dec_stream, grad_memory, dec_block_grads, dec_feed_grads, dec_norm_grads = layer_backward(
        grad_dec_out, memory_low, dec_blocks, dec_feed, gain_rows, dec_kept, batch_size
    )
    grad_enc_out, gain_two, shift_two = norm_backward_rows(grad_memory, memory_kept, gain_rows[2])
    grad_enc_stream, _, enc_block_grads, enc_feed_grads, enc_norm_grads = layer_backward(
        grad_enc_out, None, enc_blocks, enc_feed, gain_rows, enc_kept, batch_size
    )
    grad_attn_in = jnp.stack([enc_block_grads[0][0], dec_block_grads[0][0], dec_block_grads[1][0]])
    grad_attn_out = jnp.stack([enc_block_grads[0][1], dec_block_grads[0][1], dec_block_grads[1][1]])
    grad_up_all = jnp.stack([enc_feed_grads[0], dec_feed_grads[0]])
    grad_down_all = jnp.stack([enc_feed_grads[1], dec_feed_grads[1]])
    grad_norms = jnp.zeros((14, model_width), jnp.float32)
    for norm_row, grad_gain, grad_shift in (
        enc_norm_grads + dec_norm_grads + [(2, gain_two, shift_two), (6, gain_six, shift_six)]
    ):
        grad_norms = grad_norms.at[norm_row].set(grad_gain).at[norm_row + 7].set(grad_shift)
    grad_tokens = jnp.concatenate([grad_enc_stream, grad_dec_stream], axis=0) * root_width
    head_term = contract_rows(grad_logits, selected)
    lookup_term = (
        jnp.zeros((shard_rows, model_width), jnp.float32)
        .at[safe_rows]
        .add(jnp.where(inside[:, None], grad_tokens, 0.0))
    )
    g_attn_in, g_attn_out, g_up, g_down, g_norms, g_embedding = (
        lax.psum_scatter(
            grad_attn_in.astype(jnp.bfloat16), "dp", scatter_dimension=1, tiled=True
        ).astype(jnp.float32),
        lax.psum_scatter(
            grad_attn_out.astype(jnp.bfloat16), "dp", scatter_dimension=1, tiled=True
        ).astype(jnp.float32),
        lax.psum_scatter(
            grad_up_all.astype(jnp.bfloat16), "dp", scatter_dimension=1, tiled=True
        ).astype(jnp.float32),
        lax.psum_scatter(
            grad_down_all.astype(jnp.bfloat16), "dp", scatter_dimension=1, tiled=True
        ).astype(jnp.float32),
        lax.psum_scatter(
            grad_norms.astype(jnp.bfloat16), "dp", scatter_dimension=1, tiled=True
        ).astype(jnp.float32),
        lax.psum_scatter(
            (head_term + lookup_term).astype(jnp.bfloat16), "dp", scatter_dimension=1, tiled=True
        ).astype(jnp.float32),
    )
    gradients = (g_embedding, g_attn_in, g_attn_out, g_up, g_down, g_norms)
    dense_squares = sum((jnp.sum(member * member) for member in gradients[1:]))
    squares = lax.psum(
        dense_squares / lax.axis_size("vocab") + jnp.sum(g_embedding * g_embedding), ("dp", "vocab")
    )
    grad_norm = jnp.sqrt(squares)
    factor = jnp.minimum(1.0, CLIP / (grad_norm + 1e-06))
    params = (embedding, attn_in, attn_out, ffn_up, ffn_down, norms)
    firsts = (
        embedding_first,
        attn_in_first,
        attn_out_first,
        ffn_up_first,
        ffn_down_first,
        norms_first,
    )
    seconds = (
        embedding_second,
        attn_in_second,
        attn_out_second,
        ffn_up_second,
        ffn_down_second,
        norms_second,
    )
    updated = [
        adam_update(params[slot], firsts[slot], seconds[slot], gradients[slot], factor, RATES[slot])
        for slot in range(6)
    ]
    return (
        loss_sum,
        token_count,
        grad_norm,
        updated[0][0],
        updated[1][0],
        updated[2][0],
        updated[3][0],
        updated[4][0],
        updated[5][0],
        updated[0][1],
        updated[1][1],
        updated[2][1],
        updated[3][1],
        updated[4][1],
        updated[5][1],
        updated[0][2],
        updated[1][2],
        updated[2][2],
        updated[3][2],
        updated[4][2],
        updated[5][2],
    )


VMEM_BYTES = 60 * 1024 * 1024


def positions_numpy(length, model_width):
    place = np.arange(length, dtype=np.float32)[:, None]
    index = np.arange(model_width // 2, dtype=np.float32)[None, :]
    angles = place * np.exp(index * np.float32(-2.0 * math.log(10000.0) / model_width))
    return np.concatenate([np.sin(angles), np.cos(angles)], axis=1).astype(np.float32)


def hits_kernel(rows, span, ids_ref, list_ref):
    def one(step, found):
        for inner in range(8):
            slot = step * 8 + inner
            row = ids_ref[slot]
            list_ref[found] = row * span + slot
            found = found + jnp.where((row >= 0) & (row < rows), 1, 0)
        return found

    list_ref[list_ref.shape[0] - 1] = lax.fori_loop(0, ids_ref.shape[0] // 8, one, 0)


def list_hits(local_ids, rows, span):
    return pl.pallas_call(
        partial(hits_kernel, rows, span),
        out_shape=jax.ShapeDtypeStruct((span,), jnp.int32),
        in_specs=[pl.BlockSpec(memory_space=pltpu.SMEM)],
        out_specs=pl.BlockSpec(memory_space=pltpu.SMEM),
        name="list_hits",
    )(local_ids)


def over_hits(lists_ref, visit):
    groups, span = lists_ref.shape
    for group in range(groups):

        def one(step, carry):
            entry = lists_ref[group, step]
            visit(group, entry // span, lax.rem(entry, span))
            return carry

        lax.fori_loop(0, lists_ref[group, span - 1], one, 0)


def pick_kernel(lists_ref, table_ref, out_ref, across_ref, piece_ref, wide_ref, turned_ref):
    tokens = wide_ref.shape[0] // lists_ref.shape[0]
    width, rows = table_ref.shape
    total = across_ref.shape[1]
    wide_ref[...] = jnp.zeros_like(wide_ref)
    step = 1024
    for low in range(0, total, step):
        high = max(min(low + step, rows), low)
        if high > low:
            across_ref[:, low:high] = lowered(table_ref[:, low:high])
        if high < low + step:
            across_ref[:, high : low + step] = jnp.zeros((width, low + step - high), jnp.bfloat16)

    groups, _, columns = piece_ref.shape
    for group in range(groups):
        start = group * (total // groups)
        piece_ref[group] = across_ref[:, start : start + columns]

    def turn(piece, carry):
        for part in range(8):
            start = pl.multiple_of(piece * step + part * 128, 128)
            block = across_ref[:, pl.ds(start, 128)].astype(jnp.float32)
            turned_ref[pl.ds(start, 128), :] = jnp.transpose(block)
        return carry

    lax.fori_loop(0, total // step, turn, 0)

    def visit(group, row, slot):
        wide_ref[pl.ds(group * tokens + slot, 1), :] = turned_ref[pl.ds(row, 1), :]

    over_hits(lists_ref, visit)
    out_ref[...] = wide_ref[...].astype(jnp.bfloat16)


def pick_rows(lists, count, table, total, columns):
    width = table.shape[0]
    return pl.pallas_call(
        pick_kernel,
        out_shape=(
            jax.ShapeDtypeStruct((count, width), jnp.bfloat16),
            jax.ShapeDtypeStruct((width, total), jnp.bfloat16),
            jax.ShapeDtypeStruct((lists.shape[0], width, columns), jnp.bfloat16),
        ),
        in_specs=[
            pl.BlockSpec(memory_space=pltpu.SMEM),
            pl.BlockSpec(memory_space=pltpu.VMEM),
        ],
        out_specs=(
            pl.BlockSpec(memory_space=pltpu.VMEM),
            pl.BlockSpec(memory_space=pltpu.VMEM),
            pl.BlockSpec(memory_space=pltpu.VMEM),
        ),
        scratch_shapes=[
            pltpu.VMEM((count, width), jnp.float32),
            pltpu.VMEM((total, width), jnp.float32),
        ],
        compiler_params=pltpu.CompilerParams(vmem_limit_bytes=VMEM_BYTES),
        name="pick_rows",
    )(lists, table)


def spread_kernel(
    lists_ref, grads_ref, zero_ref, one_ref, out_ref, squares_ref, wide_ref, rows_ref
):
    shares, groups, _, width = grads_ref.shape
    tokens = rows_ref.shape[0] // groups
    quarter = tokens // shares
    chunks = zero_ref.shape[0]
    parts = [(ref, low) for ref in (zero_ref, one_ref) for low in range(0, ref.shape[2], 128)]
    chunk = 128 * len(parts)
    for index in range(shares):
        for number in range(groups):
            start = number * tokens + index * quarter
            rows_ref[start : start + quarter, :] = grads_ref[index, number, 0:quarter].astype(jnp.float32)
    wide_ref[...] = jnp.zeros_like(wide_ref)

    def visit(group, row, slot):
        wide_ref[pl.ds(row, 1), 0:width] += rows_ref[pl.ds(group * tokens + slot, 1), :]

    over_hits(lists_ref, visit)

    def turn(piece, total):
        for part, (head_ref, column) in enumerate(parts):
            start = pl.multiple_of(piece * chunk + part * 128, 128)
            block = jnp.transpose(wide_ref[pl.ds(start, 128), :])[:width]
            block = block + head_ref[piece, :, column : column + 128].astype(jnp.float32)
            out_ref[:, pl.ds(start, 128)] = lowered(block)
            total = total + block * block
        return total

    total = lax.fori_loop(0, chunks, turn, jnp.zeros((width, 128), jnp.float32))
    squares_ref[...] = jnp.sum(total, axis=0, keepdims=True)


def spread_rows(lists, count, grads, head):
    chunks, width, _ = head[0].shape
    chunk = sum(member.shape[2] for member in head)
    return pl.pallas_call(
        spread_kernel,
        out_shape=(
            jax.ShapeDtypeStruct((width, chunks * chunk), jnp.bfloat16),
            jax.ShapeDtypeStruct((1, 128), jnp.float32),
        ),
        in_specs=[pl.BlockSpec(memory_space=pltpu.SMEM)]
        + [pl.BlockSpec(memory_space=pltpu.VMEM)] * 3,
        out_specs=(
            pl.BlockSpec(memory_space=pltpu.VMEM),
            pl.BlockSpec(memory_space=pltpu.VMEM),
        ),
        scratch_shapes=[
            pltpu.VMEM((chunks * chunk, 128), jnp.float32),
            pltpu.VMEM((count, width), jnp.float32),
        ],
        compiler_params=pltpu.CompilerParams(vmem_limit_bytes=VMEM_BYTES),
        name="spread_rows",
    )(lists, grads, *head)


MESH = pl.DeviceIdType.MESH


def meet(devices):
    barrier = pltpu.get_barrier_semaphore()
    for device in devices:
        pl.semaphore_signal(barrier, inc=1, device_id=device, device_id_type=MESH)
    pl.semaphore_wait(barrier, len(devices))


def send(source, target, send_sem, recv_sem, device):
    copy = pltpu.make_async_remote_copy(
        src_ref=source,
        dst_ref=target,
        send_sem=send_sem,
        recv_sem=recv_sem,
        device_id=device,
        device_id_type=MESH,
    )
    copy.start()
    return copy


def places():
    group, share = lax.axis_index("dp"), lax.axis_index("vocab")
    core = lax.rem(share, 2)
    core_peer = (group, share + 1 - 2 * core)
    side_peer = (group, lax.rem(share + 2, 4))
    return group, share, core, core_peer, side_peer


def group_peers(group, share, groups):
    return [(lax.rem(group + step, groups), share) for step in range(1, groups)]


def share_peers(group, share, shares):
    return [(group, lax.rem(share + step, shares)) for step in range(1, shares)]


def total_scratch(rows, width):
    half = rows // 2
    return [
        pltpu.VMEM((rows, width), jnp.float32),
        pltpu.VMEM((4, half, width), jnp.bfloat16),
        pltpu.VMEM((rows, width), jnp.bfloat16),
        pltpu.SemaphoreType.DMA((6,)),
    ]


class Total:
    def __init__(self, refs):
        self.part, self.bufs, self.total, self.sems = refs
        _, _, core, self.core_peer, self.side_peer = places()
        half = self.part.shape[0] // 2
        self.mine = pl.ds(pl.multiple_of(core * half, half), half)
        self.other = pl.ds(pl.multiple_of((1 - core) * half, half), half)

    def begin(self, partial_rows):
        self.part[...] = partial_rows
        self.bufs[0] = lowered(self.part[self.other, :])
        self.one = send(
            self.bufs.at[0], self.bufs.at[1], self.sems.at[0], self.sems.at[1], self.core_peer
        )

    def middle(self):
        self.one.wait_recv()
        self.bufs[2] = lowered(self.part[self.mine, :] + self.bufs[1].astype(jnp.float32))
        self.two = send(
            self.bufs.at[2], self.bufs.at[3], self.sems.at[2], self.sems.at[3], self.side_peer
        )

    def last(self):
        self.two.wait_recv()
        self.total[self.mine, :] = lowered(
            self.bufs[2].astype(jnp.float32) + self.bufs[3].astype(jnp.float32)
        )
        piece = self.total.at[self.mine, :]
        self.three = send(piece, piece, self.sems.at[4], self.sems.at[5], self.core_peer)

    def finish(self):
        self.three.wait()
        self.one.wait_send()
        self.two.wait_send()
        return self.total[...].astype(jnp.float32)

    def rest(self):
        self.middle()
        self.last()
        return self.finish()


class Exchange:
    def __init__(self, block_of, target_ref, sems, groups):
        group, share = lax.axis_index("dp"), lax.axis_index("vocab")
        self.copies = [
            send(
                block_of(peer[0]), target_ref.at[group], sems.at[0, step], sems.at[1, step], peer
            )
            for step, peer in enumerate(group_peers(group, share, groups))
        ]
        self.keep = pltpu.make_async_copy(
            block_of(group), target_ref.at[group], sems.at[0, groups - 1]
        )
        self.keep.start()

    def finish(self):
        self.keep.wait()
        for copy in self.copies:
            copy.wait()


def head_blocks(source_ref, start, columns):
    return lambda group: source_ref.at[group, :, pl.ds(start, columns)]


def table_blocks(source_ref, chunk, start, columns):
    return lambda group: source_ref.at[:, pl.ds(pl.multiple_of(group * chunk + start, 128), columns)]


def pair_of(group, share):
    place = lax.rem(group, 2)
    return (group + 1 - 2 * place, share), place


def line_places(group):
    pair, place = group // 2, lax.rem(group, 2)
    high, low = pair // 2, lax.rem(pair, 2)
    far = ((1 - high) * 2 + low) * 2 + place
    near = (high * 2 + 1 - low) * 2 + place
    return high, low, far, near


def line_scratch(width, columns):
    return [
        pltpu.VMEM((2, 2, width, columns), jnp.bfloat16),
        pltpu.VMEM((2, width, columns), jnp.bfloat16),
        pltpu.VMEM((width, columns), jnp.bfloat16),
        pltpu.SemaphoreType.DMA((6,)),
    ]


class Owned:
    def __init__(self, blocks, refs):
        group, self.share = lax.axis_index("dp"), lax.axis_index("vocab")
        self.high, self.low, self.far, self.near = line_places(group)
        self.pair, self.place = pair_of(group, self.share)
        self.blocks = blocks
        self.pair_in, self.near_in, self.far_in, self.sems = refs

    def begin(self):
        source = self.blocks.at[:, :, 1 - self.place]
        self.zero = send(source, self.pair_in, self.sems.at[0], self.sems.at[1], self.pair)

    def beside(self):
        self.zero.wait()
        self.blocks[:, :, self.place] = lowered(
            self.blocks[:, :, self.place].astype(jnp.float32) + self.pair_in[...].astype(jnp.float32)
        )
        self.one = send(
            self.blocks.at[:, 1 - self.low, self.place],
            self.near_in,
            self.sems.at[2],
            self.sems.at[3],
            (self.near, self.share),
        )

    def beyond(self):
        self.one.wait()
        self.blocks[:, self.low, self.place] = lowered(
            self.blocks[:, self.low, self.place].astype(jnp.float32)
            + self.near_in[...].astype(jnp.float32)
        )
        self.two = send(
            self.blocks.at[1 - self.high, self.low, self.place],
            self.far_in,
            self.sems.at[4],
            self.sems.at[5],
            (self.far, self.share),
        )

    def finish(self):
        self.two.wait()
        return lowered(
            self.blocks[self.high, self.low, self.place].astype(jnp.float32)
            + self.far_in[...].astype(jnp.float32)
        )


class Rows:
    def __init__(self, value_ref, send_ref, recv_ref, sems):
        group, share = lax.axis_index("dp"), lax.axis_index("vocab")
        self.recv = recv_ref
        shares, _, own = send_ref.shape
        for piece in range(shares):
            send_ref[piece] = value_ref[:, piece * own : (piece + 1) * own]
        self.copies = [
            send(send_ref.at[peer[1]], recv_ref.at[share], sems.at[0, step], sems.at[1, step], peer)
            for step, peer in enumerate(share_peers(group, share, shares))
        ]
        keep = pltpu.make_async_copy(send_ref.at[share], recv_ref.at[share], sems.at[0, shares - 1])
        keep.start()
        self.copies.append(keep)

    def put(self, grads_ref, start):
        for copy in self.copies:
            copy.wait()
        shares, _, own = self.recv.shape
        part = grads_ref.shape[3]
        for piece in range(shares):
            for half in range(2):
                grads_ref[piece // 2, piece % 2, half, :, start : start + own] = self.recv[
                    piece, half * part : (half + 1) * part
                ]


class Late:
    def __init__(self, source, buffer, sem):
        self.copy, self.buffer, self.waiting = pltpu.make_async_copy(source, buffer, sem), buffer, True
        self.copy.start()

    def __call__(self):
        if self.waiting:
            self.copy.wait()
            self.waiting = False
        return self.buffer


class ShareGather:
    def __init__(self, target_ref, sems):
        _, self.share, _, self.core_peer, self.side_peer = places()
        self.target, self.sems = target_ref, sems
        block = target_ref.at[self.share]
        self.one = send(block, block, sems.at[0, 0], sems.at[1, 0], self.side_peer)

    def middle(self):
        self.one.wait()
        both = [self.target.at[index] for index in (self.share, self.side_peer[1])]
        self.two = [
            send(block, block, self.sems.at[0, 1 + step], self.sems.at[1, 1 + step], self.core_peer)
            for step, block in enumerate(both)
        ]

    def finish(self):
        for copy in self.two:
            copy.wait()


def in_vmem(count, at_rest=()):
    return [
        pl.BlockSpec(memory_space=pl.ANY if index in at_rest else pltpu.VMEM)
        for index in range(count)
    ]


def call(kernel, name, number, inputs, out_shape, scratch, flops, rest_in=(), rest_out=()):
    moved = sum(math.prod(member.shape) * member.dtype.itemsize for member in (*inputs, *out_shape))
    return pl.pallas_call(
        kernel,
        out_shape=tuple(out_shape),
        in_specs=in_vmem(len(inputs), rest_in),
        out_specs=tuple(in_vmem(len(out_shape), rest_out)),
        scratch_shapes=scratch,
        compiler_params=pltpu.CompilerParams(
            collective_id=number, has_side_effects=True, vmem_limit_bytes=VMEM_BYTES
        ),
        cost_estimate=pl.CostEstimate(flops=flops, bytes_accessed=moved, transcendentals=0),
        name=name,
    )(*inputs)


def shape_of(shape, dtype):
    return jax.ShapeDtypeStruct(shape, dtype)


def head_slice(ref, start, index):
    low = start + index * HEAD_DIM
    return ref[:, low : low + HEAD_DIM]


def masked_scores(query, key, causal):
    scores = times_transposed(query, key) * HEAD_DIM ** (-0.5)
    if causal:
        down = lax.broadcasted_iota(jnp.int32, scores.shape, 0)
        across = lax.broadcasted_iota(jnp.int32, scores.shape, 1)
        scores = jnp.where(down >= across, scores, -1e30)
    return scores


def heads_forward(q_ref, kv_ref, starts, context_ref, logs_ref, causal):
    q_start, k_start, v_start = starts
    for index in range(context_ref.shape[1] // HEAD_DIM):
        query = head_slice(q_ref, q_start, index)
        key = head_slice(kv_ref, k_start, index)
        value = head_slice(kv_ref, v_start, index)
        scores = masked_scores(query, key, causal)
        row_top = jnp.max(scores, axis=-1, keepdims=True)
        exponent = jnp.exp(scores - row_top)
        row_total = jnp.sum(exponent, axis=-1, keepdims=True)
        context = lowered(matmul(lowered(exponent / row_total), value))
        context_ref[:, index * HEAD_DIM : (index + 1) * HEAD_DIM] = context
        logs_ref[:, index : index + 1] = row_top + jnp.log(row_total)


def heads_backward(q_ref, kv_ref, starts, logs_ref, grad_ref, gq_ref, gkv_ref, g_starts, causal):
    q_start, k_start, v_start = starts
    gq_start, gk_start, gv_start = g_starts
    scale = HEAD_DIM ** (-0.5)
    for index in range(grad_ref.shape[1] // HEAD_DIM):
        low, high = index * HEAD_DIM, (index + 1) * HEAD_DIM
        query = head_slice(q_ref, q_start, index)
        key = head_slice(kv_ref, k_start, index)
        value = head_slice(kv_ref, v_start, index)
        grad = grad_ref[:, low:high]
        softmax_out = jnp.exp(
            masked_scores(query, key, causal) - logs_ref[:, index : index + 1]
        )
        gkv_ref[:, gv_start + low : gv_start + high] = lowered(
            contract_rows(lowered(softmax_out), grad)
        )
        grad_softmax = times_transposed(grad, value)
        inner = jnp.sum(grad_softmax * softmax_out, axis=-1, keepdims=True)
        grad_scores = lowered(softmax_out * (grad_softmax - inner))
        gq_ref[:, gq_start + low : gq_start + high] = lowered(matmul(grad_scores, key) * scale)
        gkv_ref[:, gk_start + low : gk_start + high] = lowered(
            contract_rows(grad_scores, query) * scale
        )


def norm_backward(grad_out, saved_parts, gain_row):
    normed, scale_inv = saved_parts
    grad_normed = grad_out * gain_row
    grad_in = scale_inv * (
        grad_normed
        - jnp.mean(grad_normed, axis=-1, keepdims=True)
        - normed * jnp.mean(grad_normed * normed, axis=-1, keepdims=True)
    )
    return (
        grad_in,
        jnp.sum(grad_out * normed, axis=0, keepdims=True),
        jnp.sum(grad_out, axis=0, keepdims=True),
    )


def gain_of(norms_ref, row):
    return norms_ref[row : row + 1, :], norms_ref[row + 7 : row + 8, :]


def stream_of(looked_ref, start, place_ref):
    rows, width = place_ref.shape
    looked = looked_ref[start : start + rows, :].astype(jnp.float32)
    return looked * math.sqrt(width) + place_ref[...]


def forward_kernel(groups, shares, base, cuts, refs_in, refs_out, *refs):
    inputs, outputs, scratch = refs[:refs_in], refs[refs_in : refs_in + refs_out], refs[refs_in + refs_out :]
    looked_ref, place_enc_ref, place_dec_ref, w_early_hbm, across_ref = inputs
    (
        table_ref, out_rows_ref, norms_ref,
        qkv_enc_ref, context_enc_ref, logs_enc_ref, stream_enc_hbm, pre_enc_hbm, stream_two_hbm, memory_ref,
        qkv_dec_ref, context_dec_ref, logs_dec_ref, stream_dec_ref,
    ) = outputs
    (
        table_sems, out_sems, load_sems, w_first_ref, w_enc_ref, stream_enc_ref, pre_enc_ref, stream_two_ref,
        blocks_ref, block_sems, local_sem,
    ) = scratch[:11]
    rest = scratch[11:]
    small_one, large_one = rest[:4], rest[4:8]
    large_two = large_one[:1] + rest[8:11]
    group, share, core, core_peer, side_peer = places()
    peers, far = share_peers(group, share, shares), group_peers(group, share, groups)
    first_wide = w_first_ref.shape[1]
    load_first = Late(w_early_hbm.at[:, pl.ds(0, first_wide)], w_first_ref, load_sems.at[0])
    load_enc = Late(
        w_early_hbm.at[:, pl.ds(first_wide, w_enc_ref.shape[1])], w_enc_ref, load_sems.at[1]
    )
    meet(peers + far)
    chunk = across_ref.shape[1] // groups
    starts = np.cumsum((0,) + cuts).tolist()

    def table_piece(index):
        at = pl.ds(starts[index], cuts[index])
        return Exchange(
            table_blocks(across_ref, chunk, base + starts[index], cuts[index]),
            table_ref.at[:, :, at],
            table_sems.at[index],
            groups,
        )

    outgoing = []

    def put_out(source, target):
        copy = pltpu.make_async_copy(source, target, out_sems.at[len(outgoing)])
        copy.start()
        outgoing.append(copy)

    table_zero = table_piece(0)
    load_first()

    own = qkv_enc_ref.shape[1] // 3
    rows, wide = blocks_ref.shape[1:]
    padded = first_wide - wide
    window = pl.ds(padded, wide)
    copies = []
    for step, (_, peer) in enumerate(peers):
        source = w_first_ref.at[pl.ds(pl.multiple_of(peer * rows, 64), rows), window]
        copies.append(
            send(source, blocks_ref.at[share], block_sems.at[0, step], block_sems.at[1, step], (group, peer))
        )
    keep = pltpu.make_async_copy(
        w_first_ref.at[pl.ds(pl.multiple_of(share * rows, 64), rows), window], blocks_ref.at[share], local_sem
    )
    keep.start()
    turned = jnp.transpose(w_first_ref[:, first_wide - 128 :].astype(jnp.float32))
    norms_ref[...] = turned[64:80]
    enc_total, dec_total = Total(large_one), Total(small_one)
    enc_len, dec_len = place_enc_ref.shape[0], place_dec_ref.shape[0]
    stream = stream_of(looked_ref, 0, place_enc_ref)
    normed, _ = norm_forward(stream, *gain_of(norms_ref, 0))
    qkv_enc_ref[...] = lowered(matmul(lowered(normed), w_first_ref[:, : 3 * own]))
    stream_enc_ref[...] = stream
    head_starts = (0, own, 2 * own)
    logs_enc_ref[...] = jnp.zeros_like(logs_enc_ref)
    heads_forward(qkv_enc_ref, qkv_enc_ref, head_starts, context_enc_ref, logs_enc_ref, False)
    table_one = table_piece(1)
    keep.wait()
    for copy in copies:
        copy.wait()
    for matrix in range(3):
        for piece in range(shares):
            out_rows_ref[matrix, :, piece * own : (piece + 1) * own] = blocks_ref[
                piece, :, matrix * own : (matrix + 1) * own
            ]
    enc_total.begin(matmul(context_enc_ref[...], out_rows_ref[0]))
    stream = stream_of(looked_ref, enc_len, place_dec_ref)
    stream_dec_ref[...] = stream
    normed, _ = norm_forward(stream, *gain_of(norms_ref, 3))
    enc_total.middle()
    dec_start = padded // 2
    qkv_dec_ref[...] = lowered(
        matmul(lowered(normed), w_first_ref[:, dec_start : dec_start + 3 * own])
    )
    logs_dec_ref[...] = jnp.zeros_like(logs_dec_ref)
    heads_forward(qkv_dec_ref, qkv_dec_ref, head_starts, context_dec_ref, logs_dec_ref, True)
    enc_total.last()
    dec_total.begin(matmul(context_dec_ref[...], out_rows_ref[1]))
    dec_total.middle()
    stream_enc_ref[...] += enc_total.finish()
    put_out(stream_enc_ref, stream_enc_hbm)
    dec_total.last()

    total = Total(large_two)
    normed, _ = norm_forward(stream_enc_ref[...], *gain_of(norms_ref, 1))
    hidden, width = pre_enc_ref.shape[1], stream_enc_ref.shape[1]
    load_enc()
    pre_enc_ref[...] = matmul(lowered(normed), w_enc_ref[:, :hidden])
    put_out(pre_enc_ref, pre_enc_hbm)
    activated = lowered(jax.nn.silu(pre_enc_ref[...]))
    total.begin(matmul(activated, w_enc_ref[:, hidden : hidden + width]))
    stream_dec_ref[...] += dec_total.finish()
    stream_two_ref[...] = stream_enc_ref[...] + total.rest()
    put_out(stream_two_ref, stream_two_hbm)
    memory, _ = norm_forward(stream_two_ref[...], *gain_of(norms_ref, 2))
    memory_ref[...] = lowered(memory)
    for piece in (table_zero, table_one):
        piece.finish()
    for copy in outgoing:
        copy.wait()


def dec_kernel(
    groups, start,
    stream_dec_ref, memory_ref, norms_ref, out_rows_ref, positions_ref, w_dec_hbm, across_ref,
    table_ref, q_ref, kv_ref, context_ref, logs_ref, stream_mid_ref, pre_dec_ref, stream_out_ref, selected_ref,
    w_dec_ref, load_sem, table_sems, own_ref, select_sems, *rest,
):
    small_one, small_two = rest[:4], rest[:1] + rest[4:7]
    group, share, core, core_peer, side_peer = places()
    far = group_peers(group, share, groups)
    load_dec = Late(w_dec_hbm, w_dec_ref, load_sem)
    meet([core_peer, side_peer] + far)
    chunk, columns = across_ref.shape[1] // groups, table_ref.shape[2]
    exchange = Exchange(
        table_blocks(across_ref, chunk, start, columns), table_ref, table_sems, groups
    )
    own, hidden = q_ref.shape[1], pre_dec_ref.shape[1]
    dec_len, width = stream_dec_ref.shape
    cross_total, feed_total = Total(small_two), Total(small_one)
    in_start = hidden + width
    normed, _ = norm_forward(stream_dec_ref[...], *gain_of(norms_ref, 4))
    load_dec()
    kv_ref[...] = lowered(
        matmul(memory_ref[...], w_dec_ref[:, in_start + own : in_start + 3 * own])
    )
    q_ref[...] = lowered(matmul(lowered(normed), w_dec_ref[:, in_start : in_start + own]))
    logs_ref[...] = jnp.zeros_like(logs_ref)
    heads_forward(q_ref, kv_ref, (0, 0, own), context_ref, logs_ref, False)
    cross_total.begin(matmul(context_ref[...], out_rows_ref[2]))
    stream_mid_ref[...] = stream_dec_ref[...] + cross_total.rest()
    normed, _ = norm_forward(stream_mid_ref[...], *gain_of(norms_ref, 5))
    pre_dec_ref[...] = matmul(lowered(normed), w_dec_ref[:, :hidden])
    activated = lowered(jax.nn.silu(pre_dec_ref[...]))
    feed_total.begin(matmul(activated, w_dec_ref[:, hidden:in_start]))
    stream_out_ref[...] = stream_mid_ref[...] + feed_total.rest()
    final, _ = norm_forward(stream_out_ref[...], *gain_of(norms_ref, 6))
    places_down = lax.broadcasted_iota(jnp.int32, (own_ref.shape[0], dec_len), 1)
    chosen = lowered(jnp.where(places_down == positions_ref[...], 1.0, 0.0))
    own_ref[...] = lowered(matmul(chosen, lowered(final)))
    selected_ref[group] = own_ref[...]
    copies = [
        send(own_ref, selected_ref.at[group], select_sems.at[0, step], select_sems.at[1, step], peer)
        for step, peer in enumerate(far)
    ]
    exchange.finish()
    for copy in copies:
        copy.wait()


def combine_stats(stats):
    row_max = stats[0][0:1]
    for member in stats[1:]:
        row_max = jnp.maximum(row_max, member[0:1])
    exp_total = smooth = target = 0.0
    for member in stats:
        exp_total = exp_total + member[1:2] * jnp.exp(member[0:1] - row_max)
        smooth = smooth + member[2:3]
        target = target + member[3:4]
    return row_max, exp_total, smooth, target


def head_kernel(
    groups, shares, shard_rows,
    selected_ref, zero_ref, one_ref, two_ref, targets_ref, weights_ref, counted_ref,
    loss_ref, grad_out_ref, head_ref, head_out_ref,
    head_sems, logits_ref, dz_ref, stats_ref, turned_ref, share_stats_ref, group_stats_ref, stat_sems,
    part_ref, core_ref, side_ref, group_ref, sum_ref, sems,
):
    group, share, core, core_peer, side_peer = places()
    side = share // 2
    near, far = share_peers(group, share, shares), group_peers(group, share, groups)
    meet(near + far)
    rows, width = selected_ref.shape
    chunk = logits_ref.shape[1]
    vocab_total = shard_rows * shares
    first = group * chunk
    limit = jnp.minimum(shard_rows - first, vocab_total - 1 - share * shard_rows - first)
    block = 384
    step_rows = 32

    tables = (zero_ref, one_ref, two_ref)
    starts = np.cumsum([0] + [ref.shape[1] for ref in tables]).tolist()
    for ref, start in zip(tables, starts):
        for low in range(0, ref.shape[1], block):
            logits_ref[:, start + low : start + low + block] = matmul(
                selected_ref[...], ref[:, low : low + block]
            )
    stats_ref[...] = jnp.zeros_like(stats_ref)

    def gather_stats(step, carry):
        at = pl.ds(pl.multiple_of(step * step_rows, step_rows), step_rows)
        logits = logits_ref[at, :]
        column = lax.broadcasted_iota(jnp.int32, logits.shape, 1)
        real = column < limit
        masked = jnp.where(real, logits, -1e30)
        top = jnp.max(masked, axis=1, keepdims=True)
        stats_ref[at, 0:1] = top
        stats_ref[at, 1:2] = jnp.sum(jnp.exp(masked - top), axis=1, keepdims=True)
        stats_ref[at, 2:3] = jnp.sum(jnp.where(real, logits, 0.0), axis=1, keepdims=True)
        hit = column == targets_ref[at, :]
        stats_ref[at, 3:4] = jnp.sum(jnp.where(hit, logits, 0.0), axis=1, keepdims=True)
        return carry

    lax.fori_loop(0, rows // step_rows, gather_stats, 0)
    share_stats_ref[share] = jnp.transpose(stats_ref[...])[0:8]
    copies = [
        send(share_stats_ref.at[share], share_stats_ref.at[share], stat_sems.at[0, step], stat_sems.at[1, step], peer)
        for step, peer in enumerate(near)
    ]
    for copy in copies:
        copy.wait()
    merged = combine_stats([share_stats_ref[index] for index in range(shares)])
    group_stats_ref[group] = jnp.concatenate(merged + (jnp.zeros((4, rows), jnp.float32),), axis=0)
    copies = [
        send(group_stats_ref.at[group], group_stats_ref.at[group], stat_sems.at[2, step], stat_sems.at[3, step], peer)
        for step, peer in enumerate(far)
    ]
    for copy in copies:
        copy.wait()
    row_max, exp_total, smooth, target = combine_stats(
        [group_stats_ref[index] for index in range(groups)]
    )
    log_total = row_max + jnp.log(exp_total)
    per_row = log_total - (1.0 - SMOOTH) * target - SMOOTH * smooth / (vocab_total - 1)
    loss = jnp.sum(counted_ref[...] * per_row, axis=1, keepdims=True)
    loss_ref[...] = jnp.broadcast_to(loss, loss_ref.shape)
    turned_ref[...] = jnp.zeros_like(turned_ref)
    turned_ref[0:1, :] = log_total
    stats_ref[...] = jnp.transpose(turned_ref[...])

    def make_dz(step, carry):
        at = pl.ds(pl.multiple_of(step * step_rows, step_rows), step_rows)
        logits = logits_ref[at, :]
        column = lax.broadcasted_iota(jnp.int32, logits.shape, 1)
        softmax_rows = jnp.exp(logits - stats_ref[at, 0:1])
        hit = jnp.where(column == targets_ref[at, :], 1.0 - SMOOTH, 0.0)
        grad = weights_ref[at, :] * (softmax_rows - hit - SMOOTH / (vocab_total - 1))
        dz_ref[at, :] = lowered(jnp.where(column < limit, grad, 0.0))
        return carry

    lax.fori_loop(0, rows // step_rows, make_dz, 0)
    loss_rows = rows // groups
    half, quarter = loss_rows // 2, loss_rows // 4

    def head_part(index):
        at = slice(index * block, (index + 1) * block)
        head_ref[:, at] = lowered(contract_rows(selected_ref[...], dz_ref[:, at]))

    early = head_out_ref.shape[2] // block
    for index in range(early):
        head_part(index)
    width_out = width // groups
    exchange = Exchange(
        lambda index: head_ref.at[
            pl.ds(pl.multiple_of(index * width_out, 16), width_out), pl.ds(0, early * block)
        ],
        head_out_ref,
        head_sems,
        groups,
    )
    grad_rows = 0.0
    for ref, start in zip(tables, starts):
        grad_rows = grad_rows + times_transposed(dz_ref[:, start : start + ref.shape[1]], ref[...])
    part_ref[...] = lowered(grad_rows).reshape(part_ref.shape)
    mine = pl.ds(pl.multiple_of(core * half, 16), half)
    other = pl.ds(pl.multiple_of((1 - core) * half, 16), half)
    copy = send(part_ref.at[:, other, :], core_ref, sems.at[0, 0], sems.at[1, 0], core_peer)
    parts = chunk // block
    middle = (early + parts) // 2
    copy.wait()
    part_ref[:, mine, :] = lowered(
        part_ref[:, mine, :].astype(jnp.float32) + core_ref[...].astype(jnp.float32)
    )
    base = core * half
    my_quarter = pl.ds(pl.multiple_of(base + side * quarter, 16), quarter)
    other_quarter = pl.ds(pl.multiple_of(base + (1 - side) * quarter, 16), quarter)
    copy = send(part_ref.at[:, other_quarter, :], side_ref, sems.at[0, 1], sems.at[1, 1], side_peer)
    for index in range(early, middle):
        head_part(index)
    copy.wait()
    side_ref[...] = lowered(
        part_ref[:, my_quarter, :].astype(jnp.float32) + side_ref[...].astype(jnp.float32)
    )
    group_ref[group] = side_ref[group]
    copies = [
        send(side_ref.at[peer[0]], group_ref.at[group], sems.at[0, 2 + step], sems.at[1, 2 + step], peer)
        for step, peer in enumerate(far)
    ]
    for index in range(middle, parts):
        head_part(index)
    for copy in copies:
        copy.wait()
    summed = group_ref[0].astype(jnp.float32)
    for index in range(1, groups):
        summed = summed + group_ref[index].astype(jnp.float32)
    sum_ref[...] = lowered(summed)
    grad_out_ref[my_quarter, :] = sum_ref[...]
    base_sem = 1 + groups
    copies = [
        send(sum_ref, grad_out_ref.at[my_quarter, :], sems.at[0, base_sem + step], sems.at[1, base_sem + step], peer)
        for step, peer in enumerate(near)
    ]
    for copy in copies:
        copy.wait()
    exchange.finish()


def put_grads(grads_ref, start, value):
    shape = grads_ref.shape[:4] + (value.shape[1],)
    grads_ref[:, :, :, :, start : start + value.shape[1]] = lowered(value).reshape(shape)


def feed_grads(grad_ref, stream_ref, pre_ref, norms_ref, row, w_ref, grads_ref, total):
    width = stream_ref.shape[1]
    hidden = pre_ref.shape[1]
    normed, _ = norm_forward(stream_ref[...], *gain_of(norms_ref, row))
    grad_low = lowered(grad_ref[...])
    pre = pre_ref[...]
    sigmoid_pre = jax.nn.sigmoid(pre)
    grad_pre = lowered(
        times_transposed(grad_low, w_ref[:, hidden : hidden + width])
        * sigmoid_pre
        * (1.0 + pre * (1.0 - sigmoid_pre))
    )
    total.begin(times_transposed(grad_pre, w_ref[:, :hidden]))
    activated = lowered(pre * sigmoid_pre)
    put_grads(grads_ref, hidden, contract_rows(activated, grad_low))
    total.middle()
    put_grads(grads_ref, 0, contract_rows(lowered(normed), grad_pre))


def norm_step(grad_ref, stream_ref, norms_ref, row, summed, rows_ref, slot):
    gain, shift = gain_of(norms_ref, row)
    _, kept = norm_forward(stream_ref[...], gain, shift)
    grad_in, grad_gain, grad_shift = norm_backward(summed, kept, gain)
    rows_ref[slot : slot + 1, :] = grad_gain
    rows_ref[slot + 1 : slot + 2, :] = grad_shift
    if grad_ref is None:
        return grad_in
    return grad_ref[...] + grad_in


def back_kernel(
    groups, shares, first_wide, refs_in, refs_out, *refs
):
    inputs, outputs, scratch = refs[:refs_in], refs[refs_in : refs_in + refs_out], refs[refs_in + refs_out :]
    (
        grad_selected_ref, positions_ref, stream_out_ref, stream_mid_ref, pre_dec_ref, norms_ref, w_dec_hbm,
        out_rows_hbm, memory_hbm, stream_dec_hbm, q_ref, kv_ref, context_cross_ref, logs_cross_ref,
        stream_two_hbm, stream_enc_hbm, pre_enc_hbm, w_early_hbm, looked_hbm, place_enc_hbm, place_dec_ref,
        qkv_dec_ref, context_dec_ref, logs_dec_ref, qkv_enc_ref, context_enc_ref, logs_enc_ref,
        head_in_ref,
    ) = inputs
    head_out_ref, own_tokens_ref, dec_shares_ref, own_ref, squares_ref = outputs
    (
        head_sems, load_sems, w_ref, w_enc_ref, out_rows_ref, memory_ref, stream_dec_ref, stream_two_ref,
        stream_enc_ref, pre_enc_ref, looked_ref,
        dec_grads_ref, mid_grads_ref, last_grads_ref,
        grad_ref, grad_enc_ref,
        context_ref, gq_ref, gkv_ref, gqkv_ref, gqkv_enc_ref, context_enc_grad_ref,
        g_enc_ref, g_self_ref, g_cross_ref, rows_dec_ref, rows_mid_ref, rows_ref,
        norm_rows_ref, block_sems, cut_ref, token_sems, share_sems, dec_sems, dec_own_ref,
        local_sems,
    ) = scratch[:36]
    row_refs = scratch[36:42]
    rest = scratch[42:]
    stream_ref = pre_enc_ref
    small_one, large_one = rest[:4], rest[4:8]
    small_two, large_two = small_one[:1] + rest[8:11], large_one[:1] + rest[11:14]
    dec_line = Owned(dec_grads_ref, rest[14:18])
    mid_line = Owned(mid_grads_ref, rest[18:22])
    last_line = Owned(last_grads_ref, rest[22:26])
    group, share, core, core_peer, side_peer = places()
    peers = share_peers(group, share, shares)
    load_w_dec = Late(w_dec_hbm, w_ref, load_sems.at[0])
    load_rows = Late(out_rows_hbm, out_rows_ref, load_sems.at[1])
    load_memory = Late(memory_hbm, memory_ref, load_sems.at[2])
    load_dec = Late(stream_dec_hbm, stream_dec_ref, load_sems.at[3])
    load_two = Late(stream_two_hbm, stream_two_ref, load_sems.at[4])
    load_enc = Late(stream_enc_hbm, stream_enc_ref, load_sems.at[5])
    load_pre = Late(pre_enc_hbm, pre_enc_ref, load_sems.at[6])
    load_w_enc = Late(
        w_early_hbm.at[:, pl.ds(first_wide, w_enc_ref.shape[1])], w_enc_ref, load_sems.at[7]
    )
    load_looked = Late(looked_hbm, looked_ref, load_sems.at[8])
    meet(peers + group_peers(group, share, groups))
    exchange = Exchange(
        head_blocks(head_in_ref, head_in_ref.shape[2] - head_out_ref.shape[2], head_out_ref.shape[2]),
        head_out_ref,
        head_sems,
        groups,
    )
    width = stream_out_ref.shape[1]
    own = q_ref.shape[1]
    hidden = pre_dec_ref.shape[1]
    in_start = hidden + width
    starts = (0, own, 2 * own)
    for rows in (rows_dec_ref, rows_mid_ref, rows_ref):
        rows[...] = jnp.zeros_like(rows)

    total = Total(small_one)
    down = lax.broadcasted_iota(jnp.int32, (stream_out_ref.shape[0], grad_selected_ref.shape[0]), 0)
    chosen = lowered(jnp.where(down == positions_ref[...], 1.0, 0.0))
    grad_final = matmul(chosen, grad_selected_ref[...])
    grad_ref[...] = norm_step(None, stream_out_ref, norms_ref, 6, grad_final, rows_dec_ref, 0)
    load_w_dec()
    feed_grads(grad_ref, stream_mid_ref, pre_dec_ref, norms_ref, 5, w_ref, dec_grads_ref, total)
    total.last()
    grad_ref[...] = norm_step(
        grad_ref, stream_mid_ref, norms_ref, 5, total.finish(), rows_dec_ref, 2
    )

    cross_total, memory_total = Total(small_two), Total(large_one)
    grad_low = lowered(grad_ref[...])
    load_rows()
    context_ref[...] = lowered(times_transposed(grad_low, out_rows_ref[2]))
    heads_backward(
        q_ref, kv_ref, (0, 0, own), logs_cross_ref, context_ref, gq_ref, gkv_ref, (0, 0, own), False
    )
    memory_total.begin(
        times_transposed(gkv_ref[...], w_ref[:, in_start + own : in_start + 3 * own])
    )
    cross_total.begin(times_transposed(gq_ref[...], w_ref[:, in_start : in_start + own]))
    load_w_first = Late(
        w_early_hbm.at[:, pl.ds(0, first_wide)], w_ref.at[:, pl.ds(0, first_wide)], load_sems.at[9]
    )
    g_cross_ref[...] = lowered(contract_rows(context_cross_ref[...], grad_low))
    cross_rows = Rows(g_cross_ref, row_refs[0], row_refs[1], block_sems.at[0])
    memory_total.middle()
    cross_total.middle()
    load_dec()
    load_memory()
    normed, _ = norm_forward(stream_dec_ref[...], *gain_of(norms_ref, 4))
    put_grads(dec_grads_ref, in_start, contract_rows(lowered(normed), gq_ref[...]))
    put_grads(dec_grads_ref, in_start + own, contract_rows(memory_ref[...], gkv_ref[...]))
    cross_rows.put(dec_grads_ref, in_start + 3 * own)
    dec_line.begin()
    memory_total.last()
    cross_total.last()
    summed = memory_total.finish()
    load_two()
    grad_enc_ref[...] = norm_step(None, stream_two_ref, norms_ref, 2, summed, rows_mid_ref, 0)
    load_place = Late(place_enc_hbm, stream_two_ref, load_sems.at[10])
    grad_ref[...] = norm_step(
        grad_ref, stream_dec_ref, norms_ref, 4, cross_total.finish(), rows_dec_ref, 4
    )

    feed_total, self_total = Total(large_two), Total(small_one)
    load_enc()
    load_pre()
    load_w_enc()
    feed_grads(
        grad_enc_ref, stream_enc_ref, pre_enc_ref, norms_ref, 1, w_enc_ref, mid_grads_ref, feed_total
    )
    grad_low = lowered(grad_ref[...])
    context_ref[...] = lowered(times_transposed(grad_low, out_rows_ref[1]))
    feed_total.last()
    heads_backward(
        qkv_dec_ref, qkv_dec_ref, starts, logs_dec_ref, context_ref, gqkv_ref, gqkv_ref, starts, True
    )
    load_w_first()
    w_start = first_wide // 3
    self_total.begin(times_transposed(gqkv_ref[...], w_ref[:, w_start : w_start + 3 * own]))
    g_self_ref[...] = lowered(contract_rows(context_dec_ref[...], grad_low))
    self_rows = Rows(g_self_ref, row_refs[2], row_refs[3], block_sems.at[1])
    self_total.middle()
    load_looked()
    enc_len = stream_enc_ref.shape[0]
    stream_dec_ref[...] = stream_of(looked_ref, enc_len, place_dec_ref)
    normed, _ = norm_forward(stream_dec_ref[...], *gain_of(norms_ref, 3))
    put_grads(mid_grads_ref, in_start, contract_rows(lowered(normed), gqkv_ref[...]))
    self_rows.put(mid_grads_ref, in_start + 3 * own)
    mid_line.begin()
    grad_enc_ref[...] = norm_step(
        grad_enc_ref, stream_enc_ref, norms_ref, 1, feed_total.finish(), rows_mid_ref, 2
    )
    self_total.last()
    tokens, part = looked_ref.shape[0], cut_ref.shape[2]
    quarter = tokens // shares
    block_rows = cut_ref.shape[1] // shares

    def put_tokens(first, rows):
        for index in range(groups):
            for piece in range(shares):
                low, high = max(first, piece * quarter), min(first + rows.shape[0], (piece + 1) * quarter)
                if low < high:
                    to = piece * block_rows - piece * quarter
                    cut_ref[index, to + low : to + high] = rows[
                        low - first : high - first, index * part : (index + 1) * part
                    ]

    grad_dec = norm_step(
        grad_ref, stream_dec_ref, norms_ref, 3, self_total.finish(), rows_mid_ref, 4
    )
    put_tokens(enc_len, lowered(grad_dec * math.sqrt(width)))

    total = Total(large_one)
    grad_low = lowered(grad_enc_ref[...])
    g_enc_ref[...] = lowered(contract_rows(context_enc_ref[...], grad_low))
    enc_rows = Rows(g_enc_ref, row_refs[4], row_refs[5], block_sems.at[2])
    context_enc_grad_ref[...] = lowered(times_transposed(grad_low, out_rows_ref[0]))
    heads_backward(
        qkv_enc_ref, qkv_enc_ref, starts, logs_enc_ref, context_enc_grad_ref, gqkv_enc_ref, gqkv_enc_ref, starts,
        False,
    )
    total.begin(times_transposed(gqkv_enc_ref[...], w_ref[:, : 3 * own]))
    load_place()
    stream_ref[...] = stream_of(looked_ref, 0, stream_two_ref)
    normed, _ = norm_forward(stream_ref[...], *gain_of(norms_ref, 0))
    total.middle()
    put_grads(last_grads_ref, 0, contract_rows(lowered(normed), gqkv_enc_ref[...]))
    enc_rows.put(last_grads_ref, 3 * own)
    last_line.begin()
    dec_line.beside()
    total.last()
    grad_enc = norm_step(grad_enc_ref, stream_ref, norms_ref, 0, total.finish(), rows_ref, 0)
    put_tokens(0, lowered(grad_enc * math.sqrt(width)))
    norm_rows_ref[...] = jnp.zeros_like(norm_rows_ref)
    order = (
        (0, rows_ref, 0),
        (1, rows_mid_ref, 2),
        (2, rows_mid_ref, 0),
        (3, rows_mid_ref, 4),
        (4, rows_dec_ref, 4),
        (5, rows_dec_ref, 2),
        (6, rows_dec_ref, 0),
    )
    for row, source, slot in order:
        norm_rows_ref[row : row + 1, :] = source[slot : slot + 1, :]
        norm_rows_ref[7 + row : 8 + row, :] = source[slot + 1 : slot + 2, :]
    norm_low = lowered(norm_rows_ref[...])
    for index in range(groups):
        for piece in range(shares):
            cut_ref[index, piece * block_rows + quarter : (piece + 1) * block_rows] = norm_low[
                :, index * part : (index + 1) * part
            ]
    own_rows = pl.ds(pl.multiple_of(share * block_rows, 16), block_rows)
    to_groups = Exchange(
        lambda index: cut_ref.at[index, own_rows, :], own_tokens_ref.at[share], token_sems, groups
    )
    mid_line.beside()
    dec_line.beyond()
    to_groups.finish()
    token_gather = ShareGather(own_tokens_ref, share_sems)
    last_line.beside()
    mid_line.beyond()
    dec_own_ref[...] = dec_line.finish()
    keep = pltpu.make_async_copy(dec_own_ref, dec_shares_ref.at[share], local_sems.at[2])
    keep.start()
    keep.wait()
    dec_gather = ShareGather(dec_shares_ref, dec_sems)
    token_gather.middle()
    last_line.beyond()
    middle = mid_grads_ref.shape[4]
    own_ref[:, :middle] = mid_line.finish()
    dec_gather.middle()
    token_gather.finish()
    own_ref[:, middle:] = last_line.finish()
    squares = 0.0
    for ref in (dec_own_ref, own_ref):
        value = ref[...].astype(jnp.float32)
        value = value * value
        squares = squares + jnp.sum(jnp.sum(value, axis=0, keepdims=True), axis=1, keepdims=True)
    lane = lax.broadcasted_iota(jnp.int32, squares_ref.shape, 1)
    squares_ref[...] = jnp.where(lane == 0, squares, 0.0)
    dec_gather.finish()
    exchange.finish()


def look_kernel(
    groups,
    picked_ref,
    looked_ref,
    send_ref, core_ref, side_ref, group_ref, sems,
):
    group, share, core, core_peer, side_peer = places()
    side = share // 2
    far = group_peers(group, share, groups)
    meet([core_peer, side_peer] + far)
    _, tokens, width = picked_ref.shape
    half, quarter = tokens // 2, tokens // 4
    mine = pl.ds(pl.multiple_of(core * half, 16), half)
    other = pl.ds(pl.multiple_of((1 - core) * half, 16), half)
    send(picked_ref.at[:, other, :], core_ref, sems.at[0, 0], sems.at[1, 0], core_peer).wait()
    core_ref[...] = core_ref[...] + picked_ref[:, mine, :]
    own_quarter = pl.ds(pl.multiple_of(side * quarter, 16), quarter)
    other_quarter = pl.ds(pl.multiple_of((1 - side) * quarter, 16), quarter)
    send(core_ref.at[:, other_quarter, :], side_ref, sems.at[0, 1], sems.at[1, 1], side_peer).wait()
    side_ref[...] = side_ref[...] + core_ref[:, own_quarter, :]
    group_ref[group] = side_ref[group]
    copies = [
        send(side_ref.at[peer[0]], group_ref.at[group], sems.at[0, 2 + step], sems.at[1, 2 + step], peer)
        for step, peer in enumerate(far)
    ]
    for copy in copies:
        copy.wait()
    for index in range(groups):
        send_ref[:, index * width : (index + 1) * width] = group_ref[index]
    at = pl.ds(pl.multiple_of(core * half + side * quarter, 16), quarter)
    looked_ref[at, :] = send_ref[...]
    end = 1 + groups
    send(send_ref, looked_ref.at[at, :], sems.at[0, end], sems.at[1, end], side_peer).wait()
    end = end + 1
    both = looked_ref.at[mine, :]
    send(both, both, sems.at[0, end], sems.at[1, end], core_peer).wait()


def squares_kernel(
    groups, shares,
    embedding_ref, dense_ref,
    out_ref,
    share_ref, group_ref, sems,
):
    group, share, _, _, _ = places()
    near, far = share_peers(group, share, shares), group_peers(group, share, groups)
    meet(near + far)
    down = lax.broadcasted_iota(jnp.int32, (8, 128), 0)
    share_ref[share] = jnp.where(down == 0, embedding_ref[...] + dense_ref[...], 0.0)
    copies = [
        send(share_ref.at[share], share_ref.at[share], sems.at[0, step], sems.at[1, step], peer)
        for step, peer in enumerate(near)
    ]
    for copy in copies:
        copy.wait()
    summed = share_ref[0]
    for index in range(1, shares):
        summed = summed + share_ref[index]
    group_ref[group] = summed
    copies = [
        send(group_ref.at[group], group_ref.at[group], sems.at[2, step], sems.at[3, step], peer)
        for step, peer in enumerate(far)
    ]
    for copy in copies:
        copy.wait()
    summed = group_ref[0]
    for index in range(1, groups):
        summed = summed + group_ref[index]
    out_ref[...] = jnp.broadcast_to(jnp.sum(summed), out_ref.shape)


def dense_kernel(
    rate, place_grads, factor_ref, *refs
):
    *grad_refs, w_ref, first_ref, second_ref, new_w_ref, new_first_ref, new_second_ref, wide_ref = refs
    place_grads(wide_ref, *grad_refs)
    updated = adam_update(
        w_ref[0],
        first_ref[0],
        second_ref[0],
        wide_ref[...].astype(jnp.float32),
        factor_ref[0],
        rate,
    )
    for out, value in zip((new_w_ref, new_first_ref, new_second_ref), updated):
        out[0] = value


def dense_update(name, rate, place_grads, factor, grads, w, first, second, parts, cut=None):
    matrices, rows, columns = w.shape
    rows = rows // parts
    own = pl.BlockSpec((1, rows, columns), lambda matrix, part: (matrix, part, 0))
    shares, width = grads[0].shape[:2]
    grad_specs = [
        pl.BlockSpec(
            (shares, width, cut[0] if cut else member.shape[2]),
            lambda matrix, part: (0, 0, cut[1] if cut else 0),
        )
        for member in grads
    ]
    return pl.pallas_call(
        partial(dense_kernel, rate, place_grads),
        grid=(matrices, parts),
        out_shape=[jax.ShapeDtypeStruct(w.shape, w.dtype)] * 3,
        in_specs=[pl.BlockSpec(memory_space=pltpu.SMEM)] + grad_specs + [own] * 3,
        out_specs=[own] * 3,
        scratch_shapes=[pltpu.VMEM((rows, columns), jnp.bfloat16)],
        compiler_params=pltpu.CompilerParams(vmem_limit_bytes=VMEM_BYTES),
        name=name,
    )(factor, *grads, w, first, second)


def place_columns(groups, matrix, source_ref, start):
    def place(wide_ref):
        @pl.when(pl.program_id(0) == matrix)
        def _():
            rows, columns = wide_ref.shape
            shares = source_ref.shape[0]
            piece = columns // groups // shares
            at = pl.ds(pl.multiple_of(pl.program_id(1) * rows, 16), rows)
            for number in range(groups):
                for share in range(shares):
                    low = (number * shares + share) * piece
                    wide_ref[:, low : low + piece] = source_ref[
                        share, at, start + number * piece : start + (number + 1) * piece
                    ]

    return place


def cut_kernel(groups, shares, gap, in_ref, out_ref, up_ref, down_ref, norms_ref, early_ref, dec_ref, square_ref):
    share = lax.axis_index("vocab")
    width, model_width = in_ref.shape[1], out_ref.shape[2]
    own = model_width // shares
    piece = up_ref.shape[2] // groups // shares
    hidden = groups * piece
    in_wide = 3 * own + gap
    early_ref[...] = jnp.zeros_like(early_ref)
    dec_ref[...] = jnp.zeros_like(dec_ref)

    def columns(target, start, source, groups_in, size, index):
        step = shares * size
        for number in range(groups_in):
            low = number * step + index * size
            target[:, start + number * size : start + (number + 1) * size] = lowered(
                source[:, low : low + size]
            )

    def put(index):
        columns(early_ref, 0, in_ref.at[0], 3, own, index)
        columns(early_ref, in_wide, in_ref.at[1], 3, own, index)
        for matrix in range(3):
            columns(early_ref, 2 * in_wide + matrix * own, out_ref.at[matrix], 1, own, index)
        rows = slice(index * (down_ref.shape[1] // shares), (index + 1) * (down_ref.shape[1] // shares))
        for matrix, (target, start) in enumerate(((early_ref, 3 * in_wide), (dec_ref, 0))):
            columns(target, start, up_ref.at[matrix], groups, piece, index)
            start = start + hidden
            target[:, start : start + model_width] = lowered(down_ref[matrix, rows, :])
        columns(dec_ref, hidden + model_width, in_ref.at[2], 3, own, index)

    for index in range(shares):
        pl.when(share == index)(partial(put, index))
    square_ref[...] = jnp.zeros_like(square_ref)
    square_ref[0 : norms_ref.shape[0], 0:width] = norms_ref[...]
    end = 3 * in_wide
    early_ref[:, end - gap : end] = lowered(jnp.transpose(square_ref[...])[0:width, 0:gap])


def cut_weights(groups, shares, gap, inputs, early_wide, dec_wide):
    width = inputs[0].shape[1]
    return pl.pallas_call(
        partial(cut_kernel, groups, shares, gap),
        out_shape=(
            jax.ShapeDtypeStruct((width, early_wide), jnp.bfloat16),
            jax.ShapeDtypeStruct((width, dec_wide), jnp.bfloat16),
        ),
        in_specs=[pl.BlockSpec(memory_space=pltpu.VMEM)] * len(inputs),
        out_specs=(pl.BlockSpec(memory_space=pltpu.VMEM),) * 2,
        scratch_shapes=[pltpu.VMEM((128, 128), jnp.float32)],
        compiler_params=pltpu.CompilerParams(vmem_limit_bytes=VMEM_BYTES),
        name="cut_weights",
    )(*inputs)


def numbers_kernel(
    groups, numbers_ref, hits_ref, all_numbers_ref, all_hits_ref, sems, local_sems
):
    group, share, _, _, _ = places()
    peers = group_peers(group, share, groups)
    meet(peers)
    copies = []
    for number, (source, target) in enumerate(
        ((numbers_ref, all_numbers_ref), (hits_ref, all_hits_ref))
    ):
        copies += [
            send(source, target.at[group], sems.at[number, 0, step], sems.at[number, 1, step], peer)
            for step, peer in enumerate(peers)
        ]
        keep = pltpu.make_async_copy(source, target.at[group], local_sems.at[number])
        keep.start()
        copies.append(keep)
    for copy in copies:
        copy.wait()


def local(
    enc_ids,
    labels,
    target_lengths,
    loss_positions,
    embedding,
    attn_in,
    attn_out,
    ffn_up,
    ffn_down,
    norms,
    embedding_first,
    attn_in_first,
    attn_out_first,
    ffn_up_first,
    ffn_down_first,
    norms_first,
    embedding_second,
    attn_in_second,
    attn_out_second,
    ffn_up_second,
    ffn_down_second,
    norms_second,
):
    groups, shares = lax.axis_size("dp"), lax.axis_size("vocab")
    group, share = lax.axis_index("dp"), lax.axis_index("vocab")
    enc_len, dec_len = enc_ids.shape[1], labels.shape[1]
    loss_count = loss_positions.shape[1]
    shard_rows, part_width = embedding.shape
    model_width = part_width * groups
    vocab_total = shard_rows * shares
    row_start = share * shard_rows
    root_width = math.sqrt(model_width)
    tokens = enc_len + dec_len

    bf16, f32 = jnp.bfloat16, jnp.float32
    sems = pltpu.SemaphoreType.DMA
    numbers = jnp.concatenate(
        [enc_ids, labels, loss_positions, target_lengths[:, None]], axis=1
    )
    number_count = numbers.shape[1]
    number_lanes = -(-number_count // 1024) * 128
    numbers = jnp.pad(numbers, ((0, 0), (0, 8 * number_lanes - number_count)))
    span = 1 << tokens.bit_length()
    own_tokens = jnp.concatenate([enc_ids[0], jnp.zeros((1,), jnp.int32), labels[0, :-1]])
    hits = list_hits(own_tokens - row_start, shard_rows, span)
    own = model_width // shares
    own_in, own_up = 3 * own, ffn_up.shape[2] // shares
    norm_rows = norms.shape[0]
    gap = -own_in % 128
    in_wide = own_in + gap
    dec_wide = own_up + model_width + in_wide
    first_wide = 3 * in_wide
    enc_wide = own_up + model_width
    chunk = -(-shard_rows // (groups * 3072)) * 3072
    table_cuts = (chunk // 4, 5 * chunk // 24, chunk // 6, 3 * chunk // 8)
    early_wide = first_wide + enc_wide
    mine_early, mine_dec = cut_weights(
        groups, shares, gap, (attn_in, attn_out, ffn_up, ffn_down, norms), early_wide, dec_wide
    )
    w_early = lax.all_gather(mine_early, "dp", axis=0, tiled=True)
    w_dec = lax.all_gather(mine_dec, "dp", axis=0, tiled=True)
    numbers, hits = call(
        partial(numbers_kernel, groups),
        "numbers",
        1,
        [numbers.reshape(8, number_lanes), hits.reshape(8, span // 8)],
        [
            shape_of((groups, 8, number_lanes), jnp.int32),
            shape_of((groups, 8, span // 8), jnp.int32),
        ],
        [sems((2, 2, groups - 1)), sems((2,))],
        0,
    )
    hits = hits.reshape(groups, span)
    numbers = numbers.reshape(groups, 8 * number_lanes)
    all_labels = numbers[:, enc_len:tokens]
    all_positions = numbers[:, tokens : tokens + loss_count]
    all_lengths = numbers[:, tokens + loss_count : number_count]
    at_place = all_positions[:, :, None] == jnp.arange(dec_len)
    all_targets = jnp.sum(jnp.where(at_place, all_labels[:, None, :], 0), axis=2).reshape(-1)
    all_counted = (all_positions < all_lengths).reshape(-1).astype(f32)
    token_count = jnp.sum(all_counted)

    picked, across, table_zero = pick_rows(
        hits, groups * tokens, embedding.T, groups * chunk, table_cuts[0]
    )
    place_enc = positions_numpy(enc_len, model_width)
    place_dec = positions_numpy(dec_len, model_width)
    enc_macs, dec_macs = enc_len * model_width, dec_len * model_width
    total_enc, total_dec = total_scratch(enc_len, model_width), total_scratch(dec_len, model_width)
    block_shape = (2, 2, 2, part_width)
    (looked,) = call(
        partial(look_kernel, groups),
        "look",
        2,
        [picked.reshape(groups, tokens, part_width)],
        [shape_of((tokens, model_width), bf16)],
        [
            pltpu.VMEM((tokens // 4, model_width), bf16),
            pltpu.VMEM((groups, tokens // 2, part_width), bf16),
            pltpu.VMEM((groups, tokens // 4, part_width), bf16),
            pltpu.VMEM((groups, tokens // 4, part_width), bf16),
            sems((2, groups + 3)),
        ],
        0,
    )
    table_zero = lax.all_to_all(table_zero, "dp", 0, 0)
    forward_inputs = [looked, place_enc, place_dec, w_early, across]
    forward_outputs = [
        shape_of((groups, part_width, sum(table_cuts[1:3])), bf16),
        shape_of((3, own, model_width), bf16),
        shape_of((16, model_width), f32),
        shape_of((enc_len, 3 * own), bf16),
        shape_of((enc_len, own), bf16),
        shape_of((enc_len, 128), f32),
        shape_of((enc_len, model_width), f32),
        shape_of((enc_len, own_up), f32),
        shape_of((enc_len, model_width), f32),
        shape_of((enc_len, model_width), bf16),
        shape_of((dec_len, 3 * own), bf16),
        shape_of((dec_len, own), bf16),
        shape_of((dec_len, 128), f32),
        shape_of((dec_len, model_width), f32),
    ]
    (
        table_one, out_rows, norm_values,
        qkv_enc, context_enc, logs_enc, stream_enc, pre_enc, stream_two, memory,
        qkv_dec, context_dec, logs_dec, stream_dec,
    ) = call(
        partial(
            forward_kernel, groups, shares, table_cuts[0], table_cuts[1:3], len(forward_inputs),
            len(forward_outputs),
        ),
        "forward",
        3,
        forward_inputs,
        forward_outputs,
        [
            sems((2, 2, groups)),
            sems((3,)),
            sems((2,)),
            pltpu.VMEM((model_width, first_wide), bf16),
            pltpu.VMEM((model_width, enc_wide), bf16),
            pltpu.VMEM((enc_len, model_width), f32),
            pltpu.VMEM((enc_len, own_up), f32),
            pltpu.VMEM((enc_len, model_width), f32),
            pltpu.VMEM((shares, own, in_wide), bf16),
            sems((2, shares - 1)),
            sems,
            *total_dec,
            *total_enc,
            *total_enc[1:],
        ],
        8 * enc_macs * own_up,
        (3, 4),
        (0, 6, 7, 8),
    )
    (
        table_two, q_cross, kv_cross, context_cross, logs_cross, stream_mid, pre_dec, stream_out, selected,
    ) = call(
        partial(dec_kernel, groups, sum(table_cuts[:3])),
        "dec",
        4,
        [
            stream_dec, memory, norm_values, out_rows, loss_positions.reshape(-1, 1), w_dec, across,
        ],
        [
            shape_of((groups, part_width, table_cuts[3]), bf16),
            shape_of((dec_len, own), bf16),
            shape_of((enc_len, 2 * own), bf16),
            shape_of((dec_len, own), bf16),
            shape_of((dec_len, 128), f32),
            shape_of((dec_len, model_width), f32),
            shape_of((dec_len, own_up), f32),
            shape_of((dec_len, model_width), f32),
            shape_of((groups, loss_count, model_width), bf16),
        ],
        [
            pltpu.VMEM((model_width, dec_wide), bf16),
            sems,
            sems((2, groups)),
            pltpu.VMEM((loss_count, model_width), bf16),
            sems((2, groups - 1)),
            *total_dec,
            *total_dec[1:],
        ],
        8 * dec_macs * own_up,
        (5, 6),
        (0,),
    )

    rows_all = groups * loss_count
    first_row = row_start + group * chunk
    targets = all_targets - first_row
    inside = (targets >= 0) & (targets < jnp.minimum(chunk, shard_rows - group * chunk))
    targets = jnp.where(inside, targets, -1)[:, None]
    head_cut = chunk // 8
    loss, grad_selected, head_grad, head_zero = call(
        partial(head_kernel, groups, shares, shard_rows),
        "head",
        6,
        [
            selected.reshape(rows_all, model_width),
            table_zero.reshape(model_width, -1),
            table_one.reshape(model_width, -1),
            table_two.reshape(model_width, -1),
            targets,
            (all_counted / token_count)[:, None],
            all_counted[None, :],
        ],
        [
            shape_of((1, 128), f32),
            shape_of((loss_count, model_width), bf16),
            shape_of((model_width, chunk), bf16),
            shape_of((groups, part_width, head_cut), bf16),
        ],
        [
            sems((2, groups)),
            pltpu.VMEM((rows_all, chunk), f32),
            pltpu.VMEM((rows_all, chunk), bf16),
            pltpu.VMEM((rows_all, 128), f32),
            pltpu.VMEM((128, rows_all), f32),
            pltpu.VMEM((shares, 8, rows_all), f32),
            pltpu.VMEM((groups, 8, rows_all), f32),
            sems((4, max(groups, shares))),
            pltpu.VMEM((groups, loss_count, model_width), bf16),
            pltpu.VMEM((groups, loss_count // 2, model_width), bf16),
            pltpu.VMEM((groups, loss_count // 4, model_width), bf16),
            pltpu.VMEM((groups, loss_count // 4, model_width), bf16),
            pltpu.VMEM((loss_count // 4, model_width), bf16),
            sems((2, groups + shares)),
        ],
        6 * rows_all * chunk * model_width,
        (),
        (3,),
    )
    loss_sum = loss[0, 0]
    head_grad = head_grad.reshape(groups, part_width, chunk)
    last_wide = own_in + own
    back_wide = own_up + model_width + last_wide
    late_wide = back_wide + last_wide
    quarter = tokens // shares
    back_inputs = [
        grad_selected, loss_positions.reshape(1, -1), stream_out, stream_mid, pre_dec, norm_values, w_dec,
        out_rows, memory, stream_dec, q_cross, kv_cross, context_cross, logs_cross,
        stream_two, stream_enc, pre_enc, w_early, looked, place_enc, place_dec,
        qkv_dec, context_dec, logs_dec, qkv_enc, context_enc, logs_enc,
        head_grad,
    ]

    head_one, grad_tokens, dec_shares, late_own, dense_squares = call(
        partial(
            back_kernel, groups, shares, first_wide, len(back_inputs), 5
        ),
        "backward",
        7,
        back_inputs,
        [
            shape_of((groups, part_width, chunk - head_cut), bf16),
            shape_of((shares, groups, quarter + 16, part_width), bf16),
            shape_of((shares, part_width, back_wide), bf16),
            shape_of((part_width, late_wide), bf16),
            shape_of((1, 128), f32),
        ],
        [
            sems((2, groups)),
            sems((11,)),
            pltpu.VMEM((model_width, dec_wide), bf16),
            pltpu.VMEM((model_width, own_up + model_width), bf16),
            pltpu.VMEM(out_rows.shape, bf16),
            pltpu.VMEM((enc_len, model_width), bf16),
            pltpu.VMEM((dec_len, model_width), f32),
            pltpu.VMEM((enc_len, model_width), f32),
            pltpu.VMEM((enc_len, model_width), f32),
            pltpu.VMEM((enc_len, own_up), f32),
            pltpu.VMEM((tokens, model_width), bf16),
            pltpu.VMEM(block_shape + (back_wide,), bf16),
            pltpu.VMEM(block_shape + (back_wide,), bf16),
            pltpu.VMEM(block_shape + (last_wide,), bf16),
            pltpu.VMEM((dec_len, model_width), f32),
            pltpu.VMEM((enc_len, model_width), f32),
            pltpu.VMEM((dec_len, own), bf16),
            pltpu.VMEM((dec_len, own), bf16),
            pltpu.VMEM((enc_len, 2 * own), bf16),
            pltpu.VMEM((dec_len, 3 * own), bf16),
            pltpu.VMEM((enc_len, 3 * own), bf16),
            pltpu.VMEM((enc_len, own), bf16),
            pltpu.VMEM((own, model_width), bf16),
            pltpu.VMEM((own, model_width), bf16),
            pltpu.VMEM((own, model_width), bf16),
            pltpu.VMEM((8, model_width), f32),
            pltpu.VMEM((8, model_width), f32),
            pltpu.VMEM((8, model_width), f32),
            pltpu.VMEM((16, model_width), f32),
            sems((3, 2, shares)),
            pltpu.VMEM((groups, tokens + 16 * shares, part_width), bf16),
            sems((2, groups)),
            sems((2, 3)),
            sems((2, 3)),
            pltpu.VMEM((part_width, back_wide), bf16),
            sems((3,)),
            *[pltpu.VMEM((shares, own, own), bf16)] * 6,
            *total_dec,
            *total_enc,
            *total_dec[1:],
            *total_enc[1:],
            *line_scratch(part_width, back_wide),
            *line_scratch(part_width, back_wide),
            *line_scratch(part_width, last_wide),
        ],
        16 * (enc_macs + dec_macs) * own_up,
        (6, 7, 8, 9, 14, 15, 16, 17, 18, 19, 27),
        (0, 1, 2),
    )
    late_shares = lax.all_gather(late_own, "vocab", axis=0, tiled=False)
    g_embedding, embedding_squares = spread_rows(
        hits, groups * tokens, grad_tokens, (head_zero, head_one)
    )
    g_embedding = g_embedding[:, :shard_rows].astype(f32).T
    g_norms = jnp.sum(grad_tokens[0, :, quarter : quarter + norm_rows].astype(f32), axis=0)
    dense_squares = dense_squares + jnp.sum(g_norms * g_norms) / (shares * dense_squares.shape[1])
    (squares,) = call(
        partial(squares_kernel, groups, shares),
        "squares",
        10,
        [embedding_squares, dense_squares],
        [shape_of((1, 128), f32)],
        [
            pltpu.VMEM((shares, 8, 128), f32),
            pltpu.VMEM((groups, 8, 128), f32),
            sems((4, max(groups, shares))),
        ],
        0,
    )
    grad_norm = jnp.sqrt(squares[0, 0])
    factor = jnp.minimum(1.0, CLIP / (grad_norm + 1e-06))
    grad_pair = [late_shares, dec_shares]
    in_start, late_in = own_up + model_width, back_wide

    def place_in(wide_ref, late_ref, dec_ref):
        place_columns(3, 0, late_ref, late_in)(wide_ref)
        place_columns(3, 1, late_ref, in_start)(wide_ref)
        place_columns(3, 2, dec_ref, in_start)(wide_ref)

    def place_out(wide_ref, late_ref, dec_ref):
        place_columns(1, 0, late_ref, late_in + own_in)(wide_ref)
        place_columns(1, 1, late_ref, in_start + own_in)(wide_ref)
        place_columns(1, 2, dec_ref, in_start + own_in)(wide_ref)

    def place_up(wide_ref, late_ref, dec_ref):
        place_columns(groups, 0, late_ref, 0)(wide_ref)
        place_columns(groups, 1, dec_ref, 0)(wide_ref)

    down_rows = ffn_down.shape[1] // shares

    def place_down(wide_ref, late_ref, dec_ref):
        for matrix, ref in enumerate((late_ref, dec_ref)):

            @pl.when(pl.program_id(0) == matrix)
            def _(ref=ref):
                for piece in range(shares):
                    wide_ref[piece * down_rows : (piece + 1) * down_rows] = ref[piece]

    scale = factor.reshape(1)
    new_in = dense_update(
        "adam_in", RATES[1], place_in, scale, grad_pair, attn_in, attn_in_first, attn_in_second, 2
    )
    new_out = dense_update(
        "adam_out", RATES[2], place_out, scale, grad_pair, attn_out, attn_out_first, attn_out_second, 1
    )
    new_up = dense_update(
        "adam_up", RATES[3], place_up, scale, grad_pair, ffn_up, ffn_up_first, ffn_up_second, 2,
        (own_up, 0),
    )
    new_down = dense_update(
        "adam_down", RATES[4], place_down, scale, grad_pair, ffn_down, ffn_down_first, ffn_down_second, 1,
        (model_width, 1),
    )
    new_embedding = adam_update(
        embedding, embedding_first, embedding_second, g_embedding, factor, RATES[0]
    )
    new_norms = adam_update(norms, norms_first, norms_second, g_norms, factor, RATES[5])
    updated = (new_embedding, new_in, new_out, new_up, new_down, new_norms)
    return (loss_sum, token_count, grad_norm) + tuple(
        updated[slot][kind] for kind in range(3) for slot in range(6)
    )


def splits_evenly(mesh):
    return HEADS % mesh.shape["vocab"] == 0 and mesh.shape["dp"] == 8


def solution(mesh):
    placed = (
        P("dp", None),
        P("dp", None),
        P("dp"),
        P("dp", None),
        P("vocab", "dp"),
        P(None, "dp", None),
        P(None, "dp", None),
        P(None, "dp", None),
        P(None, "dp", None),
        P(None, "dp"),
        P("vocab", "dp"),
        P(None, "dp", None),
        P(None, "dp", None),
        P(None, "dp", None),
        P(None, "dp", None),
        P(None, "dp"),
        P("vocab", "dp"),
        P(None, "dp", None),
        P(None, "dp", None),
        P(None, "dp", None),
        P(None, "dp", None),
        P(None, "dp"),
    )
    return jax.shard_map(
        local if splits_evenly(mesh) else local_copied,
        mesh=mesh,
        in_specs=placed,
        out_specs=(
            P(),
            P(),
            P(),
            P("vocab", "dp"),
            P(None, "dp", None),
            P(None, "dp", None),
            P(None, "dp", None),
            P(None, "dp", None),
            P(None, "dp"),
            P("vocab", "dp"),
            P(None, "dp", None),
            P(None, "dp", None),
            P(None, "dp", None),
            P(None, "dp", None),
            P(None, "dp"),
            P("vocab", "dp"),
            P(None, "dp", None),
            P(None, "dp", None),
            P(None, "dp", None),
            P(None, "dp", None),
            P(None, "dp"),
        ),
        check_vma=False,
    )
```

```python
from functools import partial
import math

import jax
import jax.numpy as jnp
import numpy as np
from jax import lax
from jax.experimental import pallas as pl
from jax.experimental.pallas import tpu as pltpu
from jax.sharding import PartitionSpec as P

HEADS = 12
HEAD_DIM = 64
STEP = 10


EPS_NORM = 1e-05
SMOOTH = 0.1
CLIP = 0.02
RATES = (0.05, 0.05, 0.4, 0.05, 0.05, 0.8)
BETA_ONE = 0.9
BETA_TWO = 0.999
ADAM_EPS = 1e-08
DECAY = 0.01


def lowered(tensor):
    return tensor.astype(jnp.bfloat16)


def matmul(left_side, right_side):
    return jnp.dot(left_side, right_side, preferred_element_type=jnp.float32)


def times_transposed(left_side, right_side):
    return lax.dot_general(
        left_side, right_side, (((1,), (1,)), ((), ())), preferred_element_type=jnp.float32
    )


def contract_rows(left_side, right_side):
    return lax.dot_general(
        left_side, right_side, (((0,), (0,)), ((), ())), preferred_element_type=jnp.float32
    )


def positions_table(length, model_width):
    position_col = jnp.arange(length, dtype=jnp.float32)[:, None]
    freq_index = jnp.arange(model_width // 2, dtype=jnp.float32)[None, :]
    angles = position_col * jnp.exp(freq_index * (-2.0 * math.log(10000.0) / model_width))
    return jnp.concatenate([jnp.sin(angles), jnp.cos(angles)], axis=1)


def norm_forward(tensor, gain_row, shift_row):
    center = tensor - jnp.mean(tensor, axis=-1, keepdims=True)
    scale_inv = lax.rsqrt(jnp.mean(center * center, axis=-1, keepdims=True) + EPS_NORM)
    normed = center * scale_inv
    return (normed * gain_row + shift_row, (normed, scale_inv))


def norm_backward_rows(grad_out, saved_parts, gain_row):
    normed, scale_inv = saved_parts
    grad_normed = grad_out * gain_row
    grad_in = scale_inv * (
        grad_normed
        - jnp.mean(grad_normed, axis=-1, keepdims=True)
        - normed * jnp.mean(grad_normed * normed, axis=-1, keepdims=True)
    )
    return (grad_in, jnp.sum(grad_out * normed, axis=0), jnp.sum(grad_out, axis=0))


def split_heads(rows, batch_size):
    return rows.reshape(batch_size, -1, HEADS, rows.shape[1] // HEADS)


def score_block(queries, key_rows, causal):
    scores = jnp.einsum(
        "qhe,khe->hqk", queries, key_rows, preferred_element_type=jnp.float32
    ) * HEAD_DIM ** (-0.5)
    if causal:
        allowed = jnp.arange(queries.shape[0])[:, None] >= jnp.arange(key_rows.shape[0])[None, :]
        scores = jnp.where(allowed[None], scores, -1e30)
    return scores


def attend_one(block_args, causal):
    queries, key_rows, value_rows = block_args
    scores = score_block(queries, key_rows, causal)
    row_top = jnp.max(scores, axis=-1, keepdims=True)
    exponent = jnp.exp(scores - row_top)
    row_total = jnp.sum(exponent, axis=-1, keepdims=True)
    softmax_out = lowered(exponent / row_total)
    context = jnp.einsum(
        "hqk,khe->qhe", softmax_out, value_rows, preferred_element_type=jnp.float32
    )
    return (lowered(context), (row_top + jnp.log(row_total))[..., 0])


def attend_back(block_args, causal):
    queries, key_rows, value_rows, log_total, grad_context = block_args
    scores = score_block(queries, key_rows, causal)
    softmax_out = jnp.exp(scores - log_total[..., None])
    grad_values = jnp.einsum(
        "hqk,qhe->khe", lowered(softmax_out), grad_context, preferred_element_type=jnp.float32
    )
    grad_softmax = jnp.einsum(
        "qhe,khe->hqk", grad_context, value_rows, preferred_element_type=jnp.float32
    )
    grad_scores = lowered(
        softmax_out * (grad_softmax - jnp.sum(grad_softmax * softmax_out, axis=-1, keepdims=True))
    )
    grad_queries = jnp.einsum(
        "hqk,khe->qhe", grad_scores, key_rows, preferred_element_type=jnp.float32
    ) * HEAD_DIM ** (-0.5)
    grad_keys = jnp.einsum(
        "hqk,qhe->khe", grad_scores, queries, preferred_element_type=jnp.float32
    ) * HEAD_DIM ** (-0.5)
    return (lowered(grad_queries), lowered(grad_keys), lowered(grad_values))


def layer_forward(stream, memory, blocks, feed_parts, gain_rows, shifts, batch_size):
    kept_values = []
    for block_order, (w_in, w_out, norm_row) in enumerate(blocks):
        normed, norm_kept = norm_forward(stream, gain_rows[norm_row], shifts[norm_row])
        query_in = lowered(normed)
        model_width = w_out.shape[0]
        if block_order == 0:
            projected = lowered(matmul(query_in, w_in))
            queries = projected[:, :model_width]
            key_rows = projected[:, model_width : 2 * model_width]
            value_rows = projected[:, 2 * model_width :]
            memory_in = query_in
        else:
            memory_in = memory
            queries = lowered(matmul(query_in, w_in[:, :model_width]))
            paired = lowered(matmul(memory, w_in[:, model_width:]))
            key_rows, value_rows = (paired[:, :model_width], paired[:, model_width:])
        causal = memory is not None and block_order == 0
        heads = (
            split_heads(queries, batch_size),
            split_heads(key_rows, batch_size),
            split_heads(value_rows, batch_size),
        )
        context, log_total = lax.map(partial(attend_one, causal=causal), heads)
        context = context.reshape(-1, model_width)
        stream = stream + matmul(context, w_out)
        kept_values.append((norm_kept, query_in, memory_in, heads, context, log_total))
    w_up, w_down, norm_row = feed_parts
    normed, norm_kept = norm_forward(stream, gain_rows[norm_row], shifts[norm_row])
    hidden_in = lowered(normed)
    hidden_pre = matmul(hidden_in, w_up)
    activated = lowered(jax.nn.silu(hidden_pre))
    stream = stream + matmul(activated, w_down)
    kept_values.append((norm_kept, hidden_in, hidden_pre, activated))
    return (stream, kept_values)


def layer_backward(grad_stream, memory, blocks, feed_parts, gain_rows, kept_values, batch_size):
    w_up, w_down, norm_row = feed_parts
    norm_kept, hidden_in, hidden_pre, activated = kept_values[-1]
    grad_low = lowered(grad_stream)
    grad_down = contract_rows(activated, grad_low)
    sigmoid_pre = jax.nn.sigmoid(hidden_pre)
    grad_pre = lowered(
        times_transposed(grad_low, w_down) * sigmoid_pre * (1.0 + hidden_pre * (1.0 - sigmoid_pre))
    )
    grad_up = contract_rows(hidden_in, grad_pre)
    grad_in, grad_gain, grad_shift = norm_backward_rows(
        times_transposed(grad_pre, w_up), norm_kept, gain_rows[norm_row]
    )
    grad_stream = grad_stream + grad_in
    norm_grads = [(norm_row, grad_gain, grad_shift)]
    block_grads = [None] * len(blocks)
    grad_memory = None
    for block_order in reversed(range(len(blocks))):
        w_in, w_out, norm_row = blocks[block_order]
        norm_kept, query_in, memory_in, heads, context, log_total = kept_values[block_order]
        model_width = w_out.shape[0]
        grad_low = lowered(grad_stream)
        grad_w_out = contract_rows(context, grad_low)
        grad_context = split_heads(lowered(times_transposed(grad_low, w_out)), batch_size)
        causal = memory is not None and block_order == 0
        grad_heads = lax.map(partial(attend_back, causal=causal), heads + (log_total, grad_context))
        grad_queries, grad_keys, grad_values = [
            member.reshape(-1, model_width) for member in grad_heads
        ]
        if block_order == 0:
            grad_proj = jnp.concatenate([grad_queries, grad_keys, grad_values], axis=1)
            grad_w_in = contract_rows(query_in, grad_proj)
            grad_normed = times_transposed(grad_proj, w_in)
        else:
            grad_pair = jnp.concatenate([grad_keys, grad_values], axis=1)
            grad_w_in = jnp.concatenate(
                [contract_rows(query_in, grad_queries), contract_rows(memory_in, grad_pair)], axis=1
            )
            grad_normed = times_transposed(grad_queries, w_in[:, :model_width])
            grad_memory = times_transposed(grad_pair, w_in[:, model_width:])
        grad_in, grad_gain, grad_shift = norm_backward_rows(grad_normed, norm_kept, gain_rows[norm_row])
        grad_stream = grad_stream + grad_in
        norm_grads.append((norm_row, grad_gain, grad_shift))
        block_grads[block_order] = (grad_w_in, grad_w_out)
    return (grad_stream, grad_memory, block_grads, (grad_up, grad_down), norm_grads)


def adam_update(weight, first_moment, second_moment, gradient, factor, rate):
    clipped = gradient * factor
    new_first = BETA_ONE * first_moment + (1.0 - BETA_ONE) * clipped
    new_second = BETA_TWO * second_moment + (1.0 - BETA_TWO) * clipped * clipped
    corrected = (
        new_first
        / (1.0 - BETA_ONE**STEP)
        / (jnp.sqrt(new_second / (1.0 - BETA_TWO**STEP)) + ADAM_EPS)
    )
    return (weight - rate * (corrected + DECAY * weight), new_first, new_second)


def local_copied(
    enc_ids,
    labels,
    target_lengths,
    loss_positions,
    embedding,
    attn_in,
    attn_out,
    ffn_up,
    ffn_down,
    norms,
    embedding_first,
    attn_in_first,
    attn_out_first,
    ffn_up_first,
    ffn_down_first,
    norms_first,
    embedding_second,
    attn_in_second,
    attn_out_second,
    ffn_up_second,
    ffn_down_second,
    norms_second,
):
    batch_size, enc_len = enc_ids.shape
    dec_len = labels.shape[1]
    emb_table, w_in_all, w_out_all, w_up_all, w_down_all, norm_table = (
        lax.all_gather(lowered(embedding), "dp", axis=1, tiled=True),
        lax.all_gather(lowered(attn_in), "dp", axis=1, tiled=True),
        lax.all_gather(lowered(attn_out), "dp", axis=1, tiled=True),
        lax.all_gather(lowered(ffn_up), "dp", axis=1, tiled=True),
        lax.all_gather(lowered(ffn_down), "dp", axis=1, tiled=True),
        lax.all_gather(lowered(norms), "dp", axis=1, tiled=True),
    )
    model_width = emb_table.shape[1]
    shard_rows = emb_table.shape[0]
    vocab_total = shard_rows * lax.axis_size("vocab")
    row_start = lax.axis_index("vocab") * shard_rows
    norm_values = norm_table.astype(jnp.float32)
    gain_rows, shifts = (norm_values[:7], norm_values[7:])
    dec_ids = jnp.concatenate([jnp.zeros((batch_size, 1), jnp.int32), labels[:, :-1]], axis=1)
    token_list = jnp.concatenate([enc_ids.reshape(-1), dec_ids.reshape(-1)])
    local_rows = token_list - row_start
    inside = (local_rows >= 0) & (local_rows < shard_rows)
    safe_rows = jnp.clip(local_rows, 0, shard_rows - 1)
    picked = jnp.where(
        inside[:, None], jnp.take(emb_table, safe_rows, axis=0).astype(jnp.float32), 0.0
    )
    looked = lax.psum(picked.astype(jnp.bfloat16), "vocab").astype(jnp.float32)
    root_width = math.sqrt(model_width)
    enc_tokens = batch_size * enc_len
    enc_stream = (
        looked[:enc_tokens].reshape(batch_size, enc_len, model_width) * root_width
        + positions_table(enc_len, model_width)
    ).reshape(enc_tokens, model_width)
    dec_stream = (
        looked[enc_tokens:].reshape(batch_size, dec_len, model_width) * root_width
        + positions_table(dec_len, model_width)
    ).reshape(batch_size * dec_len, model_width)
    enc_blocks = [(w_in_all[0], w_out_all[0], 0)]
    dec_blocks = [(w_in_all[1], w_out_all[1], 3), (w_in_all[2], w_out_all[2], 4)]
    enc_feed = (w_up_all[0], w_down_all[0], 1)
    dec_feed = (w_up_all[1], w_down_all[1], 5)
    enc_out, enc_kept = layer_forward(
        enc_stream, None, enc_blocks, enc_feed, gain_rows, shifts, batch_size
    )
    memory, memory_kept = norm_forward(enc_out, gain_rows[2], shifts[2])
    memory_low = lowered(memory)
    dec_out, dec_kept = layer_forward(
        dec_stream, memory_low, dec_blocks, dec_feed, gain_rows, shifts, batch_size
    )
    final, final_kept = norm_forward(dec_out, gain_rows[6], shifts[6])
    chosen = (jnp.arange(batch_size)[:, None] * dec_len + loss_positions).reshape(-1)
    selected = lowered(jnp.take(final, chosen, axis=0))
    logits = times_transposed(selected, emb_table)
    columns = row_start + jnp.arange(shard_rows)
    padding = columns == vocab_total - 1
    masked = jnp.where(padding[None, :], -1e30, logits)
    target_local = jnp.take_along_axis(labels, loss_positions, axis=1).reshape(-1) - row_start
    target_hit = (jnp.arange(shard_rows)[None, :] == target_local[:, None]).astype(jnp.float32)
    target_term = jnp.sum(target_hit * logits, axis=1)
    smooth_term = jnp.sum(jnp.where(padding[None, :], 0.0, logits), axis=1)
    local_max = jnp.max(masked, axis=1)
    row_max = lax.pmax(local_max, "vocab")
    exp_local = jnp.sum(jnp.exp(masked - row_max[:, None]), axis=1)
    exp_total, smooth_total, target_total = lax.psum((exp_local, smooth_term, target_term), "vocab")
    log_total = row_max + jnp.log(exp_total)
    per_row = log_total - (1.0 - SMOOTH) * target_total - SMOOTH * smooth_total / (vocab_total - 1)
    counted = (loss_positions < target_lengths[:, None]).reshape(-1).astype(jnp.float32)
    loss_sum, token_count = lax.psum((jnp.sum(counted * per_row), jnp.sum(counted)), "dp")
    softmax_rows = jnp.exp(masked - log_total[:, None])
    grad_logits = (counted / token_count)[:, None] * (
        softmax_rows - (1.0 - SMOOTH) * target_hit - SMOOTH / (vocab_total - 1)
    )
    grad_logits = lowered(jnp.where(padding[None, :], 0.0, grad_logits))
    grad_selected = lax.psum(matmul(grad_logits, emb_table).astype(jnp.bfloat16), "vocab").astype(
        jnp.float32
    )
    grad_final = jnp.zeros_like(final).at[chosen].add(grad_selected)
    grad_dec_out, gain_six, shift_six = norm_backward_rows(grad_final, final_kept, gain_rows[6])
    grad_dec_stream, grad_memory, dec_block_grads, dec_feed_grads, dec_norm_grads = layer_backward(
        grad_dec_out, memory_low, dec_blocks, dec_feed, gain_rows, dec_kept, batch_size
    )
    grad_enc_out, gain_two, shift_two = norm_backward_rows(grad_memory, memory_kept, gain_rows[2])
    grad_enc_stream, _, enc_block_grads, enc_feed_grads, enc_norm_grads = layer_backward(
        grad_enc_out, None, enc_blocks, enc_feed, gain_rows, enc_kept, batch_size
    )
    grad_attn_in = jnp.stack([enc_block_grads[0][0], dec_block_grads[0][0], dec_block_grads[1][0]])
    grad_attn_out = jnp.stack([enc_block_grads[0][1], dec_block_grads[0][1], dec_block_grads[1][1]])
    grad_up_all = jnp.stack([enc_feed_grads[0], dec_feed_grads[0]])
    grad_down_all = jnp.stack([enc_feed_grads[1], dec_feed_grads[1]])
    grad_norms = jnp.zeros((14, model_width), jnp.float32)
    for norm_row, grad_gain, grad_shift in (
        enc_norm_grads + dec_norm_grads + [(2, gain_two, shift_two), (6, gain_six, shift_six)]
    ):
        grad_norms = grad_norms.at[norm_row].set(grad_gain).at[norm_row + 7].set(grad_shift)
    grad_tokens = jnp.concatenate([grad_enc_stream, grad_dec_stream], axis=0) * root_width
    head_term = contract_rows(grad_logits, selected)
    lookup_term = (
        jnp.zeros((shard_rows, model_width), jnp.float32)
        .at[safe_rows]
        .add(jnp.where(inside[:, None], grad_tokens, 0.0))
    )
    g_attn_in, g_attn_out, g_up, g_down, g_norms, g_embedding = (
        lax.psum_scatter(
            grad_attn_in.astype(jnp.bfloat16), "dp", scatter_dimension=1, tiled=True
        ).astype(jnp.float32),
        lax.psum_scatter(
            grad_attn_out.astype(jnp.bfloat16), "dp", scatter_dimension=1, tiled=True
        ).astype(jnp.float32),
        lax.psum_scatter(
            grad_up_all.astype(jnp.bfloat16), "dp", scatter_dimension=1, tiled=True
        ).astype(jnp.float32),
        lax.psum_scatter(
            grad_down_all.astype(jnp.bfloat16), "dp", scatter_dimension=1, tiled=True
        ).astype(jnp.float32),
        lax.psum_scatter(
            grad_norms.astype(jnp.bfloat16), "dp", scatter_dimension=1, tiled=True
        ).astype(jnp.float32),
        lax.psum_scatter(
            (head_term + lookup_term).astype(jnp.bfloat16), "dp", scatter_dimension=1, tiled=True
        ).astype(jnp.float32),
    )
    gradients = (g_embedding, g_attn_in, g_attn_out, g_up, g_down, g_norms)
    dense_squares = sum((jnp.sum(member * member) for member in gradients[1:]))
    squares = lax.psum(
        dense_squares / lax.axis_size("vocab") + jnp.sum(g_embedding * g_embedding), ("dp", "vocab")
    )
    grad_norm = jnp.sqrt(squares)
    factor = jnp.minimum(1.0, CLIP / (grad_norm + 1e-06))
    params = (embedding, attn_in, attn_out, ffn_up, ffn_down, norms)
    firsts = (
        embedding_first,
        attn_in_first,
        attn_out_first,
        ffn_up_first,
        ffn_down_first,
        norms_first,
    )
    seconds = (
        embedding_second,
        attn_in_second,
        attn_out_second,
        ffn_up_second,
        ffn_down_second,
        norms_second,
    )
    updated = [
        adam_update(params[slot], firsts[slot], seconds[slot], gradients[slot], factor, RATES[slot])
        for slot in range(6)
    ]
    return (
        loss_sum,
        token_count,
        grad_norm,
        updated[0][0],
        updated[1][0],
        updated[2][0],
        updated[3][0],
        updated[4][0],
        updated[5][0],
        updated[0][1],
        updated[1][1],
        updated[2][1],
        updated[3][1],
        updated[4][1],
        updated[5][1],
        updated[0][2],
        updated[1][2],
        updated[2][2],
        updated[3][2],
        updated[4][2],
        updated[5][2],
    )


VMEM_BYTES = 60 * 1024 * 1024


def positions_numpy(length, model_width):
    place = np.arange(length, dtype=np.float32)[:, None]
    index = np.arange(model_width // 2, dtype=np.float32)[None, :]
    angles = place * np.exp(index * np.float32(-2.0 * math.log(10000.0) / model_width))
    return np.concatenate([np.sin(angles), np.cos(angles)], axis=1).astype(np.float32)


def hits_kernel(rows, span, ids_ref, list_ref):
    def one(step, found):
        for inner in range(8):
            slot = step * 8 + inner
            row = ids_ref[slot]
            list_ref[found] = row * span + slot
            found = found + jnp.where((row >= 0) & (row < rows), 1, 0)
        return found

    list_ref[list_ref.shape[0] - 1] = lax.fori_loop(0, ids_ref.shape[0] // 8, one, 0)


def list_hits(local_ids, rows, span):
    return pl.pallas_call(
        partial(hits_kernel, rows, span),
        out_shape=jax.ShapeDtypeStruct((span,), jnp.int32),
        in_specs=[pl.BlockSpec(memory_space=pltpu.SMEM)],
        out_specs=pl.BlockSpec(memory_space=pltpu.SMEM),
        name="list_hits",
    )(local_ids)


def over_hits(lists_ref, visit):
    groups, span = lists_ref.shape
    for group in range(groups):

        def one(step, carry):
            entry = lists_ref[group, step]
            visit(group, entry // span, lax.rem(entry, span))
            return carry

        lax.fori_loop(0, lists_ref[group, span - 1], one, 0)


def pick_kernel(lists_ref, table_ref, out_ref, across_ref, piece_ref, wide_ref, turned_ref):
    tokens = wide_ref.shape[0] // lists_ref.shape[0]
    width, rows = table_ref.shape
    total = across_ref.shape[1]
    wide_ref[...] = jnp.zeros_like(wide_ref)
    step = 1024
    for low in range(0, total, step):
        high = max(min(low + step, rows), low)
        if high > low:
            across_ref[:, low:high] = lowered(table_ref[:, low:high])
        if high < low + step:
            across_ref[:, high : low + step] = jnp.zeros((width, low + step - high), jnp.bfloat16)

    groups, _, columns = piece_ref.shape
    for group in range(groups):
        start = group * (total // groups)
        piece_ref[group] = across_ref[:, start : start + columns]

    def turn(piece, carry):
        for part in range(8):
            start = pl.multiple_of(piece * step + part * 128, 128)
            block = across_ref[:, pl.ds(start, 128)].astype(jnp.float32)
            turned_ref[pl.ds(start, 128), :] = jnp.transpose(block)
        return carry

    lax.fori_loop(0, total // step, turn, 0)

    def visit(group, row, slot):
        wide_ref[pl.ds(group * tokens + slot, 1), :] = turned_ref[pl.ds(row, 1), :]

    over_hits(lists_ref, visit)
    out_ref[...] = wide_ref[...].astype(jnp.bfloat16)


def pick_rows(lists, count, table, total, columns):
    width = table.shape[0]
    return pl.pallas_call(
        pick_kernel,
        out_shape=(
            jax.ShapeDtypeStruct((count, width), jnp.bfloat16),
            jax.ShapeDtypeStruct((width, total), jnp.bfloat16),
            jax.ShapeDtypeStruct((lists.shape[0], width, columns), jnp.bfloat16),
        ),
        in_specs=[
            pl.BlockSpec(memory_space=pltpu.SMEM),
            pl.BlockSpec(memory_space=pltpu.VMEM),
        ],
        out_specs=(
            pl.BlockSpec(memory_space=pltpu.VMEM),
            pl.BlockSpec(memory_space=pltpu.VMEM),
            pl.BlockSpec(memory_space=pltpu.VMEM),
        ),
        scratch_shapes=[
            pltpu.VMEM((count, width), jnp.float32),
            pltpu.VMEM((total, width), jnp.float32),
        ],
        compiler_params=pltpu.CompilerParams(vmem_limit_bytes=VMEM_BYTES),
        name="pick_rows",
    )(lists, table)


def spread_kernel(
    lists_ref, grads_ref, zero_ref, one_ref, out_ref, squares_ref, wide_ref, rows_ref
):
    shares, groups, _, width = grads_ref.shape
    tokens = rows_ref.shape[0] // groups
    quarter = tokens // shares
    chunks = zero_ref.shape[0]
    parts = [(ref, low) for ref in (zero_ref, one_ref) for low in range(0, ref.shape[2], 128)]
    chunk = 128 * len(parts)
    for index in range(shares):
        for number in range(groups):
            start = number * tokens + index * quarter
            rows_ref[start : start + quarter, :] = grads_ref[index, number, 0:quarter].astype(jnp.float32)
    wide_ref[...] = jnp.zeros_like(wide_ref)

    def visit(group, row, slot):
        wide_ref[pl.ds(row, 1), 0:width] += rows_ref[pl.ds(group * tokens + slot, 1), :]

    over_hits(lists_ref, visit)

    def turn(piece, total):
        for part, (head_ref, column) in enumerate(parts):
            start = pl.multiple_of(piece * chunk + part * 128, 128)
            block = jnp.transpose(wide_ref[pl.ds(start, 128), :])[:width]
            block = block + head_ref[piece, :, column : column + 128].astype(jnp.float32)
            out_ref[:, pl.ds(start, 128)] = lowered(block)
            total = total + block * block
        return total

    total = lax.fori_loop(0, chunks, turn, jnp.zeros((width, 128), jnp.float32))
    squares_ref[...] = jnp.sum(total, axis=0, keepdims=True)


def spread_rows(lists, count, grads, head):
    chunks, width, _ = head[0].shape
    chunk = sum(member.shape[2] for member in head)
    return pl.pallas_call(
        spread_kernel,
        out_shape=(
            jax.ShapeDtypeStruct((width, chunks * chunk), jnp.bfloat16),
            jax.ShapeDtypeStruct((1, 128), jnp.float32),
        ),
        in_specs=[pl.BlockSpec(memory_space=pltpu.SMEM)]
        + [pl.BlockSpec(memory_space=pltpu.VMEM)] * 3,
        out_specs=(
            pl.BlockSpec(memory_space=pltpu.VMEM),
            pl.BlockSpec(memory_space=pltpu.VMEM),
        ),
        scratch_shapes=[
            pltpu.VMEM((chunks * chunk, 128), jnp.float32),
            pltpu.VMEM((count, width), jnp.float32),
        ],
        compiler_params=pltpu.CompilerParams(vmem_limit_bytes=VMEM_BYTES),
        name="spread_rows",
    )(lists, grads, *head)


MESH = pl.DeviceIdType.MESH


def meet(devices):
    barrier = pltpu.get_barrier_semaphore()
    for device in devices:
        pl.semaphore_signal(barrier, inc=1, device_id=device, device_id_type=MESH)
    pl.semaphore_wait(barrier, len(devices))


def send(source, target, send_sem, recv_sem, device):
    copy = pltpu.make_async_remote_copy(
        src_ref=source,
        dst_ref=target,
        send_sem=send_sem,
        recv_sem=recv_sem,
        device_id=device,
        device_id_type=MESH,
    )
    copy.start()
    return copy


def places():
    group, share = lax.axis_index("dp"), lax.axis_index("vocab")
    core = lax.rem(share, 2)
    core_peer = (group, share + 1 - 2 * core)
    side_peer = (group, lax.rem(share + 2, 4))
    return group, share, core, core_peer, side_peer


def group_peers(group, share, groups):
    return [(lax.rem(group + step, groups), share) for step in range(1, groups)]


def share_peers(group, share, shares):
    return [(group, lax.rem(share + step, shares)) for step in range(1, shares)]


def total_scratch(rows, width):
    half = rows // 2
    return [
        pltpu.VMEM((rows, width), jnp.float32),
        pltpu.VMEM((4, half, width), jnp.bfloat16),
        pltpu.VMEM((rows, width), jnp.bfloat16),
        pltpu.SemaphoreType.DMA((6,)),
    ]


class Total:
    def __init__(self, refs):
        self.part, self.bufs, self.total, self.sems = refs
        _, _, core, self.core_peer, self.side_peer = places()
        half = self.part.shape[0] // 2
        self.mine = pl.ds(pl.multiple_of(core * half, half), half)
        self.other = pl.ds(pl.multiple_of((1 - core) * half, half), half)

    def begin(self, partial_rows):
        self.part[...] = partial_rows
        self.bufs[0] = lowered(self.part[self.other, :])
        self.one = send(
            self.bufs.at[0], self.bufs.at[1], self.sems.at[0], self.sems.at[1], self.core_peer
        )

    def middle(self):
        self.one.wait_recv()
        self.bufs[2] = lowered(self.part[self.mine, :] + self.bufs[1].astype(jnp.float32))
        self.two = send(
            self.bufs.at[2], self.bufs.at[3], self.sems.at[2], self.sems.at[3], self.side_peer
        )

    def last(self):
        self.two.wait_recv()
        self.total[self.mine, :] = lowered(
            self.bufs[2].astype(jnp.float32) + self.bufs[3].astype(jnp.float32)
        )
        piece = self.total.at[self.mine, :]
        self.three = send(piece, piece, self.sems.at[4], self.sems.at[5], self.core_peer)

    def finish(self):
        self.three.wait()
        self.one.wait_send()
        self.two.wait_send()
        return self.total[...].astype(jnp.float32)

    def rest(self):
        self.middle()
        self.last()
        return self.finish()


class Exchange:
    def __init__(self, block_of, target_ref, sems, groups):
        group, share = lax.axis_index("dp"), lax.axis_index("vocab")
        self.copies = [
            send(
                block_of(peer[0]), target_ref.at[group], sems.at[0, step], sems.at[1, step], peer
            )
            for step, peer in enumerate(group_peers(group, share, groups))
        ]
        self.keep = pltpu.make_async_copy(
            block_of(group), target_ref.at[group], sems.at[0, groups - 1]
        )
        self.keep.start()

    def finish(self):
        self.keep.wait()
        for copy in self.copies:
            copy.wait()


def head_blocks(source_ref, start, columns):
    return lambda group: source_ref.at[group, :, pl.ds(start, columns)]


def table_blocks(source_ref, chunk, start, columns):
    return lambda group: source_ref.at[:, pl.ds(pl.multiple_of(group * chunk + start, 128), columns)]


def pair_of(group, share):
    place = lax.rem(group, 2)
    return (group + 1 - 2 * place, share), place


def line_places(group):
    pair, place = group // 2, lax.rem(group, 2)
    high, low = pair // 2, lax.rem(pair, 2)
    far = ((1 - high) * 2 + low) * 2 + place
    near = (high * 2 + 1 - low) * 2 + place
    return high, low, far, near


def line_scratch(width, columns):
    return [
        pltpu.VMEM((2, 2, width, columns), jnp.bfloat16),
        pltpu.VMEM((2, width, columns), jnp.bfloat16),
        pltpu.VMEM((width, columns), jnp.bfloat16),
        pltpu.SemaphoreType.DMA((6,)),
    ]


class Owned:
    def __init__(self, blocks, refs):
        group, self.share = lax.axis_index("dp"), lax.axis_index("vocab")
        self.high, self.low, self.far, self.near = line_places(group)
        self.pair, self.place = pair_of(group, self.share)
        self.blocks = blocks
        self.pair_in, self.near_in, self.far_in, self.sems = refs

    def begin(self):
        source = self.blocks.at[:, :, 1 - self.place]
        self.zero = send(source, self.pair_in, self.sems.at[0], self.sems.at[1], self.pair)

    def beside(self):
        self.zero.wait()
        self.blocks[:, :, self.place] = lowered(
            self.blocks[:, :, self.place].astype(jnp.float32) + self.pair_in[...].astype(jnp.float32)
        )
        self.one = send(
            self.blocks.at[:, 1 - self.low, self.place],
            self.near_in,
            self.sems.at[2],
            self.sems.at[3],
            (self.near, self.share),
        )

    def beyond(self):
        self.one.wait()
        self.blocks[:, self.low, self.place] = lowered(
            self.blocks[:, self.low, self.place].astype(jnp.float32)
            + self.near_in[...].astype(jnp.float32)
        )
        self.two = send(
            self.blocks.at[1 - self.high, self.low, self.place],
            self.far_in,
            self.sems.at[4],
            self.sems.at[5],
            (self.far, self.share),
        )

    def finish(self):
        self.two.wait()
        return lowered(
            self.blocks[self.high, self.low, self.place].astype(jnp.float32)
            + self.far_in[...].astype(jnp.float32)
        )


class Rows:
    def __init__(self, value_ref, send_ref, recv_ref, sems):
        group, share = lax.axis_index("dp"), lax.axis_index("vocab")
        self.recv = recv_ref
        shares, _, own = send_ref.shape
        for piece in range(shares):
            send_ref[piece] = value_ref[:, piece * own : (piece + 1) * own]
        self.copies = [
            send(send_ref.at[peer[1]], recv_ref.at[share], sems.at[0, step], sems.at[1, step], peer)
            for step, peer in enumerate(share_peers(group, share, shares))
        ]
        keep = pltpu.make_async_copy(send_ref.at[share], recv_ref.at[share], sems.at[0, shares - 1])
        keep.start()
        self.copies.append(keep)

    def put(self, grads_ref, start):
        for copy in self.copies:
            copy.wait()
        shares, _, own = self.recv.shape
        part = grads_ref.shape[3]
        for piece in range(shares):
            for half in range(2):
                grads_ref[piece // 2, piece % 2, half, :, start : start + own] = self.recv[
                    piece, half * part : (half + 1) * part
                ]


class Late:
    def __init__(self, source, buffer, sem):
        self.copy, self.buffer, self.waiting = pltpu.make_async_copy(source, buffer, sem), buffer, True
        self.copy.start()

    def __call__(self):
        if self.waiting:
            self.copy.wait()
            self.waiting = False
        return self.buffer


class ShareGather:
    def __init__(self, target_ref, sems):
        _, self.share, _, self.core_peer, self.side_peer = places()
        self.target, self.sems = target_ref, sems
        block = target_ref.at[self.share]
        self.one = send(block, block, sems.at[0, 0], sems.at[1, 0], self.side_peer)

    def middle(self):
        self.one.wait()
        both = [self.target.at[index] for index in (self.share, self.side_peer[1])]
        self.two = [
            send(block, block, self.sems.at[0, 1 + step], self.sems.at[1, 1 + step], self.core_peer)
            for step, block in enumerate(both)
        ]

    def finish(self):
        for copy in self.two:
            copy.wait()


def in_vmem(count, at_rest=()):
    return [
        pl.BlockSpec(memory_space=pl.ANY if index in at_rest else pltpu.VMEM)
        for index in range(count)
    ]


def call(kernel, name, number, inputs, out_shape, scratch, flops, rest_in=(), rest_out=()):
    moved = sum(math.prod(member.shape) * member.dtype.itemsize for member in (*inputs, *out_shape))
    return pl.pallas_call(
        kernel,
        out_shape=tuple(out_shape),
        in_specs=in_vmem(len(inputs), rest_in),
        out_specs=tuple(in_vmem(len(out_shape), rest_out)),
        scratch_shapes=scratch,
        compiler_params=pltpu.CompilerParams(
            collective_id=number, has_side_effects=True, vmem_limit_bytes=VMEM_BYTES
        ),
        cost_estimate=pl.CostEstimate(flops=flops, bytes_accessed=moved, transcendentals=0),
        name=name,
    )(*inputs)


def shape_of(shape, dtype):
    return jax.ShapeDtypeStruct(shape, dtype)


def head_slice(ref, start, index):
    low = start + index * HEAD_DIM
    return ref[:, low : low + HEAD_DIM]


def masked_scores(query, key, causal):
    scores = times_transposed(query, key) * HEAD_DIM ** (-0.5)
    if causal:
        down = lax.broadcasted_iota(jnp.int32, scores.shape, 0)
        across = lax.broadcasted_iota(jnp.int32, scores.shape, 1)
        scores = jnp.where(down >= across, scores, -1e30)
    return scores


def heads_forward(q_ref, kv_ref, starts, context_ref, logs_ref, causal):
    q_start, k_start, v_start = starts
    for index in range(context_ref.shape[1] // HEAD_DIM):
        query = head_slice(q_ref, q_start, index)
        key = head_slice(kv_ref, k_start, index)
        value = head_slice(kv_ref, v_start, index)
        scores = masked_scores(query, key, causal)
        row_top = jnp.max(scores, axis=-1, keepdims=True)
        exponent = jnp.exp(scores - row_top)
        row_total = jnp.sum(exponent, axis=-1, keepdims=True)
        context = lowered(matmul(lowered(exponent / row_total), value))
        context_ref[:, index * HEAD_DIM : (index + 1) * HEAD_DIM] = context
        logs_ref[:, index : index + 1] = row_top + jnp.log(row_total)


def heads_backward(q_ref, kv_ref, starts, logs_ref, grad_ref, gq_ref, gkv_ref, g_starts, causal):
    q_start, k_start, v_start = starts
    gq_start, gk_start, gv_start = g_starts
    scale = HEAD_DIM ** (-0.5)
    for index in range(grad_ref.shape[1] // HEAD_DIM):
        low, high = index * HEAD_DIM, (index + 1) * HEAD_DIM
        query = head_slice(q_ref, q_start, index)
        key = head_slice(kv_ref, k_start, index)
        value = head_slice(kv_ref, v_start, index)
        grad = grad_ref[:, low:high]
        softmax_out = jnp.exp(
            masked_scores(query, key, causal) - logs_ref[:, index : index + 1]
        )
        gkv_ref[:, gv_start + low : gv_start + high] = lowered(
            contract_rows(lowered(softmax_out), grad)
        )
        grad_softmax = times_transposed(grad, value)
        inner = jnp.sum(grad_softmax * softmax_out, axis=-1, keepdims=True)
        grad_scores = lowered(softmax_out * (grad_softmax - inner))
        gq_ref[:, gq_start + low : gq_start + high] = lowered(matmul(grad_scores, key) * scale)
        gkv_ref[:, gk_start + low : gk_start + high] = lowered(
            contract_rows(grad_scores, query) * scale
        )


def norm_backward(grad_out, saved_parts, gain_row):
    normed, scale_inv = saved_parts
    grad_normed = grad_out * gain_row
    grad_in = scale_inv * (
        grad_normed
        - jnp.mean(grad_normed, axis=-1, keepdims=True)
        - normed * jnp.mean(grad_normed * normed, axis=-1, keepdims=True)
    )
    return (
        grad_in,
        jnp.sum(grad_out * normed, axis=0, keepdims=True),
        jnp.sum(grad_out, axis=0, keepdims=True),
    )


def gain_of(norms_ref, row):
    return norms_ref[row : row + 1, :], norms_ref[row + 7 : row + 8, :]


def stream_of(looked_ref, start, place_ref):
    rows, width = place_ref.shape
    looked = looked_ref[start : start + rows, :].astype(jnp.float32)
    return looked * math.sqrt(width) + place_ref[...]


def forward_kernel(groups, shares, base, cuts, refs_in, refs_out, *refs):
    inputs, outputs, scratch = refs[:refs_in], refs[refs_in : refs_in + refs_out], refs[refs_in + refs_out :]
    looked_ref, place_enc_ref, place_dec_ref, w_early_hbm, across_ref = inputs
    (
        table_ref, out_rows_ref, norms_ref,
        qkv_enc_ref, context_enc_ref, logs_enc_ref, stream_enc_hbm, pre_enc_hbm, stream_two_hbm, memory_ref,
        qkv_dec_ref, context_dec_ref, logs_dec_ref, stream_dec_ref,
    ) = outputs
    (
        table_sems, out_sems, load_sems, w_first_ref, w_enc_ref, stream_enc_ref, pre_enc_ref, stream_two_ref,
        blocks_ref, block_sems, local_sem,
    ) = scratch[:11]
    rest = scratch[11:]
    small_one, large_one = rest[:4], rest[4:8]
    large_two = large_one[:1] + rest[8:11]
    group, share, core, core_peer, side_peer = places()
    peers, far = share_peers(group, share, shares), group_peers(group, share, groups)
    first_wide = w_first_ref.shape[1]
    load_first = Late(w_early_hbm.at[:, pl.ds(0, first_wide)], w_first_ref, load_sems.at[0])
    load_enc = Late(
        w_early_hbm.at[:, pl.ds(first_wide, w_enc_ref.shape[1])], w_enc_ref, load_sems.at[1]
    )
    meet(peers + far)
    chunk = across_ref.shape[1] // groups
    starts = np.cumsum((0,) + cuts).tolist()

    def table_piece(index):
        at = pl.ds(starts[index], cuts[index])
        return Exchange(
            table_blocks(across_ref, chunk, base + starts[index], cuts[index]),
            table_ref.at[:, :, at],
            table_sems.at[index],
            groups,
        )

    outgoing = []

    def put_out(source, target):
        copy = pltpu.make_async_copy(source, target, out_sems.at[len(outgoing)])
        copy.start()
        outgoing.append(copy)

    table_zero = table_piece(0)
    load_first()

    own = qkv_enc_ref.shape[1] // 3
    rows, wide = blocks_ref.shape[1:]
    padded = first_wide - wide
    window = pl.ds(padded, wide)
    copies = []
    for step, (_, peer) in enumerate(peers):
        source = w_first_ref.at[pl.ds(pl.multiple_of(peer * rows, 64), rows), window]
        copies.append(
            send(source, blocks_ref.at[share], block_sems.at[0, step], block_sems.at[1, step], (group, peer))
        )
    keep = pltpu.make_async_copy(
        w_first_ref.at[pl.ds(pl.multiple_of(share * rows, 64), rows), window], blocks_ref.at[share], local_sem
    )
    keep.start()
    turned = jnp.transpose(w_first_ref[:, first_wide - 128 :].astype(jnp.float32))
    norms_ref[...] = turned[64:80]
    enc_total, dec_total = Total(large_one), Total(small_one)
    enc_len, dec_len = place_enc_ref.shape[0], place_dec_ref.shape[0]
    stream = stream_of(looked_ref, 0, place_enc_ref)
    normed, _ = norm_forward(stream, *gain_of(norms_ref, 0))
    qkv_enc_ref[...] = lowered(matmul(lowered(normed), w_first_ref[:, : 3 * own]))
    stream_enc_ref[...] = stream
    head_starts = (0, own, 2 * own)
    logs_enc_ref[...] = jnp.zeros_like(logs_enc_ref)
    heads_forward(qkv_enc_ref, qkv_enc_ref, head_starts, context_enc_ref, logs_enc_ref, False)
    table_one = table_piece(1)
    keep.wait()
    for copy in copies:
        copy.wait()
    for matrix in range(3):
        for piece in range(shares):
            out_rows_ref[matrix, :, piece * own : (piece + 1) * own] = blocks_ref[
                piece, :, matrix * own : (matrix + 1) * own
            ]
    enc_total.begin(matmul(context_enc_ref[...], out_rows_ref[0]))
    stream = stream_of(looked_ref, enc_len, place_dec_ref)
    stream_dec_ref[...] = stream
    normed, _ = norm_forward(stream, *gain_of(norms_ref, 3))
    enc_total.middle()
    dec_start = padded // 2
    qkv_dec_ref[...] = lowered(
        matmul(lowered(normed), w_first_ref[:, dec_start : dec_start + 3 * own])
    )
    logs_dec_ref[...] = jnp.zeros_like(logs_dec_ref)
    heads_forward(qkv_dec_ref, qkv_dec_ref, head_starts, context_dec_ref, logs_dec_ref, True)
    enc_total.last()
    dec_total.begin(matmul(context_dec_ref[...], out_rows_ref[1]))
    dec_total.middle()
    stream_enc_ref[...] += enc_total.finish()
    put_out(stream_enc_ref, stream_enc_hbm)
    dec_total.last()

    total = Total(large_two)
    normed, _ = norm_forward(stream_enc_ref[...], *gain_of(norms_ref, 1))
    hidden, width = pre_enc_ref.shape[1], stream_enc_ref.shape[1]
    load_enc()
    pre_enc_ref[...] = matmul(lowered(normed), w_enc_ref[:, :hidden])
    put_out(pre_enc_ref, pre_enc_hbm)
    activated = lowered(jax.nn.silu(pre_enc_ref[...]))
    total.begin(matmul(activated, w_enc_ref[:, hidden : hidden + width]))
    stream_dec_ref[...] += dec_total.finish()
    stream_two_ref[...] = stream_enc_ref[...] + total.rest()
    put_out(stream_two_ref, stream_two_hbm)
    memory, _ = norm_forward(stream_two_ref[...], *gain_of(norms_ref, 2))
    memory_ref[...] = lowered(memory)
    for piece in (table_zero, table_one):
        piece.finish()
    for copy in outgoing:
        copy.wait()


def dec_kernel(
    groups, start,
    stream_dec_ref, memory_ref, norms_ref, out_rows_ref, positions_ref, w_dec_hbm, across_ref,
    table_ref, q_ref, kv_ref, context_ref, logs_ref, stream_mid_ref, pre_dec_ref, stream_out_ref, selected_ref,
    w_dec_ref, load_sem, table_sems, own_ref, select_sems, *rest,
):
    small_one, small_two = rest[:4], rest[:1] + rest[4:7]
    group, share, core, core_peer, side_peer = places()
    far = group_peers(group, share, groups)
    load_dec = Late(w_dec_hbm, w_dec_ref, load_sem)
    meet([core_peer, side_peer] + far)
    chunk, columns = across_ref.shape[1] // groups, table_ref.shape[2]
    exchange = Exchange(
        table_blocks(across_ref, chunk, start, columns), table_ref, table_sems, groups
    )
    own, hidden = q_ref.shape[1], pre_dec_ref.shape[1]
    dec_len, width = stream_dec_ref.shape
    cross_total, feed_total = Total(small_two), Total(small_one)
    in_start = hidden + width
    normed, _ = norm_forward(stream_dec_ref[...], *gain_of(norms_ref, 4))
    load_dec()
    kv_ref[...] = lowered(
        matmul(memory_ref[...], w_dec_ref[:, in_start + own : in_start + 3 * own])
    )
    q_ref[...] = lowered(matmul(lowered(normed), w_dec_ref[:, in_start : in_start + own]))
    logs_ref[...] = jnp.zeros_like(logs_ref)
    heads_forward(q_ref, kv_ref, (0, 0, own), context_ref, logs_ref, False)
    cross_total.begin(matmul(context_ref[...], out_rows_ref[2]))
    stream_mid_ref[...] = stream_dec_ref[...] + cross_total.rest()
    normed, _ = norm_forward(stream_mid_ref[...], *gain_of(norms_ref, 5))
    pre_dec_ref[...] = matmul(lowered(normed), w_dec_ref[:, :hidden])
    activated = lowered(jax.nn.silu(pre_dec_ref[...]))
    feed_total.begin(matmul(activated, w_dec_ref[:, hidden:in_start]))
    stream_out_ref[...] = stream_mid_ref[...] + feed_total.rest()
    final, _ = norm_forward(stream_out_ref[...], *gain_of(norms_ref, 6))
    places_down = lax.broadcasted_iota(jnp.int32, (own_ref.shape[0], dec_len), 1)
    chosen = lowered(jnp.where(places_down == positions_ref[...], 1.0, 0.0))
    own_ref[...] = lowered(matmul(chosen, lowered(final)))
    selected_ref[group] = own_ref[...]
    copies = [
        send(own_ref, selected_ref.at[group], select_sems.at[0, step], select_sems.at[1, step], peer)
        for step, peer in enumerate(far)
    ]
    exchange.finish()
    for copy in copies:
        copy.wait()


def combine_stats(stats):
    row_max = stats[0][0:1]
    for member in stats[1:]:
        row_max = jnp.maximum(row_max, member[0:1])
    exp_total = smooth = target = 0.0
    for member in stats:
        exp_total = exp_total + member[1:2] * jnp.exp(member[0:1] - row_max)
        smooth = smooth + member[2:3]
        target = target + member[3:4]
    return row_max, exp_total, smooth, target


def head_kernel(
    groups, shares, shard_rows,
    selected_ref, zero_ref, one_ref, two_ref, targets_ref, weights_ref, counted_ref,
    loss_ref, grad_out_ref, head_ref, head_out_ref,
    head_sems, logits_ref, dz_ref, stats_ref, turned_ref, share_stats_ref, group_stats_ref, stat_sems,
    part_ref, core_ref, side_ref, group_ref, sum_ref, sems,
):
    group, share, core, core_peer, side_peer = places()
    side = share // 2
    near, far = share_peers(group, share, shares), group_peers(group, share, groups)
    meet(near + far)
    rows, width = selected_ref.shape
    chunk = logits_ref.shape[1]
    vocab_total = shard_rows * shares
    first = group * chunk
    limit = jnp.minimum(shard_rows - first, vocab_total - 1 - share * shard_rows - first)
    block = 384
    step_rows = 32

    tables = (zero_ref, one_ref, two_ref)
    starts = np.cumsum([0] + [ref.shape[1] for ref in tables]).tolist()
    for ref, start in zip(tables, starts):
        for low in range(0, ref.shape[1], block):
            logits_ref[:, start + low : start + low + block] = matmul(
                selected_ref[...], ref[:, low : low + block]
            )
    stats_ref[...] = jnp.zeros_like(stats_ref)

    def gather_stats(step, carry):
        at = pl.ds(pl.multiple_of(step * step_rows, step_rows), step_rows)
        logits = logits_ref[at, :]
        column = lax.broadcasted_iota(jnp.int32, logits.shape, 1)
        real = column < limit
        masked = jnp.where(real, logits, -1e30)
        top = jnp.max(masked, axis=1, keepdims=True)
        stats_ref[at, 0:1] = top
        stats_ref[at, 1:2] = jnp.sum(jnp.exp(masked - top), axis=1, keepdims=True)
        stats_ref[at, 2:3] = jnp.sum(jnp.where(real, logits, 0.0), axis=1, keepdims=True)
        hit = column == targets_ref[at, :]
        stats_ref[at, 3:4] = jnp.sum(jnp.where(hit, logits, 0.0), axis=1, keepdims=True)
        return carry

    lax.fori_loop(0, rows // step_rows, gather_stats, 0)
    share_stats_ref[share] = jnp.transpose(stats_ref[...])[0:8]
    copies = [
        send(share_stats_ref.at[share], share_stats_ref.at[share], stat_sems.at[0, step], stat_sems.at[1, step], peer)
        for step, peer in enumerate(near)
    ]
    for copy in copies:
        copy.wait()
    merged = combine_stats([share_stats_ref[index] for index in range(shares)])
    group_stats_ref[group] = jnp.concatenate(merged + (jnp.zeros((4, rows), jnp.float32),), axis=0)
    copies = [
        send(group_stats_ref.at[group], group_stats_ref.at[group], stat_sems.at[2, step], stat_sems.at[3, step], peer)
        for step, peer in enumerate(far)
    ]
    for copy in copies:
        copy.wait()
    row_max, exp_total, smooth, target = combine_stats(
        [group_stats_ref[index] for index in range(groups)]
    )
    log_total = row_max + jnp.log(exp_total)
    per_row = log_total - (1.0 - SMOOTH) * target - SMOOTH * smooth / (vocab_total - 1)
    loss = jnp.sum(counted_ref[...] * per_row, axis=1, keepdims=True)
    loss_ref[...] = jnp.broadcast_to(loss, loss_ref.shape)
    turned_ref[...] = jnp.zeros_like(turned_ref)
    turned_ref[0:1, :] = log_total
    stats_ref[...] = jnp.transpose(turned_ref[...])

    def make_dz(step, carry):
        at = pl.ds(pl.multiple_of(step * step_rows, step_rows), step_rows)
        logits = logits_ref[at, :]
        column = lax.broadcasted_iota(jnp.int32, logits.shape, 1)
        softmax_rows = jnp.exp(logits - stats_ref[at, 0:1])
        hit = jnp.where(column == targets_ref[at, :], 1.0 - SMOOTH, 0.0)
        grad = weights_ref[at, :] * (softmax_rows - hit - SMOOTH / (vocab_total - 1))
        dz_ref[at, :] = lowered(jnp.where(column < limit, grad, 0.0))
        return carry

    lax.fori_loop(0, rows // step_rows, make_dz, 0)
    loss_rows = rows // groups
    half, quarter = loss_rows // 2, loss_rows // 4

    def head_part(index):
        at = slice(index * block, (index + 1) * block)
        head_ref[:, at] = lowered(contract_rows(selected_ref[...], dz_ref[:, at]))

    early = head_out_ref.shape[2] // block
    for index in range(early):
        head_part(index)
    width_out = width // groups
    exchange = Exchange(
        lambda index: head_ref.at[
            pl.ds(pl.multiple_of(index * width_out, 16), width_out), pl.ds(0, early * block)
        ],
        head_out_ref,
        head_sems,
        groups,
    )
    grad_rows = 0.0
    for ref, start in zip(tables, starts):
        grad_rows = grad_rows + times_transposed(dz_ref[:, start : start + ref.shape[1]], ref[...])
    part_ref[...] = lowered(grad_rows).reshape(part_ref.shape)
    mine = pl.ds(pl.multiple_of(core * half, 16), half)
    other = pl.ds(pl.multiple_of((1 - core) * half, 16), half)
    copy = send(part_ref.at[:, other, :], core_ref, sems.at[0, 0], sems.at[1, 0], core_peer)
    parts = chunk // block
    middle = (early + parts) // 2
    copy.wait()
    part_ref[:, mine, :] = lowered(
        part_ref[:, mine, :].astype(jnp.float32) + core_ref[...].astype(jnp.float32)
    )
    base = core * half
    my_quarter = pl.ds(pl.multiple_of(base + side * quarter, 16), quarter)
    other_quarter = pl.ds(pl.multiple_of(base + (1 - side) * quarter, 16), quarter)
    copy = send(part_ref.at[:, other_quarter, :], side_ref, sems.at[0, 1], sems.at[1, 1], side_peer)
    for index in range(early, middle):
        head_part(index)
    copy.wait()
    side_ref[...] = lowered(
        part_ref[:, my_quarter, :].astype(jnp.float32) + side_ref[...].astype(jnp.float32)
    )
    group_ref[group] = side_ref[group]
    copies = [
        send(side_ref.at[peer[0]], group_ref.at[group], sems.at[0, 2 + step], sems.at[1, 2 + step], peer)
        for step, peer in enumerate(far)
    ]
    for index in range(middle, parts):
        head_part(index)
    for copy in copies:
        copy.wait()
    summed = group_ref[0].astype(jnp.float32)
    for index in range(1, groups):
        summed = summed + group_ref[index].astype(jnp.float32)
    sum_ref[...] = lowered(summed)
    grad_out_ref[my_quarter, :] = sum_ref[...]
    base_sem = 1 + groups
    copies = [
        send(sum_ref, grad_out_ref.at[my_quarter, :], sems.at[0, base_sem + step], sems.at[1, base_sem + step], peer)
        for step, peer in enumerate(near)
    ]
    for copy in copies:
        copy.wait()
    exchange.finish()


def put_grads(grads_ref, start, value):
    shape = grads_ref.shape[:4] + (value.shape[1],)
    grads_ref[:, :, :, :, start : start + value.shape[1]] = lowered(value).reshape(shape)


def feed_grads(grad_ref, stream_ref, pre_ref, norms_ref, row, w_ref, grads_ref, total):
    width = stream_ref.shape[1]
    hidden = pre_ref.shape[1]
    normed, _ = norm_forward(stream_ref[...], *gain_of(norms_ref, row))
    grad_low = lowered(grad_ref[...])
    pre = pre_ref[...]
    sigmoid_pre = jax.nn.sigmoid(pre)
    grad_pre = lowered(
        times_transposed(grad_low, w_ref[:, hidden : hidden + width])
        * sigmoid_pre
        * (1.0 + pre * (1.0 - sigmoid_pre))
    )
    total.begin(times_transposed(grad_pre, w_ref[:, :hidden]))
    activated = lowered(pre * sigmoid_pre)
    put_grads(grads_ref, hidden, contract_rows(activated, grad_low))
    total.middle()
    put_grads(grads_ref, 0, contract_rows(lowered(normed), grad_pre))


def norm_step(grad_ref, stream_ref, norms_ref, row, summed, rows_ref, slot):
    gain, shift = gain_of(norms_ref, row)
    _, kept = norm_forward(stream_ref[...], gain, shift)
    grad_in, grad_gain, grad_shift = norm_backward(summed, kept, gain)
    rows_ref[slot : slot + 1, :] = grad_gain
    rows_ref[slot + 1 : slot + 2, :] = grad_shift
    if grad_ref is None:
        return grad_in
    return grad_ref[...] + grad_in


def back_kernel(
    groups, shares, first_wide, refs_in, refs_out, *refs
):
    inputs, outputs, scratch = refs[:refs_in], refs[refs_in : refs_in + refs_out], refs[refs_in + refs_out :]
    (
        grad_selected_ref, positions_ref, stream_out_ref, stream_mid_ref, pre_dec_ref, norms_ref, w_dec_hbm,
        out_rows_hbm, memory_hbm, stream_dec_hbm, q_ref, kv_ref, context_cross_ref, logs_cross_ref,
        stream_two_hbm, stream_enc_hbm, pre_enc_hbm, w_early_hbm, looked_hbm, place_enc_hbm, place_dec_ref,
        qkv_dec_ref, context_dec_ref, logs_dec_ref, qkv_enc_ref, context_enc_ref, logs_enc_ref,
        head_in_ref,
    ) = inputs
    head_out_ref, own_tokens_ref, dec_shares_ref, own_ref, squares_ref = outputs
    (
        head_sems, load_sems, w_ref, w_enc_ref, out_rows_ref, memory_ref, stream_dec_ref, stream_two_ref,
        stream_enc_ref, pre_enc_ref, looked_ref,
        dec_grads_ref, mid_grads_ref, last_grads_ref,
        grad_ref, grad_enc_ref,
        context_ref, gq_ref, gkv_ref, gqkv_ref, gqkv_enc_ref, context_enc_grad_ref,
        g_enc_ref, g_self_ref, g_cross_ref, rows_dec_ref, rows_mid_ref, rows_ref,
        norm_rows_ref, block_sems, cut_ref, token_sems, share_sems, dec_sems, dec_own_ref,
        local_sems,
    ) = scratch[:36]
    row_refs = scratch[36:42]
    rest = scratch[42:]
    stream_ref = pre_enc_ref
    small_one, large_one = rest[:4], rest[4:8]
    small_two, large_two = small_one[:1] + rest[8:11], large_one[:1] + rest[11:14]
    dec_line = Owned(dec_grads_ref, rest[14:18])
    mid_line = Owned(mid_grads_ref, rest[18:22])
    last_line = Owned(last_grads_ref, rest[22:26])
    group, share, core, core_peer, side_peer = places()
    peers = share_peers(group, share, shares)
    load_w_dec = Late(w_dec_hbm, w_ref, load_sems.at[0])
    load_rows = Late(out_rows_hbm, out_rows_ref, load_sems.at[1])
    load_memory = Late(memory_hbm, memory_ref, load_sems.at[2])
    load_dec = Late(stream_dec_hbm, stream_dec_ref, load_sems.at[3])
    load_two = Late(stream_two_hbm, stream_two_ref, load_sems.at[4])
    load_enc = Late(stream_enc_hbm, stream_enc_ref, load_sems.at[5])
    load_pre = Late(pre_enc_hbm, pre_enc_ref, load_sems.at[6])
    load_w_enc = Late(
        w_early_hbm.at[:, pl.ds(first_wide, w_enc_ref.shape[1])], w_enc_ref, load_sems.at[7]
    )
    load_looked = Late(looked_hbm, looked_ref, load_sems.at[8])
    meet(peers + group_peers(group, share, groups))
    columns = head_out_ref.shape[2]
    skipped = head_in_ref.shape[2] - columns
    cuts = (0, 3 * columns // 7, 5 * columns // 7, columns)

    def head_piece(index):
        low, wide = cuts[index], cuts[index + 1] - cuts[index]
        return Exchange(
            head_blocks(head_in_ref, skipped + low, wide),
            head_out_ref.at[:, :, pl.ds(low, wide)],
            head_sems.at[index],
            groups,
        )

    pieces = [head_piece(0)]
    width = stream_out_ref.shape[1]
    own = q_ref.shape[1]
    hidden = pre_dec_ref.shape[1]
    in_start = hidden + width
    starts = (0, own, 2 * own)
    for rows in (rows_dec_ref, rows_mid_ref, rows_ref):
        rows[...] = jnp.zeros_like(rows)

    total = Total(small_one)
    down = lax.broadcasted_iota(jnp.int32, (stream_out_ref.shape[0], grad_selected_ref.shape[0]), 0)
    chosen = lowered(jnp.where(down == positions_ref[...], 1.0, 0.0))
    grad_final = matmul(chosen, grad_selected_ref[...])
    grad_ref[...] = norm_step(None, stream_out_ref, norms_ref, 6, grad_final, rows_dec_ref, 0)
    load_w_dec()
    feed_grads(grad_ref, stream_mid_ref, pre_dec_ref, norms_ref, 5, w_ref, dec_grads_ref, total)
    total.last()
    grad_ref[...] = norm_step(
        grad_ref, stream_mid_ref, norms_ref, 5, total.finish(), rows_dec_ref, 2
    )

    cross_total, memory_total = Total(small_two), Total(large_one)
    grad_low = lowered(grad_ref[...])
    load_rows()
    context_ref[...] = lowered(times_transposed(grad_low, out_rows_ref[2]))
    heads_backward(
        q_ref, kv_ref, (0, 0, own), logs_cross_ref, context_ref, gq_ref, gkv_ref, (0, 0, own), False
    )
    memory_total.begin(
        times_transposed(gkv_ref[...], w_ref[:, in_start + own : in_start + 3 * own])
    )
    cross_total.begin(times_transposed(gq_ref[...], w_ref[:, in_start : in_start + own]))
    load_w_first = Late(
        w_early_hbm.at[:, pl.ds(0, first_wide)], w_ref.at[:, pl.ds(0, first_wide)], load_sems.at[9]
    )
    g_cross_ref[...] = lowered(contract_rows(context_cross_ref[...], grad_low))
    cross_rows = Rows(g_cross_ref, row_refs[0], row_refs[1], block_sems.at[0])
    memory_total.middle()
    cross_total.middle()
    load_dec()
    load_memory()
    normed, _ = norm_forward(stream_dec_ref[...], *gain_of(norms_ref, 4))
    put_grads(dec_grads_ref, in_start, contract_rows(lowered(normed), gq_ref[...]))
    put_grads(dec_grads_ref, in_start + own, contract_rows(memory_ref[...], gkv_ref[...]))
    cross_rows.put(dec_grads_ref, in_start + 3 * own)
    dec_line.begin()
    pieces.append(head_piece(1))
    memory_total.last()
    cross_total.last()
    summed = memory_total.finish()
    load_two()
    grad_enc_ref[...] = norm_step(None, stream_two_ref, norms_ref, 2, summed, rows_mid_ref, 0)
    load_place = Late(place_enc_hbm, stream_two_ref, load_sems.at[10])
    grad_ref[...] = norm_step(
        grad_ref, stream_dec_ref, norms_ref, 4, cross_total.finish(), rows_dec_ref, 4
    )

    feed_total, self_total = Total(large_two), Total(small_one)
    load_enc()
    load_pre()
    load_w_enc()
    feed_grads(
        grad_enc_ref, stream_enc_ref, pre_enc_ref, norms_ref, 1, w_enc_ref, mid_grads_ref, feed_total
    )
    grad_low = lowered(grad_ref[...])
    context_ref[...] = lowered(times_transposed(grad_low, out_rows_ref[1]))
    feed_total.last()
    heads_backward(
        qkv_dec_ref, qkv_dec_ref, starts, logs_dec_ref, context_ref, gqkv_ref, gqkv_ref, starts, True
    )
    load_w_first()
    w_start = first_wide // 3
    self_total.begin(times_transposed(gqkv_ref[...], w_ref[:, w_start : w_start + 3 * own]))
    g_self_ref[...] = lowered(contract_rows(context_dec_ref[...], grad_low))
    self_rows = Rows(g_self_ref, row_refs[2], row_refs[3], block_sems.at[1])
    self_total.middle()
    load_looked()
    enc_len = stream_enc_ref.shape[0]
    stream_dec_ref[...] = stream_of(looked_ref, enc_len, place_dec_ref)
    normed, _ = norm_forward(stream_dec_ref[...], *gain_of(norms_ref, 3))
    put_grads(mid_grads_ref, in_start, contract_rows(lowered(normed), gqkv_ref[...]))
    self_rows.put(mid_grads_ref, in_start + 3 * own)
    mid_line.begin()
    pieces.append(head_piece(2))
    grad_enc_ref[...] = norm_step(
        grad_enc_ref, stream_enc_ref, norms_ref, 1, feed_total.finish(), rows_mid_ref, 2
    )
    self_total.last()
    tokens, part = looked_ref.shape[0], cut_ref.shape[2]
    quarter = tokens // shares
    block_rows = cut_ref.shape[1] // shares

    def put_tokens(first, rows):
        for index in range(groups):
            for piece in range(shares):
                low, high = max(first, piece * quarter), min(first + rows.shape[0], (piece + 1) * quarter)
                if low < high:
                    to = piece * block_rows - piece * quarter
                    cut_ref[index, to + low : to + high] = rows[
                        low - first : high - first, index * part : (index + 1) * part
                    ]

    grad_dec = norm_step(
        grad_ref, stream_dec_ref, norms_ref, 3, self_total.finish(), rows_mid_ref, 4
    )
    put_tokens(enc_len, lowered(grad_dec * math.sqrt(width)))

    total = Total(large_one)
    grad_low = lowered(grad_enc_ref[...])
    g_enc_ref[...] = lowered(contract_rows(context_enc_ref[...], grad_low))
    enc_rows = Rows(g_enc_ref, row_refs[4], row_refs[5], block_sems.at[2])
    context_enc_grad_ref[...] = lowered(times_transposed(grad_low, out_rows_ref[0]))
    heads_backward(
        qkv_enc_ref, qkv_enc_ref, starts, logs_enc_ref, context_enc_grad_ref, gqkv_enc_ref, gqkv_enc_ref, starts,
        False,
    )
    total.begin(times_transposed(gqkv_enc_ref[...], w_ref[:, : 3 * own]))
    load_place()
    stream_ref[...] = stream_of(looked_ref, 0, stream_two_ref)
    normed, _ = norm_forward(stream_ref[...], *gain_of(norms_ref, 0))
    total.middle()
    put_grads(last_grads_ref, 0, contract_rows(lowered(normed), gqkv_enc_ref[...]))
    enc_rows.put(last_grads_ref, 3 * own)
    last_line.begin()
    dec_line.beside()
    total.last()
    grad_enc = norm_step(grad_enc_ref, stream_ref, norms_ref, 0, total.finish(), rows_ref, 0)
    put_tokens(0, lowered(grad_enc * math.sqrt(width)))
    norm_rows_ref[...] = jnp.zeros_like(norm_rows_ref)
    order = (
        (0, rows_ref, 0),
        (1, rows_mid_ref, 2),
        (2, rows_mid_ref, 0),
        (3, rows_mid_ref, 4),
        (4, rows_dec_ref, 4),
        (5, rows_dec_ref, 2),
        (6, rows_dec_ref, 0),
    )
    for row, source, slot in order:
        norm_rows_ref[row : row + 1, :] = source[slot : slot + 1, :]
        norm_rows_ref[7 + row : 8 + row, :] = source[slot + 1 : slot + 2, :]
    norm_low = lowered(norm_rows_ref[...])
    for index in range(groups):
        for piece in range(shares):
            cut_ref[index, piece * block_rows + quarter : (piece + 1) * block_rows] = norm_low[
                :, index * part : (index + 1) * part
            ]
    own_rows = pl.ds(pl.multiple_of(share * block_rows, 16), block_rows)
    to_groups = Exchange(
        lambda index: cut_ref.at[index, own_rows, :], own_tokens_ref.at[share], token_sems, groups
    )
    mid_line.beside()
    dec_line.beyond()
    to_groups.finish()
    token_gather = ShareGather(own_tokens_ref, share_sems)
    last_line.beside()
    mid_line.beyond()
    dec_own_ref[...] = dec_line.finish()
    keep = pltpu.make_async_copy(dec_own_ref, dec_shares_ref.at[share], local_sems.at[2])
    keep.start()
    keep.wait()
    dec_gather = ShareGather(dec_shares_ref, dec_sems)
    token_gather.middle()
    last_line.beyond()
    middle = mid_grads_ref.shape[4]
    own_ref[:, :middle] = mid_line.finish()
    dec_gather.middle()
    token_gather.finish()
    own_ref[:, middle:] = last_line.finish()
    squares = 0.0
    for ref in (dec_own_ref, own_ref):
        value = ref[...].astype(jnp.float32)
        value = value * value
        squares = squares + jnp.sum(jnp.sum(value, axis=0, keepdims=True), axis=1, keepdims=True)
    lane = lax.broadcasted_iota(jnp.int32, squares_ref.shape, 1)
    squares_ref[...] = jnp.where(lane == 0, squares, 0.0)
    dec_gather.finish()
    for piece in pieces:
        piece.finish()


def look_kernel(
    groups,
    picked_ref, piece_ref,
    looked_ref, table_ref,
    send_ref, core_ref, side_ref, group_ref, sems, table_sems,
):
    group, share, core, core_peer, side_peer = places()
    side = share // 2
    far = group_peers(group, share, groups)
    meet([core_peer, side_peer] + far)
    _, tokens, width = picked_ref.shape
    half, quarter = tokens // 2, tokens // 4
    mine = pl.ds(pl.multiple_of(core * half, 16), half)
    other = pl.ds(pl.multiple_of((1 - core) * half, 16), half)
    send(picked_ref.at[:, other, :], core_ref, sems.at[0, 0], sems.at[1, 0], core_peer).wait()
    core_ref[...] = core_ref[...] + picked_ref[:, mine, :]
    own_quarter = pl.ds(pl.multiple_of(side * quarter, 16), quarter)
    other_quarter = pl.ds(pl.multiple_of((1 - side) * quarter, 16), quarter)
    send(core_ref.at[:, other_quarter, :], side_ref, sems.at[0, 1], sems.at[1, 1], side_peer).wait()
    side_ref[...] = side_ref[...] + core_ref[:, own_quarter, :]
    group_ref[group] = side_ref[group]
    copies = [
        send(side_ref.at[peer[0]], group_ref.at[group], sems.at[0, 2 + step], sems.at[1, 2 + step], peer)
        for step, peer in enumerate(far)
    ]
    exchange = Exchange(lambda index: piece_ref.at[index], table_ref, table_sems, groups)
    for copy in copies:
        copy.wait()
    for index in range(groups):
        send_ref[:, index * width : (index + 1) * width] = group_ref[index]
    at = pl.ds(pl.multiple_of(core * half + side * quarter, 16), quarter)
    looked_ref[at, :] = send_ref[...]
    end = 1 + groups
    send(send_ref, looked_ref.at[at, :], sems.at[0, end], sems.at[1, end], side_peer).wait()
    end = end + 1
    both = looked_ref.at[mine, :]
    send(both, both, sems.at[0, end], sems.at[1, end], core_peer).wait()
    exchange.finish()


def squares_kernel(
    groups, shares,
    embedding_ref, dense_ref,
    out_ref,
    share_ref, group_ref, sems,
):
    group, share, _, _, _ = places()
    near, far = share_peers(group, share, shares), group_peers(group, share, groups)
    meet(near + far)
    down = lax.broadcasted_iota(jnp.int32, (8, 128), 0)
    share_ref[share] = jnp.where(down == 0, embedding_ref[...] + dense_ref[...], 0.0)
    copies = [
        send(share_ref.at[share], share_ref.at[share], sems.at[0, step], sems.at[1, step], peer)
        for step, peer in enumerate(near)
    ]
    for copy in copies:
        copy.wait()
    summed = share_ref[0]
    for index in range(1, shares):
        summed = summed + share_ref[index]
    group_ref[group] = summed
    copies = [
        send(group_ref.at[group], group_ref.at[group], sems.at[2, step], sems.at[3, step], peer)
        for step, peer in enumerate(far)
    ]
    for copy in copies:
        copy.wait()
    summed = group_ref[0]
    for index in range(1, groups):
        summed = summed + group_ref[index]
    out_ref[...] = jnp.broadcast_to(jnp.sum(summed), out_ref.shape)


def dense_kernel(
    rate, place_grads, factor_ref, *refs
):
    *grad_refs, w_ref, first_ref, second_ref, new_w_ref, new_first_ref, new_second_ref, wide_ref = refs
    place_grads(wide_ref, *grad_refs)
    updated = adam_update(
        w_ref[0],
        first_ref[0],
        second_ref[0],
        wide_ref[...].astype(jnp.float32),
        factor_ref[0],
        rate,
    )
    for out, value in zip((new_w_ref, new_first_ref, new_second_ref), updated):
        out[0] = value


def dense_update(name, rate, place_grads, factor, grads, w, first, second, parts, cut=None):
    matrices, rows, columns = w.shape
    rows = rows // parts
    own = pl.BlockSpec((1, rows, columns), lambda matrix, part: (matrix, part, 0))
    shares, width = grads[0].shape[:2]
    grad_specs = [
        pl.BlockSpec(
            (shares, width, cut[0] if cut else member.shape[2]),
            lambda matrix, part: (0, 0, cut[1] if cut else 0),
        )
        for member in grads
    ]
    return pl.pallas_call(
        partial(dense_kernel, rate, place_grads),
        grid=(matrices, parts),
        out_shape=[jax.ShapeDtypeStruct(w.shape, w.dtype)] * 3,
        in_specs=[pl.BlockSpec(memory_space=pltpu.SMEM)] + grad_specs + [own] * 3,
        out_specs=[own] * 3,
        scratch_shapes=[pltpu.VMEM((rows, columns), jnp.bfloat16)],
        compiler_params=pltpu.CompilerParams(vmem_limit_bytes=VMEM_BYTES),
        name=name,
    )(factor, *grads, w, first, second)


def place_columns(groups, matrix, source_ref, start):
    def place(wide_ref):
        @pl.when(pl.program_id(0) == matrix)
        def _():
            rows, columns = wide_ref.shape
            shares = source_ref.shape[0]
            piece = columns // groups // shares
            at = pl.ds(pl.multiple_of(pl.program_id(1) * rows, 16), rows)
            for number in range(groups):
                for share in range(shares):
                    low = (number * shares + share) * piece
                    wide_ref[:, low : low + piece] = source_ref[
                        share, at, start + number * piece : start + (number + 1) * piece
                    ]

    return place


def cut_kernel(groups, shares, gap, in_ref, out_ref, up_ref, down_ref, norms_ref, early_ref, dec_ref, square_ref):
    share = lax.axis_index("vocab")
    width, model_width = in_ref.shape[1], out_ref.shape[2]
    own = model_width // shares
    piece = up_ref.shape[2] // groups // shares
    hidden = groups * piece
    in_wide = 3 * own + gap
    early_ref[...] = jnp.zeros_like(early_ref)
    dec_ref[...] = jnp.zeros_like(dec_ref)

    def columns(target, start, source, groups_in, size, index):
        step = shares * size
        for number in range(groups_in):
            low = number * step + index * size
            target[:, start + number * size : start + (number + 1) * size] = lowered(
                source[:, low : low + size]
            )

    def put(index):
        columns(early_ref, 0, in_ref.at[0], 3, own, index)
        columns(early_ref, in_wide, in_ref.at[1], 3, own, index)
        for matrix in range(3):
            columns(early_ref, 2 * in_wide + matrix * own, out_ref.at[matrix], 1, own, index)
        rows = slice(index * (down_ref.shape[1] // shares), (index + 1) * (down_ref.shape[1] // shares))
        for matrix, (target, start) in enumerate(((early_ref, 3 * in_wide), (dec_ref, 0))):
            columns(target, start, up_ref.at[matrix], groups, piece, index)
            start = start + hidden
            target[:, start : start + model_width] = lowered(down_ref[matrix, rows, :])
        columns(dec_ref, hidden + model_width, in_ref.at[2], 3, own, index)

    for index in range(shares):
        pl.when(share == index)(partial(put, index))
    square_ref[...] = jnp.zeros_like(square_ref)
    square_ref[0 : norms_ref.shape[0], 0:width] = norms_ref[...]
    end = 3 * in_wide
    early_ref[:, end - gap : end] = lowered(jnp.transpose(square_ref[...])[0:width, 0:gap])


def cut_weights(groups, shares, gap, inputs, early_wide, dec_wide):
    width = inputs[0].shape[1]
    return pl.pallas_call(
        partial(cut_kernel, groups, shares, gap),
        out_shape=(
            jax.ShapeDtypeStruct((width, early_wide), jnp.bfloat16),
            jax.ShapeDtypeStruct((width, dec_wide), jnp.bfloat16),
        ),
        in_specs=[pl.BlockSpec(memory_space=pltpu.VMEM)] * len(inputs),
        out_specs=(pl.BlockSpec(memory_space=pltpu.VMEM),) * 2,
        scratch_shapes=[pltpu.VMEM((128, 128), jnp.float32)],
        compiler_params=pltpu.CompilerParams(vmem_limit_bytes=VMEM_BYTES),
        name="cut_weights",
    )(*inputs)


def numbers_kernel(
    groups, numbers_ref, hits_ref, all_numbers_ref, all_hits_ref, sems, local_sems
):
    group, share, _, _, _ = places()
    peers = group_peers(group, share, groups)
    meet(peers)
    copies = []
    for number, (source, target) in enumerate(
        ((numbers_ref, all_numbers_ref), (hits_ref, all_hits_ref))
    ):
        copies += [
            send(source, target.at[group], sems.at[number, 0, step], sems.at[number, 1, step], peer)
            for step, peer in enumerate(peers)
        ]
        keep = pltpu.make_async_copy(source, target.at[group], local_sems.at[number])
        keep.start()
        copies.append(keep)
    for copy in copies:
        copy.wait()


def local(
    enc_ids,
    labels,
    target_lengths,
    loss_positions,
    embedding,
    attn_in,
    attn_out,
    ffn_up,
    ffn_down,
    norms,
    embedding_first,
    attn_in_first,
    attn_out_first,
    ffn_up_first,
    ffn_down_first,
    norms_first,
    embedding_second,
    attn_in_second,
    attn_out_second,
    ffn_up_second,
    ffn_down_second,
    norms_second,
):
    groups, shares = lax.axis_size("dp"), lax.axis_size("vocab")
    group, share = lax.axis_index("dp"), lax.axis_index("vocab")
    enc_len, dec_len = enc_ids.shape[1], labels.shape[1]
    loss_count = loss_positions.shape[1]
    shard_rows, part_width = embedding.shape
    model_width = part_width * groups
    vocab_total = shard_rows * shares
    row_start = share * shard_rows
    root_width = math.sqrt(model_width)
    tokens = enc_len + dec_len

    bf16, f32 = jnp.bfloat16, jnp.float32
    sems = pltpu.SemaphoreType.DMA
    numbers = jnp.concatenate(
        [enc_ids, labels, loss_positions, target_lengths[:, None]], axis=1
    )
    number_count = numbers.shape[1]
    number_lanes = -(-number_count // 1024) * 128
    numbers = jnp.pad(numbers, ((0, 0), (0, 8 * number_lanes - number_count)))
    span = 1 << tokens.bit_length()
    own_tokens = jnp.concatenate([enc_ids[0], jnp.zeros((1,), jnp.int32), labels[0, :-1]])
    hits = list_hits(own_tokens - row_start, shard_rows, span)
    own = model_width // shares
    own_in, own_up = 3 * own, ffn_up.shape[2] // shares
    norm_rows = norms.shape[0]
    gap = -own_in % 128
    in_wide = own_in + gap
    dec_wide = own_up + model_width + in_wide
    first_wide = 3 * in_wide
    enc_wide = own_up + model_width
    chunk = -(-shard_rows // (groups * 3072)) * 3072
    table_cuts = (chunk // 8, chunk // 4, chunk // 4, 3 * chunk // 8)
    early_wide = first_wide + enc_wide
    mine_early, mine_dec = cut_weights(
        groups, shares, gap, (attn_in, attn_out, ffn_up, ffn_down, norms), early_wide, dec_wide
    )
    w_early = lax.all_gather(mine_early, "dp", axis=0, tiled=True)
    w_dec = lax.all_gather(mine_dec, "dp", axis=0, tiled=True)
    numbers, hits = call(
        partial(numbers_kernel, groups),
        "numbers",
        1,
        [numbers.reshape(8, number_lanes), hits.reshape(8, span // 8)],
        [
            shape_of((groups, 8, number_lanes), jnp.int32),
            shape_of((groups, 8, span // 8), jnp.int32),
        ],
        [sems((2, 2, groups - 1)), sems((2,))],
        0,
    )
    hits = hits.reshape(groups, span)
    numbers = numbers.reshape(groups, 8 * number_lanes)
    all_labels = numbers[:, enc_len:tokens]
    all_positions = numbers[:, tokens : tokens + loss_count]
    all_lengths = numbers[:, tokens + loss_count : number_count]
    at_place = all_positions[:, :, None] == jnp.arange(dec_len)
    all_targets = jnp.sum(jnp.where(at_place, all_labels[:, None, :], 0), axis=2).reshape(-1)
    all_counted = (all_positions < all_lengths).reshape(-1).astype(f32)
    token_count = jnp.sum(all_counted)

    picked, across, table_zero = pick_rows(
        hits, groups * tokens, embedding.T, groups * chunk, table_cuts[0]
    )
    place_enc = positions_numpy(enc_len, model_width)
    place_dec = positions_numpy(dec_len, model_width)
    enc_macs, dec_macs = enc_len * model_width, dec_len * model_width
    total_enc, total_dec = total_scratch(enc_len, model_width), total_scratch(dec_len, model_width)
    block_shape = (2, 2, 2, part_width)
    looked, table_zero = call(
        partial(look_kernel, groups),
        "look",
        2,
        [picked.reshape(groups, tokens, part_width), table_zero],
        [
            shape_of((tokens, model_width), bf16),
            shape_of((groups, part_width, table_cuts[0]), bf16),
        ],
        [
            pltpu.VMEM((tokens // 4, model_width), bf16),
            pltpu.VMEM((groups, tokens // 2, part_width), bf16),
            pltpu.VMEM((groups, tokens // 4, part_width), bf16),
            pltpu.VMEM((groups, tokens // 4, part_width), bf16),
            sems((2, groups + 3)),
            sems((2, groups)),
        ],
        0,
        (1,),
        (1,),
    )
    forward_inputs = [looked, place_enc, place_dec, w_early, across]
    forward_outputs = [
        shape_of((groups, part_width, sum(table_cuts[1:3])), bf16),
        shape_of((3, own, model_width), bf16),
        shape_of((16, model_width), f32),
        shape_of((enc_len, 3 * own), bf16),
        shape_of((enc_len, own), bf16),
        shape_of((enc_len, 128), f32),
        shape_of((enc_len, model_width), f32),
        shape_of((enc_len, own_up), f32),
        shape_of((enc_len, model_width), f32),
        shape_of((enc_len, model_width), bf16),
        shape_of((dec_len, 3 * own), bf16),
        shape_of((dec_len, own), bf16),
        shape_of((dec_len, 128), f32),
        shape_of((dec_len, model_width), f32),
    ]
    (
        table_one, out_rows, norm_values,
        qkv_enc, context_enc, logs_enc, stream_enc, pre_enc, stream_two, memory,
        qkv_dec, context_dec, logs_dec, stream_dec,
    ) = call(
        partial(
            forward_kernel, groups, shares, table_cuts[0], table_cuts[1:3], len(forward_inputs),
            len(forward_outputs),
        ),
        "forward",
        3,
        forward_inputs,
        forward_outputs,
        [
            sems((2, 2, groups)),
            sems((3,)),
            sems((2,)),
            pltpu.VMEM((model_width, first_wide), bf16),
            pltpu.VMEM((model_width, enc_wide), bf16),
            pltpu.VMEM((enc_len, model_width), f32),
            pltpu.VMEM((enc_len, own_up), f32),
            pltpu.VMEM((enc_len, model_width), f32),
            pltpu.VMEM((shares, own, in_wide), bf16),
            sems((2, shares - 1)),
            sems,
            *total_dec,
            *total_enc,
            *total_enc[1:],
        ],
        8 * enc_macs * own_up,
        (3, 4),
        (0, 6, 7, 8),
    )
    (
        table_two, q_cross, kv_cross, context_cross, logs_cross, stream_mid, pre_dec, stream_out, selected,
    ) = call(
        partial(dec_kernel, groups, sum(table_cuts[:3])),
        "dec",
        4,
        [
            stream_dec, memory, norm_values, out_rows, loss_positions.reshape(-1, 1), w_dec, across,
        ],
        [
            shape_of((groups, part_width, table_cuts[3]), bf16),
            shape_of((dec_len, own), bf16),
            shape_of((enc_len, 2 * own), bf16),
            shape_of((dec_len, own), bf16),
            shape_of((dec_len, 128), f32),
            shape_of((dec_len, model_width), f32),
            shape_of((dec_len, own_up), f32),
            shape_of((dec_len, model_width), f32),
            shape_of((groups, loss_count, model_width), bf16),
        ],
        [
            pltpu.VMEM((model_width, dec_wide), bf16),
            sems,
            sems((2, groups)),
            pltpu.VMEM((loss_count, model_width), bf16),
            sems((2, groups - 1)),
            *total_dec,
            *total_dec[1:],
        ],
        8 * dec_macs * own_up,
        (5, 6),
        (0,),
    )

    rows_all = groups * loss_count
    first_row = row_start + group * chunk
    targets = all_targets - first_row
    inside = (targets >= 0) & (targets < jnp.minimum(chunk, shard_rows - group * chunk))
    targets = jnp.where(inside, targets, -1)[:, None]
    head_cut = chunk // 8
    loss, grad_selected, head_grad, head_zero = call(
        partial(head_kernel, groups, shares, shard_rows),
        "head",
        6,
        [
            selected.reshape(rows_all, model_width),
            table_zero.reshape(model_width, -1),
            table_one.reshape(model_width, -1),
            table_two.reshape(model_width, -1),
            targets,
            (all_counted / token_count)[:, None],
            all_counted[None, :],
        ],
        [
            shape_of((1, 128), f32),
            shape_of((loss_count, model_width), bf16),
            shape_of((model_width, chunk), bf16),
            shape_of((groups, part_width, head_cut), bf16),
        ],
        [
            sems((2, groups)),
            pltpu.VMEM((rows_all, chunk), f32),
            pltpu.VMEM((rows_all, chunk), bf16),
            pltpu.VMEM((rows_all, 128), f32),
            pltpu.VMEM((128, rows_all), f32),
            pltpu.VMEM((shares, 8, rows_all), f32),
            pltpu.VMEM((groups, 8, rows_all), f32),
            sems((4, max(groups, shares))),
            pltpu.VMEM((groups, loss_count, model_width), bf16),
            pltpu.VMEM((groups, loss_count // 2, model_width), bf16),
            pltpu.VMEM((groups, loss_count // 4, model_width), bf16),
            pltpu.VMEM((groups, loss_count // 4, model_width), bf16),
            pltpu.VMEM((loss_count // 4, model_width), bf16),
            sems((2, groups + shares)),
        ],
        6 * rows_all * chunk * model_width,
        (),
        (3,),
    )
    loss_sum = loss[0, 0]
    head_grad = head_grad.reshape(groups, part_width, chunk)
    last_wide = own_in + own
    back_wide = own_up + model_width + last_wide
    late_wide = back_wide + last_wide
    quarter = tokens // shares
    back_inputs = [
        grad_selected, loss_positions.reshape(1, -1), stream_out, stream_mid, pre_dec, norm_values, w_dec,
        out_rows, memory, stream_dec, q_cross, kv_cross, context_cross, logs_cross,
        stream_two, stream_enc, pre_enc, w_early, looked, place_enc, place_dec,
        qkv_dec, context_dec, logs_dec, qkv_enc, context_enc, logs_enc,
        head_grad,
    ]

    head_one, grad_tokens, dec_shares, late_own, dense_squares = call(
        partial(
            back_kernel, groups, shares, first_wide, len(back_inputs), 5
        ),
        "backward",
        7,
        back_inputs,
        [
            shape_of((groups, part_width, chunk - head_cut), bf16),
            shape_of((shares, groups, quarter + 16, part_width), bf16),
            shape_of((shares, part_width, back_wide), bf16),
            shape_of((part_width, late_wide), bf16),
            shape_of((1, 128), f32),
        ],
        [
            sems((3, 2, groups)),
            sems((11,)),
            pltpu.VMEM((model_width, dec_wide), bf16),
            pltpu.VMEM((model_width, own_up + model_width), bf16),
            pltpu.VMEM(out_rows.shape, bf16),
            pltpu.VMEM((enc_len, model_width), bf16),
            pltpu.VMEM((dec_len, model_width), f32),
            pltpu.VMEM((enc_len, model_width), f32),
            pltpu.VMEM((enc_len, model_width), f32),
            pltpu.VMEM((enc_len, own_up), f32),
            pltpu.VMEM((tokens, model_width), bf16),
            pltpu.VMEM(block_shape + (back_wide,), bf16),
            pltpu.VMEM(block_shape + (back_wide,), bf16),
            pltpu.VMEM(block_shape + (last_wide,), bf16),
            pltpu.VMEM((dec_len, model_width), f32),
            pltpu.VMEM((enc_len, model_width), f32),
            pltpu.VMEM((dec_len, own), bf16),
            pltpu.VMEM((dec_len, own), bf16),
            pltpu.VMEM((enc_len, 2 * own), bf16),
            pltpu.VMEM((dec_len, 3 * own), bf16),
            pltpu.VMEM((enc_len, 3 * own), bf16),
            pltpu.VMEM((enc_len, own), bf16),
            pltpu.VMEM((own, model_width), bf16),
            pltpu.VMEM((own, model_width), bf16),
            pltpu.VMEM((own, model_width), bf16),
            pltpu.VMEM((8, model_width), f32),
            pltpu.VMEM((8, model_width), f32),
            pltpu.VMEM((8, model_width), f32),
            pltpu.VMEM((16, model_width), f32),
            sems((3, 2, shares)),
            pltpu.VMEM((groups, tokens + 16 * shares, part_width), bf16),
            sems((2, groups)),
            sems((2, 3)),
            sems((2, 3)),
            pltpu.VMEM((part_width, back_wide), bf16),
            sems((3,)),
            *[pltpu.VMEM((shares, own, own), bf16)] * 6,
            *total_dec,
            *total_enc,
            *total_dec[1:],
            *total_enc[1:],
            *line_scratch(part_width, back_wide),
            *line_scratch(part_width, back_wide),
            *line_scratch(part_width, last_wide),
        ],
        16 * (enc_macs + dec_macs) * own_up,
        (6, 7, 8, 9, 14, 15, 16, 17, 18, 19, 27),
        (0, 1, 2),
    )
    late_shares = lax.all_gather(late_own, "vocab", axis=0, tiled=False)
    g_embedding, embedding_squares = spread_rows(
        hits, groups * tokens, grad_tokens, (head_zero, head_one)
    )
    g_embedding = g_embedding[:, :shard_rows].astype(f32).T
    g_norms = jnp.sum(grad_tokens[0, :, quarter : quarter + norm_rows].astype(f32), axis=0)
    dense_squares = dense_squares + jnp.sum(g_norms * g_norms) / (shares * dense_squares.shape[1])
    (squares,) = call(
        partial(squares_kernel, groups, shares),
        "squares",
        10,
        [embedding_squares, dense_squares],
        [shape_of((1, 128), f32)],
        [
            pltpu.VMEM((shares, 8, 128), f32),
            pltpu.VMEM((groups, 8, 128), f32),
            sems((4, max(groups, shares))),
        ],
        0,
    )
    grad_norm = jnp.sqrt(squares[0, 0])
    factor = jnp.minimum(1.0, CLIP / (grad_norm + 1e-06))
    grad_pair = [late_shares, dec_shares]
    in_start, late_in = own_up + model_width, back_wide

    def place_in(wide_ref, late_ref, dec_ref):
        place_columns(3, 0, late_ref, late_in)(wide_ref)
        place_columns(3, 1, late_ref, in_start)(wide_ref)
        place_columns(3, 2, dec_ref, in_start)(wide_ref)

    def place_out(wide_ref, late_ref, dec_ref):
        place_columns(1, 0, late_ref, late_in + own_in)(wide_ref)
        place_columns(1, 1, late_ref, in_start + own_in)(wide_ref)
        place_columns(1, 2, dec_ref, in_start + own_in)(wide_ref)

    def place_up(wide_ref, late_ref, dec_ref):
        place_columns(groups, 0, late_ref, 0)(wide_ref)
        place_columns(groups, 1, dec_ref, 0)(wide_ref)

    down_rows = ffn_down.shape[1] // shares

    def place_down(wide_ref, late_ref, dec_ref):
        for matrix, ref in enumerate((late_ref, dec_ref)):

            @pl.when(pl.program_id(0) == matrix)
            def _(ref=ref):
                for piece in range(shares):
                    wide_ref[piece * down_rows : (piece + 1) * down_rows] = ref[piece]

    scale = factor.reshape(1)
    new_in = dense_update(
        "adam_in", RATES[1], place_in, scale, grad_pair, attn_in, attn_in_first, attn_in_second, 2
    )
    new_out = dense_update(
        "adam_out", RATES[2], place_out, scale, grad_pair, attn_out, attn_out_first, attn_out_second, 1
    )
    new_up = dense_update(
        "adam_up", RATES[3], place_up, scale, grad_pair, ffn_up, ffn_up_first, ffn_up_second, 2,
        (own_up, 0),
    )
    new_down = dense_update(
        "adam_down", RATES[4], place_down, scale, grad_pair, ffn_down, ffn_down_first, ffn_down_second, 1,
        (model_width, 1),
    )
    new_embedding = adam_update(
        embedding, embedding_first, embedding_second, g_embedding, factor, RATES[0]
    )
    new_norms = adam_update(norms, norms_first, norms_second, g_norms, factor, RATES[5])
    updated = (new_embedding, new_in, new_out, new_up, new_down, new_norms)
    return (loss_sum, token_count, grad_norm) + tuple(
        updated[slot][kind] for kind in range(3) for slot in range(6)
    )


def splits_evenly(mesh):
    return HEADS % mesh.shape["vocab"] == 0 and mesh.shape["dp"] == 8


def solution(mesh):
    placed = (
        P("dp", None),
        P("dp", None),
        P("dp"),
        P("dp", None),
        P("vocab", "dp"),
        P(None, "dp", None),
        P(None, "dp", None),
        P(None, "dp", None),
        P(None, "dp", None),
        P(None, "dp"),
        P("vocab", "dp"),
        P(None, "dp", None),
        P(None, "dp", None),
        P(None, "dp", None),
        P(None, "dp", None),
        P(None, "dp"),
        P("vocab", "dp"),
        P(None, "dp", None),
        P(None, "dp", None),
        P(None, "dp", None),
        P(None, "dp", None),
        P(None, "dp"),
    )
    return jax.shard_map(
        local if splits_evenly(mesh) else local_copied,
        mesh=mesh,
        in_specs=placed,
        out_specs=(
            P(),
            P(),
            P(),
            P("vocab", "dp"),
            P(None, "dp", None),
            P(None, "dp", None),
            P(None, "dp", None),
            P(None, "dp", None),
            P(None, "dp"),
            P("vocab", "dp"),
            P(None, "dp", None),
            P(None, "dp", None),
            P(None, "dp", None),
            P(None, "dp", None),
            P(None, "dp"),
            P("vocab", "dp"),
            P(None, "dp", None),
            P(None, "dp", None),
            P(None, "dp", None),
            P(None, "dp", None),
            P(None, "dp"),
        ),
        check_vma=False,
    )
```

```python
from functools import partial
import math

import jax
import jax.numpy as jnp
import numpy as np
from jax import lax
from jax.experimental import pallas as pl
from jax.experimental.pallas import tpu as pltpu
from jax.sharding import PartitionSpec as P

HEADS = 12
HEAD_DIM = 64
STEP = 10


EPS_NORM = 1e-05
SMOOTH = 0.1
CLIP = 0.02
RATES = (0.05, 0.05, 0.4, 0.05, 0.05, 0.8)
BETA_ONE = 0.9
BETA_TWO = 0.999
ADAM_EPS = 1e-08
DECAY = 0.01


def lowered(tensor):
    return tensor.astype(jnp.bfloat16)


def matmul(left_side, right_side):
    return jnp.dot(left_side, right_side, preferred_element_type=jnp.float32)


def times_transposed(left_side, right_side):
    return lax.dot_general(
        left_side, right_side, (((1,), (1,)), ((), ())), preferred_element_type=jnp.float32
    )


def contract_rows(left_side, right_side):
    return lax.dot_general(
        left_side, right_side, (((0,), (0,)), ((), ())), preferred_element_type=jnp.float32
    )


def positions_table(length, model_width):
    position_col = jnp.arange(length, dtype=jnp.float32)[:, None]
    freq_index = jnp.arange(model_width // 2, dtype=jnp.float32)[None, :]
    angles = position_col * jnp.exp(freq_index * (-2.0 * math.log(10000.0) / model_width))
    return jnp.concatenate([jnp.sin(angles), jnp.cos(angles)], axis=1)


def norm_forward(tensor, gain_row, shift_row):
    center = tensor - jnp.mean(tensor, axis=-1, keepdims=True)
    scale_inv = lax.rsqrt(jnp.mean(center * center, axis=-1, keepdims=True) + EPS_NORM)
    normed = center * scale_inv
    return (normed * gain_row + shift_row, (normed, scale_inv))


def norm_backward_rows(grad_out, saved_parts, gain_row):
    normed, scale_inv = saved_parts
    grad_normed = grad_out * gain_row
    grad_in = scale_inv * (
        grad_normed
        - jnp.mean(grad_normed, axis=-1, keepdims=True)
        - normed * jnp.mean(grad_normed * normed, axis=-1, keepdims=True)
    )
    return (grad_in, jnp.sum(grad_out * normed, axis=0), jnp.sum(grad_out, axis=0))


def split_heads(rows, batch_size):
    return rows.reshape(batch_size, -1, HEADS, rows.shape[1] // HEADS)


def score_block(queries, key_rows, causal):
    scores = jnp.einsum(
        "qhe,khe->hqk", queries, key_rows, preferred_element_type=jnp.float32
    ) * HEAD_DIM ** (-0.5)
    if causal:
        allowed = jnp.arange(queries.shape[0])[:, None] >= jnp.arange(key_rows.shape[0])[None, :]
        scores = jnp.where(allowed[None], scores, -1e30)
    return scores


def attend_one(block_args, causal):
    queries, key_rows, value_rows = block_args
    scores = score_block(queries, key_rows, causal)
    row_top = jnp.max(scores, axis=-1, keepdims=True)
    exponent = jnp.exp(scores - row_top)
    row_total = jnp.sum(exponent, axis=-1, keepdims=True)
    softmax_out = lowered(exponent / row_total)
    context = jnp.einsum(
        "hqk,khe->qhe", softmax_out, value_rows, preferred_element_type=jnp.float32
    )
    return (lowered(context), (row_top + jnp.log(row_total))[..., 0])


def attend_back(block_args, causal):
    queries, key_rows, value_rows, log_total, grad_context = block_args
    scores = score_block(queries, key_rows, causal)
    softmax_out = jnp.exp(scores - log_total[..., None])
    grad_values = jnp.einsum(
        "hqk,qhe->khe", lowered(softmax_out), grad_context, preferred_element_type=jnp.float32
    )
    grad_softmax = jnp.einsum(
        "qhe,khe->hqk", grad_context, value_rows, preferred_element_type=jnp.float32
    )
    grad_scores = lowered(
        softmax_out * (grad_softmax - jnp.sum(grad_softmax * softmax_out, axis=-1, keepdims=True))
    )
    grad_queries = jnp.einsum(
        "hqk,khe->qhe", grad_scores, key_rows, preferred_element_type=jnp.float32
    ) * HEAD_DIM ** (-0.5)
    grad_keys = jnp.einsum(
        "hqk,qhe->khe", grad_scores, queries, preferred_element_type=jnp.float32
    ) * HEAD_DIM ** (-0.5)
    return (lowered(grad_queries), lowered(grad_keys), lowered(grad_values))


def layer_forward(stream, memory, blocks, feed_parts, gain_rows, shifts, batch_size):
    kept_values = []
    for block_order, (w_in, w_out, norm_row) in enumerate(blocks):
        normed, norm_kept = norm_forward(stream, gain_rows[norm_row], shifts[norm_row])
        query_in = lowered(normed)
        model_width = w_out.shape[0]
        if block_order == 0:
            projected = lowered(matmul(query_in, w_in))
            queries = projected[:, :model_width]
            key_rows = projected[:, model_width : 2 * model_width]
            value_rows = projected[:, 2 * model_width :]
            memory_in = query_in
        else:
            memory_in = memory
            queries = lowered(matmul(query_in, w_in[:, :model_width]))
            paired = lowered(matmul(memory, w_in[:, model_width:]))
            key_rows, value_rows = (paired[:, :model_width], paired[:, model_width:])
        causal = memory is not None and block_order == 0
        heads = (
            split_heads(queries, batch_size),
            split_heads(key_rows, batch_size),
            split_heads(value_rows, batch_size),
        )
        context, log_total = lax.map(partial(attend_one, causal=causal), heads)
        context = context.reshape(-1, model_width)
        stream = stream + matmul(context, w_out)
        kept_values.append((norm_kept, query_in, memory_in, heads, context, log_total))
    w_up, w_down, norm_row = feed_parts
    normed, norm_kept = norm_forward(stream, gain_rows[norm_row], shifts[norm_row])
    hidden_in = lowered(normed)
    hidden_pre = matmul(hidden_in, w_up)
    activated = lowered(jax.nn.silu(hidden_pre))
    stream = stream + matmul(activated, w_down)
    kept_values.append((norm_kept, hidden_in, hidden_pre, activated))
    return (stream, kept_values)


def layer_backward(grad_stream, memory, blocks, feed_parts, gain_rows, kept_values, batch_size):
    w_up, w_down, norm_row = feed_parts
    norm_kept, hidden_in, hidden_pre, activated = kept_values[-1]
    grad_low = lowered(grad_stream)
    grad_down = contract_rows(activated, grad_low)
    sigmoid_pre = jax.nn.sigmoid(hidden_pre)
    grad_pre = lowered(
        times_transposed(grad_low, w_down) * sigmoid_pre * (1.0 + hidden_pre * (1.0 - sigmoid_pre))
    )
    grad_up = contract_rows(hidden_in, grad_pre)
    grad_in, grad_gain, grad_shift = norm_backward_rows(
        times_transposed(grad_pre, w_up), norm_kept, gain_rows[norm_row]
    )
    grad_stream = grad_stream + grad_in
    norm_grads = [(norm_row, grad_gain, grad_shift)]
    block_grads = [None] * len(blocks)
    grad_memory = None
    for block_order in reversed(range(len(blocks))):
        w_in, w_out, norm_row = blocks[block_order]
        norm_kept, query_in, memory_in, heads, context, log_total = kept_values[block_order]
        model_width = w_out.shape[0]
        grad_low = lowered(grad_stream)
        grad_w_out = contract_rows(context, grad_low)
        grad_context = split_heads(lowered(times_transposed(grad_low, w_out)), batch_size)
        causal = memory is not None and block_order == 0
        grad_heads = lax.map(partial(attend_back, causal=causal), heads + (log_total, grad_context))
        grad_queries, grad_keys, grad_values = [
            member.reshape(-1, model_width) for member in grad_heads
        ]
        if block_order == 0:
            grad_proj = jnp.concatenate([grad_queries, grad_keys, grad_values], axis=1)
            grad_w_in = contract_rows(query_in, grad_proj)
            grad_normed = times_transposed(grad_proj, w_in)
        else:
            grad_pair = jnp.concatenate([grad_keys, grad_values], axis=1)
            grad_w_in = jnp.concatenate(
                [contract_rows(query_in, grad_queries), contract_rows(memory_in, grad_pair)], axis=1
            )
            grad_normed = times_transposed(grad_queries, w_in[:, :model_width])
            grad_memory = times_transposed(grad_pair, w_in[:, model_width:])
        grad_in, grad_gain, grad_shift = norm_backward_rows(grad_normed, norm_kept, gain_rows[norm_row])
        grad_stream = grad_stream + grad_in
        norm_grads.append((norm_row, grad_gain, grad_shift))
        block_grads[block_order] = (grad_w_in, grad_w_out)
    return (grad_stream, grad_memory, block_grads, (grad_up, grad_down), norm_grads)


def adam_update(weight, first_moment, second_moment, gradient, factor, rate):
    clipped = gradient * factor
    new_first = BETA_ONE * first_moment + (1.0 - BETA_ONE) * clipped
    new_second = BETA_TWO * second_moment + (1.0 - BETA_TWO) * clipped * clipped
    corrected = (
        new_first
        / (1.0 - BETA_ONE**STEP)
        / (jnp.sqrt(new_second / (1.0 - BETA_TWO**STEP)) + ADAM_EPS)
    )
    return (weight - rate * (corrected + DECAY * weight), new_first, new_second)


def local_copied(
    enc_ids,
    labels,
    target_lengths,
    loss_positions,
    embedding,
    attn_in,
    attn_out,
    ffn_up,
    ffn_down,
    norms,
    embedding_first,
    attn_in_first,
    attn_out_first,
    ffn_up_first,
    ffn_down_first,
    norms_first,
    embedding_second,
    attn_in_second,
    attn_out_second,
    ffn_up_second,
    ffn_down_second,
    norms_second,
):
    batch_size, enc_len = enc_ids.shape
    dec_len = labels.shape[1]
    emb_table, w_in_all, w_out_all, w_up_all, w_down_all, norm_table = (
        lax.all_gather(lowered(embedding), "dp", axis=1, tiled=True),
        lax.all_gather(lowered(attn_in), "dp", axis=1, tiled=True),
        lax.all_gather(lowered(attn_out), "dp", axis=1, tiled=True),
        lax.all_gather(lowered(ffn_up), "dp", axis=1, tiled=True),
        lax.all_gather(lowered(ffn_down), "dp", axis=1, tiled=True),
        lax.all_gather(lowered(norms), "dp", axis=1, tiled=True),
    )
    model_width = emb_table.shape[1]
    shard_rows = emb_table.shape[0]
    vocab_total = shard_rows * lax.axis_size("vocab")
    row_start = lax.axis_index("vocab") * shard_rows
    norm_values = norm_table.astype(jnp.float32)
    gain_rows, shifts = (norm_values[:7], norm_values[7:])
    dec_ids = jnp.concatenate([jnp.zeros((batch_size, 1), jnp.int32), labels[:, :-1]], axis=1)
    token_list = jnp.concatenate([enc_ids.reshape(-1), dec_ids.reshape(-1)])
    local_rows = token_list - row_start
    inside = (local_rows >= 0) & (local_rows < shard_rows)
    safe_rows = jnp.clip(local_rows, 0, shard_rows - 1)
    picked = jnp.where(
        inside[:, None], jnp.take(emb_table, safe_rows, axis=0).astype(jnp.float32), 0.0
    )
    looked = lax.psum(picked.astype(jnp.bfloat16), "vocab").astype(jnp.float32)
    root_width = math.sqrt(model_width)
    enc_tokens = batch_size * enc_len
    enc_stream = (
        looked[:enc_tokens].reshape(batch_size, enc_len, model_width) * root_width
        + positions_table(enc_len, model_width)
    ).reshape(enc_tokens, model_width)
    dec_stream = (
        looked[enc_tokens:].reshape(batch_size, dec_len, model_width) * root_width
        + positions_table(dec_len, model_width)
    ).reshape(batch_size * dec_len, model_width)
    enc_blocks = [(w_in_all[0], w_out_all[0], 0)]
    dec_blocks = [(w_in_all[1], w_out_all[1], 3), (w_in_all[2], w_out_all[2], 4)]
    enc_feed = (w_up_all[0], w_down_all[0], 1)
    dec_feed = (w_up_all[1], w_down_all[1], 5)
    enc_out, enc_kept = layer_forward(
        enc_stream, None, enc_blocks, enc_feed, gain_rows, shifts, batch_size
    )
    memory, memory_kept = norm_forward(enc_out, gain_rows[2], shifts[2])
    memory_low = lowered(memory)
    dec_out, dec_kept = layer_forward(
        dec_stream, memory_low, dec_blocks, dec_feed, gain_rows, shifts, batch_size
    )
    final, final_kept = norm_forward(dec_out, gain_rows[6], shifts[6])
    chosen = (jnp.arange(batch_size)[:, None] * dec_len + loss_positions).reshape(-1)
    selected = lowered(jnp.take(final, chosen, axis=0))
    logits = times_transposed(selected, emb_table)
    columns = row_start + jnp.arange(shard_rows)
    padding = columns == vocab_total - 1
    masked = jnp.where(padding[None, :], -1e30, logits)
    target_local = jnp.take_along_axis(labels, loss_positions, axis=1).reshape(-1) - row_start
    target_hit = (jnp.arange(shard_rows)[None, :] == target_local[:, None]).astype(jnp.float32)
    target_term = jnp.sum(target_hit * logits, axis=1)
    smooth_term = jnp.sum(jnp.where(padding[None, :], 0.0, logits), axis=1)
    local_max = jnp.max(masked, axis=1)
    row_max = lax.pmax(local_max, "vocab")
    exp_local = jnp.sum(jnp.exp(masked - row_max[:, None]), axis=1)
    exp_total, smooth_total, target_total = lax.psum((exp_local, smooth_term, target_term), "vocab")
    log_total = row_max + jnp.log(exp_total)
    per_row = log_total - (1.0 - SMOOTH) * target_total - SMOOTH * smooth_total / (vocab_total - 1)
    counted = (loss_positions < target_lengths[:, None]).reshape(-1).astype(jnp.float32)
    loss_sum, token_count = lax.psum((jnp.sum(counted * per_row), jnp.sum(counted)), "dp")
    softmax_rows = jnp.exp(masked - log_total[:, None])
    grad_logits = (counted / token_count)[:, None] * (
        softmax_rows - (1.0 - SMOOTH) * target_hit - SMOOTH / (vocab_total - 1)
    )
    grad_logits = lowered(jnp.where(padding[None, :], 0.0, grad_logits))
    grad_selected = lax.psum(matmul(grad_logits, emb_table).astype(jnp.bfloat16), "vocab").astype(
        jnp.float32
    )
    grad_final = jnp.zeros_like(final).at[chosen].add(grad_selected)
    grad_dec_out, gain_six, shift_six = norm_backward_rows(grad_final, final_kept, gain_rows[6])
    grad_dec_stream, grad_memory, dec_block_grads, dec_feed_grads, dec_norm_grads = layer_backward(
        grad_dec_out, memory_low, dec_blocks, dec_feed, gain_rows, dec_kept, batch_size
    )
    grad_enc_out, gain_two, shift_two = norm_backward_rows(grad_memory, memory_kept, gain_rows[2])
    grad_enc_stream, _, enc_block_grads, enc_feed_grads, enc_norm_grads = layer_backward(
        grad_enc_out, None, enc_blocks, enc_feed, gain_rows, enc_kept, batch_size
    )
    grad_attn_in = jnp.stack([enc_block_grads[0][0], dec_block_grads[0][0], dec_block_grads[1][0]])
    grad_attn_out = jnp.stack([enc_block_grads[0][1], dec_block_grads[0][1], dec_block_grads[1][1]])
    grad_up_all = jnp.stack([enc_feed_grads[0], dec_feed_grads[0]])
    grad_down_all = jnp.stack([enc_feed_grads[1], dec_feed_grads[1]])
    grad_norms = jnp.zeros((14, model_width), jnp.float32)
    for norm_row, grad_gain, grad_shift in (
        enc_norm_grads + dec_norm_grads + [(2, gain_two, shift_two), (6, gain_six, shift_six)]
    ):
        grad_norms = grad_norms.at[norm_row].set(grad_gain).at[norm_row + 7].set(grad_shift)
    grad_tokens = jnp.concatenate([grad_enc_stream, grad_dec_stream], axis=0) * root_width
    head_term = contract_rows(grad_logits, selected)
    lookup_term = (
        jnp.zeros((shard_rows, model_width), jnp.float32)
        .at[safe_rows]
        .add(jnp.where(inside[:, None], grad_tokens, 0.0))
    )
    g_attn_in, g_attn_out, g_up, g_down, g_norms, g_embedding = (
        lax.psum_scatter(
            grad_attn_in.astype(jnp.bfloat16), "dp", scatter_dimension=1, tiled=True
        ).astype(jnp.float32),
        lax.psum_scatter(
            grad_attn_out.astype(jnp.bfloat16), "dp", scatter_dimension=1, tiled=True
        ).astype(jnp.float32),
        lax.psum_scatter(
            grad_up_all.astype(jnp.bfloat16), "dp", scatter_dimension=1, tiled=True
        ).astype(jnp.float32),
        lax.psum_scatter(
            grad_down_all.astype(jnp.bfloat16), "dp", scatter_dimension=1, tiled=True
        ).astype(jnp.float32),
        lax.psum_scatter(
            grad_norms.astype(jnp.bfloat16), "dp", scatter_dimension=1, tiled=True
        ).astype(jnp.float32),
        lax.psum_scatter(
            (head_term + lookup_term).astype(jnp.bfloat16), "dp", scatter_dimension=1, tiled=True
        ).astype(jnp.float32),
    )
    gradients = (g_embedding, g_attn_in, g_attn_out, g_up, g_down, g_norms)
    dense_squares = sum((jnp.sum(member * member) for member in gradients[1:]))
    squares = lax.psum(
        dense_squares / lax.axis_size("vocab") + jnp.sum(g_embedding * g_embedding), ("dp", "vocab")
    )
    grad_norm = jnp.sqrt(squares)
    factor = jnp.minimum(1.0, CLIP / (grad_norm + 1e-06))
    params = (embedding, attn_in, attn_out, ffn_up, ffn_down, norms)
    firsts = (
        embedding_first,
        attn_in_first,
        attn_out_first,
        ffn_up_first,
        ffn_down_first,
        norms_first,
    )
    seconds = (
        embedding_second,
        attn_in_second,
        attn_out_second,
        ffn_up_second,
        ffn_down_second,
        norms_second,
    )
    updated = [
        adam_update(params[slot], firsts[slot], seconds[slot], gradients[slot], factor, RATES[slot])
        for slot in range(6)
    ]
    return (
        loss_sum,
        token_count,
        grad_norm,
        updated[0][0],
        updated[1][0],
        updated[2][0],
        updated[3][0],
        updated[4][0],
        updated[5][0],
        updated[0][1],
        updated[1][1],
        updated[2][1],
        updated[3][1],
        updated[4][1],
        updated[5][1],
        updated[0][2],
        updated[1][2],
        updated[2][2],
        updated[3][2],
        updated[4][2],
        updated[5][2],
    )


VMEM_BYTES = 60 * 1024 * 1024


def positions_numpy(length, model_width):
    place = np.arange(length, dtype=np.float32)[:, None]
    index = np.arange(model_width // 2, dtype=np.float32)[None, :]
    angles = place * np.exp(index * np.float32(-2.0 * math.log(10000.0) / model_width))
    return np.concatenate([np.sin(angles), np.cos(angles)], axis=1).astype(np.float32)


def hits_kernel(rows, span, ids_ref, list_ref):
    def one(step, found):
        for inner in range(8):
            slot = step * 8 + inner
            row = ids_ref[slot]
            list_ref[found] = row * span + slot
            found = found + jnp.where((row >= 0) & (row < rows), 1, 0)
        return found

    list_ref[list_ref.shape[0] - 1] = lax.fori_loop(0, ids_ref.shape[0] // 8, one, 0)


def list_hits(local_ids, rows, span):
    return pl.pallas_call(
        partial(hits_kernel, rows, span),
        out_shape=jax.ShapeDtypeStruct((span,), jnp.int32),
        in_specs=[pl.BlockSpec(memory_space=pltpu.SMEM)],
        out_specs=pl.BlockSpec(memory_space=pltpu.SMEM),
        name="list_hits",
    )(local_ids)


def over_hits(lists_ref, visit):
    groups, span = lists_ref.shape
    for group in range(groups):

        def one(step, carry):
            entry = lists_ref[group, step]
            visit(group, entry // span, lax.rem(entry, span))
            return carry

        lax.fori_loop(0, lists_ref[group, span - 1], one, 0)


def pick_kernel(lists_ref, table_ref, out_ref, across_ref, piece_ref, wide_ref, turned_ref):
    tokens = wide_ref.shape[0] // lists_ref.shape[0]
    width, rows = table_ref.shape
    total = across_ref.shape[1]
    wide_ref[...] = jnp.zeros_like(wide_ref)
    step = 1024
    for low in range(0, total, step):
        high = max(min(low + step, rows), low)
        if high > low:
            across_ref[:, low:high] = lowered(table_ref[:, low:high])
        if high < low + step:
            across_ref[:, high : low + step] = jnp.zeros((width, low + step - high), jnp.bfloat16)

    groups, _, columns = piece_ref.shape
    for group in range(groups):
        start = group * (total // groups)
        piece_ref[group] = across_ref[:, start : start + columns]

    def turn(piece, carry):
        for part in range(8):
            start = pl.multiple_of(piece * step + part * 128, 128)
            block = across_ref[:, pl.ds(start, 128)].astype(jnp.float32)
            turned_ref[pl.ds(start, 128), :] = jnp.transpose(block)
        return carry

    lax.fori_loop(0, total // step, turn, 0)

    def visit(group, row, slot):
        wide_ref[pl.ds(group * tokens + slot, 1), :] = turned_ref[pl.ds(row, 1), :]

    over_hits(lists_ref, visit)
    out_ref[...] = wide_ref[...].astype(jnp.bfloat16)


def pick_rows(lists, count, table, total, columns):
    width = table.shape[0]
    return pl.pallas_call(
        pick_kernel,
        out_shape=(
            jax.ShapeDtypeStruct((count, width), jnp.bfloat16),
            jax.ShapeDtypeStruct((width, total), jnp.bfloat16),
            jax.ShapeDtypeStruct((lists.shape[0], width, columns), jnp.bfloat16),
        ),
        in_specs=[
            pl.BlockSpec(memory_space=pltpu.SMEM),
            pl.BlockSpec(memory_space=pltpu.VMEM),
        ],
        out_specs=(
            pl.BlockSpec(memory_space=pltpu.VMEM),
            pl.BlockSpec(memory_space=pltpu.VMEM),
            pl.BlockSpec(memory_space=pltpu.VMEM),
        ),
        scratch_shapes=[
            pltpu.VMEM((count, width), jnp.float32),
            pltpu.VMEM((total, width), jnp.float32),
        ],
        compiler_params=pltpu.CompilerParams(vmem_limit_bytes=VMEM_BYTES),
        name="pick_rows",
    )(lists, table)


def spread_kernel(
    lists_ref, grads_ref, zero_ref, one_ref, out_ref, squares_ref, wide_ref, rows_ref
):
    shares, groups, _, width = grads_ref.shape
    tokens = rows_ref.shape[0] // groups
    quarter = tokens // shares
    chunks = zero_ref.shape[0]
    parts = [(ref, low) for ref in (zero_ref, one_ref) for low in range(0, ref.shape[2], 128)]
    chunk = 128 * len(parts)
    for index in range(shares):
        for number in range(groups):
            start = number * tokens + index * quarter
            rows_ref[start : start + quarter, :] = grads_ref[index, number, 0:quarter].astype(jnp.float32)
    wide_ref[...] = jnp.zeros_like(wide_ref)

    def visit(group, row, slot):
        wide_ref[pl.ds(row, 1), 0:width] += rows_ref[pl.ds(group * tokens + slot, 1), :]

    over_hits(lists_ref, visit)

    def turn(piece, total):
        for part, (head_ref, column) in enumerate(parts):
            start = pl.multiple_of(piece * chunk + part * 128, 128)
            block = jnp.transpose(wide_ref[pl.ds(start, 128), :])[:width]
            block = block + head_ref[piece, :, column : column + 128].astype(jnp.float32)
            out_ref[:, pl.ds(start, 128)] = lowered(block)
            total = total + block * block
        return total

    total = lax.fori_loop(0, chunks, turn, jnp.zeros((width, 128), jnp.float32))
    squares_ref[...] = jnp.sum(total, axis=0, keepdims=True)


def spread_rows(lists, count, grads, head):
    chunks, width, _ = head[0].shape
    chunk = sum(member.shape[2] for member in head)
    return pl.pallas_call(
        spread_kernel,
        out_shape=(
            jax.ShapeDtypeStruct((width, chunks * chunk), jnp.bfloat16),
            jax.ShapeDtypeStruct((1, 128), jnp.float32),
        ),
        in_specs=[pl.BlockSpec(memory_space=pltpu.SMEM)]
        + [pl.BlockSpec(memory_space=pltpu.VMEM)] * 3,
        out_specs=(
            pl.BlockSpec(memory_space=pltpu.VMEM),
            pl.BlockSpec(memory_space=pltpu.VMEM),
        ),
        scratch_shapes=[
            pltpu.VMEM((chunks * chunk, 128), jnp.float32),
            pltpu.VMEM((count, width), jnp.float32),
        ],
        compiler_params=pltpu.CompilerParams(vmem_limit_bytes=VMEM_BYTES),
        name="spread_rows",
    )(lists, grads, *head)


MESH = pl.DeviceIdType.MESH


def meet(devices):
    barrier = pltpu.get_barrier_semaphore()
    for device in devices:
        pl.semaphore_signal(barrier, inc=1, device_id=device, device_id_type=MESH)
    pl.semaphore_wait(barrier, len(devices))


def send(source, target, send_sem, recv_sem, device):
    copy = pltpu.make_async_remote_copy(
        src_ref=source,
        dst_ref=target,
        send_sem=send_sem,
        recv_sem=recv_sem,
        device_id=device,
        device_id_type=MESH,
    )
    copy.start()
    return copy


def places():
    group, share = lax.axis_index("dp"), lax.axis_index("vocab")
    core = lax.rem(share, 2)
    core_peer = (group, share + 1 - 2 * core)
    side_peer = (group, lax.rem(share + 2, 4))
    return group, share, core, core_peer, side_peer


def group_peers(group, share, groups):
    return [(lax.rem(group + step, groups), share) for step in range(1, groups)]


def share_peers(group, share, shares):
    return [(group, lax.rem(share + step, shares)) for step in range(1, shares)]


def total_scratch(rows, width):
    half = rows // 2
    return [
        pltpu.VMEM((rows, width), jnp.float32),
        pltpu.VMEM((4, half, width), jnp.bfloat16),
        pltpu.VMEM((rows, width), jnp.bfloat16),
        pltpu.SemaphoreType.DMA((6,)),
    ]


class Total:
    def __init__(self, refs):
        self.part, self.bufs, self.total, self.sems = refs
        _, _, core, self.core_peer, self.side_peer = places()
        half = self.part.shape[0] // 2
        self.mine = pl.ds(pl.multiple_of(core * half, half), half)
        self.other = pl.ds(pl.multiple_of((1 - core) * half, half), half)

    def begin(self, partial_rows):
        self.part[...] = partial_rows
        self.bufs[0] = lowered(self.part[self.other, :])
        self.one = send(
            self.bufs.at[0], self.bufs.at[1], self.sems.at[0], self.sems.at[1], self.core_peer
        )

    def middle(self):
        self.one.wait_recv()
        self.bufs[2] = lowered(self.part[self.mine, :] + self.bufs[1].astype(jnp.float32))
        self.two = send(
            self.bufs.at[2], self.bufs.at[3], self.sems.at[2], self.sems.at[3], self.side_peer
        )

    def last(self):
        self.two.wait_recv()
        self.total[self.mine, :] = lowered(
            self.bufs[2].astype(jnp.float32) + self.bufs[3].astype(jnp.float32)
        )
        piece = self.total.at[self.mine, :]
        self.three = send(piece, piece, self.sems.at[4], self.sems.at[5], self.core_peer)

    def finish(self):
        self.three.wait()
        self.one.wait_send()
        self.two.wait_send()
        return self.total[...].astype(jnp.float32)

    def rest(self):
        self.middle()
        self.last()
        return self.finish()


class Exchange:
    def __init__(self, block_of, target_ref, sems, groups):
        group, share = lax.axis_index("dp"), lax.axis_index("vocab")
        self.copies = [
            send(
                block_of(peer[0]), target_ref.at[group], sems.at[0, step], sems.at[1, step], peer
            )
            for step, peer in enumerate(group_peers(group, share, groups))
        ]
        self.keep = pltpu.make_async_copy(
            block_of(group), target_ref.at[group], sems.at[0, groups - 1]
        )
        self.keep.start()

    def finish(self):
        self.keep.wait()
        for copy in self.copies:
            copy.wait()


def head_blocks(source_ref, start, columns):
    return lambda group: source_ref.at[group, :, pl.ds(start, columns)]


def table_blocks(source_ref, chunk, start, columns):
    return lambda group: source_ref.at[:, pl.ds(pl.multiple_of(group * chunk + start, 128), columns)]


def pair_of(group, share):
    place = lax.rem(group, 2)
    return (group + 1 - 2 * place, share), place


def line_places(group):
    pair, place = group // 2, lax.rem(group, 2)
    high, low = pair // 2, lax.rem(pair, 2)
    far = ((1 - high) * 2 + low) * 2 + place
    near = (high * 2 + 1 - low) * 2 + place
    return high, low, far, near


def line_scratch(width, columns):
    return [
        pltpu.VMEM((2, 2, width, columns), jnp.bfloat16),
        pltpu.VMEM((2, width, columns), jnp.bfloat16),
        pltpu.VMEM((width, columns), jnp.bfloat16),
        pltpu.SemaphoreType.DMA((6,)),
    ]


class Owned:
    def __init__(self, blocks, refs):
        group, self.share = lax.axis_index("dp"), lax.axis_index("vocab")
        self.high, self.low, self.far, self.near = line_places(group)
        self.pair, self.place = pair_of(group, self.share)
        self.blocks = blocks
        self.pair_in, self.near_in, self.far_in, self.sems = refs

    def begin(self):
        source = self.blocks.at[:, :, 1 - self.place]
        self.zero = send(source, self.pair_in, self.sems.at[0], self.sems.at[1], self.pair)

    def beside(self):
        self.zero.wait()
        self.blocks[:, :, self.place] = lowered(
            self.blocks[:, :, self.place].astype(jnp.float32) + self.pair_in[...].astype(jnp.float32)
        )
        self.one = send(
            self.blocks.at[:, 1 - self.low, self.place],
            self.near_in,
            self.sems.at[2],
            self.sems.at[3],
            (self.near, self.share),
        )

    def beyond(self):
        self.one.wait()
        self.blocks[:, self.low, self.place] = lowered(
            self.blocks[:, self.low, self.place].astype(jnp.float32)
            + self.near_in[...].astype(jnp.float32)
        )
        self.two = send(
            self.blocks.at[1 - self.high, self.low, self.place],
            self.far_in,
            self.sems.at[4],
            self.sems.at[5],
            (self.far, self.share),
        )

    def finish(self):
        self.two.wait()
        return lowered(
            self.blocks[self.high, self.low, self.place].astype(jnp.float32)
            + self.far_in[...].astype(jnp.float32)
        )


class Rows:
    def __init__(self, value_ref, send_ref, recv_ref, sems):
        group, share = lax.axis_index("dp"), lax.axis_index("vocab")
        self.recv = recv_ref
        shares, _, own = send_ref.shape
        for piece in range(shares):
            send_ref[piece] = value_ref[:, piece * own : (piece + 1) * own]
        self.copies = [
            send(send_ref.at[peer[1]], recv_ref.at[share], sems.at[0, step], sems.at[1, step], peer)
            for step, peer in enumerate(share_peers(group, share, shares))
        ]
        keep = pltpu.make_async_copy(send_ref.at[share], recv_ref.at[share], sems.at[0, shares - 1])
        keep.start()
        self.copies.append(keep)

    def put(self, grads_ref, start):
        for copy in self.copies:
            copy.wait()
        shares, _, own = self.recv.shape
        part = grads_ref.shape[3]
        for piece in range(shares):
            for half in range(2):
                grads_ref[piece // 2, piece % 2, half, :, start : start + own] = self.recv[
                    piece, half * part : (half + 1) * part
                ]


class Late:
    def __init__(self, source, buffer, sem):
        self.copy, self.buffer, self.waiting = pltpu.make_async_copy(source, buffer, sem), buffer, True
        self.copy.start()

    def __call__(self):
        if self.waiting:
            self.copy.wait()
            self.waiting = False
        return self.buffer


class ShareGather:
    def __init__(self, target_ref, sems):
        _, self.share, _, self.core_peer, self.side_peer = places()
        self.target, self.sems = target_ref, sems
        block = target_ref.at[self.share]
        self.one = send(block, block, sems.at[0, 0], sems.at[1, 0], self.side_peer)

    def middle(self):
        self.one.wait()
        both = [self.target.at[index] for index in (self.share, self.side_peer[1])]
        self.two = [
            send(block, block, self.sems.at[0, 1 + step], self.sems.at[1, 1 + step], self.core_peer)
            for step, block in enumerate(both)
        ]

    def finish(self):
        for copy in self.two:
            copy.wait()


def in_vmem(count, at_rest=()):
    return [
        pl.BlockSpec(memory_space=pl.ANY if index in at_rest else pltpu.VMEM)
        for index in range(count)
    ]


def call(kernel, name, number, inputs, out_shape, scratch, flops, rest_in=(), rest_out=()):
    moved = sum(math.prod(member.shape) * member.dtype.itemsize for member in (*inputs, *out_shape))
    return pl.pallas_call(
        kernel,
        out_shape=tuple(out_shape),
        in_specs=in_vmem(len(inputs), rest_in),
        out_specs=tuple(in_vmem(len(out_shape), rest_out)),
        scratch_shapes=scratch,
        compiler_params=pltpu.CompilerParams(
            collective_id=number, has_side_effects=True, vmem_limit_bytes=VMEM_BYTES
        ),
        cost_estimate=pl.CostEstimate(flops=flops, bytes_accessed=moved, transcendentals=0),
        name=name,
    )(*inputs)


def shape_of(shape, dtype):
    return jax.ShapeDtypeStruct(shape, dtype)


def head_slice(ref, start, index):
    low = start + index * HEAD_DIM
    return ref[:, low : low + HEAD_DIM]


def masked_scores(query, key, causal):
    scores = times_transposed(query, key) * HEAD_DIM ** (-0.5)
    if causal:
        down = lax.broadcasted_iota(jnp.int32, scores.shape, 0)
        across = lax.broadcasted_iota(jnp.int32, scores.shape, 1)
        scores = jnp.where(down >= across, scores, -1e30)
    return scores


def heads_forward(q_ref, kv_ref, starts, context_ref, logs_ref, causal):
    q_start, k_start, v_start = starts
    for index in range(context_ref.shape[1] // HEAD_DIM):
        query = head_slice(q_ref, q_start, index)
        key = head_slice(kv_ref, k_start, index)
        value = head_slice(kv_ref, v_start, index)
        scores = masked_scores(query, key, causal)
        row_top = jnp.max(scores, axis=-1, keepdims=True)
        exponent = jnp.exp(scores - row_top)
        row_total = jnp.sum(exponent, axis=-1, keepdims=True)
        context = lowered(matmul(lowered(exponent / row_total), value))
        context_ref[:, index * HEAD_DIM : (index + 1) * HEAD_DIM] = context
        logs_ref[:, index : index + 1] = row_top + jnp.log(row_total)


def heads_backward(q_ref, kv_ref, starts, logs_ref, grad_ref, gq_ref, gkv_ref, g_starts, causal):
    q_start, k_start, v_start = starts
    gq_start, gk_start, gv_start = g_starts
    scale = HEAD_DIM ** (-0.5)
    for index in range(grad_ref.shape[1] // HEAD_DIM):
        low, high = index * HEAD_DIM, (index + 1) * HEAD_DIM
        query = head_slice(q_ref, q_start, index)
        key = head_slice(kv_ref, k_start, index)
        value = head_slice(kv_ref, v_start, index)
        grad = grad_ref[:, low:high]
        softmax_out = jnp.exp(
            masked_scores(query, key, causal) - logs_ref[:, index : index + 1]
        )
        gkv_ref[:, gv_start + low : gv_start + high] = lowered(
            contract_rows(lowered(softmax_out), grad)
        )
        grad_softmax = times_transposed(grad, value)
        inner = jnp.sum(grad_softmax * softmax_out, axis=-1, keepdims=True)
        grad_scores = lowered(softmax_out * (grad_softmax - inner))
        gq_ref[:, gq_start + low : gq_start + high] = lowered(matmul(grad_scores, key) * scale)
        gkv_ref[:, gk_start + low : gk_start + high] = lowered(
            contract_rows(grad_scores, query) * scale
        )


def norm_backward(grad_out, saved_parts, gain_row):
    normed, scale_inv = saved_parts
    grad_normed = grad_out * gain_row
    grad_in = scale_inv * (
        grad_normed
        - jnp.mean(grad_normed, axis=-1, keepdims=True)
        - normed * jnp.mean(grad_normed * normed, axis=-1, keepdims=True)
    )
    return (
        grad_in,
        jnp.sum(grad_out * normed, axis=0, keepdims=True),
        jnp.sum(grad_out, axis=0, keepdims=True),
    )


def gain_of(norms_ref, row):
    return norms_ref[row : row + 1, :], norms_ref[row + 7 : row + 8, :]


def stream_of(looked_ref, start, place_ref):
    rows, width = place_ref.shape
    looked = looked_ref[start : start + rows, :].astype(jnp.float32)
    return looked * math.sqrt(width) + place_ref[...]


def forward_kernel(groups, shares, base, cuts, refs_in, refs_out, *refs):
    inputs, outputs, scratch = refs[:refs_in], refs[refs_in : refs_in + refs_out], refs[refs_in + refs_out :]
    looked_ref, place_enc_ref, place_dec_ref, w_early_hbm, across_ref = inputs
    (
        table_ref, out_rows_ref, norms_ref,
        qkv_enc_ref, context_enc_ref, logs_enc_ref, stream_enc_hbm, pre_enc_hbm, stream_two_hbm, memory_ref,
        qkv_dec_ref, context_dec_ref, logs_dec_ref, stream_dec_ref,
    ) = outputs
    (
        table_sems, out_sems, load_sems, w_first_ref, w_enc_ref, stream_enc_ref, pre_enc_ref, stream_two_ref,
        blocks_ref, block_sems, local_sem,
    ) = scratch[:11]
    rest = scratch[11:]
    small_one, large_one = rest[:4], rest[4:8]
    large_two = large_one[:1] + rest[8:11]
    group, share, core, core_peer, side_peer = places()
    peers, far = share_peers(group, share, shares), group_peers(group, share, groups)
    first_wide = w_first_ref.shape[1]
    load_first = Late(w_early_hbm.at[:, pl.ds(0, first_wide)], w_first_ref, load_sems.at[0])
    load_enc = Late(
        w_early_hbm.at[:, pl.ds(first_wide, w_enc_ref.shape[1])], w_enc_ref, load_sems.at[1]
    )
    meet(peers + far)
    chunk = across_ref.shape[1] // groups
    starts = np.cumsum((0,) + cuts).tolist()

    def table_piece(index):
        at = pl.ds(starts[index], cuts[index])
        return Exchange(
            table_blocks(across_ref, chunk, base + starts[index], cuts[index]),
            table_ref.at[:, :, at],
            table_sems.at[index],
            groups,
        )

    outgoing = []

    def put_out(source, target):
        copy = pltpu.make_async_copy(source, target, out_sems.at[len(outgoing)])
        copy.start()
        outgoing.append(copy)

    table_zero = table_piece(0)
    load_first()

    own = qkv_enc_ref.shape[1] // 3
    rows, wide = blocks_ref.shape[1:]
    padded = first_wide - wide
    window = pl.ds(padded, wide)
    copies = []
    for step, (_, peer) in enumerate(peers):
        source = w_first_ref.at[pl.ds(pl.multiple_of(peer * rows, 64), rows), window]
        copies.append(
            send(source, blocks_ref.at[share], block_sems.at[0, step], block_sems.at[1, step], (group, peer))
        )
    keep = pltpu.make_async_copy(
        w_first_ref.at[pl.ds(pl.multiple_of(share * rows, 64), rows), window], blocks_ref.at[share], local_sem
    )
    keep.start()
    turned = jnp.transpose(w_first_ref[:, first_wide - 128 :].astype(jnp.float32))
    norms_ref[...] = turned[64:80]
    enc_total, dec_total = Total(large_one), Total(small_one)
    enc_len, dec_len = place_enc_ref.shape[0], place_dec_ref.shape[0]
    stream = stream_of(looked_ref, 0, place_enc_ref)
    normed, _ = norm_forward(stream, *gain_of(norms_ref, 0))
    qkv_enc_ref[...] = lowered(matmul(lowered(normed), w_first_ref[:, : 3 * own]))
    stream_enc_ref[...] = stream
    head_starts = (0, own, 2 * own)
    logs_enc_ref[...] = jnp.zeros_like(logs_enc_ref)
    heads_forward(qkv_enc_ref, qkv_enc_ref, head_starts, context_enc_ref, logs_enc_ref, False)
    table_one = table_piece(1)
    keep.wait()
    for copy in copies:
        copy.wait()
    for matrix in range(3):
        for piece in range(shares):
            out_rows_ref[matrix, :, piece * own : (piece + 1) * own] = blocks_ref[
                piece, :, matrix * own : (matrix + 1) * own
            ]
    enc_total.begin(matmul(context_enc_ref[...], out_rows_ref[0]))
    stream = stream_of(looked_ref, enc_len, place_dec_ref)
    stream_dec_ref[...] = stream
    normed, _ = norm_forward(stream, *gain_of(norms_ref, 3))
    enc_total.middle()
    dec_start = padded // 2
    qkv_dec_ref[...] = lowered(
        matmul(lowered(normed), w_first_ref[:, dec_start : dec_start + 3 * own])
    )
    logs_dec_ref[...] = jnp.zeros_like(logs_dec_ref)
    heads_forward(qkv_dec_ref, qkv_dec_ref, head_starts, context_dec_ref, logs_dec_ref, True)
    enc_total.last()
    dec_total.begin(matmul(context_dec_ref[...], out_rows_ref[1]))
    dec_total.middle()
    stream_enc_ref[...] += enc_total.finish()
    put_out(stream_enc_ref, stream_enc_hbm)
    dec_total.last()

    total = Total(large_two)
    normed, _ = norm_forward(stream_enc_ref[...], *gain_of(norms_ref, 1))
    hidden, width = pre_enc_ref.shape[1], stream_enc_ref.shape[1]
    load_enc()
    pre_enc_ref[...] = matmul(lowered(normed), w_enc_ref[:, :hidden])
    put_out(pre_enc_ref, pre_enc_hbm)
    activated = lowered(jax.nn.silu(pre_enc_ref[...]))
    total.begin(matmul(activated, w_enc_ref[:, hidden : hidden + width]))
    stream_dec_ref[...] += dec_total.finish()
    stream_two_ref[...] = stream_enc_ref[...] + total.rest()
    put_out(stream_two_ref, stream_two_hbm)
    memory, _ = norm_forward(stream_two_ref[...], *gain_of(norms_ref, 2))
    memory_ref[...] = lowered(memory)
    for piece in (table_zero, table_one):
        piece.finish()
    for copy in outgoing:
        copy.wait()


def dec_kernel(
    groups, start,
    stream_dec_ref, memory_ref, norms_ref, out_rows_ref, positions_ref, w_dec_hbm, across_ref,
    table_ref, q_ref, kv_ref, context_ref, logs_ref, stream_mid_ref, pre_dec_ref, stream_out_ref, selected_ref,
    w_dec_ref, load_sem, table_sems, own_ref, select_sems, *rest,
):
    small_one, small_two = rest[:4], rest[:1] + rest[4:7]
    group, share, core, core_peer, side_peer = places()
    far = group_peers(group, share, groups)
    load_dec = Late(w_dec_hbm, w_dec_ref, load_sem)
    meet([core_peer, side_peer] + far)
    chunk, columns = across_ref.shape[1] // groups, table_ref.shape[2]
    exchange = Exchange(
        table_blocks(across_ref, chunk, start, columns), table_ref, table_sems, groups
    )
    own, hidden = q_ref.shape[1], pre_dec_ref.shape[1]
    dec_len, width = stream_dec_ref.shape
    cross_total, feed_total = Total(small_two), Total(small_one)
    in_start = hidden + width
    normed, _ = norm_forward(stream_dec_ref[...], *gain_of(norms_ref, 4))
    load_dec()
    kv_ref[...] = lowered(
        matmul(memory_ref[...], w_dec_ref[:, in_start + own : in_start + 3 * own])
    )
    q_ref[...] = lowered(matmul(lowered(normed), w_dec_ref[:, in_start : in_start + own]))
    logs_ref[...] = jnp.zeros_like(logs_ref)
    heads_forward(q_ref, kv_ref, (0, 0, own), context_ref, logs_ref, False)
    cross_total.begin(matmul(context_ref[...], out_rows_ref[2]))
    stream_mid_ref[...] = stream_dec_ref[...] + cross_total.rest()
    normed, _ = norm_forward(stream_mid_ref[...], *gain_of(norms_ref, 5))
    pre_dec_ref[...] = matmul(lowered(normed), w_dec_ref[:, :hidden])
    activated = lowered(jax.nn.silu(pre_dec_ref[...]))
    feed_total.begin(matmul(activated, w_dec_ref[:, hidden:in_start]))
    stream_out_ref[...] = stream_mid_ref[...] + feed_total.rest()
    final, _ = norm_forward(stream_out_ref[...], *gain_of(norms_ref, 6))
    places_down = lax.broadcasted_iota(jnp.int32, (own_ref.shape[0], dec_len), 1)
    chosen = lowered(jnp.where(places_down == positions_ref[...], 1.0, 0.0))
    own_ref[...] = lowered(matmul(chosen, lowered(final)))
    selected_ref[group] = own_ref[...]
    copies = [
        send(own_ref, selected_ref.at[group], select_sems.at[0, step], select_sems.at[1, step], peer)
        for step, peer in enumerate(far)
    ]
    exchange.finish()
    for copy in copies:
        copy.wait()


def combine_stats(stats):
    row_max = stats[0][0:1]
    for member in stats[1:]:
        row_max = jnp.maximum(row_max, member[0:1])
    exp_total = smooth = target = 0.0
    for member in stats:
        exp_total = exp_total + member[1:2] * jnp.exp(member[0:1] - row_max)
        smooth = smooth + member[2:3]
        target = target + member[3:4]
    return row_max, exp_total, smooth, target


def head_kernel(
    groups, shares, shard_rows,
    selected_ref, zero_ref, one_ref, two_ref, targets_ref, weights_ref, counted_ref,
    loss_ref, grad_out_ref, head_ref, head_out_ref,
    head_sems, logits_ref, dz_ref, stats_ref, turned_ref, share_stats_ref, group_stats_ref, stat_sems,
    part_ref, core_ref, side_ref, group_ref, sum_ref, sems,
):
    group, share, core, core_peer, side_peer = places()
    side = share // 2
    near, far = share_peers(group, share, shares), group_peers(group, share, groups)
    meet(near + far)
    rows, width = selected_ref.shape
    chunk = logits_ref.shape[1]
    vocab_total = shard_rows * shares
    first = group * chunk
    limit = jnp.minimum(shard_rows - first, vocab_total - 1 - share * shard_rows - first)
    block = 384
    step_rows = 32

    tables = (zero_ref, one_ref, two_ref)
    starts = np.cumsum([0] + [ref.shape[1] for ref in tables]).tolist()
    for ref, start in zip(tables, starts):
        for low in range(0, ref.shape[1], block):
            logits_ref[:, start + low : start + low + block] = matmul(
                selected_ref[...], ref[:, low : low + block]
            )
    stats_ref[...] = jnp.zeros_like(stats_ref)

    def gather_stats(step, carry):
        at = pl.ds(pl.multiple_of(step * step_rows, step_rows), step_rows)
        logits = logits_ref[at, :]
        column = lax.broadcasted_iota(jnp.int32, logits.shape, 1)
        real = column < limit
        masked = jnp.where(real, logits, -1e30)
        top = jnp.max(masked, axis=1, keepdims=True)
        stats_ref[at, 0:1] = top
        stats_ref[at, 1:2] = jnp.sum(jnp.exp(masked - top), axis=1, keepdims=True)
        stats_ref[at, 2:3] = jnp.sum(jnp.where(real, logits, 0.0), axis=1, keepdims=True)
        hit = column == targets_ref[at, :]
        stats_ref[at, 3:4] = jnp.sum(jnp.where(hit, logits, 0.0), axis=1, keepdims=True)
        return carry

    lax.fori_loop(0, rows // step_rows, gather_stats, 0)
    share_stats_ref[share] = jnp.transpose(stats_ref[...])[0:8]
    copies = [
        send(share_stats_ref.at[share], share_stats_ref.at[share], stat_sems.at[0, step], stat_sems.at[1, step], peer)
        for step, peer in enumerate(near)
    ]
    for copy in copies:
        copy.wait()
    merged = combine_stats([share_stats_ref[index] for index in range(shares)])
    group_stats_ref[group] = jnp.concatenate(merged + (jnp.zeros((4, rows), jnp.float32),), axis=0)
    copies = [
        send(group_stats_ref.at[group], group_stats_ref.at[group], stat_sems.at[2, step], stat_sems.at[3, step], peer)
        for step, peer in enumerate(far)
    ]
    for copy in copies:
        copy.wait()
    row_max, exp_total, smooth, target = combine_stats(
        [group_stats_ref[index] for index in range(groups)]
    )
    log_total = row_max + jnp.log(exp_total)
    per_row = log_total - (1.0 - SMOOTH) * target - SMOOTH * smooth / (vocab_total - 1)
    loss = jnp.sum(counted_ref[...] * per_row, axis=1, keepdims=True)
    loss_ref[...] = jnp.broadcast_to(loss, loss_ref.shape)
    turned_ref[...] = jnp.zeros_like(turned_ref)
    turned_ref[0:1, :] = log_total
    stats_ref[...] = jnp.transpose(turned_ref[...])

    def make_dz(step, carry):
        at = pl.ds(pl.multiple_of(step * step_rows, step_rows), step_rows)
        logits = logits_ref[at, :]
        column = lax.broadcasted_iota(jnp.int32, logits.shape, 1)
        softmax_rows = jnp.exp(logits - stats_ref[at, 0:1])
        hit = jnp.where(column == targets_ref[at, :], 1.0 - SMOOTH, 0.0)
        grad = weights_ref[at, :] * (softmax_rows - hit - SMOOTH / (vocab_total - 1))
        dz_ref[at, :] = lowered(jnp.where(column < limit, grad, 0.0))
        return carry

    lax.fori_loop(0, rows // step_rows, make_dz, 0)
    loss_rows = rows // groups
    half, quarter = loss_rows // 2, loss_rows // 4

    def head_part(index):
        at = slice(index * block, (index + 1) * block)
        head_ref[:, at] = lowered(contract_rows(selected_ref[...], dz_ref[:, at]))

    early = head_out_ref.shape[2] // block
    for index in range(early):
        head_part(index)
    width_out = width // groups
    exchange = Exchange(
        lambda index: head_ref.at[
            pl.ds(pl.multiple_of(index * width_out, 16), width_out), pl.ds(0, early * block)
        ],
        head_out_ref,
        head_sems,
        groups,
    )
    grad_rows = 0.0
    for ref, start in zip(tables, starts):
        grad_rows = grad_rows + times_transposed(dz_ref[:, start : start + ref.shape[1]], ref[...])
    part_ref[...] = lowered(grad_rows).reshape(part_ref.shape)
    mine = pl.ds(pl.multiple_of(core * half, 16), half)
    other = pl.ds(pl.multiple_of((1 - core) * half, 16), half)
    copy = send(part_ref.at[:, other, :], core_ref, sems.at[0, 0], sems.at[1, 0], core_peer)
    parts = chunk // block
    middle = (early + parts) // 2
    copy.wait()
    part_ref[:, mine, :] = lowered(
        part_ref[:, mine, :].astype(jnp.float32) + core_ref[...].astype(jnp.float32)
    )
    base = core * half
    my_quarter = pl.ds(pl.multiple_of(base + side * quarter, 16), quarter)
    other_quarter = pl.ds(pl.multiple_of(base + (1 - side) * quarter, 16), quarter)
    copy = send(part_ref.at[:, other_quarter, :], side_ref, sems.at[0, 1], sems.at[1, 1], side_peer)
    for index in range(early, middle):
        head_part(index)
    copy.wait()
    side_ref[...] = lowered(
        part_ref[:, my_quarter, :].astype(jnp.float32) + side_ref[...].astype(jnp.float32)
    )
    group_ref[group] = side_ref[group]
    copies = [
        send(side_ref.at[peer[0]], group_ref.at[group], sems.at[0, 2 + step], sems.at[1, 2 + step], peer)
        for step, peer in enumerate(far)
    ]
    for index in range(middle, parts):
        head_part(index)
    for copy in copies:
        copy.wait()
    summed = group_ref[0].astype(jnp.float32)
    for index in range(1, groups):
        summed = summed + group_ref[index].astype(jnp.float32)
    sum_ref[...] = lowered(summed)
    grad_out_ref[my_quarter, :] = sum_ref[...]
    base_sem = 1 + groups
    copies = [
        send(sum_ref, grad_out_ref.at[my_quarter, :], sems.at[0, base_sem + step], sems.at[1, base_sem + step], peer)
        for step, peer in enumerate(near)
    ]
    for copy in copies:
        copy.wait()
    exchange.finish()


def put_grads(grads_ref, start, value):
    shape = grads_ref.shape[:4] + (value.shape[1],)
    grads_ref[:, :, :, :, start : start + value.shape[1]] = lowered(value).reshape(shape)


def feed_grads(grad_ref, stream_ref, pre_ref, norms_ref, row, w_ref, grads_ref, total):
    width = stream_ref.shape[1]
    hidden = pre_ref.shape[1]
    normed, _ = norm_forward(stream_ref[...], *gain_of(norms_ref, row))
    grad_low = lowered(grad_ref[...])
    pre = pre_ref[...]
    sigmoid_pre = jax.nn.sigmoid(pre)
    grad_pre = lowered(
        times_transposed(grad_low, w_ref[:, hidden : hidden + width])
        * sigmoid_pre
        * (1.0 + pre * (1.0 - sigmoid_pre))
    )
    total.begin(times_transposed(grad_pre, w_ref[:, :hidden]))
    activated = lowered(pre * sigmoid_pre)
    put_grads(grads_ref, hidden, contract_rows(activated, grad_low))
    total.middle()
    put_grads(grads_ref, 0, contract_rows(lowered(normed), grad_pre))


def norm_step(grad_ref, stream_ref, norms_ref, row, summed, rows_ref, slot):
    gain, shift = gain_of(norms_ref, row)
    _, kept = norm_forward(stream_ref[...], gain, shift)
    grad_in, grad_gain, grad_shift = norm_backward(summed, kept, gain)
    rows_ref[slot : slot + 1, :] = grad_gain
    rows_ref[slot + 1 : slot + 2, :] = grad_shift
    if grad_ref is None:
        return grad_in
    return grad_ref[...] + grad_in


def back_kernel(
    groups, shares, first_wide, refs_in, refs_out, *refs
):
    inputs, outputs, scratch = refs[:refs_in], refs[refs_in : refs_in + refs_out], refs[refs_in + refs_out :]
    (
        grad_selected_ref, positions_ref, stream_out_ref, stream_mid_ref, pre_dec_ref, norms_ref, w_dec_hbm,
        out_rows_hbm, memory_hbm, stream_dec_hbm, q_ref, kv_ref, context_cross_ref, logs_cross_ref,
        stream_two_hbm, stream_enc_hbm, pre_enc_hbm, w_early_hbm, looked_hbm, place_enc_hbm, place_dec_ref,
        qkv_dec_ref, context_dec_ref, logs_dec_ref, qkv_enc_ref, context_enc_ref, logs_enc_ref,
        head_in_ref,
    ) = inputs
    head_out_ref, own_tokens_ref, dec_shares_ref, own_ref, squares_ref = outputs
    (
        head_sems, load_sems, w_ref, w_enc_ref, out_rows_ref, memory_ref, stream_dec_ref, stream_two_ref,
        stream_enc_ref, pre_enc_ref, looked_ref,
        dec_grads_ref, mid_grads_ref, last_grads_ref,
        grad_ref, grad_enc_ref,
        context_ref, gq_ref, gkv_ref, gqkv_ref, gqkv_enc_ref, context_enc_grad_ref,
        g_enc_ref, g_self_ref, g_cross_ref, rows_dec_ref, rows_mid_ref, rows_ref,
        norm_rows_ref, block_sems, cut_ref, token_sems, share_sems, dec_sems, dec_own_ref,
        local_sems,
    ) = scratch[:36]
    row_refs = scratch[36:42]
    rest = scratch[42:]
    stream_ref = pre_enc_ref
    small_one, large_one = rest[:4], rest[4:8]
    small_two, large_two = small_one[:1] + rest[8:11], large_one[:1] + rest[11:14]
    dec_line = Owned(dec_grads_ref, rest[14:18])
    mid_line = Owned(mid_grads_ref, rest[18:22])
    last_line = Owned(last_grads_ref, rest[22:26])
    group, share, core, core_peer, side_peer = places()
    peers = share_peers(group, share, shares)
    load_w_dec = Late(w_dec_hbm, w_ref, load_sems.at[0])
    load_rows = Late(out_rows_hbm, out_rows_ref, load_sems.at[1])
    load_memory = Late(memory_hbm, memory_ref, load_sems.at[2])
    load_dec = Late(stream_dec_hbm, stream_dec_ref, load_sems.at[3])
    load_two = Late(stream_two_hbm, stream_two_ref, load_sems.at[4])
    load_enc = Late(stream_enc_hbm, stream_enc_ref, load_sems.at[5])
    load_pre = Late(pre_enc_hbm, pre_enc_ref, load_sems.at[6])
    load_w_enc = Late(
        w_early_hbm.at[:, pl.ds(first_wide, w_enc_ref.shape[1])], w_enc_ref, load_sems.at[7]
    )
    load_looked = Late(looked_hbm, looked_ref, load_sems.at[8])
    meet(peers + group_peers(group, share, groups))
    columns = head_out_ref.shape[2]
    skipped = head_in_ref.shape[2] - columns
    cuts = (0, 3 * columns // 7, 5 * columns // 7, columns)

    def head_piece(index):
        low, wide = cuts[index], cuts[index + 1] - cuts[index]
        return Exchange(
            head_blocks(head_in_ref, skipped + low, wide),
            head_out_ref.at[:, :, pl.ds(low, wide)],
            head_sems.at[index],
            groups,
        )

    pieces = [head_piece(index) for index in range(3)]
    width = stream_out_ref.shape[1]
    own = q_ref.shape[1]
    hidden = pre_dec_ref.shape[1]
    in_start = hidden + width
    starts = (0, own, 2 * own)
    for rows in (rows_dec_ref, rows_mid_ref, rows_ref):
        rows[...] = jnp.zeros_like(rows)

    total = Total(small_one)
    down = lax.broadcasted_iota(jnp.int32, (stream_out_ref.shape[0], grad_selected_ref.shape[0]), 0)
    chosen = lowered(jnp.where(down == positions_ref[...], 1.0, 0.0))
    grad_final = matmul(chosen, grad_selected_ref[...])
    grad_ref[...] = norm_step(None, stream_out_ref, norms_ref, 6, grad_final, rows_dec_ref, 0)
    load_w_dec()
    feed_grads(grad_ref, stream_mid_ref, pre_dec_ref, norms_ref, 5, w_ref, dec_grads_ref, total)
    total.last()
    grad_ref[...] = norm_step(
        grad_ref, stream_mid_ref, norms_ref, 5, total.finish(), rows_dec_ref, 2
    )

    cross_total, memory_total = Total(small_two), Total(large_one)
    grad_low = lowered(grad_ref[...])
    load_rows()
    context_ref[...] = lowered(times_transposed(grad_low, out_rows_ref[2]))
    heads_backward(
        q_ref, kv_ref, (0, 0, own), logs_cross_ref, context_ref, gq_ref, gkv_ref, (0, 0, own), False
    )
    memory_total.begin(
        times_transposed(gkv_ref[...], w_ref[:, in_start + own : in_start + 3 * own])
    )
    cross_total.begin(times_transposed(gq_ref[...], w_ref[:, in_start : in_start + own]))
    load_w_first = Late(
        w_early_hbm.at[:, pl.ds(0, first_wide)], w_ref.at[:, pl.ds(0, first_wide)], load_sems.at[9]
    )
    g_cross_ref[...] = lowered(contract_rows(context_cross_ref[...], grad_low))
    cross_rows = Rows(g_cross_ref, row_refs[0], row_refs[1], block_sems.at[0])
    memory_total.middle()
    cross_total.middle()
    load_dec()
    load_memory()
    normed, _ = norm_forward(stream_dec_ref[...], *gain_of(norms_ref, 4))
    put_grads(dec_grads_ref, in_start, contract_rows(lowered(normed), gq_ref[...]))
    put_grads(dec_grads_ref, in_start + own, contract_rows(memory_ref[...], gkv_ref[...]))
    cross_rows.put(dec_grads_ref, in_start + 3 * own)
    dec_line.begin()
    memory_total.last()
    cross_total.last()
    summed = memory_total.finish()
    load_two()
    grad_enc_ref[...] = norm_step(None, stream_two_ref, norms_ref, 2, summed, rows_mid_ref, 0)
    load_place = Late(place_enc_hbm, stream_two_ref, load_sems.at[10])
    grad_ref[...] = norm_step(
        grad_ref, stream_dec_ref, norms_ref, 4, cross_total.finish(), rows_dec_ref, 4
    )

    feed_total, self_total = Total(large_two), Total(small_one)
    load_enc()
    load_pre()
    load_w_enc()
    feed_grads(
        grad_enc_ref, stream_enc_ref, pre_enc_ref, norms_ref, 1, w_enc_ref, mid_grads_ref, feed_total
    )
    grad_low = lowered(grad_ref[...])
    context_ref[...] = lowered(times_transposed(grad_low, out_rows_ref[1]))
    feed_total.last()
    heads_backward(
        qkv_dec_ref, qkv_dec_ref, starts, logs_dec_ref, context_ref, gqkv_ref, gqkv_ref, starts, True
    )
    load_w_first()
    w_start = first_wide // 3
    self_total.begin(times_transposed(gqkv_ref[...], w_ref[:, w_start : w_start + 3 * own]))
    g_self_ref[...] = lowered(contract_rows(context_dec_ref[...], grad_low))
    self_rows = Rows(g_self_ref, row_refs[2], row_refs[3], block_sems.at[1])
    self_total.middle()
    load_looked()
    enc_len = stream_enc_ref.shape[0]
    stream_dec_ref[...] = stream_of(looked_ref, enc_len, place_dec_ref)
    normed, _ = norm_forward(stream_dec_ref[...], *gain_of(norms_ref, 3))
    put_grads(mid_grads_ref, in_start, contract_rows(lowered(normed), gqkv_ref[...]))
    self_rows.put(mid_grads_ref, in_start + 3 * own)
    mid_line.begin()
    grad_enc_ref[...] = norm_step(
        grad_enc_ref, stream_enc_ref, norms_ref, 1, feed_total.finish(), rows_mid_ref, 2
    )
    self_total.last()
    tokens, part = looked_ref.shape[0], cut_ref.shape[2]
    quarter = tokens // shares
    block_rows = cut_ref.shape[1] // shares

    def put_tokens(first, rows):
        for index in range(groups):
            for piece in range(shares):
                low, high = max(first, piece * quarter), min(first + rows.shape[0], (piece + 1) * quarter)
                if low < high:
                    to = piece * block_rows - piece * quarter
                    cut_ref[index, to + low : to + high] = rows[
                        low - first : high - first, index * part : (index + 1) * part
                    ]

    grad_dec = norm_step(
        grad_ref, stream_dec_ref, norms_ref, 3, self_total.finish(), rows_mid_ref, 4
    )
    put_tokens(enc_len, lowered(grad_dec * math.sqrt(width)))

    total = Total(large_one)
    grad_low = lowered(grad_enc_ref[...])
    g_enc_ref[...] = lowered(contract_rows(context_enc_ref[...], grad_low))
    enc_rows = Rows(g_enc_ref, row_refs[4], row_refs[5], block_sems.at[2])
    context_enc_grad_ref[...] = lowered(times_transposed(grad_low, out_rows_ref[0]))
    heads_backward(
        qkv_enc_ref, qkv_enc_ref, starts, logs_enc_ref, context_enc_grad_ref, gqkv_enc_ref, gqkv_enc_ref, starts,
        False,
    )
    total.begin(times_transposed(gqkv_enc_ref[...], w_ref[:, : 3 * own]))
    load_place()
    stream_ref[...] = stream_of(looked_ref, 0, stream_two_ref)
    normed, _ = norm_forward(stream_ref[...], *gain_of(norms_ref, 0))
    total.middle()
    put_grads(last_grads_ref, 0, contract_rows(lowered(normed), gqkv_enc_ref[...]))
    enc_rows.put(last_grads_ref, 3 * own)
    last_line.begin()
    dec_line.beside()
    total.last()
    grad_enc = norm_step(grad_enc_ref, stream_ref, norms_ref, 0, total.finish(), rows_ref, 0)
    put_tokens(0, lowered(grad_enc * math.sqrt(width)))
    norm_rows_ref[...] = jnp.zeros_like(norm_rows_ref)
    order = (
        (0, rows_ref, 0),
        (1, rows_mid_ref, 2),
        (2, rows_mid_ref, 0),
        (3, rows_mid_ref, 4),
        (4, rows_dec_ref, 4),
        (5, rows_dec_ref, 2),
        (6, rows_dec_ref, 0),
    )
    for row, source, slot in order:
        norm_rows_ref[row : row + 1, :] = source[slot : slot + 1, :]
        norm_rows_ref[7 + row : 8 + row, :] = source[slot + 1 : slot + 2, :]
    norm_low = lowered(norm_rows_ref[...])
    for index in range(groups):
        for piece in range(shares):
            cut_ref[index, piece * block_rows + quarter : (piece + 1) * block_rows] = norm_low[
                :, index * part : (index + 1) * part
            ]
    own_rows = pl.ds(pl.multiple_of(share * block_rows, 16), block_rows)
    to_groups = Exchange(
        lambda index: cut_ref.at[index, own_rows, :], own_tokens_ref.at[share], token_sems, groups
    )
    mid_line.beside()
    dec_line.beyond()
    to_groups.finish()
    token_gather = ShareGather(own_tokens_ref, share_sems)
    last_line.beside()
    mid_line.beyond()
    dec_own_ref[...] = dec_line.finish()
    keep = pltpu.make_async_copy(dec_own_ref, dec_shares_ref.at[share], local_sems.at[2])
    keep.start()
    keep.wait()
    dec_gather = ShareGather(dec_shares_ref, dec_sems)
    token_gather.middle()
    last_line.beyond()
    middle = mid_grads_ref.shape[4]
    own_ref[:, :middle] = mid_line.finish()
    dec_gather.middle()
    token_gather.finish()
    own_ref[:, middle:] = last_line.finish()
    squares = 0.0
    for ref in (dec_own_ref, own_ref):
        value = ref[...].astype(jnp.float32)
        value = value * value
        squares = squares + jnp.sum(jnp.sum(value, axis=0, keepdims=True), axis=1, keepdims=True)
    lane = lax.broadcasted_iota(jnp.int32, squares_ref.shape, 1)
    squares_ref[...] = jnp.where(lane == 0, squares, 0.0)
    dec_gather.finish()
    for piece in pieces:
        piece.finish()


def look_kernel(
    groups,
    picked_ref, piece_ref,
    looked_ref, table_ref,
    send_ref, core_ref, side_ref, group_ref, sems, table_sems,
):
    group, share, core, core_peer, side_peer = places()
    side = share // 2
    far = group_peers(group, share, groups)
    meet([core_peer, side_peer] + far)
    _, tokens, width = picked_ref.shape
    half, quarter = tokens // 2, tokens // 4
    mine = pl.ds(pl.multiple_of(core * half, 16), half)
    other = pl.ds(pl.multiple_of((1 - core) * half, 16), half)
    send(picked_ref.at[:, other, :], core_ref, sems.at[0, 0], sems.at[1, 0], core_peer).wait()
    core_ref[...] = core_ref[...] + picked_ref[:, mine, :]
    own_quarter = pl.ds(pl.multiple_of(side * quarter, 16), quarter)
    other_quarter = pl.ds(pl.multiple_of((1 - side) * quarter, 16), quarter)
    send(core_ref.at[:, other_quarter, :], side_ref, sems.at[0, 1], sems.at[1, 1], side_peer).wait()
    side_ref[...] = side_ref[...] + core_ref[:, own_quarter, :]
    group_ref[group] = side_ref[group]
    copies = [
        send(side_ref.at[peer[0]], group_ref.at[group], sems.at[0, 2 + step], sems.at[1, 2 + step], peer)
        for step, peer in enumerate(far)
    ]
    exchange = Exchange(lambda index: piece_ref.at[index], table_ref, table_sems, groups)
    for copy in copies:
        copy.wait()
    for index in range(groups):
        send_ref[:, index * width : (index + 1) * width] = group_ref[index]
    at = pl.ds(pl.multiple_of(core * half + side * quarter, 16), quarter)
    looked_ref[at, :] = send_ref[...]
    end = 1 + groups
    send(send_ref, looked_ref.at[at, :], sems.at[0, end], sems.at[1, end], side_peer).wait()
    end = end + 1
    both = looked_ref.at[mine, :]
    send(both, both, sems.at[0, end], sems.at[1, end], core_peer).wait()
    exchange.finish()


def squares_kernel(
    groups, shares,
    embedding_ref, dense_ref,
    out_ref,
    share_ref, group_ref, sems,
):
    group, share, _, _, _ = places()
    near, far = share_peers(group, share, shares), group_peers(group, share, groups)
    meet(near + far)
    down = lax.broadcasted_iota(jnp.int32, (8, 128), 0)
    share_ref[share] = jnp.where(down == 0, embedding_ref[...] + dense_ref[...], 0.0)
    copies = [
        send(share_ref.at[share], share_ref.at[share], sems.at[0, step], sems.at[1, step], peer)
        for step, peer in enumerate(near)
    ]
    for copy in copies:
        copy.wait()
    summed = share_ref[0]
    for index in range(1, shares):
        summed = summed + share_ref[index]
    group_ref[group] = summed
    copies = [
        send(group_ref.at[group], group_ref.at[group], sems.at[2, step], sems.at[3, step], peer)
        for step, peer in enumerate(far)
    ]
    for copy in copies:
        copy.wait()
    summed = group_ref[0]
    for index in range(1, groups):
        summed = summed + group_ref[index]
    out_ref[...] = jnp.broadcast_to(jnp.sum(summed), out_ref.shape)


def dense_kernel(
    rate, place_grads, factor_ref, *refs
):
    *grad_refs, w_ref, first_ref, second_ref, new_w_ref, new_first_ref, new_second_ref, wide_ref = refs
    place_grads(wide_ref, *grad_refs)
    updated = adam_update(
        w_ref[0],
        first_ref[0],
        second_ref[0],
        wide_ref[...].astype(jnp.float32),
        factor_ref[0],
        rate,
    )
    for out, value in zip((new_w_ref, new_first_ref, new_second_ref), updated):
        out[0] = value


def dense_update(name, rate, place_grads, factor, grads, w, first, second, parts, cut=None):
    matrices, rows, columns = w.shape
    rows = rows // parts
    own = pl.BlockSpec((1, rows, columns), lambda matrix, part: (matrix, part, 0))
    shares, width = grads[0].shape[:2]
    grad_specs = [
        pl.BlockSpec(
            (shares, width, cut[0] if cut else member.shape[2]),
            lambda matrix, part: (0, 0, cut[1] if cut else 0),
        )
        for member in grads
    ]
    return pl.pallas_call(
        partial(dense_kernel, rate, place_grads),
        grid=(matrices, parts),
        out_shape=[jax.ShapeDtypeStruct(w.shape, w.dtype)] * 3,
        in_specs=[pl.BlockSpec(memory_space=pltpu.SMEM)] + grad_specs + [own] * 3,
        out_specs=[own] * 3,
        scratch_shapes=[pltpu.VMEM((rows, columns), jnp.bfloat16)],
        compiler_params=pltpu.CompilerParams(vmem_limit_bytes=VMEM_BYTES),
        name=name,
    )(factor, *grads, w, first, second)


def place_columns(groups, matrix, source_ref, start):
    def place(wide_ref):
        @pl.when(pl.program_id(0) == matrix)
        def _():
            rows, columns = wide_ref.shape
            shares = source_ref.shape[0]
            piece = columns // groups // shares
            at = pl.ds(pl.multiple_of(pl.program_id(1) * rows, 16), rows)
            for number in range(groups):
                for share in range(shares):
                    low = (number * shares + share) * piece
                    wide_ref[:, low : low + piece] = source_ref[
                        share, at, start + number * piece : start + (number + 1) * piece
                    ]

    return place


def cut_kernel(groups, shares, gap, in_ref, out_ref, up_ref, down_ref, norms_ref, early_ref, dec_ref, square_ref):
    share = lax.axis_index("vocab")
    width, model_width = in_ref.shape[1], out_ref.shape[2]
    own = model_width // shares
    piece = up_ref.shape[2] // groups // shares
    hidden = groups * piece
    in_wide = 3 * own + gap
    early_ref[...] = jnp.zeros_like(early_ref)
    dec_ref[...] = jnp.zeros_like(dec_ref)

    def columns(target, start, source, groups_in, size, index):
        step = shares * size
        for number in range(groups_in):
            low = number * step + index * size
            target[:, start + number * size : start + (number + 1) * size] = lowered(
                source[:, low : low + size]
            )

    def put(index):
        columns(early_ref, 0, in_ref.at[0], 3, own, index)
        columns(early_ref, in_wide, in_ref.at[1], 3, own, index)
        for matrix in range(3):
            columns(early_ref, 2 * in_wide + matrix * own, out_ref.at[matrix], 1, own, index)
        rows = slice(index * (down_ref.shape[1] // shares), (index + 1) * (down_ref.shape[1] // shares))
        for matrix, (target, start) in enumerate(((early_ref, 3 * in_wide), (dec_ref, 0))):
            columns(target, start, up_ref.at[matrix], groups, piece, index)
            start = start + hidden
            target[:, start : start + model_width] = lowered(down_ref[matrix, rows, :])
        columns(dec_ref, hidden + model_width, in_ref.at[2], 3, own, index)

    for index in range(shares):
        pl.when(share == index)(partial(put, index))
    square_ref[...] = jnp.zeros_like(square_ref)
    square_ref[0 : norms_ref.shape[0], 0:width] = norms_ref[...]
    end = 3 * in_wide
    early_ref[:, end - gap : end] = lowered(jnp.transpose(square_ref[...])[0:width, 0:gap])


def cut_weights(groups, shares, gap, inputs, early_wide, dec_wide):
    width = inputs[0].shape[1]
    return pl.pallas_call(
        partial(cut_kernel, groups, shares, gap),
        out_shape=(
            jax.ShapeDtypeStruct((width, early_wide), jnp.bfloat16),
            jax.ShapeDtypeStruct((width, dec_wide), jnp.bfloat16),
        ),
        in_specs=[pl.BlockSpec(memory_space=pltpu.VMEM)] * len(inputs),
        out_specs=(pl.BlockSpec(memory_space=pltpu.VMEM),) * 2,
        scratch_shapes=[pltpu.VMEM((128, 128), jnp.float32)],
        compiler_params=pltpu.CompilerParams(vmem_limit_bytes=VMEM_BYTES),
        name="cut_weights",
    )(*inputs)


def numbers_kernel(
    groups, numbers_ref, hits_ref, all_numbers_ref, all_hits_ref, sems, local_sems
):
    group, share, _, _, _ = places()
    peers = group_peers(group, share, groups)
    meet(peers)
    copies = []
    for number, (source, target) in enumerate(
        ((numbers_ref, all_numbers_ref), (hits_ref, all_hits_ref))
    ):
        copies += [
            send(source, target.at[group], sems.at[number, 0, step], sems.at[number, 1, step], peer)
            for step, peer in enumerate(peers)
        ]
        keep = pltpu.make_async_copy(source, target.at[group], local_sems.at[number])
        keep.start()
        copies.append(keep)
    for copy in copies:
        copy.wait()


def local(
    enc_ids,
    labels,
    target_lengths,
    loss_positions,
    embedding,
    attn_in,
    attn_out,
    ffn_up,
    ffn_down,
    norms,
    embedding_first,
    attn_in_first,
    attn_out_first,
    ffn_up_first,
    ffn_down_first,
    norms_first,
    embedding_second,
    attn_in_second,
    attn_out_second,
    ffn_up_second,
    ffn_down_second,
    norms_second,
):
    groups, shares = lax.axis_size("dp"), lax.axis_size("vocab")
    group, share = lax.axis_index("dp"), lax.axis_index("vocab")
    enc_len, dec_len = enc_ids.shape[1], labels.shape[1]
    loss_count = loss_positions.shape[1]
    shard_rows, part_width = embedding.shape
    model_width = part_width * groups
    vocab_total = shard_rows * shares
    row_start = share * shard_rows
    root_width = math.sqrt(model_width)
    tokens = enc_len + dec_len

    bf16, f32 = jnp.bfloat16, jnp.float32
    sems = pltpu.SemaphoreType.DMA
    numbers = jnp.concatenate(
        [enc_ids, labels, loss_positions, target_lengths[:, None]], axis=1
    )
    number_count = numbers.shape[1]
    number_lanes = -(-number_count // 1024) * 128
    numbers = jnp.pad(numbers, ((0, 0), (0, 8 * number_lanes - number_count)))
    span = 1 << tokens.bit_length()
    own_tokens = jnp.concatenate([enc_ids[0], jnp.zeros((1,), jnp.int32), labels[0, :-1]])
    hits = list_hits(own_tokens - row_start, shard_rows, span)
    own = model_width // shares
    own_in, own_up = 3 * own, ffn_up.shape[2] // shares
    norm_rows = norms.shape[0]
    gap = -own_in % 128
    in_wide = own_in + gap
    dec_wide = own_up + model_width + in_wide
    first_wide = 3 * in_wide
    enc_wide = own_up + model_width
    chunk = -(-shard_rows // (groups * 3072)) * 3072
    table_cuts = (chunk // 8, chunk // 4, chunk // 4, 3 * chunk // 8)
    early_wide = first_wide + enc_wide
    mine_early, mine_dec = cut_weights(
        groups, shares, gap, (attn_in, attn_out, ffn_up, ffn_down, norms), early_wide, dec_wide
    )
    w_early = lax.all_gather(mine_early, "dp", axis=0, tiled=True)
    w_dec = lax.all_gather(mine_dec, "dp", axis=0, tiled=True)
    numbers, hits = call(
        partial(numbers_kernel, groups),
        "numbers",
        1,
        [numbers.reshape(8, number_lanes), hits.reshape(8, span // 8)],
        [
            shape_of((groups, 8, number_lanes), jnp.int32),
            shape_of((groups, 8, span // 8), jnp.int32),
        ],
        [sems((2, 2, groups - 1)), sems((2,))],
        0,
    )
    hits = hits.reshape(groups, span)
    numbers = numbers.reshape(groups, 8 * number_lanes)
    all_labels = numbers[:, enc_len:tokens]
    all_positions = numbers[:, tokens : tokens + loss_count]
    all_lengths = numbers[:, tokens + loss_count : number_count]
    at_place = all_positions[:, :, None] == jnp.arange(dec_len)
    all_targets = jnp.sum(jnp.where(at_place, all_labels[:, None, :], 0), axis=2).reshape(-1)
    all_counted = (all_positions < all_lengths).reshape(-1).astype(f32)
    token_count = jnp.sum(all_counted)

    picked, across, table_zero = pick_rows(
        hits, groups * tokens, embedding.T, groups * chunk, table_cuts[0]
    )
    place_enc = positions_numpy(enc_len, model_width)
    place_dec = positions_numpy(dec_len, model_width)
    enc_macs, dec_macs = enc_len * model_width, dec_len * model_width
    total_enc, total_dec = total_scratch(enc_len, model_width), total_scratch(dec_len, model_width)
    block_shape = (2, 2, 2, part_width)
    looked, table_zero = call(
        partial(look_kernel, groups),
        "look",
        2,
        [picked.reshape(groups, tokens, part_width), table_zero],
        [
            shape_of((tokens, model_width), bf16),
            shape_of((groups, part_width, table_cuts[0]), bf16),
        ],
        [
            pltpu.VMEM((tokens // 4, model_width), bf16),
            pltpu.VMEM((groups, tokens // 2, part_width), bf16),
            pltpu.VMEM((groups, tokens // 4, part_width), bf16),
            pltpu.VMEM((groups, tokens // 4, part_width), bf16),
            sems((2, groups + 3)),
            sems((2, groups)),
        ],
        0,
        (1,),
        (1,),
    )
    forward_inputs = [looked, place_enc, place_dec, w_early, across]
    forward_outputs = [
        shape_of((groups, part_width, sum(table_cuts[1:3])), bf16),
        shape_of((3, own, model_width), bf16),
        shape_of((16, model_width), f32),
        shape_of((enc_len, 3 * own), bf16),
        shape_of((enc_len, own), bf16),
        shape_of((enc_len, 128), f32),
        shape_of((enc_len, model_width), f32),
        shape_of((enc_len, own_up), f32),
        shape_of((enc_len, model_width), f32),
        shape_of((enc_len, model_width), bf16),
        shape_of((dec_len, 3 * own), bf16),
        shape_of((dec_len, own), bf16),
        shape_of((dec_len, 128), f32),
        shape_of((dec_len, model_width), f32),
    ]
    (
        table_one, out_rows, norm_values,
        qkv_enc, context_enc, logs_enc, stream_enc, pre_enc, stream_two, memory,
        qkv_dec, context_dec, logs_dec, stream_dec,
    ) = call(
        partial(
            forward_kernel, groups, shares, table_cuts[0], table_cuts[1:3], len(forward_inputs),
            len(forward_outputs),
        ),
        "forward",
        3,
        forward_inputs,
        forward_outputs,
        [
            sems((2, 2, groups)),
            sems((3,)),
            sems((2,)),
            pltpu.VMEM((model_width, first_wide), bf16),
            pltpu.VMEM((model_width, enc_wide), bf16),
            pltpu.VMEM((enc_len, model_width), f32),
            pltpu.VMEM((enc_len, own_up), f32),
            pltpu.VMEM((enc_len, model_width), f32),
            pltpu.VMEM((shares, own, in_wide), bf16),
            sems((2, shares - 1)),
            sems,
            *total_dec,
            *total_enc,
            *total_enc[1:],
        ],
        8 * enc_macs * own_up,
        (3, 4),
        (0, 6, 7, 8),
    )
    (
        table_two, q_cross, kv_cross, context_cross, logs_cross, stream_mid, pre_dec, stream_out, selected,
    ) = call(
        partial(dec_kernel, groups, sum(table_cuts[:3])),
        "dec",
        4,
        [
            stream_dec, memory, norm_values, out_rows, loss_positions.reshape(-1, 1), w_dec, across,
        ],
        [
            shape_of((groups, part_width, table_cuts[3]), bf16),
            shape_of((dec_len, own), bf16),
            shape_of((enc_len, 2 * own), bf16),
            shape_of((dec_len, own), bf16),
            shape_of((dec_len, 128), f32),
            shape_of((dec_len, model_width), f32),
            shape_of((dec_len, own_up), f32),
            shape_of((dec_len, model_width), f32),
            shape_of((groups, loss_count, model_width), bf16),
        ],
        [
            pltpu.VMEM((model_width, dec_wide), bf16),
            sems,
            sems((2, groups)),
            pltpu.VMEM((loss_count, model_width), bf16),
            sems((2, groups - 1)),
            *total_dec,
            *total_dec[1:],
        ],
        8 * dec_macs * own_up,
        (5, 6),
        (0,),
    )

    rows_all = groups * loss_count
    first_row = row_start + group * chunk
    targets = all_targets - first_row
    inside = (targets >= 0) & (targets < jnp.minimum(chunk, shard_rows - group * chunk))
    targets = jnp.where(inside, targets, -1)[:, None]
    head_cut = chunk // 8
    loss, grad_selected, head_grad, head_zero = call(
        partial(head_kernel, groups, shares, shard_rows),
        "head",
        6,
        [
            selected.reshape(rows_all, model_width),
            table_zero.reshape(model_width, -1),
            table_one.reshape(model_width, -1),
            table_two.reshape(model_width, -1),
            targets,
            (all_counted / token_count)[:, None],
            all_counted[None, :],
        ],
        [
            shape_of((1, 128), f32),
            shape_of((loss_count, model_width), bf16),
            shape_of((model_width, chunk), bf16),
            shape_of((groups, part_width, head_cut), bf16),
        ],
        [
            sems((2, groups)),
            pltpu.VMEM((rows_all, chunk), f32),
            pltpu.VMEM((rows_all, chunk), bf16),
            pltpu.VMEM((rows_all, 128), f32),
            pltpu.VMEM((128, rows_all), f32),
            pltpu.VMEM((shares, 8, rows_all), f32),
            pltpu.VMEM((groups, 8, rows_all), f32),
            sems((4, max(groups, shares))),
            pltpu.VMEM((groups, loss_count, model_width), bf16),
            pltpu.VMEM((groups, loss_count // 2, model_width), bf16),
            pltpu.VMEM((groups, loss_count // 4, model_width), bf16),
            pltpu.VMEM((groups, loss_count // 4, model_width), bf16),
            pltpu.VMEM((loss_count // 4, model_width), bf16),
            sems((2, groups + shares)),
        ],
        6 * rows_all * chunk * model_width,
        (),
        (3,),
    )
    loss_sum = loss[0, 0]
    head_grad = head_grad.reshape(groups, part_width, chunk)
    last_wide = own_in + own
    back_wide = own_up + model_width + last_wide
    late_wide = back_wide + last_wide
    quarter = tokens // shares
    back_inputs = [
        grad_selected, loss_positions.reshape(1, -1), stream_out, stream_mid, pre_dec, norm_values, w_dec,
        out_rows, memory, stream_dec, q_cross, kv_cross, context_cross, logs_cross,
        stream_two, stream_enc, pre_enc, w_early, looked, place_enc, place_dec,
        qkv_dec, context_dec, logs_dec, qkv_enc, context_enc, logs_enc,
        head_grad,
    ]

    head_one, grad_tokens, dec_shares, late_own, dense_squares = call(
        partial(
            back_kernel, groups, shares, first_wide, len(back_inputs), 5
        ),
        "backward",
        7,
        back_inputs,
        [
            shape_of((groups, part_width, chunk - head_cut), bf16),
            shape_of((shares, groups, quarter + 16, part_width), bf16),
            shape_of((shares, part_width, back_wide), bf16),
            shape_of((part_width, late_wide), bf16),
            shape_of((1, 128), f32),
        ],
        [
            sems((3, 2, groups)),
            sems((11,)),
            pltpu.VMEM((model_width, dec_wide), bf16),
            pltpu.VMEM((model_width, own_up + model_width), bf16),
            pltpu.VMEM(out_rows.shape, bf16),
            pltpu.VMEM((enc_len, model_width), bf16),
            pltpu.VMEM((dec_len, model_width), f32),
            pltpu.VMEM((enc_len, model_width), f32),
            pltpu.VMEM((enc_len, model_width), f32),
            pltpu.VMEM((enc_len, own_up), f32),
            pltpu.VMEM((tokens, model_width), bf16),
            pltpu.VMEM(block_shape + (back_wide,), bf16),
            pltpu.VMEM(block_shape + (back_wide,), bf16),
            pltpu.VMEM(block_shape + (last_wide,), bf16),
            pltpu.VMEM((dec_len, model_width), f32),
            pltpu.VMEM((enc_len, model_width), f32),
            pltpu.VMEM((dec_len, own), bf16),
            pltpu.VMEM((dec_len, own), bf16),
            pltpu.VMEM((enc_len, 2 * own), bf16),
            pltpu.VMEM((dec_len, 3 * own), bf16),
            pltpu.VMEM((enc_len, 3 * own), bf16),
            pltpu.VMEM((enc_len, own), bf16),
            pltpu.VMEM((own, model_width), bf16),
            pltpu.VMEM((own, model_width), bf16),
            pltpu.VMEM((own, model_width), bf16),
            pltpu.VMEM((8, model_width), f32),
            pltpu.VMEM((8, model_width), f32),
            pltpu.VMEM((8, model_width), f32),
            pltpu.VMEM((16, model_width), f32),
            sems((3, 2, shares)),
            pltpu.VMEM((groups, tokens + 16 * shares, part_width), bf16),
            sems((2, groups)),
            sems((2, 3)),
            sems((2, 3)),
            pltpu.VMEM((part_width, back_wide), bf16),
            sems((3,)),
            *[pltpu.VMEM((shares, own, own), bf16)] * 6,
            *total_dec,
            *total_enc,
            *total_dec[1:],
            *total_enc[1:],
            *line_scratch(part_width, back_wide),
            *line_scratch(part_width, back_wide),
            *line_scratch(part_width, last_wide),
        ],
        16 * (enc_macs + dec_macs) * own_up,
        (6, 7, 8, 9, 14, 15, 16, 17, 18, 19, 27),
        (0, 1, 2),
    )
    late_shares = lax.all_gather(late_own, "vocab", axis=0, tiled=False)
    g_embedding, embedding_squares = spread_rows(
        hits, groups * tokens, grad_tokens, (head_zero, head_one)
    )
    g_embedding = g_embedding[:, :shard_rows].astype(f32).T
    g_norms = jnp.sum(grad_tokens[0, :, quarter : quarter + norm_rows].astype(f32), axis=0)
    dense_squares = dense_squares + jnp.sum(g_norms * g_norms) / (shares * dense_squares.shape[1])
    (squares,) = call(
        partial(squares_kernel, groups, shares),
        "squares",
        10,
        [embedding_squares, dense_squares],
        [shape_of((1, 128), f32)],
        [
            pltpu.VMEM((shares, 8, 128), f32),
            pltpu.VMEM((groups, 8, 128), f32),
            sems((4, max(groups, shares))),
        ],
        0,
    )
    grad_norm = jnp.sqrt(squares[0, 0])
    factor = jnp.minimum(1.0, CLIP / (grad_norm + 1e-06))
    grad_pair = [late_shares, dec_shares]
    in_start, late_in = own_up + model_width, back_wide

    def place_in(wide_ref, late_ref, dec_ref):
        place_columns(3, 0, late_ref, late_in)(wide_ref)
        place_columns(3, 1, late_ref, in_start)(wide_ref)
        place_columns(3, 2, dec_ref, in_start)(wide_ref)

    def place_out(wide_ref, late_ref, dec_ref):
        place_columns(1, 0, late_ref, late_in + own_in)(wide_ref)
        place_columns(1, 1, late_ref, in_start + own_in)(wide_ref)
        place_columns(1, 2, dec_ref, in_start + own_in)(wide_ref)

    def place_up(wide_ref, late_ref, dec_ref):
        place_columns(groups, 0, late_ref, 0)(wide_ref)
        place_columns(groups, 1, dec_ref, 0)(wide_ref)

    down_rows = ffn_down.shape[1] // shares

    def place_down(wide_ref, late_ref, dec_ref):
        for matrix, ref in enumerate((late_ref, dec_ref)):

            @pl.when(pl.program_id(0) == matrix)
            def _(ref=ref):
                for piece in range(shares):
                    wide_ref[piece * down_rows : (piece + 1) * down_rows] = ref[piece]

    scale = factor.reshape(1)
    new_in = dense_update(
        "adam_in", RATES[1], place_in, scale, grad_pair, attn_in, attn_in_first, attn_in_second, 2
    )
    new_out = dense_update(
        "adam_out", RATES[2], place_out, scale, grad_pair, attn_out, attn_out_first, attn_out_second, 1
    )
    new_up = dense_update(
        "adam_up", RATES[3], place_up, scale, grad_pair, ffn_up, ffn_up_first, ffn_up_second, 2,
        (own_up, 0),
    )
    new_down = dense_update(
        "adam_down", RATES[4], place_down, scale, grad_pair, ffn_down, ffn_down_first, ffn_down_second, 1,
        (model_width, 1),
    )
    new_embedding = adam_update(
        embedding, embedding_first, embedding_second, g_embedding, factor, RATES[0]
    )
    new_norms = adam_update(norms, norms_first, norms_second, g_norms, factor, RATES[5])
    updated = (new_embedding, new_in, new_out, new_up, new_down, new_norms)
    return (loss_sum, token_count, grad_norm) + tuple(
        updated[slot][kind] for kind in range(3) for slot in range(6)
    )


def splits_evenly(mesh):
    return HEADS % mesh.shape["vocab"] == 0 and mesh.shape["dp"] == 8


def solution(mesh):
    placed = (
        P("dp", None),
        P("dp", None),
        P("dp"),
        P("dp", None),
        P("vocab", "dp"),
        P(None, "dp", None),
        P(None, "dp", None),
        P(None, "dp", None),
        P(None, "dp", None),
        P(None, "dp"),
        P("vocab", "dp"),
        P(None, "dp", None),
        P(None, "dp", None),
        P(None, "dp", None),
        P(None, "dp", None),
        P(None, "dp"),
        P("vocab", "dp"),
        P(None, "dp", None),
        P(None, "dp", None),
        P(None, "dp", None),
        P(None, "dp", None),
        P(None, "dp"),
    )
    return jax.shard_map(
        local if splits_evenly(mesh) else local_copied,
        mesh=mesh,
        in_specs=placed,
        out_specs=(
            P(),
            P(),
            P(),
            P("vocab", "dp"),
            P(None, "dp", None),
            P(None, "dp", None),
            P(None, "dp", None),
            P(None, "dp", None),
            P(None, "dp"),
            P("vocab", "dp"),
            P(None, "dp", None),
            P(None, "dp", None),
            P(None, "dp", None),
            P(None, "dp", None),
            P(None, "dp"),
            P("vocab", "dp"),
            P(None, "dp", None),
            P(None, "dp", None),
            P(None, "dp", None),
            P(None, "dp", None),
            P(None, "dp"),
        ),
        check_vma=False,
    )
```
